32 devices in a mesh: dp: 4 (over z), seq: 8 (over y, x, core).
Axes of the slice: x: 2, y: 2, z: 4, core: 2. Of those that a mesh axis runs over, the one named last changes fastest.
Arguments:
- enc_input: bfloat16 [8, 512, 768], P('dp', 'seq'), may hold values from -6 to 6
- dec_input: bfloat16 [8, 512, 768], P('dp', 'seq'), may hold values from -6 to 6
- enc_lengths: int32 [8], P('dp'), may hold values from 128 to 512, as said below
- dec_lengths: int32 [8], P('dp'), may hold values from 128 to 512, as said below
- enc_buckets: int32 [1023], replicated, may hold values from 0 to 31
- dec_buckets: int32 [512], replicated, may hold values from 0 to 31
- attention_in: bfloat16 [3, 3, 768, 768], P(None, None, ('dp', 'seq')), may hold values from -0.21875 to 0.21875
- attention_out: bfloat16 [3, 768, 768], P(None, ('dp', 'seq')), may hold values from -0.875 to 0.875
- hidden_in: bfloat16 [2, 2, 768, 2048], P(None, None, ('dp', 'seq')), may hold values from -0.21875 to 0.21875
- hidden_out: bfloat16 [2, 2048, 768], P(None, ('dp', 'seq')), may hold values from -0.25 to 0.25
- norm_gains: bfloat16 [7, 768], P(None, ('dp', 'seq')), may hold values from 0.5 to 1.5
- position_bias: float32 [2, 32, 12], replicated, may hold values from -4 to 4
- enc_cotangent: bfloat16 [8, 512, 768], P('dp', 'seq'), may hold values from -6 to 6
- dec_cotangent: bfloat16 [8, 512, 768], P('dp', 'seq'), may hold values from -6 to 6
Outputs:
- enc_output: bfloat16 [8, 512, 768], P('dp', 'seq')
- dec_output: bfloat16 [8, 512, 768], P('dp', 'seq')
- grad_enc_input: float32 [8, 512, 768], P('dp', 'seq')
- grad_dec_input: float32 [8, 512, 768], P('dp', 'seq')
- grad_attention_in: float32 [3, 3, 768, 768], P(None, None, ('dp', 'seq'))
- grad_attention_out: float32 [3, 768, 768], P(None, ('dp', 'seq'))
- grad_hidden_in: float32 [2, 2, 768, 2048], P(None, None, ('dp', 'seq'))
- grad_hidden_out: float32 [2, 2048, 768], P(None, ('dp', 'seq'))
- grad_norm_gains: float32 [7, 768], P(None, ('dp', 'seq'))
- grad_position_bias: float32 [2, 32, 12], replicated
- row_attention_in: float32 [3, 3, 768], P(None, None, ('dp', 'seq'))
- col_attention_in: float32 [3, 3, 768], replicated
- row_attention_out: float32 [3, 768], P(None, ('dp', 'seq'))
- col_attention_out: float32 [3, 768], replicated
- row_hidden_in: float32 [2, 2, 768], P(None, None, ('dp', 'seq'))
- col_hidden_in: float32 [2, 2, 2048], replicated
- row_hidden_out: float32 [2, 2048], P(None, ('dp', 'seq'))
- col_hidden_out: float32 [2, 768], replicated
The draws below stay inside these ranges and needn't reach their ends.
Inputs may be any that keep to these rules, and one draw needn't show every extreme that they name: `enc_lengths`: among the 2 sequences of one dp index at least one has all 512 valid tokens. `dec_lengths`: among the 2 sequences of one dp index at least one has all 512 valid tokens.
All inputs are finite; a program needn't handle non-finite values.
Results may differ from the reference program's by a relative error of at most 0.04.
Values may be sent and summed in bfloat16 or wider, within the bound.
No kernel may reach another device: no remote copies, remote signals or barrier semaphores. Data moves between devices by JAX's collectives and lax.ppermute only.
A program may use at most 384 MiB of HBM per device.

```python
import math
import jax
import jax.numpy as jnp
from jax import lax

D = 768
HEADS = 12
HEAD = 64
FF = 2048
BUCKETS = 32
SEQS = 2
BATCH = 8
LEN_ENC = 512
LEN_DEC = 512


def ragged_lengths(key, longest):
    first_key, second_key, third_key = jax.random.split(key, 3)
    groups = BATCH // SEQS
    drawn = jax.random.randint(first_key, (BATCH,), longest // 4, longest + 1)
    chosen = jax.random.randint(second_key, (groups,), 0, SEQS)
    short_group = jax.random.randint(third_key, (), 0, groups)
    slot_ids = jnp.arange(BATCH) % SEQS
    group_ids = jnp.arange(BATCH) // SEQS
    full_row = slot_ids == jnp.repeat(chosen, SEQS)
    short_row = (group_ids == short_group) & (slot_ids == jnp.repeat((chosen + 1) % SEQS, SEQS))
    shortest = jnp.full((BATCH,), longest // 4)
    return jnp.where(full_row, longest, jnp.where(short_row, shortest, drawn)).astype(jnp.int32)


def draw_enc_lengths(key, part):
    return ragged_lengths(jax.random.fold_in(key, 11), LEN_ENC)


def draw_dec_lengths(key, part):
    return ragged_lengths(jax.random.fold_in(key, 23), LEN_DEC)


def plant(entries, stream_key, smallest, high):
    longest = entries.shape.index(max(entries.shape))
    spots = []
    for shift in (0, 1):
        where = [jax.random.randint(jax.random.fold_in(stream_key, axis), (), 0, length) for axis, length in enumerate(entries.shape)]
        where[longest] = (where[longest] + shift) % entries.shape[longest]
        spots.append(tuple(where))
    return entries.at[spots[0]].set(smallest).at[spots[1]].set(high)


def shard_levels(rng, shape, pieces, low, high):
    loudness, own = 1.0, jax.random.fold_in(rng, 6)
    for dim, blocks in pieces:
        steps = jnp.exp(jax.random.uniform(jax.random.fold_in(own, dim), (blocks,), jnp.float32, low / len(pieces), high / len(pieces)))
        loudness = loudness * jnp.repeat(steps, shape[dim] // blocks).reshape([-1 if axis == dim else 1 for axis in range(len(shape))])
    return loudness


def noise(key, extent, spread, bound, cuts=(), held_as=jnp.bfloat16):
    values = spread * jax.random.normal(key, extent, jnp.float32)
    if cuts:
        values = values * shard_levels(key, extent, cuts, -0.22, 0.18)
    return jnp.clip(values, -bound, bound).astype(held_as)


def setup_inputs(seed: int = 0) -> dict:
    keys = jax.random.split(jax.random.key(seed), 15)
    enc_input = noise(keys[0], (BATCH, LEN_ENC, D), 1.0, 6.0, ((0, 4), (1, 8)))
    dec_input = noise(keys[1], (BATCH, LEN_DEC, D), 1.0, 6.0, ((0, 4), (1, 8)))
    enc_lengths = draw_enc_lengths(jax.random.fold_in(keys[14], 71), 0)
    dec_lengths = draw_dec_lengths(jax.random.fold_in(keys[14], 71), 0)
    enc_buckets = plant(jax.random.randint(keys[4], (2 * LEN_ENC - 1,), 0, BUCKETS), jax.random.fold_in(keys[4], 1), 0, BUCKETS - 1).astype(jnp.int32)
    dec_buckets = plant(jax.random.randint(keys[5], (LEN_DEC,), 0, BUCKETS), jax.random.fold_in(keys[5], 1), 0, BUCKETS - 1).astype(jnp.int32)
    attention_in = noise(keys[6], (3, 3, D, D), D ** -0.5, 0.21875, ((2, 32),))
    attention_out = noise(keys[7], (3, D, D), (D // 16) ** -0.5, 0.875, ((1, 32),))
    hidden_in = noise(keys[8], (2, 2, D, FF), D ** -0.5, 0.21875, ((2, 32),))
    hidden_out = noise(keys[9], (2, FF, D), (FF // 4) ** -0.5, 0.25, ((1, 32),))
    norm_gains = jnp.clip(1.0 + 0.1 * jax.random.normal(keys[10], (7, D), jnp.float32), 0.5, 1.5).astype(jnp.bfloat16)
    position_bias = noise(keys[11], (2, BUCKETS, HEADS), 1.0, 4.0, (), jnp.float32)
    enc_cotangent = noise(keys[12], (BATCH, LEN_ENC, D), 1.0, 6.0, ((0, 4), (1, 8)))
    dec_cotangent = noise(keys[13], (BATCH, LEN_DEC, D), 1.0, 6.0, ((0, 4), (1, 8)))
    return dict(enc_input=enc_input, dec_input=dec_input, enc_lengths=enc_lengths, dec_lengths=dec_lengths, enc_buckets=enc_buckets, dec_buckets=dec_buckets, attention_in=attention_in, attention_out=attention_out, hidden_in=hidden_in, hidden_out=hidden_out, norm_gains=norm_gains, position_bias=position_bias, enc_cotangent=enc_cotangent, dec_cotangent=dec_cotangent)


@jax.custom_vjp
def low(v):
    return lax.optimization_barrier(v.astype(jnp.bfloat16)).astype(jnp.float32)

@jax.custom_vjp
def low_back(v):
    return v

def low_keep(v):
    return (low(v), None)

def low_pass(kept, grad):
    return (grad,)

def back_keep(v):
    return (v, None)

def back_low(kept, grad):
    return (low(grad),)
low.defvjp(low_keep, low_pass)
low_back.defvjp(back_keep, back_low)
EPSILON = 1e-06
NEGATIVE = -1e+30
HIGHEST = lax.Precision.HIGHEST

def rms_norm(values, gain_row):
    return values * lax.rsqrt(lax.optimization_barrier(jnp.mean(values * values, axis=-1, keepdims=True)) + EPSILON) * gain_row

def project(values, weights):
    return jnp.dot(values, weights, precision=HIGHEST, preferred_element_type=jnp.float32)

def heads_of(normed, weights):
    return low(low_back(project(normed, weights)))

def attention(queries, key_rows, value_rows, visible_fn, bias_fn):
    length = queries.shape[0]
    block_len = math.gcd(length, 512)
    key_count = key_rows.shape[0]
    key_heads = key_rows.reshape(key_count, HEADS, HEAD)
    value_heads = value_rows.reshape(key_count, HEADS, HEAD)
    col_ids = jnp.arange(key_count, dtype=jnp.int32)
    factor = HEAD ** (-0.5)

    def one_block(inputs):
        query_block, first_row = inputs
        row_ids = first_row + jnp.arange(block_len, dtype=jnp.int32)
        raw_scores = jnp.einsum('qhe,khe->hqk', query_block, key_heads, precision=HIGHEST)
        scores = low_back(raw_scores) * factor + bias_fn(row_ids, col_ids)
        scores = jnp.where(visible_fn(row_ids, col_ids)[None], scores, NEGATIVE)
        row_max = lax.optimization_barrier(jnp.max(scores, axis=-1, keepdims=True))
        expo = jnp.exp(scores - row_max)
        weights = expo / lax.optimization_barrier(jnp.sum(expo, axis=-1, keepdims=True))
        return jnp.einsum('hqk,khe->qhe', low(weights), value_heads, precision=HIGHEST)
    query_blocks = queries.reshape(length // block_len, block_len, HEADS, HEAD)
    firsts = jnp.arange(length // block_len, dtype=jnp.int32) * block_len
    context = lax.map(jax.checkpoint(one_block), (query_blocks, firsts))
    return low(low_back(context.reshape(length, HEADS * HEAD)))

def feed_forward(residual, gain_row, weights_in, weights_out):
    normed = low(rms_norm(residual, gain_row))
    gate = low_back(project(normed, weights_in[0]))
    upper = low_back(project(normed, weights_in[1]))
    hidden = low(jax.nn.gelu(gate, approximate=True) * upper)
    return residual + low_back(project(hidden, weights_out))

def forward(params, enc_values, dec_values, enc_length, dec_length, enc_buckets, dec_buckets):
    attention_in, attention_out, hidden_in, hidden_out, norm_gains, position_bias = params
    enc_table = jnp.take(position_bias[0], enc_buckets, axis=0).T
    dec_table = jnp.take(position_bias[1], dec_buckets, axis=0).T

    def enc_bias(row_ids, col_ids):
        return jnp.take(enc_table, col_ids[None, :] - row_ids[:, None] + (LEN_ENC - 1), axis=1)

    def dec_bias(row_ids, col_ids):
        return jnp.take(dec_table, jnp.clip(row_ids[:, None] - col_ids[None, :], 0, LEN_DEC - 1), axis=1)

    def no_bias(row_ids, col_ids):
        return jnp.zeros((), jnp.float32)

    def enc_visible(row_ids, col_ids):
        return jnp.broadcast_to(col_ids[None, :] < enc_length, (row_ids.shape[0], col_ids.shape[0]))

    def dec_visible(row_ids, col_ids):
        return (col_ids[None, :] < dec_length) & (col_ids[None, :] <= row_ids[:, None])
    normed = low(rms_norm(enc_values, norm_gains[0]))
    queries = heads_of(normed, attention_in[0, 0])
    key_rows = heads_of(normed, attention_in[0, 1])
    value_rows = heads_of(normed, attention_in[0, 2])
    context = attention(queries, key_rows, value_rows, enc_visible, enc_bias)
    enc_mid = enc_values + low_back(project(context, attention_out[0]))
    enc_last = feed_forward(enc_mid, norm_gains[1], hidden_in[0], hidden_out[0])
    memory = rms_norm(enc_last, norm_gains[2])
    memory_low = low(memory)
    normed = low(rms_norm(dec_values, norm_gains[3]))
    queries = heads_of(normed, attention_in[1, 0])
    key_rows = heads_of(normed, attention_in[1, 1])
    value_rows = heads_of(normed, attention_in[1, 2])
    context = attention(queries, key_rows, value_rows, dec_visible, dec_bias)
    dec_mid = dec_values + low_back(project(context, attention_out[1]))
    normed = low(rms_norm(dec_mid, norm_gains[4]))
    queries = heads_of(normed, attention_in[2, 0])
    key_rows = heads_of(memory_low, attention_in[2, 1])
    value_rows = heads_of(memory_low, attention_in[2, 2])
    context = attention(queries, key_rows, value_rows, enc_visible, no_bias)
    dec_cross = dec_mid + low_back(project(context, attention_out[2]))
    dec_last = feed_forward(dec_cross, norm_gains[5], hidden_in[1], hidden_out[1])
    return (memory, rms_norm(dec_last, norm_gains[6]))

def moments(grad_matrix):
    squares = grad_matrix * grad_matrix
    return (0.5 * lax.optimization_barrier(jnp.mean(squares, axis=-1)), 0.5 * lax.optimization_barrier(jnp.mean(squares, axis=-2)))

def reference(enc_input, dec_input, enc_lengths, dec_lengths, enc_buckets, dec_buckets, attention_in, attention_out, hidden_in, hidden_out, norm_gains, position_bias, enc_cotangent, dec_cotangent):
    params = (attention_in.astype(jnp.float32), attention_out.astype(jnp.float32), hidden_in.astype(jnp.float32), hidden_out.astype(jnp.float32), norm_gains.astype(jnp.float32), position_bias.astype(jnp.float32))

    def per_sequence(totals, inputs):
        enc_seq, dec_seq, enc_cot, dec_cot, enc_length, dec_length = inputs

        def run_layers(weights, enc_values, dec_values):
            return forward(weights, enc_values, dec_values, enc_length, dec_length, enc_buckets, dec_buckets)
        outputs, pullback = jax.vjp(run_layers, params, enc_seq.astype(jnp.float32), dec_seq.astype(jnp.float32))
        grad_params, grad_enc, grad_dec = pullback((enc_cot.astype(jnp.float32), dec_cot.astype(jnp.float32)))
        totals = jax.tree.map(lambda summed, added: summed + added, totals, grad_params)
        return (totals, (outputs[0].astype(jnp.bfloat16), outputs[1].astype(jnp.bfloat16), grad_enc, grad_dec))
    zero_grads = jax.tree.map(jnp.zeros_like, params)
    totals, stacked = lax.scan(per_sequence, zero_grads, (enc_input, dec_input, enc_cotangent, dec_cotangent, enc_lengths, dec_lengths))
    enc_output, dec_output, grad_enc_input, grad_dec_input = stacked
    grad_in, grad_out, grad_hin, grad_hout, grad_gains, grad_position = totals
    row_in, col_in = moments(grad_in)
    row_out, col_out = moments(grad_out)
    row_hin, col_hin = moments(grad_hin)
    row_hout, col_hout = moments(grad_hout)
    return (enc_output, dec_output, grad_enc_input, grad_dec_input, grad_in, grad_out, grad_hin, grad_hout, grad_gains, grad_position, row_in, col_in, row_out, col_out, row_hin, col_hin, row_hout, col_hout)
```

```python
import functools
import math

import jax
import jax.numpy as jnp
from jax import lax
from jax.experimental import pallas as pl
from jax.experimental.pallas import tpu as pltpu
from jax.sharding import PartitionSpec as P

D = 768
HEADS = 12
HEAD = 64
FF = 2048


EPSILON = 1e-06
NEGATIVE = -1e30
HIGHEST = lax.Precision.HIGHEST


def rounded(values):
    return values.astype(jnp.bfloat16)


def rows_first(values):
    return values.transpose(0, 2, 1)


def rms_norm(values, gain_row):
    return (
        values * lax.rsqrt(jnp.mean(values * values, axis=-1, keepdims=True) + EPSILON) * gain_row
    )


def rms_back(values, gain_row, upstream):
    _, pullback = jax.vjp(rms_norm, values, gain_row)
    return pullback(upstream)


def gated_unit(gate_up):
    return jax.nn.gelu(gate_up[0], approximate=True) * gate_up[1]


def offset_table(buckets, layer_bias):
    choose = (buckets[:, None] == jnp.arange(layer_bias.shape[0], dtype=jnp.int32)[None, :]).astype(
        jnp.float32
    )
    return jnp.dot(choose, layer_bias, precision=HIGHEST).T


def bucket_grad(buckets, grad_bias, bucket_count):
    choose = (buckets[:, None] == jnp.arange(bucket_count, dtype=jnp.int32)[None, :]).astype(
        jnp.float32
    )
    return jnp.dot(choose.T, grad_bias.T, precision=HIGHEST)


def hankel_block(window, rows, cols):
    heads_here, length = (window.shape[0], window.shape[1])
    tiled = jnp.tile(window, (1, rows + 1))[:, : rows * (length + 1)]
    return tiled.reshape(heads_here, rows, length + 1)[:, :, :cols]


def bias_block(variant, table, row_start, col_start, rows, cols, extent):
    span = rows + cols - 1
    if variant == "enc":
        base = col_start - row_start - (rows - 1) + (extent - 1)
        window = lax.dynamic_slice_in_dim(table, base, span, 1)
        return hankel_block(window, rows, cols)[:, ::-1, :]
    widened = jnp.concatenate(
        [jnp.broadcast_to(table[:, :1], (table.shape[0], extent - 1)), table], axis=1
    )
    base = row_start - col_start - (cols - 1) + (extent - 1)
    window = lax.dynamic_slice_in_dim(widened, base, span, 1)
    return hankel_block(window, rows, cols)[:, :, ::-1]


def visible_mask(variant, row_ids, col_ids, lengths):
    visible = col_ids[None, None, :] < lengths[:, None, None]
    if variant == "dec":
        visible = visible & (col_ids[None, None, :] <= row_ids[None, :, None])
    return visible[:, None]


def block_scores(query_heads, key_heads, row_ids, col_ids, lengths, variant, offset_bias, extent):
    factor = HEAD ** (-0.5)
    scores = (
        jnp.einsum("sqhe,skhe->shqk", query_heads, key_heads, preferred_element_type=jnp.float32)
        * factor
    )
    if offset_bias is not None:
        scores = (
            scores
            + bias_block(
                variant,
                offset_bias,
                row_ids[0],
                col_ids[0],
                row_ids.shape[0],
                col_ids.shape[0],
                extent,
            )[None]
        )
    return (scores, visible_mask(variant, row_ids, col_ids, lengths))


def row_products(grad_context, context):
    seqs_here, rows_here = (context.shape[0], context.shape[1])
    return jnp.sum(
        (grad_context.astype(jnp.float32) * context).reshape(seqs_here, rows_here, HEADS, HEAD),
        axis=-1,
    ).transpose(0, 2, 1)


def attend(queries, row_ids, lengths, variant, offset_bias, extent, fold_keys):
    seqs_here, rows_here = (queries.shape[0], queries.shape[1])
    query_heads = queries.reshape(seqs_here, rows_here, HEADS, HEAD)

    def fold_step(carried, pieces, begin_at):
        key_rows, value_rows = pieces
        block_len = math.gcd(key_rows.shape[1], 512)

        def block_step(block_id, running):
            row_max, row_sum, weighted = running
            offset_in = block_id * block_len
            key_heads = lax.dynamic_slice_in_dim(key_rows, offset_in, block_len, 1).reshape(
                seqs_here, block_len, HEADS, HEAD
            )
            value_heads = lax.dynamic_slice_in_dim(value_rows, offset_in, block_len, 1).reshape(
                seqs_here, block_len, HEADS, HEAD
            )
            col_ids = offset_in + jnp.arange(block_len, dtype=jnp.int32)
            scores, visible = block_scores(
                query_heads, key_heads, row_ids, col_ids, lengths, variant, offset_bias, extent
            )
            new_max = jnp.maximum(row_max, jnp.max(jnp.where(visible, scores, NEGATIVE), axis=-1))
            weights = jnp.where(visible, jnp.exp(scores - new_max[..., None]), 0.0)
            shrink = jnp.exp(row_max - new_max)
            row_sum = row_sum * shrink + jnp.sum(weights, axis=-1)
            weighted = weighted * shrink[..., None] + jnp.einsum(
                "shqk,skhe->shqe", rounded(weights), value_heads, preferred_element_type=jnp.float32
            )
            return (new_max, row_sum, weighted)

        return lax.fori_loop(0, key_rows.shape[1] // block_len, block_step, carried)

    initial = (
        jnp.full((seqs_here, HEADS, rows_here), NEGATIVE, jnp.float32),
        jnp.zeros((seqs_here, HEADS, rows_here), jnp.float32),
        jnp.zeros((seqs_here, HEADS, rows_here, HEAD), jnp.float32),
    )
    row_max, row_sum, weighted = fold_keys(fold_step, initial)
    context = (
        (weighted / row_sum[..., None])
        .transpose(0, 2, 1, 3)
        .reshape(seqs_here, rows_here, HEADS * HEAD)
    )
    return (context, row_max + jnp.log(row_sum))


def attend_back(
    queries,
    log_sums,
    row_dots,
    grad_context,
    row_ids,
    lengths,
    variant,
    offset_bias,
    extent,
    fold_keys,
):
    seqs_here, rows_here = (queries.shape[0], queries.shape[1])
    query_heads = queries.reshape(seqs_here, rows_here, HEADS, HEAD)
    grad_heads = grad_context.reshape(seqs_here, rows_here, HEADS, HEAD)
    bias_width = offset_bias.shape[1] if offset_bias is not None else 1
    factor = HEAD ** (-0.5)

    def fold_step(carried, pieces, begin_at):
        key_rows, value_rows = pieces
        block_len = math.gcd(key_rows.shape[1], 512)

        def block_step(block_id, running):
            grad_query, grad_bias = (running[0], running[-1])
            offset_in = block_id * block_len
            key_heads = lax.dynamic_slice_in_dim(key_rows, offset_in, block_len, 1).reshape(
                seqs_here, block_len, HEADS, HEAD
            )
            value_heads = lax.dynamic_slice_in_dim(value_rows, offset_in, block_len, 1).reshape(
                seqs_here, block_len, HEADS, HEAD
            )
            col_ids = offset_in + jnp.arange(block_len, dtype=jnp.int32)
            scores, visible = block_scores(
                query_heads, key_heads, row_ids, col_ids, lengths, variant, offset_bias, extent
            )
            weights = jnp.where(visible, jnp.exp(scores - log_sums[..., None]), 0.0)
            grad_weights = jnp.einsum(
                "sqhe,skhe->shqk", grad_heads, value_heads, preferred_element_type=jnp.float32
            )
            grad_scores = weights * (grad_weights - row_dots[..., None])
            if offset_bias is not None:

                def table_block(table_values):
                    return bias_block(
                        variant,
                        table_values,
                        row_ids[0],
                        col_ids[0],
                        row_ids.shape[0],
                        col_ids.shape[0],
                        extent,
                    )

                _, table_pull = jax.vjp(table_block, offset_bias)
                grad_bias = grad_bias + table_pull(jnp.sum(grad_scores, axis=0))[0]
            grad_raw = rounded(grad_scores * factor)
            grad_query = grad_query + jnp.einsum(
                "shqk,skhe->shqe", grad_raw, key_heads, preferred_element_type=jnp.float32
            )
            return (grad_query, grad_bias)

        return lax.fori_loop(0, key_rows.shape[1] // block_len, block_step, carried)

    query_start = jnp.zeros((seqs_here, HEADS, rows_here, HEAD), jnp.float32)
    bias_start = jnp.zeros((HEADS, bias_width), jnp.float32)
    initial = (query_start, bias_start)
    result = fold_keys(fold_step, initial)
    grad_query = result[0].transpose(0, 2, 1, 3).reshape(seqs_here, rows_here, HEADS * HEAD)
    return (grad_query, None, None, result[1])


def owned_key_grads(
    key_rows, value_rows, col_ids, lengths, variant, offset_bias, extent, fold_queries
):
    seqs_here, keys_here = (key_rows.shape[0], key_rows.shape[1])
    key_heads = key_rows.reshape(seqs_here, keys_here, HEADS, HEAD)
    value_heads = value_rows.reshape(seqs_here, keys_here, HEADS, HEAD)
    factor = HEAD ** (-0.5)

    def fold_step(carried, pieces, begin_at):
        query_rows, grad_rows, log_rows, dot_rows = pieces
        block_len = math.gcd(query_rows.shape[1], 512)

        def block_step(block_id, running):
            grad_keys, grad_values = running
            offset_in = block_id * block_len
            query_heads = lax.dynamic_slice_in_dim(query_rows, offset_in, block_len, 1).reshape(
                seqs_here, block_len, HEADS, HEAD
            )
            grad_heads = lax.dynamic_slice_in_dim(grad_rows, offset_in, block_len, 1).reshape(
                seqs_here, block_len, HEADS, HEAD
            )
            log_block = lax.dynamic_slice_in_dim(log_rows, offset_in, block_len, 1).transpose(
                0, 2, 1
            )
            dot_block = lax.dynamic_slice_in_dim(dot_rows, offset_in, block_len, 1).transpose(
                0, 2, 1
            )
            row_ids = offset_in + jnp.arange(block_len, dtype=jnp.int32)
            scores, visible = block_scores(
                query_heads, key_heads, row_ids, col_ids, lengths, variant, offset_bias, extent
            )
            weights = jnp.where(visible, jnp.exp(scores - log_block[..., None]), 0.0)
            grad_weights = jnp.einsum(
                "sqhe,skhe->shqk", grad_heads, value_heads, preferred_element_type=jnp.float32
            )
            grad_scores = weights * (grad_weights - dot_block[..., None])
            grad_raw = rounded(grad_scores * factor)
            grad_keys = grad_keys + jnp.einsum(
                "shqk,sqhe->skhe", grad_raw, query_heads, preferred_element_type=jnp.float32
            ).reshape(seqs_here, keys_here, HEADS * HEAD)
            grad_values = grad_values + jnp.einsum(
                "shqk,sqhe->skhe", rounded(weights), grad_heads, preferred_element_type=jnp.float32
            ).reshape(seqs_here, keys_here, HEADS * HEAD)
            return (grad_keys, grad_values)

        return lax.fori_loop(0, query_rows.shape[1] // block_len, block_step, carried)

    initial = (
        jnp.zeros((seqs_here, keys_here, HEADS * HEAD), jnp.float32),
        jnp.zeros((seqs_here, keys_here, HEADS * HEAD), jnp.float32),
    )
    return fold_queries(fold_step, initial)


def feed_forward(residual, gain_row, weights_in, weights_out):
    normed_low = rounded(rms_norm(residual, gain_row))
    gate_up = jnp.einsum(
        "srd,jdf->jsrf", normed_low, weights_in, preferred_element_type=jnp.float32
    )
    hidden = rounded(gated_unit(gate_up))
    output = jnp.einsum("srf,fd->srd", hidden, weights_out, preferred_element_type=jnp.float32)
    return (residual + output, (normed_low, gate_up, hidden))


def feed_back(residual, gain_row, weights_in, weights_out, kept_values, upstream):
    normed_low, gate_up, hidden = kept_values
    upstream_low = rounded(upstream)
    grad_out_weights = jnp.einsum(
        "srf,srd->fd", hidden, upstream_low, preferred_element_type=jnp.float32
    )
    grad_hidden = jnp.einsum(
        "srd,fd->srf", upstream_low, weights_out, preferred_element_type=jnp.float32
    )
    _, pullback = jax.vjp(gated_unit, gate_up)
    grad_gate_up = rounded(pullback(grad_hidden)[0])
    grad_in_weights = jnp.einsum(
        "srd,jsrf->jdf", normed_low, grad_gate_up, preferred_element_type=jnp.float32
    )
    grad_normed = jnp.einsum(
        "jsrf,jdf->srd", grad_gate_up, weights_in, preferred_element_type=jnp.float32
    )
    grad_residual, grad_gain = rms_back(residual, gain_row, grad_normed)
    return (upstream + grad_residual, grad_gain, grad_in_weights, grad_out_weights)


def local(
    enc_input,
    dec_input,
    enc_lengths,
    dec_lengths,
    enc_buckets,
    dec_buckets,
    attention_in,
    attention_out,
    hidden_in,
    hidden_out,
    norm_gains,
    position_bias,
    enc_cotangent,
    dec_cotangent,
):
    full_in, full_out, full_hidden_in, full_hidden_out, full_gains = (
        lax.all_gather(attention_in, ("dp", "seq"), axis=2, tiled=True),
        lax.all_gather(attention_out, ("dp", "seq"), axis=1, tiled=True),
        lax.all_gather(hidden_in, ("dp", "seq"), axis=2, tiled=True),
        lax.all_gather(hidden_out, ("dp", "seq"), axis=1, tiled=True),
        lax.all_gather(norm_gains, ("dp", "seq"), axis=1, tiled=True),
    )
    gain_rows = full_gains.astype(jnp.float32)
    enc_rows = enc_input.shape[1]
    dec_rows = dec_input.shape[1]
    seq_index = lax.axis_index("seq")
    enc_ids = seq_index * enc_rows + jnp.arange(enc_rows, dtype=jnp.int32)
    dec_ids = seq_index * dec_rows + jnp.arange(dec_rows, dtype=jnp.int32)
    enc_extent = (enc_buckets.shape[0] + 1) // 2
    dec_extent = dec_buckets.shape[0]
    enc_table = offset_table(enc_buckets, position_bias[0])
    dec_table = offset_table(dec_buckets, position_bias[1])
    enc_values = enc_input.astype(jnp.float32)
    norm_a_low = rounded(rms_norm(enc_values, gain_rows[0]))
    enc_qkv = rounded(
        jnp.einsum("srd,jde->jsre", norm_a_low, full_in[0], preferred_element_type=jnp.float32)
    )
    enc_context, enc_logs = attend(
        enc_qkv[0],
        enc_ids,
        enc_lengths,
        "enc",
        enc_table,
        enc_extent,
        lambda folder, initial: folder(
            initial,
            (
                lax.all_gather(enc_qkv[1], "seq", axis=1, tiled=True),
                lax.all_gather(enc_qkv[2], "seq", axis=1, tiled=True),
            ),
            jnp.int32(0),
        ),
    )
    enc_context_low = rounded(enc_context)
    enc_mid = enc_values + jnp.einsum(
        "srd,de->sre", enc_context_low, full_out[0], preferred_element_type=jnp.float32
    )
    enc_last, enc_ffn_kept = feed_forward(
        enc_mid, gain_rows[1], full_hidden_in[0], full_hidden_out[0]
    )
    memory = rms_norm(enc_last, gain_rows[2])
    memory_low = rounded(memory)
    dec_values = dec_input.astype(jnp.float32)
    norm_b_low = rounded(rms_norm(dec_values, gain_rows[3]))
    dec_qkv = rounded(
        jnp.einsum("srd,jde->jsre", norm_b_low, full_in[1], preferred_element_type=jnp.float32)
    )
    dec_context, dec_logs = attend(
        dec_qkv[0],
        dec_ids,
        dec_lengths,
        "dec",
        dec_table,
        dec_extent,
        lambda folder, initial: folder(
            initial,
            (
                lax.all_gather(dec_qkv[1], "seq", axis=1, tiled=True),
                lax.all_gather(dec_qkv[2], "seq", axis=1, tiled=True),
            ),
            jnp.int32(0),
        ),
    )
    dec_context_low = rounded(dec_context)
    dec_mid = dec_values + jnp.einsum(
        "srd,de->sre", dec_context_low, full_out[1], preferred_element_type=jnp.float32
    )
    norm_c_low = rounded(rms_norm(dec_mid, gain_rows[4]))
    cross_query = rounded(
        jnp.einsum("srd,de->sre", norm_c_low, full_in[2, 0], preferred_element_type=jnp.float32)
    )
    cross_pair = rounded(
        jnp.einsum("srd,jde->jsre", memory_low, full_in[2, 1:], preferred_element_type=jnp.float32)
    )
    cross_context, cross_logs = attend(
        cross_query,
        dec_ids,
        enc_lengths,
        "cross",
        None,
        0,
        lambda folder, initial: folder(
            initial,
            (
                lax.all_gather(cross_pair[0], "seq", axis=1, tiled=True),
                lax.all_gather(cross_pair[1], "seq", axis=1, tiled=True),
            ),
            jnp.int32(0),
        ),
    )
    cross_low = rounded(cross_context)
    dec_cross = dec_mid + jnp.einsum(
        "srd,de->sre", cross_low, full_out[2], preferred_element_type=jnp.float32
    )
    dec_last, dec_ffn_kept = feed_forward(
        dec_cross, gain_rows[5], full_hidden_in[1], full_hidden_out[1]
    )
    dec_final = rms_norm(dec_last, gain_rows[6])
    grad_dec_last, grad_gain_six = rms_back(
        dec_last, gain_rows[6], dec_cotangent.astype(jnp.float32)
    )
    grad_dec_cross, grad_gain_five, grad_hin_one, grad_hout_one = feed_back(
        dec_cross, gain_rows[5], full_hidden_in[1], full_hidden_out[1], dec_ffn_kept, grad_dec_last
    )
    upstream_low = rounded(grad_dec_cross)
    grad_out_two = jnp.einsum(
        "srd,sre->de", cross_low, upstream_low, preferred_element_type=jnp.float32
    )
    grad_cross_context = rounded(
        jnp.einsum("sre,de->srd", upstream_low, full_out[2], preferred_element_type=jnp.float32)
    )
    cross_dots = row_products(grad_cross_context, cross_context)
    cross_grad_query, cross_grad_keys, cross_grad_values, _ = attend_back(
        cross_query,
        cross_logs,
        cross_dots,
        grad_cross_context,
        dec_ids,
        enc_lengths,
        "cross",
        None,
        0,
        lambda folder, initial: folder(
            initial,
            (
                lax.all_gather(cross_pair[0], "seq", axis=1, tiled=True),
                lax.all_gather(cross_pair[1], "seq", axis=1, tiled=True),
            ),
            jnp.int32(0),
        ),
    )
    cross_query_low = rounded(cross_grad_query)
    grad_query_two = jnp.einsum(
        "srd,sre->de", norm_c_low, cross_query_low, preferred_element_type=jnp.float32
    )
    grad_norm_c = jnp.einsum(
        "sre,de->srd", cross_query_low, full_in[2, 0], preferred_element_type=jnp.float32
    )
    grad_mid_part, grad_gain_four = rms_back(dec_mid, gain_rows[4], grad_norm_c)
    grad_dec_mid = grad_dec_cross + grad_mid_part
    upstream_low = rounded(grad_dec_mid)
    grad_out_one = jnp.einsum(
        "srd,sre->de", dec_context_low, upstream_low, preferred_element_type=jnp.float32
    )
    grad_dec_context = rounded(
        jnp.einsum("sre,de->srd", upstream_low, full_out[1], preferred_element_type=jnp.float32)
    )
    dec_dots = row_products(grad_dec_context, dec_context)
    dec_grad_query, dec_grad_keys, dec_grad_values, grad_dec_bias = attend_back(
        dec_qkv[0],
        dec_logs,
        dec_dots,
        grad_dec_context,
        dec_ids,
        dec_lengths,
        "dec",
        dec_table,
        dec_extent,
        lambda folder, initial: folder(
            initial,
            (
                lax.all_gather(dec_qkv[1], "seq", axis=1, tiled=True),
                lax.all_gather(dec_qkv[2], "seq", axis=1, tiled=True),
            ),
            jnp.int32(0),
        ),
    )
    cross_key_grad, cross_value_grad = owned_key_grads(
        cross_pair[0],
        cross_pair[1],
        enc_ids,
        enc_lengths,
        "cross",
        None,
        0,
        lambda folder, initial: folder(
            initial,
            (
                lax.all_gather(cross_query, "seq", axis=1, tiled=True),
                lax.all_gather(grad_cross_context, "seq", axis=1, tiled=True),
                lax.all_gather(
                    rows_first(cross_logs).astype(jnp.bfloat16), "seq", axis=1, tiled=True
                ).astype(jnp.float32),
                lax.all_gather(
                    rows_first(cross_dots).astype(jnp.bfloat16), "seq", axis=1, tiled=True
                ).astype(jnp.float32),
            ),
            jnp.int32(0),
        ),
    )
    dec_key_grad, dec_value_grad = owned_key_grads(
        dec_qkv[1],
        dec_qkv[2],
        dec_ids,
        dec_lengths,
        "dec",
        dec_table,
        dec_extent,
        lambda folder, initial: folder(
            initial,
            (
                lax.all_gather(dec_qkv[0], "seq", axis=1, tiled=True),
                lax.all_gather(grad_dec_context, "seq", axis=1, tiled=True),
                lax.all_gather(
                    rows_first(dec_logs).astype(jnp.bfloat16), "seq", axis=1, tiled=True
                ).astype(jnp.float32),
                lax.all_gather(
                    rows_first(dec_dots).astype(jnp.bfloat16), "seq", axis=1, tiled=True
                ).astype(jnp.float32),
            ),
            jnp.int32(0),
        ),
    )
    pair_grads = rounded(jnp.stack([cross_key_grad, cross_value_grad]))
    grad_pair_two = jnp.einsum(
        "srd,jsre->jde", memory_low, pair_grads, preferred_element_type=jnp.float32
    )
    grad_memory = jnp.einsum(
        "jsre,jde->srd", pair_grads, full_in[2, 1:], preferred_element_type=jnp.float32
    )
    dec_grads = rounded(jnp.stack([dec_grad_query, dec_key_grad, dec_value_grad]))
    grad_in_one = jnp.einsum(
        "srd,jsre->jde", norm_b_low, dec_grads, preferred_element_type=jnp.float32
    )
    grad_norm_b = jnp.einsum(
        "jsre,jde->srd", dec_grads, full_in[1], preferred_element_type=jnp.float32
    )
    grad_dec_part, grad_gain_three = rms_back(dec_values, gain_rows[3], grad_norm_b)
    grad_dec_input = grad_dec_mid + grad_dec_part
    grad_memory_total = enc_cotangent.astype(jnp.float32) + grad_memory
    grad_enc_last, grad_gain_two = rms_back(enc_last, gain_rows[2], grad_memory_total)
    grad_enc_mid, grad_gain_one, grad_hin_zero, grad_hout_zero = feed_back(
        enc_mid, gain_rows[1], full_hidden_in[0], full_hidden_out[0], enc_ffn_kept, grad_enc_last
    )
    upstream_low = rounded(grad_enc_mid)
    grad_out_zero = jnp.einsum(
        "srd,sre->de", enc_context_low, upstream_low, preferred_element_type=jnp.float32
    )
    grad_enc_context = rounded(
        jnp.einsum("sre,de->srd", upstream_low, full_out[0], preferred_element_type=jnp.float32)
    )
    enc_dots = row_products(grad_enc_context, enc_context)
    enc_grad_query, enc_grad_keys, enc_grad_values, grad_enc_bias = attend_back(
        enc_qkv[0],
        enc_logs,
        enc_dots,
        grad_enc_context,
        enc_ids,
        enc_lengths,
        "enc",
        enc_table,
        enc_extent,
        lambda folder, initial: folder(
            initial,
            (
                lax.all_gather(enc_qkv[1], "seq", axis=1, tiled=True),
                lax.all_gather(enc_qkv[2], "seq", axis=1, tiled=True),
            ),
            jnp.int32(0),
        ),
    )
    enc_key_grad, enc_value_grad = owned_key_grads(
        enc_qkv[1],
        enc_qkv[2],
        enc_ids,
        enc_lengths,
        "enc",
        enc_table,
        enc_extent,
        lambda folder, initial: folder(
            initial,
            (
                lax.all_gather(enc_qkv[0], "seq", axis=1, tiled=True),
                lax.all_gather(grad_enc_context, "seq", axis=1, tiled=True),
                lax.all_gather(
                    rows_first(enc_logs).astype(jnp.bfloat16), "seq", axis=1, tiled=True
                ).astype(jnp.float32),
                lax.all_gather(
                    rows_first(enc_dots).astype(jnp.bfloat16), "seq", axis=1, tiled=True
                ).astype(jnp.float32),
            ),
            jnp.int32(0),
        ),
    )
    enc_grads = rounded(jnp.stack([enc_grad_query, enc_key_grad, enc_value_grad]))
    grad_in_zero = jnp.einsum(
        "srd,jsre->jde", norm_a_low, enc_grads, preferred_element_type=jnp.float32
    )
    grad_norm_a = jnp.einsum(
        "jsre,jde->srd", enc_grads, full_in[0], preferred_element_type=jnp.float32
    )
    grad_enc_part, grad_gain_zero = rms_back(enc_values, gain_rows[0], grad_norm_a)
    grad_enc_input = grad_enc_mid + grad_enc_part
    grad_cross_in = jnp.concatenate([grad_query_two[None], grad_pair_two], axis=0)
    grad_attention_in = jnp.stack([grad_in_zero, grad_in_one, grad_cross_in])
    grad_attention_out = jnp.stack([grad_out_zero, grad_out_one, grad_out_two])
    grad_hidden_in = jnp.stack([grad_hin_zero, grad_hin_one])
    grad_hidden_out = jnp.stack([grad_hout_zero, grad_hout_one])
    grad_gains = jnp.stack(
        [
            grad_gain_zero,
            grad_gain_one,
            grad_gain_two,
            grad_gain_three,
            grad_gain_four,
            grad_gain_five,
            grad_gain_six,
        ]
    )
    shard_in, shard_out, shard_hin, shard_hout, shard_gains = (
        lax.psum_scatter(grad_attention_in, ("dp", "seq"), scatter_dimension=2, tiled=True),
        lax.psum_scatter(grad_attention_out, ("dp", "seq"), scatter_dimension=1, tiled=True),
        lax.psum_scatter(grad_hidden_in, ("dp", "seq"), scatter_dimension=2, tiled=True),
        lax.psum_scatter(grad_hidden_out, ("dp", "seq"), scatter_dimension=1, tiled=True),
        lax.psum_scatter(grad_gains, ("dp", "seq"), scatter_dimension=1, tiled=True),
    )
    bucket_count = position_bias.shape[1]
    grad_position = jnp.stack(
        [
            bucket_grad(enc_buckets, grad_enc_bias, bucket_count),
            bucket_grad(dec_buckets, grad_dec_bias, bucket_count),
        ]
    )
    squares_in = shard_in * shard_in
    squares_out = shard_out * shard_out
    squares_hin = shard_hin * shard_hin
    squares_hout = shard_hout * shard_hout
    col_in, col_out, col_hin, col_hout, grad_position = lax.psum(
        (
            jnp.sum(squares_in, axis=2),
            jnp.sum(squares_out, axis=1),
            jnp.sum(squares_hin, axis=2),
            jnp.sum(squares_hout, axis=1),
            grad_position,
        ),
        ("dp", "seq"),
    )
    return (
        rounded(memory),
        rounded(dec_final),
        grad_enc_input,
        grad_dec_input,
        shard_in,
        shard_out,
        shard_hin,
        shard_hout,
        shard_gains,
        grad_position,
        0.5 * jnp.mean(squares_in, axis=-1),
        0.5 * col_in / D,
        0.5 * jnp.mean(squares_out, axis=-1),
        0.5 * col_out / D,
        0.5 * jnp.mean(squares_hin, axis=-1),
        0.5 * col_hin / D,
        0.5 * jnp.mean(squares_hout, axis=-1),
        0.5 * col_hout / FF,
    )


WAYS = 4


def swap(values, bits):
    return lax.ppermute(values, "seq", [(s, s ^ bits) for s in range(8)])


def swap_core(values):
    return swap(values, 1)


def swap_x(values):
    return swap(values, 2)


def swap_y(values):
    return swap(values, 4)


def shift_z(values, hops, count):
    return lax.ppermute(values, "dp", [(i, (i + hops) % count) for i in range(count)])


def pair_up(mine, other, bit):
    first = bit == 0
    return jnp.stack([jnp.where(first, mine, other), jnp.where(first, other, mine)])


def pick(values, index, axis=0):
    return lax.dynamic_index_in_dim(values, index, axis, keepdims=False)


class Place:
    def __init__(self, depth):
        self.depth = depth
        self.z = lax.axis_index("dp")
        s = lax.axis_index("seq")
        self.y, self.x, self.c = s // 4, (s // 2) % 2, s % 2
        self.q = s % 4


def exchange_columns(place, pieces):
    halves = pieces.reshape((2, 2) + pieces.shape[1:])
    got = swap_x(pick(halves, 1 - place.x))
    both = pair_up(pick(halves, place.x), got, place.x)
    got = swap_core(pick(both, 1 - place.c, 1))
    whole = pair_up(pick(both, place.c, 1), got, place.c)
    return jnp.swapaxes(whole, 0, 1).reshape(pieces.shape)


def gather_rows(place, piece):
    depth = place.depth
    held = jnp.zeros((depth,) + piece.shape, piece.dtype)
    arrivals = [(0, piece)] + [(k, shift_z(piece, k, depth)) for k in range(1, depth)]
    for hops, block in arrivals:
        held = lax.dynamic_update_index_in_dim(held, block, (place.z - hops) % depth, 0)
    other = swap_y(held)
    first = place.y == 0
    return jnp.stack([jnp.where(first, held, other), jnp.where(first, other, held)], axis=1)


def scatter_rows(place, parts):
    depth = place.depth
    sent = swap_y(rounded(pick(parts, 1 - place.y, 1)))
    halves = pick(parts, place.y, 1) + sent.astype(jnp.float32)
    halves_low = rounded(halves)
    total = pick(halves, place.z)
    for hops in range(1, depth):
        total = total + shift_z(pick(halves_low, (place.z + hops) % depth), hops, depth).astype(
            jnp.float32
        )
    return total


def turn(values, depth, back=False):
    pairs = []
    for d in range(depth):
        for y in range(2):
            for q in range(WAYS):
                pairs.append((d * 8 + y * 4 + q, q * 8 + y * 4 + d))
    return lax.ppermute(values, ("dp", "seq"), pairs)


def sum_group(place, partial):
    half = partial.shape[0] // 2
    parts = partial.reshape(2, half, partial.shape[1])
    chip = pick(parts, place.c) + swap_core(rounded(pick(parts, 1 - place.c))).astype(jnp.float32)
    return chip + swap_x(rounded(chip)).astype(jnp.float32)


def both_cores(place, half):
    whole = pair_up(half, swap_core(half), place.c)
    return whole.reshape((2 * half.shape[0],) + half.shape[1:])


def matmul(a, b):
    return jnp.dot(a, b, preferred_element_type=jnp.float32)


def matmul_nt(a, b):
    return lax.dot_general(a, b, (((1,), (1,)), ((), ())), preferred_element_type=jnp.float32)


def matmul_tn(a, b):
    return lax.dot_general(a, b, (((0,), (0,)), ((), ())), preferred_element_type=jnp.float32)


def inner_block(block):
    y, x, c = block // 4, (block // 2) % 2, block % 2
    return c * 4 + y * 2 + x


def in_order(ref, first, width):
    step = ref.shape[0] // 8
    return jnp.concatenate(
        [
            ref[inner_block(n) * step : (inner_block(n) + 1) * step, first : first + width]
            for n in range(8)
        ],
        axis=0,
    )


def out_of_order(ref, first, values):
    step = ref.shape[0] // 8
    for n in range(8):
        at = inner_block(n)
        ref[at * step : (at + 1) * step, first : first + values.shape[1]] = values[
            n * step : (n + 1) * step
        ].astype(ref.dtype)


TILE = 128


def attend_kernel(heads, causal, biased, *refs):
    if biased:
        length_ref, q_ref, kv_ref, table_ref, ctx_ref, p_ref = refs
    else:
        length_ref, q_ref, kv_ref, ctx_ref, p_ref = refs
    rows = q_ref.shape[0]
    tiles = rows // TILE
    length = length_ref[0]
    width = heads * HEAD
    cols = lax.broadcasted_iota(jnp.int32, (TILE, rows), 1)
    for h in range(heads):
        q = in_order(q_ref, h * HEAD, HEAD)
        k = in_order(kv_ref, kv_ref.shape[1] - 2 * width + h * HEAD, HEAD)
        v = in_order(kv_ref, kv_ref.shape[1] - width + h * HEAD, HEAD)
        if biased:
            line = jnp.broadcast_to(table_ref[h : h + 1, :], (TILE, 2 * rows))
            skew = pltpu.roll(line, 2 * rows - (TILE - 1), 1, stride=1, stride_axis=0)
        contexts = []
        for i in range(tiles):
            s = matmul_nt(q[i * TILE : (i + 1) * TILE], k) * (HEAD**-0.5)
            if biased:
                begin = (tiles - 1 - i) * TILE
                s = s + skew[:, begin : begin + rows]
            visible = cols < length
            if causal:
                ids = lax.broadcasted_iota(jnp.int32, (TILE, rows), 0) + i * TILE
                visible = visible & (cols <= ids)
            s = jnp.where(visible, s, NEGATIVE)
            e = jnp.exp(s - jnp.max(s, axis=-1, keepdims=True))
            p = (e / jnp.sum(e, axis=-1, keepdims=True)).astype(jnp.bfloat16)
            p_ref[h, i * TILE : (i + 1) * TILE, :] = p
            contexts.append(matmul(p, v))
        out_of_order(ctx_ref, h * HEAD, jnp.concatenate(contexts, axis=0))


def attend_local(q, kv, table, length, causal):
    rows = q.shape[0]
    heads = HEADS // WAYS
    biased = table is not None
    vmem = pl.BlockSpec(memory_space=pltpu.VMEM)
    operands = [length.reshape(1), q, kv] + ([table] if biased else [])
    return pl.pallas_call(
        functools.partial(attend_kernel, heads, causal, biased),
        out_shape=(
            jax.ShapeDtypeStruct((rows, heads * HEAD), jnp.float32),
            jax.ShapeDtypeStruct((heads, rows, rows), jnp.bfloat16),
        ),
        in_specs=[pl.BlockSpec(memory_space=pltpu.SMEM)] + [vmem] * (len(operands) - 1),
        out_specs=(vmem, vmem),
        compiler_params=pltpu.CompilerParams(vmem_limit_bytes=40 * 2**20),
        cost_estimate=pl.CostEstimate(
            flops=4 * heads * rows * rows * HEAD,
            bytes_accessed=2 * heads * rows * (rows + 5 * HEAD),
            transcendentals=heads * rows * rows,
        ),
        name="attend",
    )(*operands)


def attend_back_kernel(heads, biased, *refs):
    if biased:
        q_ref, kv_ref, p_ref, ctx_ref, g_ref, dqkv_ref, dtable_ref, ds_ref = refs
    else:
        q_ref, kv_ref, p_ref, ctx_ref, g_ref, dqkv_ref, ds_ref = refs
    rows = q_ref.shape[0]
    tiles = rows // TILE
    width = heads * HEAD
    factor = HEAD**-0.5
    for h in range(heads):
        q = in_order(q_ref, h * HEAD, HEAD)
        k = in_order(kv_ref, kv_ref.shape[1] - 2 * width + h * HEAD, HEAD)
        v = in_order(kv_ref, kv_ref.shape[1] - width + h * HEAD, HEAD)
        g = in_order(g_ref, h * HEAD, HEAD)
        context = in_order(ctx_ref, h * HEAD, HEAD)
        dots = jnp.sum(g.astype(jnp.float32) * context, axis=-1, keepdims=True)
        if biased:
            sums = [None] * (2 * tiles - 1)
        for i in range(tiles):
            at = slice(i * TILE, (i + 1) * TILE)
            dp = matmul_nt(g[at], v)
            ds = p_ref[h, at, :].astype(jnp.float32) * (dp - dots[at])
            if biased:
                for j in range(tiles):
                    slot = tiles - 1 - i + j
                    part = ds[:, j * TILE : (j + 1) * TILE]
                    sums[slot] = part if sums[slot] is None else sums[slot] + part
            ds_ref[at, :] = (ds * factor).astype(jnp.bfloat16)
        ds_low = ds_ref[...]
        out_of_order(dqkv_ref, h * HEAD, matmul(ds_low, k))
        out_of_order(dqkv_ref, width + h * HEAD, matmul_tn(ds_low, q))
        out_of_order(dqkv_ref, 2 * width + h * HEAD, matmul_tn(p_ref[h], g))
        if biased:
            band = jnp.concatenate(sums + [jnp.zeros((TILE, TILE), jnp.float32)], axis=1)
            ids = lax.broadcasted_iota(jnp.int32, band.shape, 0)
            bit = 1
            while bit < TILE:
                moved = pltpu.roll(band, 2 * rows - bit, 1)
                band = jnp.where((ids & bit) != 0, moved, band)
                bit *= 2
            line = jnp.sum(band, axis=0, keepdims=True)
            dtable_ref[h : h + 1, :] = pltpu.roll(line, TILE - 1, 1)


def attend_local_back(q, kv, p, ctx, g, biased):
    rows = q.shape[0]
    heads = HEADS // WAYS
    vmem = pl.BlockSpec(memory_space=pltpu.VMEM)
    shapes = [jax.ShapeDtypeStruct((rows, 3 * heads * HEAD), jnp.bfloat16)]
    if biased:
        shapes.append(jax.ShapeDtypeStruct((heads, 2 * rows), jnp.float32))
    result = pl.pallas_call(
        functools.partial(attend_back_kernel, heads, biased),
        out_shape=tuple(shapes),
        in_specs=[vmem] * 5,
        out_specs=(vmem,) * len(shapes),
        scratch_shapes=[pltpu.VMEM((rows, rows), jnp.bfloat16)],
        compiler_params=pltpu.CompilerParams(vmem_limit_bytes=40 * 2**20),
        cost_estimate=pl.CostEstimate(
            flops=8 * heads * rows * rows * HEAD,
            bytes_accessed=2 * heads * rows * (rows + 8 * HEAD),
            transcendentals=0,
        ),
        name="attend_back",
    )(q, kv, p, ctx, g)
    return result if biased else (result[0], None)


def gather_own_rows(place, mine, other_seq):
    near = pair_up(mine, swap_y(other_seq), place.y)
    far = pair_up(near, swap_x(near), place.x)
    far = far.transpose(2, 1, 0, 3, 4)
    return far.reshape(far.shape[0], -1, far.shape[4])


def give_back(place, half):
    blocks = half.reshape(2, 2, -1, half.shape[1])
    blocks = pick(blocks, place.x, 1)
    other = swap_y(pick(blocks, 1 - place.y))
    return pair_up(pick(blocks, place.y), other, place.y)


def group_feed_back(place, residual, gain, weights_in, weights_out, kept, upstream):
    normed, gate, up, hidden = kept
    up_low = both_cores(place, rounded(upstream))
    grad_hidden = matmul_nt(up_low, weights_out)
    _, pullback = jax.vjp(lambda a, b: jax.nn.gelu(a, approximate=True) * b, gate, up)
    grad_gate, grad_up = pullback(grad_hidden)
    grad_gate_up = jnp.concatenate([rounded(grad_gate), rounded(grad_up)], axis=1)
    grad_normed = sum_group(place, matmul_nt(grad_gate_up, weights_in))
    grad_out = matmul_tn(hidden, up_low)
    grad_in = matmul_tn(normed, grad_gate_up)
    grad_residual, grad_gain = rms_back(residual, gain, grad_normed)
    return (upstream + grad_residual, grad_gain, grad_in, grad_out)


def group_feed_forward(place, residual, gain, weights_in, weights_out):
    normed = both_cores(place, rounded(rms_norm(residual, gain)))
    gate_up = matmul(normed, weights_in)
    gate, up = jnp.split(gate_up, 2, axis=1)
    hidden = rounded(jax.nn.gelu(gate, approximate=True) * up)
    output = sum_group(place, matmul(hidden, weights_out))
    return (residual + output, (normed, gate, up, hidden))


def sum_everywhere(place, values):
    depth = place.depth
    for bits in (1, 2, 4):
        values = values + swap(values, bits)
    return values + sum(shift_z(values, k, depth) for k in range(1, depth))


def split_columns(weights):
    pieces = weights.reshape(weights.shape[:-1] + (WAYS, -1))
    return jnp.moveaxis(pieces, -2, 0)


def grouped(
    depth,
    enc_input,
    dec_input,
    enc_lengths,
    dec_lengths,
    enc_buckets,
    dec_buckets,
    attention_in,
    attention_out,
    hidden_in,
    hidden_out,
    norm_gains,
    position_bias,
    enc_cotangent,
    dec_cotangent,
):
    place = Place(depth)
    y, q = place.y, place.q
    length = enc_input.shape[1] * 8
    own = attention_in.shape[2]
    ff_own = hidden_out.shape[1]
    ff = ff_own * 2 * depth
    heads = HEADS // WAYS
    width = heads * HEAD

    in_pieces = split_columns(attention_in)
    in_pieces = in_pieces.transpose(0, 1, 3, 2, 4).reshape(WAYS, 3, own, 3 * width)
    enc_piece = exchange_columns(place, in_pieces[:, 0]).reshape(WAYS * own, 3 * width)
    w_enc = gather_rows(place, enc_piece).reshape(D, 3 * width)
    turned = turn(attention_out, depth)
    w_out_enc = gather_rows(place, turned[0])
    hidden_pieces = hidden_in.reshape(2, 2, own, 2 * depth, WAYS, ff_own)
    hidden_pieces = hidden_pieces.transpose(4, 0, 2, 1, 3, 5).reshape(WAYS, 2, own, 2 * ff)
    hid_enc = exchange_columns(place, hidden_pieces[:, 0]).reshape(WAYS * own, 2 * ff)
    w_hin_enc = gather_rows(place, hid_enc).reshape(D, 2 * ff)
    w_hout_enc = gather_rows(place, hidden_out[0]).reshape(ff, D)
    rest = exchange_columns(place, in_pieces[:, 1:])
    rest = rest.transpose(1, 0, 2, 3).reshape(2 * WAYS * own, 3 * width)
    w_rest = gather_rows(place, rest).reshape(2 * depth, 2, WAYS * own, 3 * width)
    w_dec = w_rest[:, 0].reshape(D, 3 * width)
    w_cross = w_rest[:, 1].reshape(D, 3 * width)
    w_out_rest = gather_rows(place, turned[1:])
    hid_dec = exchange_columns(place, hidden_pieces[:, 1]).reshape(WAYS * own, 2 * ff)
    w_hin_dec = gather_rows(place, hid_dec).reshape(D, 2 * ff)
    w_hout_dec = gather_rows(place, hidden_out[1]).reshape(ff, D)

    def out_rows(gathered):
        return gathered.transpose(1, 0, 2, 3).reshape(width, D)

    w_out_enc = out_rows(w_out_enc)
    w_out_dec, w_out_cross = out_rows(w_out_rest[:, :, 0]), out_rows(w_out_rest[:, :, 1])
    gains_full = lax.all_gather(norm_gains, ("dp", "seq"), axis=1, tiled=True)
    gains = gains_full.astype(jnp.float32)

    def mine_other(array):
        return (pick(array, y), pick(array, 1 - y))

    enc_mine, enc_other = mine_other(enc_input)
    dec_mine, dec_other = mine_other(dec_input)
    enc_half = gather_own_rows(place, enc_mine[None], enc_other[None])[0]
    enc_full = both_cores(place, enc_half)
    dec_half = gather_own_rows(place, dec_mine[None], dec_other[None])[0]
    dec_full = both_cores(place, dec_half)
    cot_mine = jnp.stack([pick(dec_cotangent, y), pick(enc_cotangent, y)])
    cot_other = jnp.stack([pick(dec_cotangent, 1 - y), pick(enc_cotangent, 1 - y)])
    cots = gather_own_rows(place, cot_mine, cot_other).astype(jnp.float32)
    enc_length = pick(enc_lengths, y)
    dec_length = pick(dec_lengths, y)

    enc_table = offset_table(enc_buckets, position_bias[0])
    enc_table = jnp.pad(enc_table, ((0, 0), (0, 1)))
    dec_table = offset_table(dec_buckets, position_bias[1])
    dec_table = jnp.concatenate(
        [dec_table[:, ::-1], jnp.broadcast_to(dec_table[:, :1], (HEADS, length))], axis=1
    )
    enc_table = lax.dynamic_slice_in_dim(enc_table, q * heads, heads, 0)
    dec_table = lax.dynamic_slice_in_dim(dec_table, q * heads, heads, 0)

    enc_values = enc_half.astype(jnp.float32)
    norm_a = rounded(rms_norm(enc_full.astype(jnp.float32), gains[0]))
    qkv_enc = rounded(matmul(norm_a, w_enc))
    ctx_enc, p_enc = attend_local(qkv_enc, qkv_enc, enc_table, enc_length, False)
    ctx_enc_low = rounded(ctx_enc)
    enc_mid = enc_values + sum_group(place, matmul(ctx_enc_low, w_out_enc))
    enc_last, enc_kept = group_feed_forward(place, enc_mid, gains[1], w_hin_enc, w_hout_enc)
    memory = rms_norm(enc_last, gains[2])
    memory_low = both_cores(place, rounded(memory))

    dec_values = dec_half.astype(jnp.float32)
    norm_b = rounded(rms_norm(dec_full.astype(jnp.float32), gains[3]))
    qkv_dec = rounded(matmul(norm_b, w_dec))
    ctx_dec, p_dec = attend_local(qkv_dec, qkv_dec, dec_table, dec_length, True)
    ctx_dec_low = rounded(ctx_dec)
    dec_mid = dec_values + sum_group(place, matmul(ctx_dec_low, w_out_dec))
    norm_c = both_cores(place, rounded(rms_norm(dec_mid, gains[4])))
    q_cross = rounded(matmul(norm_c, w_cross[:, :width]))
    kv_cross = rounded(matmul(memory_low, w_cross[:, width:]))
    ctx_cross, p_cross = attend_local(q_cross, kv_cross, None, enc_length, False)
    ctx_cross_low = rounded(ctx_cross)
    dec_cross = dec_mid + sum_group(place, matmul(ctx_cross_low, w_out_cross))
    dec_last, dec_kept = group_feed_forward(place, dec_cross, gains[5], w_hin_dec, w_hout_dec)
    dec_final = rms_norm(dec_last, gains[6])

    g_dec_last, gg6 = rms_back(dec_last, gains[6], cots[0])
    g_dec_cross, gg5, d_hin_dec, d_hout_dec = group_feed_back(
        place, dec_cross, gains[5], w_hin_dec, w_hout_dec, dec_kept, g_dec_last
    )
    up_low = both_cores(place, rounded(g_dec_cross))
    g_ctx = rounded(matmul_nt(up_low, w_out_cross))
    d_out_cross = matmul_tn(ctx_cross_low, up_low)
    dqkv_cross, _ = attend_local_back(q_cross, kv_cross, p_cross, ctx_cross, g_ctx, False)
    g_memory = cots[1] + sum_group(place, matmul_nt(dqkv_cross[:, width:], w_cross[:, width:]))
    g_norm_c = sum_group(place, matmul_nt(dqkv_cross[:, :width], w_cross[:, :width]))
    d_cross = jnp.concatenate(
        [
            matmul_tn(norm_c, dqkv_cross[:, :width]),
            matmul_tn(memory_low, dqkv_cross[:, width:]),
        ],
        axis=1,
    )
    g_part, gg4 = rms_back(dec_mid, gains[4], g_norm_c)
    g_dec_mid = g_dec_cross + g_part
    up_low = both_cores(place, rounded(g_dec_mid))
    g_ctx = rounded(matmul_nt(up_low, w_out_dec))
    d_out_dec = matmul_tn(ctx_dec_low, up_low)
    dqkv_dec, d_table_dec = attend_local_back(qkv_dec, qkv_dec, p_dec, ctx_dec, g_ctx, True)
    g_norm_b = sum_group(place, matmul_nt(dqkv_dec, w_dec))
    d_dec = matmul_tn(norm_b, dqkv_dec)
    g_part, gg3 = rms_back(dec_values, gains[3], g_norm_b)
    grad_dec_half = g_dec_mid + g_part

    g_enc_last, gg2 = rms_back(enc_last, gains[2], g_memory)
    g_enc_mid, gg1, d_hin_enc, d_hout_enc = group_feed_back(
        place, enc_mid, gains[1], w_hin_enc, w_hout_enc, enc_kept, g_enc_last
    )
    up_low = both_cores(place, rounded(g_enc_mid))
    g_ctx = rounded(matmul_nt(up_low, w_out_enc))
    d_out_enc = matmul_tn(ctx_enc_low, up_low)
    dqkv_enc, d_table_enc = attend_local_back(qkv_enc, qkv_enc, p_enc, ctx_enc, g_ctx, True)
    g_norm_a = sum_group(place, matmul_nt(dqkv_enc, w_enc))
    d_enc = matmul_tn(norm_a, dqkv_enc)
    g_part, gg0 = rms_back(enc_values, gains[0], g_norm_a)
    grad_enc_half = g_enc_mid + g_part

    def in_parts(grads):
        return grads.reshape(depth, 2, WAYS * own, grads.shape[1])

    def out_parts(grads):
        return grads.reshape(2, depth, own, D).transpose(1, 0, 2, 3)

    def to_rows(shard):
        return exchange_columns(place, rounded(shard).reshape(WAYS, own, -1)).astype(jnp.float32)

    shard_hin_dec = to_rows(scatter_rows(place, in_parts(d_hin_dec)))
    shard_hout_dec = scatter_rows(place, d_hout_dec.reshape(depth, 2, ff_own, D))
    shard_cross = to_rows(scatter_rows(place, in_parts(d_cross)))
    shard_dec = to_rows(scatter_rows(place, in_parts(d_dec)))
    shard_hin_enc = to_rows(scatter_rows(place, in_parts(d_hin_enc)))
    shard_hout_enc = scatter_rows(place, d_hout_enc.reshape(depth, 2, ff_own, D))
    outs = [scatter_rows(place, out_parts(g)) for g in (d_out_cross, d_out_dec, d_out_enc)]
    shard_enc = to_rows(scatter_rows(place, in_parts(d_enc)))
    shard_out = turn(rounded(jnp.stack(outs[::-1])), depth).astype(jnp.float32)
    shard_out = jnp.stack([shard_out[0], shard_out[1], shard_out[2]])
    shard_in = jnp.stack([shard_enc, shard_dec, shard_cross])
    shard_in = shard_in.reshape(3, WAYS, own, 3, width).transpose(0, 3, 2, 1, 4)
    shard_in = shard_in.reshape(3, 3, own, D)
    shard_hin = jnp.stack([shard_hin_enc, shard_hin_dec])
    shard_hin = shard_hin.reshape(2, WAYS, own, 2, 2 * depth, ff_own).transpose(0, 3, 2, 4, 1, 5)
    shard_hin = shard_hin.reshape(2, 2, own, WAYS * ff)
    shard_hout = jnp.stack([shard_hout_enc, shard_hout_dec])

    buckets = position_bias.shape[1]
    grad_enc_bias = d_table_enc[:, : 2 * length - 1]
    grad_dec_bias = d_table_dec[:, :length][:, ::-1]
    grad_position = jnp.stack(
        [
            bucket_grad(enc_buckets, grad_enc_bias, buckets),
            bucket_grad(dec_buckets, grad_dec_bias, buckets),
        ]
    )
    grad_position = lax.dynamic_update_slice_in_dim(
        jnp.zeros_like(position_bias), grad_position, q * heads, 2
    )
    grad_gains = jnp.stack([gg0, gg1, gg2, gg3, gg4, gg5, gg6])
    grad_gains = jnp.where(place.x == 0, grad_gains, 0.0)
    small = jnp.concatenate([grad_gains.reshape(-1, 128), grad_position.reshape(-1, 128)])
    small = sum_everywhere(place, small)
    cut = grad_gains.size // 128
    grad_gains = small[:cut].reshape(grad_gains.shape)
    grad_position = small[cut:].reshape(grad_position.shape)
    shard_gains = lax.dynamic_slice_in_dim(
        grad_gains, (place.z * 8 + lax.axis_index("seq")) * own, own, 1
    )

    squares = [v * v for v in (shard_in, shard_out, shard_hin, shard_hout)]
    columns = [jnp.sum(v, axis=-2) for v in squares]
    flat = sum_everywhere(place, jnp.concatenate([v.reshape(-1, 128) for v in columns]))
    totals = []
    at = 0
    for v in columns:
        count = v.size // 128
        totals.append(flat[at : at + count].reshape(v.shape))
        at += count

    def mean_rows(v):
        return 0.5 * jnp.mean(v, axis=-1)

    return (
        give_back(place, rounded(memory)),
        give_back(place, rounded(dec_final)),
        give_back(place, grad_enc_half),
        give_back(place, grad_dec_half),
        shard_in,
        shard_out,
        shard_hin,
        shard_hout,
        shard_gains,
        grad_position,
        mean_rows(squares[0]),
        0.5 * totals[0] / D,
        mean_rows(squares[1]),
        0.5 * totals[1] / D,
        mean_rows(squares[2]),
        0.5 * totals[2] / D,
        mean_rows(squares[3]),
        0.5 * totals[3] / FF,
    )


def body(mesh):
    depth, seq = mesh.shape["dp"], mesh.shape["seq"]

    def run(*args):
        seqs, rows = args[0].shape[:2]
        fits = (
            depth == WAYS
            and seq == 8
            and seqs == 2
            and (rows * 8) % TILE == 0
            and args[1].shape == args[0].shape
        )
        return grouped(depth, *args) if fits else local(*args)

    return run


def solution(mesh):
    return jax.shard_map(
        body(mesh),
        mesh=mesh,
        in_specs=(
            P("dp", "seq", None),
            P("dp", "seq", None),
            P("dp"),
            P("dp"),
            P(),
            P(),
            P(None, None, ("dp", "seq"), None),
            P(None, ("dp", "seq"), None),
            P(None, None, ("dp", "seq"), None),
            P(None, ("dp", "seq"), None),
            P(None, ("dp", "seq")),
            P(),
            P("dp", "seq", None),
            P("dp", "seq", None),
        ),
        out_specs=(
            P("dp", "seq", None),
            P("dp", "seq", None),
            P("dp", "seq", None),
            P("dp", "seq", None),
            P(None, None, ("dp", "seq"), None),
            P(None, ("dp", "seq"), None),
            P(None, None, ("dp", "seq"), None),
            P(None, ("dp", "seq"), None),
            P(None, ("dp", "seq")),
            P(),
            P(None, None, ("dp", "seq")),
            P(),
            P(None, ("dp", "seq")),
            P(),
            P(None, None, ("dp", "seq")),
            P(),
            P(None, ("dp", "seq")),
            P(),
        ),
        check_vma=False,
    )
```

```python
import functools
import math

import jax
import jax.numpy as jnp
from jax import lax
from jax.experimental import pallas as pl
from jax.experimental.pallas import tpu as pltpu
from jax.sharding import Mesh, PartitionSpec as P

D = 768
HEADS = 12
HEAD = 64
FF = 2048


EPSILON = 1e-06
NEGATIVE = -1e30
HIGHEST = lax.Precision.HIGHEST


def rounded(values):
    return values.astype(jnp.bfloat16)


def rows_first(values):
    return values.transpose(0, 2, 1)


def rms_norm(values, gain_row):
    return (
        values * lax.rsqrt(jnp.mean(values * values, axis=-1, keepdims=True) + EPSILON) * gain_row
    )


def rms_back(values, gain_row, upstream):
    _, pullback = jax.vjp(rms_norm, values, gain_row)
    return pullback(upstream)


def gated_unit(gate_up):
    return jax.nn.gelu(gate_up[0], approximate=True) * gate_up[1]


def offset_table(buckets, layer_bias):
    choose = (buckets[:, None] == jnp.arange(layer_bias.shape[0], dtype=jnp.int32)[None, :]).astype(
        jnp.float32
    )
    return jnp.dot(choose, layer_bias, precision=HIGHEST).T


def bucket_grad(buckets, grad_bias, bucket_count):
    choose = (buckets[:, None] == jnp.arange(bucket_count, dtype=jnp.int32)[None, :]).astype(
        jnp.float32
    )
    return jnp.dot(choose.T, grad_bias.T, precision=HIGHEST)


def hankel_block(window, rows, cols):
    heads_here, length = (window.shape[0], window.shape[1])
    tiled = jnp.tile(window, (1, rows + 1))[:, : rows * (length + 1)]
    return tiled.reshape(heads_here, rows, length + 1)[:, :, :cols]


def bias_block(variant, table, row_start, col_start, rows, cols, extent):
    span = rows + cols - 1
    if variant == "enc":
        base = col_start - row_start - (rows - 1) + (extent - 1)
        window = lax.dynamic_slice_in_dim(table, base, span, 1)
        return hankel_block(window, rows, cols)[:, ::-1, :]
    widened = jnp.concatenate(
        [jnp.broadcast_to(table[:, :1], (table.shape[0], extent - 1)), table], axis=1
    )
    base = row_start - col_start - (cols - 1) + (extent - 1)
    window = lax.dynamic_slice_in_dim(widened, base, span, 1)
    return hankel_block(window, rows, cols)[:, :, ::-1]


def visible_mask(variant, row_ids, col_ids, lengths):
    visible = col_ids[None, None, :] < lengths[:, None, None]
    if variant == "dec":
        visible = visible & (col_ids[None, None, :] <= row_ids[None, :, None])
    return visible[:, None]


def block_scores(query_heads, key_heads, row_ids, col_ids, lengths, variant, offset_bias, extent):
    factor = HEAD ** (-0.5)
    scores = (
        jnp.einsum("sqhe,skhe->shqk", query_heads, key_heads, preferred_element_type=jnp.float32)
        * factor
    )
    if offset_bias is not None:
        scores = (
            scores
            + bias_block(
                variant,
                offset_bias,
                row_ids[0],
                col_ids[0],
                row_ids.shape[0],
                col_ids.shape[0],
                extent,
            )[None]
        )
    return (scores, visible_mask(variant, row_ids, col_ids, lengths))


def row_products(grad_context, context):
    seqs_here, rows_here = (context.shape[0], context.shape[1])
    return jnp.sum(
        (grad_context.astype(jnp.float32) * context).reshape(seqs_here, rows_here, HEADS, HEAD),
        axis=-1,
    ).transpose(0, 2, 1)


def attend(queries, row_ids, lengths, variant, offset_bias, extent, fold_keys):
    seqs_here, rows_here = (queries.shape[0], queries.shape[1])
    query_heads = queries.reshape(seqs_here, rows_here, HEADS, HEAD)

    def fold_step(carried, pieces, begin_at):
        key_rows, value_rows = pieces
        block_len = math.gcd(key_rows.shape[1], 512)

        def block_step(block_id, running):
            row_max, row_sum, weighted = running
            offset_in = block_id * block_len
            key_heads = lax.dynamic_slice_in_dim(key_rows, offset_in, block_len, 1).reshape(
                seqs_here, block_len, HEADS, HEAD
            )
            value_heads = lax.dynamic_slice_in_dim(value_rows, offset_in, block_len, 1).reshape(
                seqs_here, block_len, HEADS, HEAD
            )
            col_ids = offset_in + jnp.arange(block_len, dtype=jnp.int32)
            scores, visible = block_scores(
                query_heads, key_heads, row_ids, col_ids, lengths, variant, offset_bias, extent
            )
            new_max = jnp.maximum(row_max, jnp.max(jnp.where(visible, scores, NEGATIVE), axis=-1))
            weights = jnp.where(visible, jnp.exp(scores - new_max[..., None]), 0.0)
            shrink = jnp.exp(row_max - new_max)
            row_sum = row_sum * shrink + jnp.sum(weights, axis=-1)
            weighted = weighted * shrink[..., None] + jnp.einsum(
                "shqk,skhe->shqe", rounded(weights), value_heads, preferred_element_type=jnp.float32
            )
            return (new_max, row_sum, weighted)

        return lax.fori_loop(0, key_rows.shape[1] // block_len, block_step, carried)

    initial = (
        jnp.full((seqs_here, HEADS, rows_here), NEGATIVE, jnp.float32),
        jnp.zeros((seqs_here, HEADS, rows_here), jnp.float32),
        jnp.zeros((seqs_here, HEADS, rows_here, HEAD), jnp.float32),
    )
    row_max, row_sum, weighted = fold_keys(fold_step, initial)
    context = (
        (weighted / row_sum[..., None])
        .transpose(0, 2, 1, 3)
        .reshape(seqs_here, rows_here, HEADS * HEAD)
    )
    return (context, row_max + jnp.log(row_sum))


def attend_back(
    queries,
    log_sums,
    row_dots,
    grad_context,
    row_ids,
    lengths,
    variant,
    offset_bias,
    extent,
    fold_keys,
):
    seqs_here, rows_here = (queries.shape[0], queries.shape[1])
    query_heads = queries.reshape(seqs_here, rows_here, HEADS, HEAD)
    grad_heads = grad_context.reshape(seqs_here, rows_here, HEADS, HEAD)
    bias_width = offset_bias.shape[1] if offset_bias is not None else 1
    factor = HEAD ** (-0.5)

    def fold_step(carried, pieces, begin_at):
        key_rows, value_rows = pieces
        block_len = math.gcd(key_rows.shape[1], 512)

        def block_step(block_id, running):
            grad_query, grad_bias = (running[0], running[-1])
            offset_in = block_id * block_len
            key_heads = lax.dynamic_slice_in_dim(key_rows, offset_in, block_len, 1).reshape(
                seqs_here, block_len, HEADS, HEAD
            )
            value_heads = lax.dynamic_slice_in_dim(value_rows, offset_in, block_len, 1).reshape(
                seqs_here, block_len, HEADS, HEAD
            )
            col_ids = offset_in + jnp.arange(block_len, dtype=jnp.int32)
            scores, visible = block_scores(
                query_heads, key_heads, row_ids, col_ids, lengths, variant, offset_bias, extent
            )
            weights = jnp.where(visible, jnp.exp(scores - log_sums[..., None]), 0.0)
            grad_weights = jnp.einsum(
                "sqhe,skhe->shqk", grad_heads, value_heads, preferred_element_type=jnp.float32
            )
            grad_scores = weights * (grad_weights - row_dots[..., None])
            if offset_bias is not None:

                def table_block(table_values):
                    return bias_block(
                        variant,
                        table_values,
                        row_ids[0],
                        col_ids[0],
                        row_ids.shape[0],
                        col_ids.shape[0],
                        extent,
                    )

                _, table_pull = jax.vjp(table_block, offset_bias)
                grad_bias = grad_bias + table_pull(jnp.sum(grad_scores, axis=0))[0]
            grad_raw = rounded(grad_scores * factor)
            grad_query = grad_query + jnp.einsum(
                "shqk,skhe->shqe", grad_raw, key_heads, preferred_element_type=jnp.float32
            )
            return (grad_query, grad_bias)

        return lax.fori_loop(0, key_rows.shape[1] // block_len, block_step, carried)

    query_start = jnp.zeros((seqs_here, HEADS, rows_here, HEAD), jnp.float32)
    bias_start = jnp.zeros((HEADS, bias_width), jnp.float32)
    initial = (query_start, bias_start)
    result = fold_keys(fold_step, initial)
    grad_query = result[0].transpose(0, 2, 1, 3).reshape(seqs_here, rows_here, HEADS * HEAD)
    return (grad_query, None, None, result[1])


def owned_key_grads(
    key_rows, value_rows, col_ids, lengths, variant, offset_bias, extent, fold_queries
):
    seqs_here, keys_here = (key_rows.shape[0], key_rows.shape[1])
    key_heads = key_rows.reshape(seqs_here, keys_here, HEADS, HEAD)
    value_heads = value_rows.reshape(seqs_here, keys_here, HEADS, HEAD)
    factor = HEAD ** (-0.5)

    def fold_step(carried, pieces, begin_at):
        query_rows, grad_rows, log_rows, dot_rows = pieces
        block_len = math.gcd(query_rows.shape[1], 512)

        def block_step(block_id, running):
            grad_keys, grad_values = running
            offset_in = block_id * block_len
            query_heads = lax.dynamic_slice_in_dim(query_rows, offset_in, block_len, 1).reshape(
                seqs_here, block_len, HEADS, HEAD
            )
            grad_heads = lax.dynamic_slice_in_dim(grad_rows, offset_in, block_len, 1).reshape(
                seqs_here, block_len, HEADS, HEAD
            )
            log_block = lax.dynamic_slice_in_dim(log_rows, offset_in, block_len, 1).transpose(
                0, 2, 1
            )
            dot_block = lax.dynamic_slice_in_dim(dot_rows, offset_in, block_len, 1).transpose(
                0, 2, 1
            )
            row_ids = offset_in + jnp.arange(block_len, dtype=jnp.int32)
            scores, visible = block_scores(
                query_heads, key_heads, row_ids, col_ids, lengths, variant, offset_bias, extent
            )
            weights = jnp.where(visible, jnp.exp(scores - log_block[..., None]), 0.0)
            grad_weights = jnp.einsum(
                "sqhe,skhe->shqk", grad_heads, value_heads, preferred_element_type=jnp.float32
            )
            grad_scores = weights * (grad_weights - dot_block[..., None])
            grad_raw = rounded(grad_scores * factor)
            grad_keys = grad_keys + jnp.einsum(
                "shqk,sqhe->skhe", grad_raw, query_heads, preferred_element_type=jnp.float32
            ).reshape(seqs_here, keys_here, HEADS * HEAD)
            grad_values = grad_values + jnp.einsum(
                "shqk,sqhe->skhe", rounded(weights), grad_heads, preferred_element_type=jnp.float32
            ).reshape(seqs_here, keys_here, HEADS * HEAD)
            return (grad_keys, grad_values)

        return lax.fori_loop(0, query_rows.shape[1] // block_len, block_step, carried)

    initial = (
        jnp.zeros((seqs_here, keys_here, HEADS * HEAD), jnp.float32),
        jnp.zeros((seqs_here, keys_here, HEADS * HEAD), jnp.float32),
    )
    return fold_queries(fold_step, initial)


def feed_forward(residual, gain_row, weights_in, weights_out):
    normed_low = rounded(rms_norm(residual, gain_row))
    gate_up = jnp.einsum(
        "srd,jdf->jsrf", normed_low, weights_in, preferred_element_type=jnp.float32
    )
    hidden = rounded(gated_unit(gate_up))
    output = jnp.einsum("srf,fd->srd", hidden, weights_out, preferred_element_type=jnp.float32)
    return (residual + output, (normed_low, gate_up, hidden))


def feed_back(residual, gain_row, weights_in, weights_out, kept_values, upstream):
    normed_low, gate_up, hidden = kept_values
    upstream_low = rounded(upstream)
    grad_out_weights = jnp.einsum(
        "srf,srd->fd", hidden, upstream_low, preferred_element_type=jnp.float32
    )
    grad_hidden = jnp.einsum(
        "srd,fd->srf", upstream_low, weights_out, preferred_element_type=jnp.float32
    )
    _, pullback = jax.vjp(gated_unit, gate_up)
    grad_gate_up = rounded(pullback(grad_hidden)[0])
    grad_in_weights = jnp.einsum(
        "srd,jsrf->jdf", normed_low, grad_gate_up, preferred_element_type=jnp.float32
    )
    grad_normed = jnp.einsum(
        "jsrf,jdf->srd", grad_gate_up, weights_in, preferred_element_type=jnp.float32
    )
    grad_residual, grad_gain = rms_back(residual, gain_row, grad_normed)
    return (upstream + grad_residual, grad_gain, grad_in_weights, grad_out_weights)


def local(
    enc_input,
    dec_input,
    enc_lengths,
    dec_lengths,
    enc_buckets,
    dec_buckets,
    attention_in,
    attention_out,
    hidden_in,
    hidden_out,
    norm_gains,
    position_bias,
    enc_cotangent,
    dec_cotangent,
):
    full_in, full_out, full_hidden_in, full_hidden_out, full_gains = (
        lax.all_gather(attention_in, ("dp", "seq"), axis=2, tiled=True),
        lax.all_gather(attention_out, ("dp", "seq"), axis=1, tiled=True),
        lax.all_gather(hidden_in, ("dp", "seq"), axis=2, tiled=True),
        lax.all_gather(hidden_out, ("dp", "seq"), axis=1, tiled=True),
        lax.all_gather(norm_gains, ("dp", "seq"), axis=1, tiled=True),
    )
    gain_rows = full_gains.astype(jnp.float32)
    enc_rows = enc_input.shape[1]
    dec_rows = dec_input.shape[1]
    seq_index = lax.axis_index("seq")
    enc_ids = seq_index * enc_rows + jnp.arange(enc_rows, dtype=jnp.int32)
    dec_ids = seq_index * dec_rows + jnp.arange(dec_rows, dtype=jnp.int32)
    enc_extent = (enc_buckets.shape[0] + 1) // 2
    dec_extent = dec_buckets.shape[0]
    enc_table = offset_table(enc_buckets, position_bias[0])
    dec_table = offset_table(dec_buckets, position_bias[1])
    enc_values = enc_input.astype(jnp.float32)
    norm_a_low = rounded(rms_norm(enc_values, gain_rows[0]))
    enc_qkv = rounded(
        jnp.einsum("srd,jde->jsre", norm_a_low, full_in[0], preferred_element_type=jnp.float32)
    )
    enc_context, enc_logs = attend(
        enc_qkv[0],
        enc_ids,
        enc_lengths,
        "enc",
        enc_table,
        enc_extent,
        lambda folder, initial: folder(
            initial,
            (
                lax.all_gather(enc_qkv[1], "seq", axis=1, tiled=True),
                lax.all_gather(enc_qkv[2], "seq", axis=1, tiled=True),
            ),
            jnp.int32(0),
        ),
    )
    enc_context_low = rounded(enc_context)
    enc_mid = enc_values + jnp.einsum(
        "srd,de->sre", enc_context_low, full_out[0], preferred_element_type=jnp.float32
    )
    enc_last, enc_ffn_kept = feed_forward(
        enc_mid, gain_rows[1], full_hidden_in[0], full_hidden_out[0]
    )
    memory = rms_norm(enc_last, gain_rows[2])
    memory_low = rounded(memory)
    dec_values = dec_input.astype(jnp.float32)
    norm_b_low = rounded(rms_norm(dec_values, gain_rows[3]))
    dec_qkv = rounded(
        jnp.einsum("srd,jde->jsre", norm_b_low, full_in[1], preferred_element_type=jnp.float32)
    )
    dec_context, dec_logs = attend(
        dec_qkv[0],
        dec_ids,
        dec_lengths,
        "dec",
        dec_table,
        dec_extent,
        lambda folder, initial: folder(
            initial,
            (
                lax.all_gather(dec_qkv[1], "seq", axis=1, tiled=True),
                lax.all_gather(dec_qkv[2], "seq", axis=1, tiled=True),
            ),
            jnp.int32(0),
        ),
    )
    dec_context_low = rounded(dec_context)
    dec_mid = dec_values + jnp.einsum(
        "srd,de->sre", dec_context_low, full_out[1], preferred_element_type=jnp.float32
    )
    norm_c_low = rounded(rms_norm(dec_mid, gain_rows[4]))
    cross_query = rounded(
        jnp.einsum("srd,de->sre", norm_c_low, full_in[2, 0], preferred_element_type=jnp.float32)
    )
    cross_pair = rounded(
        jnp.einsum("srd,jde->jsre", memory_low, full_in[2, 1:], preferred_element_type=jnp.float32)
    )
    cross_context, cross_logs = attend(
        cross_query,
        dec_ids,
        enc_lengths,
        "cross",
        None,
        0,
        lambda folder, initial: folder(
            initial,
            (
                lax.all_gather(cross_pair[0], "seq", axis=1, tiled=True),
                lax.all_gather(cross_pair[1], "seq", axis=1, tiled=True),
            ),
            jnp.int32(0),
        ),
    )
    cross_low = rounded(cross_context)
    dec_cross = dec_mid + jnp.einsum(
        "srd,de->sre", cross_low, full_out[2], preferred_element_type=jnp.float32
    )
    dec_last, dec_ffn_kept = feed_forward(
        dec_cross, gain_rows[5], full_hidden_in[1], full_hidden_out[1]
    )
    dec_final = rms_norm(dec_last, gain_rows[6])
    grad_dec_last, grad_gain_six = rms_back(
        dec_last, gain_rows[6], dec_cotangent.astype(jnp.float32)
    )
    grad_dec_cross, grad_gain_five, grad_hin_one, grad_hout_one = feed_back(
        dec_cross, gain_rows[5], full_hidden_in[1], full_hidden_out[1], dec_ffn_kept, grad_dec_last
    )
    upstream_low = rounded(grad_dec_cross)
    grad_out_two = jnp.einsum(
        "srd,sre->de", cross_low, upstream_low, preferred_element_type=jnp.float32
    )
    grad_cross_context = rounded(
        jnp.einsum("sre,de->srd", upstream_low, full_out[2], preferred_element_type=jnp.float32)
    )
    cross_dots = row_products(grad_cross_context, cross_context)
    cross_grad_query, cross_grad_keys, cross_grad_values, _ = attend_back(
        cross_query,
        cross_logs,
        cross_dots,
        grad_cross_context,
        dec_ids,
        enc_lengths,
        "cross",
        None,
        0,
        lambda folder, initial: folder(
            initial,
            (
                lax.all_gather(cross_pair[0], "seq", axis=1, tiled=True),
                lax.all_gather(cross_pair[1], "seq", axis=1, tiled=True),
            ),
            jnp.int32(0),
        ),
    )
    cross_query_low = rounded(cross_grad_query)
    grad_query_two = jnp.einsum(
        "srd,sre->de", norm_c_low, cross_query_low, preferred_element_type=jnp.float32
    )
    grad_norm_c = jnp.einsum(
        "sre,de->srd", cross_query_low, full_in[2, 0], preferred_element_type=jnp.float32
    )
    grad_mid_part, grad_gain_four = rms_back(dec_mid, gain_rows[4], grad_norm_c)
    grad_dec_mid = grad_dec_cross + grad_mid_part
    upstream_low = rounded(grad_dec_mid)
    grad_out_one = jnp.einsum(
        "srd,sre->de", dec_context_low, upstream_low, preferred_element_type=jnp.float32
    )
    grad_dec_context = rounded(
        jnp.einsum("sre,de->srd", upstream_low, full_out[1], preferred_element_type=jnp.float32)
    )
    dec_dots = row_products(grad_dec_context, dec_context)
    dec_grad_query, dec_grad_keys, dec_grad_values, grad_dec_bias = attend_back(
        dec_qkv[0],
        dec_logs,
        dec_dots,
        grad_dec_context,
        dec_ids,
        dec_lengths,
        "dec",
        dec_table,
        dec_extent,
        lambda folder, initial: folder(
            initial,
            (
                lax.all_gather(dec_qkv[1], "seq", axis=1, tiled=True),
                lax.all_gather(dec_qkv[2], "seq", axis=1, tiled=True),
            ),
            jnp.int32(0),
        ),
    )
    cross_key_grad, cross_value_grad = owned_key_grads(
        cross_pair[0],
        cross_pair[1],
        enc_ids,
        enc_lengths,
        "cross",
        None,
        0,
        lambda folder, initial: folder(
            initial,
            (
                lax.all_gather(cross_query, "seq", axis=1, tiled=True),
                lax.all_gather(grad_cross_context, "seq", axis=1, tiled=True),
                lax.all_gather(
                    rows_first(cross_logs).astype(jnp.bfloat16), "seq", axis=1, tiled=True
                ).astype(jnp.float32),
                lax.all_gather(
                    rows_first(cross_dots).astype(jnp.bfloat16), "seq", axis=1, tiled=True
                ).astype(jnp.float32),
            ),
            jnp.int32(0),
        ),
    )
    dec_key_grad, dec_value_grad = owned_key_grads(
        dec_qkv[1],
        dec_qkv[2],
        dec_ids,
        dec_lengths,
        "dec",
        dec_table,
        dec_extent,
        lambda folder, initial: folder(
            initial,
            (
                lax.all_gather(dec_qkv[0], "seq", axis=1, tiled=True),
                lax.all_gather(grad_dec_context, "seq", axis=1, tiled=True),
                lax.all_gather(
                    rows_first(dec_logs).astype(jnp.bfloat16), "seq", axis=1, tiled=True
                ).astype(jnp.float32),
                lax.all_gather(
                    rows_first(dec_dots).astype(jnp.bfloat16), "seq", axis=1, tiled=True
                ).astype(jnp.float32),
            ),
            jnp.int32(0),
        ),
    )
    pair_grads = rounded(jnp.stack([cross_key_grad, cross_value_grad]))
    grad_pair_two = jnp.einsum(
        "srd,jsre->jde", memory_low, pair_grads, preferred_element_type=jnp.float32
    )
    grad_memory = jnp.einsum(
        "jsre,jde->srd", pair_grads, full_in[2, 1:], preferred_element_type=jnp.float32
    )
    dec_grads = rounded(jnp.stack([dec_grad_query, dec_key_grad, dec_value_grad]))
    grad_in_one = jnp.einsum(
        "srd,jsre->jde", norm_b_low, dec_grads, preferred_element_type=jnp.float32
    )
    grad_norm_b = jnp.einsum(
        "jsre,jde->srd", dec_grads, full_in[1], preferred_element_type=jnp.float32
    )
    grad_dec_part, grad_gain_three = rms_back(dec_values, gain_rows[3], grad_norm_b)
    grad_dec_input = grad_dec_mid + grad_dec_part
    grad_memory_total = enc_cotangent.astype(jnp.float32) + grad_memory
    grad_enc_last, grad_gain_two = rms_back(enc_last, gain_rows[2], grad_memory_total)
    grad_enc_mid, grad_gain_one, grad_hin_zero, grad_hout_zero = feed_back(
        enc_mid, gain_rows[1], full_hidden_in[0], full_hidden_out[0], enc_ffn_kept, grad_enc_last
    )
    upstream_low = rounded(grad_enc_mid)
    grad_out_zero = jnp.einsum(
        "srd,sre->de", enc_context_low, upstream_low, preferred_element_type=jnp.float32
    )
    grad_enc_context = rounded(
        jnp.einsum("sre,de->srd", upstream_low, full_out[0], preferred_element_type=jnp.float32)
    )
    enc_dots = row_products(grad_enc_context, enc_context)
    enc_grad_query, enc_grad_keys, enc_grad_values, grad_enc_bias = attend_back(
        enc_qkv[0],
        enc_logs,
        enc_dots,
        grad_enc_context,
        enc_ids,
        enc_lengths,
        "enc",
        enc_table,
        enc_extent,
        lambda folder, initial: folder(
            initial,
            (
                lax.all_gather(enc_qkv[1], "seq", axis=1, tiled=True),
                lax.all_gather(enc_qkv[2], "seq", axis=1, tiled=True),
            ),
            jnp.int32(0),
        ),
    )
    enc_key_grad, enc_value_grad = owned_key_grads(
        enc_qkv[1],
        enc_qkv[2],
        enc_ids,
        enc_lengths,
        "enc",
        enc_table,
        enc_extent,
        lambda folder, initial: folder(
            initial,
            (
                lax.all_gather(enc_qkv[0], "seq", axis=1, tiled=True),
                lax.all_gather(grad_enc_context, "seq", axis=1, tiled=True),
                lax.all_gather(
                    rows_first(enc_logs).astype(jnp.bfloat16), "seq", axis=1, tiled=True
                ).astype(jnp.float32),
                lax.all_gather(
                    rows_first(enc_dots).astype(jnp.bfloat16), "seq", axis=1, tiled=True
                ).astype(jnp.float32),
            ),
            jnp.int32(0),
        ),
    )
    enc_grads = rounded(jnp.stack([enc_grad_query, enc_key_grad, enc_value_grad]))
    grad_in_zero = jnp.einsum(
        "srd,jsre->jde", norm_a_low, enc_grads, preferred_element_type=jnp.float32
    )
    grad_norm_a = jnp.einsum(
        "jsre,jde->srd", enc_grads, full_in[0], preferred_element_type=jnp.float32
    )
    grad_enc_part, grad_gain_zero = rms_back(enc_values, gain_rows[0], grad_norm_a)
    grad_enc_input = grad_enc_mid + grad_enc_part
    grad_cross_in = jnp.concatenate([grad_query_two[None], grad_pair_two], axis=0)
    grad_attention_in = jnp.stack([grad_in_zero, grad_in_one, grad_cross_in])
    grad_attention_out = jnp.stack([grad_out_zero, grad_out_one, grad_out_two])
    grad_hidden_in = jnp.stack([grad_hin_zero, grad_hin_one])
    grad_hidden_out = jnp.stack([grad_hout_zero, grad_hout_one])
    grad_gains = jnp.stack(
        [
            grad_gain_zero,
            grad_gain_one,
            grad_gain_two,
            grad_gain_three,
            grad_gain_four,
            grad_gain_five,
            grad_gain_six,
        ]
    )
    shard_in, shard_out, shard_hin, shard_hout, shard_gains = (
        lax.psum_scatter(grad_attention_in, ("dp", "seq"), scatter_dimension=2, tiled=True),
        lax.psum_scatter(grad_attention_out, ("dp", "seq"), scatter_dimension=1, tiled=True),
        lax.psum_scatter(grad_hidden_in, ("dp", "seq"), scatter_dimension=2, tiled=True),
        lax.psum_scatter(grad_hidden_out, ("dp", "seq"), scatter_dimension=1, tiled=True),
        lax.psum_scatter(grad_gains, ("dp", "seq"), scatter_dimension=1, tiled=True),
    )
    bucket_count = position_bias.shape[1]
    grad_position = jnp.stack(
        [
            bucket_grad(enc_buckets, grad_enc_bias, bucket_count),
            bucket_grad(dec_buckets, grad_dec_bias, bucket_count),
        ]
    )
    squares_in = shard_in * shard_in
    squares_out = shard_out * shard_out
    squares_hin = shard_hin * shard_hin
    squares_hout = shard_hout * shard_hout
    col_in, col_out, col_hin, col_hout, grad_position = lax.psum(
        (
            jnp.sum(squares_in, axis=2),
            jnp.sum(squares_out, axis=1),
            jnp.sum(squares_hin, axis=2),
            jnp.sum(squares_hout, axis=1),
            grad_position,
        ),
        ("dp", "seq"),
    )
    return (
        rounded(memory),
        rounded(dec_final),
        grad_enc_input,
        grad_dec_input,
        shard_in,
        shard_out,
        shard_hin,
        shard_hout,
        shard_gains,
        grad_position,
        0.5 * jnp.mean(squares_in, axis=-1),
        0.5 * col_in / D,
        0.5 * jnp.mean(squares_out, axis=-1),
        0.5 * col_out / D,
        0.5 * jnp.mean(squares_hin, axis=-1),
        0.5 * col_hin / D,
        0.5 * jnp.mean(squares_hout, axis=-1),
        0.5 * col_hout / FF,
    )


WAYS = 4
SETS = HEADS // WAYS
WIDTH = SETS * HEAD
VMEM_LIMIT = 16 * 2**20


def swap(values, axis):
    return lax.ppermute(values, axis, [(0, 1), (1, 0)])


def shift_z(values, hops, count):
    return lax.ppermute(values, "dp", [(i, (i + hops) % count) for i in range(count)])


def pair_up(mine, other, bit):
    first = bit == 0
    return jnp.stack([jnp.where(first, mine, other), jnp.where(first, other, mine)])


def pick(values, index, axis=0):
    return lax.dynamic_index_in_dim(values, index, axis, keepdims=False)


class Place:
    def __init__(self, depth):
        self.depth = depth
        self.z, self.y, self.x, self.c = [lax.axis_index(a) for a in ("dp", "y", "x", "c")]
        self.q = 2 * self.x + self.c
        self.index = (self.z * 2 + self.y) * WAYS + self.q


def exchange_columns(place, pieces):
    halves = pieces.reshape((2, 2) + pieces.shape[1:])
    got = swap(pick(halves, 1 - place.x), "x")
    both = pair_up(pick(halves, place.x), got, place.x)
    got = swap(pick(both, 1 - place.c, 1), "c")
    whole = pair_up(pick(both, place.c, 1), got, place.c)
    return jnp.swapaxes(whole, 0, 1).reshape(pieces.shape)


def along_z(place, piece, *earlier):
    depth = place.depth
    held = jnp.zeros((depth,) + piece.shape, piece.dtype)
    arrivals = [shift_z(piece, k, depth) for k in range(1, depth)]
    if earlier:
        arrivals = [after(block, *earlier) for block in arrivals]
    for hops, block in enumerate([piece] + arrivals):
        held = lax.dynamic_update_index_in_dim(held, block, (place.z - hops) % depth, 0)
    return held


def along_y(place, held):
    other = swap(held, "y")
    first = place.y == 0
    pair = [jnp.where(first, held, other), jnp.where(first, other, held)]
    return jnp.stack(pair, axis=1).reshape(-1, held.shape[-1])


def scatter_y(place, parts):
    parts = parts.reshape((place.depth, 2) + parts.shape[1:])
    sent = swap(pick(parts, 1 - place.y, 1), "y")
    return pick(parts, place.y, 1).astype(F32) + sent.astype(F32)


def scatter_z(place, halves):
    depth = place.depth
    low = rounded(halves)
    total = pick(halves, place.z)
    for hops in range(1, depth):
        sent = shift_z(pick(low, (place.z + hops) % depth), hops, depth)
        total = total + sent.astype(F32)
    return total


def after(values, *earlier):
    return lax.optimization_barrier((values,) + earlier)[0]


def turn(values, depth):
    pairs = []
    for d in range(depth):
        for y in range(2):
            for q in range(WAYS):
                pairs.append((d * 8 + y * 4 + q, q * 8 + y * 4 + d))
    return lax.ppermute(values, ("dp", "y", "x", "c"), pairs)


def matmul(a, b):
    return jnp.dot(a, b, preferred_element_type=jnp.float32)


def matmul_nt(a, b):
    return lax.dot_general(a, b, (((1,), (1,)), ((), ())), preferred_element_type=jnp.float32)


def matmul_tn(a, b):
    return lax.dot_general(a, b, (((0,), (0,)), ((), ())), preferred_element_type=jnp.float32)


def call(kernel, name, outs, args, micros, scratch=()):
    whole = pl.BlockSpec(memory_space=pltpu.VMEM)
    arrays = [a[0] if isinstance(a, tuple) else a for a in args]
    specs = [a[1] if isinstance(a, tuple) else whole for a in args]
    shapes = tuple(jax.ShapeDtypeStruct(s, t) for s, t in outs)
    moved = sum(a.size * a.dtype.itemsize for a in list(arrays) + list(shapes))
    windows = any(isinstance(a, tuple) and a[1] is not SCALARS for a in args)
    return pl.pallas_call(
        kernel,
        grid=(1,) if windows else (),
        out_shape=shapes,
        in_specs=specs,
        out_specs=(whole,) * len(shapes),
        scratch_shapes=list(scratch),
        compiler_params=pltpu.CompilerParams(vmem_limit_bytes=VMEM_LIMIT),
        cost_estimate=pl.CostEstimate(
            flops=int(micros * 5e7), bytes_accessed=moved, transcendentals=0
        ),
        name=name,
    )(*arrays)


SCALARS = pl.BlockSpec(memory_space=pltpu.SMEM)
BF, F32 = jnp.bfloat16, jnp.float32


def column_block(array, index):
    rows, columns = array.shape
    return (array, pl.BlockSpec((rows, 2 * WIDTH), lambda _: (0, index)))


def norm_rows(values, gain):
    return values * lax.rsqrt(jnp.mean(values * values, axis=-1, keepdims=True) + EPSILON) * gain


def norm_back(values, gain, upstream):
    scale = lax.rsqrt(jnp.mean(values * values, axis=-1, keepdims=True) + EPSILON)
    unit = values * scale
    inner = upstream * gain
    grad = scale * (inner - unit * jnp.mean(inner * unit, axis=-1, keepdims=True))
    return grad, jnp.sum(upstream * unit, axis=0, keepdims=True)


def self_kernel(gain, q_at, x_ref, gains_ref, kva_ref, qa_ref, kvb_ref, qb_ref, *outs):
    n_ref, q_ref, kv_ref = outs
    n = norm_rows(x_ref[...].astype(F32), gains_ref[gain : gain + 1, :]).astype(BF)
    n_ref[...] = n
    for e, (kv, q) in enumerate(((kva_ref, qa_ref), (kvb_ref, qb_ref))):
        kv_ref[e] = matmul(n, kv[:, : 2 * WIDTH]).astype(BF)
        q_ref[e] = matmul(n, q[:, q_at : q_at + WIDTH]).astype(BF)


def self_project(x, gains, gain, kv_own, q_own, kv_sib, q_sib, q_at, name):
    rows = x.shape[0]
    return call(
        functools.partial(self_kernel, gain, q_at),
        name,
        [((rows, D), BF), ((2, rows, WIDTH), BF), ((2, rows, 2 * WIDTH), BF)],
        [x, gains, kv_own, q_own, kv_sib, q_sib],
        2.5,
    )


def memory_kernel(res_ref, part_ref, got_ref, gains_ref, kva_ref, kvb_ref, *outs):
    last_ref, low_ref, kv_ref = outs
    last = res_ref[...].astype(F32) + part_ref[...] + got_ref[...].astype(F32)
    last_ref[...] = last
    low = norm_rows(last, gains_ref[2:3, :]).astype(BF)
    low_ref[...] = low
    for e, kv in enumerate((kva_ref, kvb_ref)):
        kv_ref[e] = matmul(low, kv[...]).astype(BF)


def cross_kernel(q_at, res_ref, part_ref, got_ref, gains_ref, qa_ref, qb_ref, *outs):
    mid_ref, low_ref, q_ref = outs
    mid = res_ref[...].astype(F32) + part_ref[...] + got_ref[...].astype(F32)
    mid_ref[...] = mid
    low = norm_rows(mid, gains_ref[4:5, :]).astype(BF)
    low_ref[...] = low
    for e, q in enumerate((qa_ref, qb_ref)):
        q_ref[e] = matmul(low, q[:, q_at : q_at + WIDTH]).astype(BF)


def lay_out_keys(core, kv_ref, got_ref, keys):
    block = kv_ref.shape[1] // 4
    for e in range(2):
        for k in range(4):
            at = pl.multiple_of(block * (2 * k + core), block)
            keys[e, pl.ds(at, block), :] = kv_ref[e, k * block : (k + 1) * block, :]
            at = pl.multiple_of(block * (2 * k + 1 - core), block)
            keys[e, pl.ds(at, block), :] = got_ref[1 - e, k * block : (k + 1) * block, :]


def attend_kernel(causal, biased, *refs):
    if biased:
        scalars, q_ref, kv_ref, got_ref, table_ref, oa_ref, ob_ref = refs[:7]
    else:
        scalars, q_ref, kv_ref, got_ref, oa_ref, ob_ref = refs[:6]
    ctx_ref, p_ref, part_ref, low_ref, keys = refs[-5:]
    core, length = scalars[0], scalars[1]
    lay_out_keys(core, kv_ref, got_ref, keys)
    rows, extent = q_ref.shape[1], keys.shape[1]
    block = rows // 4
    cols = lax.broadcasted_iota(jnp.int32, (block, extent), 1)
    ids = lax.broadcasted_iota(jnp.int32, (block, extent), 0)
    total = None
    for e in range(2):
        for h in range(SETS):
            at = slice(h * HEAD, (h + 1) * HEAD)
            k = keys[e, :, at]
            v = keys[e, :, WIDTH + h * HEAD : WIDTH + (h + 1) * HEAD]
            scores = matmul_nt(q_ref[e, :, at], k)
            if biased:
                line = table_ref[e * SETS + h : e * SETS + h + 1, :]
                skew = pltpu.roll(
                    jnp.broadcast_to(line, (block, 2 * extent)),
                    2 * extent - (block - 1),
                    1,
                    stride=1,
                    stride_axis=0,
                )
            for i in range(4):
                here = slice(i * block, (i + 1) * block)
                s = scores[here] * (HEAD**-0.5)
                if biased:
                    begin = (3 - i) * 2 * block
                    s = s + skew[:, begin : begin + extent]
                visible = cols < length
                if causal:
                    visible = visible & (cols <= ids + (i * 2 * block + core * block))
                s = jnp.where(visible, s, NEGATIVE)
                weights = jnp.exp(s - jnp.max(s, axis=-1, keepdims=True))
                weights = weights * (1.0 / jnp.sum(weights, axis=-1, keepdims=True))
                p_ref[e * SETS + h, here, :] = weights.astype(BF)
            ctx_ref[e, :, at] = matmul(p_ref[e * SETS + h], v)
        term = matmul(ctx_ref[e].astype(BF), (oa_ref, ob_ref)[e][...])
        total = term if total is None else total + term
    part_ref[...] = total
    low_ref[...] = total.astype(BF)


def attend_local(scalars, q, kv, got, table, out_own, out_sib, causal, name):
    rows = q.shape[1]
    extent = 2 * rows
    args = [(scalars, SCALARS), q, kv, got] + ([] if table is None else [table])
    return call(
        functools.partial(attend_kernel, causal, table is not None),
        name,
        [
            ((2, rows, WIDTH), F32),
            ((2 * SETS, rows, extent), BF),
            ((rows, D), F32),
            ((rows, D), BF),
        ],
        args + [out_own, out_sib],
        5.5,
        [pltpu.VMEM((2, extent, 2 * WIDTH), BF)],
    )


def unpack_into(w_ref, columns, down):
    blocks, rows = 8, down.shape[0] // 8
    half, third = rows // 2, down.shape[1] // 3
    step = rows + half
    for b in range(blocks):
        down[b * rows : (b + 1) * rows, : 2 * third] = w_ref[
            b * step : b * step + rows, columns : columns + 2 * third
        ]
        for k in range(2):
            down[b * rows + k * half : b * rows + (k + 1) * half, 2 * third :] = w_ref[
                b * step + rows : (b + 1) * step,
                columns + k * third : columns + (k + 1) * third,
            ]


GELU_A, GELU_B = (2 / math.pi) ** 0.5, 0.044715


def gelu_tanh(gate):
    return jnp.tanh(GELU_A * (gate + GELU_B * gate * gate * gate))


def ffn_kernel(gain, res_ref, part_ref, got_ref, gains_ref, wa_ref, wb_ref, *refs):
    mid_ref, n_ref, gu_ref, hid_ref, out_ref, low_ref, down = refs
    mid = res_ref[...].astype(F32) + part_ref[...] + got_ref[...].astype(F32)
    mid_ref[...] = mid
    n = norm_rows(mid, gains_ref[gain : gain + 1, :]).astype(BF)
    n_ref[...] = n
    units = down.shape[0]
    total = None
    for e, w_ref in enumerate((wa_ref, wb_ref)):
        gu_ref[e] = matmul(n, w_ref[:, : 2 * units])
        gate, up = gu_ref[e, :, :units], gu_ref[e, :, units:]
        hid_ref[e] = (0.5 * gate * (1.0 + gelu_tanh(gate)) * up).astype(BF)
        unpack_into(w_ref, 2 * units, down)
        term = matmul(hid_ref[e], down[...])
        total = term if total is None else total + term
    out_ref[...] = total
    low_ref[...] = total.astype(BF)


def ffn_local(res, part, got, gains, gain, w_own, w_sib, units, name):
    rows = res.shape[0]
    return call(
        functools.partial(ffn_kernel, gain),
        name,
        [
            ((rows, D), F32),
            ((rows, D), BF),
            ((2, rows, 2 * units), F32),
            ((2, rows, units), BF),
            ((rows, D), F32),
            ((rows, D), BF),
        ],
        [res, part, got, gains, w_own, w_sib],
        3.0,
        [pltpu.VMEM((units, D), BF)],
    )


def ffn_back_kernel(decoder, val_ref, part_ref, got_ref, cot_ref, gains_ref, *refs):
    gu_ref, wa_ref, wb_ref = refs[:3]
    down = refs[-1]
    sent = part_ref[...] + got_ref[...].astype(F32)
    if decoder:
        final_ref, g_ref, dgain_ref, low_ref, dgu_ref, out_ref, out_low_ref = refs[3:-1]
        gain = gains_ref[6:7, :]
        values = val_ref[...] + sent
        upstream = cot_ref[...].astype(F32)
        final_ref[...] = norm_rows(values, gain).astype(BF)
    else:
        g_ref, dgain_ref, low_ref, dgu_ref, out_ref, out_low_ref = refs[3:-1]
        gain = gains_ref[2:3, :]
        values = val_ref[...]
        upstream = cot_ref[...].astype(F32) + sent
    grad, dgain_ref[...] = norm_back(values, gain, upstream)
    g_ref[...] = grad
    low = grad.astype(BF)
    low_ref[...] = low
    units = down.shape[0]
    total = None
    for e, w_ref in enumerate((wa_ref, wb_ref)):
        unpack_into(w_ref, 2 * units, down)
        grad_hidden = matmul_nt(low, down[...])
        gate, up = gu_ref[e, :, :units], gu_ref[e, :, units:]
        t = gelu_tanh(gate)
        slope = 0.5 * (1.0 + t) + 0.5 * gate * (1.0 - t * t) * GELU_A * (
            1.0 + 3.0 * GELU_B * gate * gate
        )
        dgu_ref[e, :, :units] = (grad_hidden * up * slope).astype(BF)
        dgu_ref[e, :, units:] = (grad_hidden * (0.5 * gate * (1.0 + t))).astype(BF)
        term = matmul_nt(dgu_ref[e], w_ref[:, : 2 * units])
        total = term if total is None else total + term
    out_ref[...] = total
    out_low_ref[...] = total.astype(BF)


def ffn_back(decoder, values, part, got, cot, gains, gate_up, w_own, w_sib, name):
    rows, units = values.shape[0], gate_up.shape[2] // 2
    outs = [((rows, D), BF)] if decoder else []
    outs += [
        ((rows, D), F32),
        ((1, D), F32),
        ((rows, D), BF),
        ((2, rows, 2 * units), BF),
        ((rows, D), F32),
        ((rows, D), BF),
    ]
    return call(
        functools.partial(ffn_back_kernel, decoder),
        name,
        outs,
        [values, part, got, cot, gains, gate_up, w_own, w_sib],
        4.0,
        [pltpu.VMEM((units, D), BF)],
    )


def ffn_weights_kernel(n_ref, dgu_ref, hid_ref, low_ref, own_ref, sib_ref):
    units = hid_ref.shape[2]
    rows, half, third = units // 8, units // 16, D // 3
    step = rows + half
    for e, out in enumerate((own_ref, sib_ref)):
        out[:, : 2 * units] = matmul_tn(n_ref[...], dgu_ref[e]).astype(BF)
        down = matmul_tn(hid_ref[e], low_ref[...]).astype(BF)
        for b in range(8):
            out[b * step : b * step + rows, 2 * units :] = down[
                b * rows : (b + 1) * rows, : 2 * third
            ]
            for k in range(2):
                out[
                    b * step + rows : (b + 1) * step,
                    2 * units + k * third : 2 * units + (k + 1) * third,
                ] = down[b * rows + k * half : b * rows + (k + 1) * half, 2 * third :]


def ffn_weights(n, dgu, hid, low, name):
    units = hid.shape[2]
    shape = ((D, 2 * units + 2 * D // 3), BF)
    return call(
        ffn_weights_kernel, name, [shape, shape], [n, dgu, hid, low], 1.5
    )


def attend_back_kernel(gain, biased, scalars, up_ref, val_ref, part_ref, got_ref, *refs):
    gains_ref, oa_ref, ob_ref, q_ref, kv_ref, kvgot_ref, p_ref, ctx_ref = refs[:8]
    g_ref, dgain_ref, low_ref, dq_ref, mine_ref, other_ref = refs[8:14]
    keys, dkeys, ds_ref = refs[-3:]
    core = scalars[0]
    grad, dgain_ref[...] = norm_back(
        val_ref[...], gains_ref[gain : gain + 1, :], part_ref[...] + got_ref[...].astype(F32)
    )
    grad = up_ref[...] + grad
    g_ref[...] = grad
    low = grad.astype(BF)
    low_ref[...] = low
    lay_out_keys(core, kv_ref, kvgot_ref, keys)
    rows, extent = q_ref.shape[1], keys.shape[1]
    block = rows // 4
    factor = HEAD**-0.5
    for e in range(2):
        g = matmul_nt(low, (oa_ref, ob_ref)[e][...]).astype(BF)
        products = g.astype(F32) * ctx_ref[e]
        for h in range(SETS):
            at = slice(h * HEAD, (h + 1) * HEAD)
            k = keys[e, :, at]
            v = keys[e, :, WIDTH + h * HEAD : WIDTH + (h + 1) * HEAD]
            dots = jnp.sum(products[:, at], axis=-1, keepdims=True)
            dp = matmul_nt(g[:, at], v)
            sums = [None] * 7
            for i in range(4):
                here = slice(i * block, (i + 1) * block)
                ds = p_ref[e * SETS + h, here, :].astype(F32) * (dp[here] - dots[here])
                if biased:
                    for j in range(4):
                        part = ds[:, j * 2 * block : (j + 1) * 2 * block]
                        slot = 3 - i + j
                        sums[slot] = part if sums[slot] is None else sums[slot] + part
                ds_ref[here, :] = (ds * factor).astype(BF)
            dq_ref[e, :, at] = matmul(ds_ref[...], k).astype(BF)
            dkeys[:, at] = matmul_tn(ds_ref[...], q_ref[e, :, at])
            dkeys[:, WIDTH + h * HEAD : WIDTH + (h + 1) * HEAD] = matmul_tn(
                p_ref[e * SETS + h], g[:, at]
            )
            if biased:
                dtable_ref = refs[14]
                band = jnp.concatenate(sums + [jnp.zeros_like(sums[0])], axis=1)
                ids = lax.broadcasted_iota(jnp.int32, band.shape, 0)
                bit = 1
                while bit < block:
                    moved = pltpu.roll(band, 2 * extent - bit, 1)
                    band = jnp.where((ids & bit) != 0, moved, band)
                    bit *= 2
                line = jnp.sum(band, axis=0, keepdims=True)
                dtable_ref[e * SETS + h : e * SETS + h + 1, :] = pltpu.roll(line, block - 1, 1)
        for k in range(4):
            at = pl.multiple_of(block * (2 * k + core), block)
            mine_ref[e, k * block : (k + 1) * block, :] = dkeys[pl.ds(at, block), :]
            at = pl.multiple_of(block * (2 * k + 1 - core), block)
            other_ref[1 - e, k * block : (k + 1) * block, :] = dkeys[
                pl.ds(at, block), :
            ].astype(BF)


def attend_local_back(gain, biased, scalars, upstream, values, part, got, gains, *rest, name):
    rows, extent = upstream.shape[0], 2 * upstream.shape[0]
    outs = [
        ((rows, D), F32),
        ((1, D), F32),
        ((rows, D), BF),
        ((2, rows, WIDTH), BF),
        ((2, rows, 2 * WIDTH), F32),
        ((2, rows, 2 * WIDTH), BF),
    ]
    if biased:
        outs.append(((2 * SETS, 2 * extent), F32))
    return call(
        functools.partial(attend_back_kernel, gain, biased),
        name,
        outs,
        [(scalars, SCALARS), upstream, values, part, got, gains] + list(rest),
        9.0 if biased else 6.0,
        [
            pltpu.VMEM((2, extent, 2 * WIDTH), BF),
            pltpu.VMEM((extent, 2 * WIDTH), F32),
            pltpu.VMEM((rows, extent), BF),
        ],
    )


def project_back_kernel(split, q_at, dq_ref, mine_ref, got_ref, *refs):
    kva_ref, qa_ref, kvb_ref, qb_ref = refs[:4]
    dkv_ref = refs[4]
    from_keys = from_queries = None
    for e, (kv, q) in enumerate(((kva_ref, qa_ref), (kvb_ref, qb_ref))):
        dkv = (mine_ref[e] + got_ref[e].astype(F32)).astype(BF)
        dkv_ref[e] = dkv
        term = matmul_nt(dkv, kv[:, : 2 * WIDTH])
        from_keys = term if e == 0 else from_keys + term
        term = matmul_nt(dq_ref[e], q[:, q_at : q_at + WIDTH])
        from_queries = term if e == 0 else from_queries + term
    outs = [from_keys, from_queries] if split else [from_keys + from_queries]
    for k, total in enumerate(outs):
        refs[5 + 2 * k][...] = total
        refs[6 + 2 * k][...] = total.astype(BF)


def project_back(split, dq, mine, got, kv_own, q_own, kv_sib, q_sib, q_at, name):
    rows = dq.shape[1]
    outs = [((2, rows, 2 * WIDTH), BF)] + [((rows, D), F32), ((rows, D), BF)] * (1 + split)
    return call(
        functools.partial(project_back_kernel, split, q_at),
        name,
        outs,
        [dq, mine, got, kv_own, q_own, kv_sib, q_sib],
        2.5,
    )


def attend_weights_kernel(count, *refs):
    ins, (own_ref, sib_ref, out_own_ref, out_sib_ref) = refs[:-4], refs[-4:]
    for k in range(count):
        nq_ref, nkv_ref, dq_ref, dkv_ref, ctx_ref, low_ref = ins[6 * k : 6 * k + 6]
        kv_at, q_at = 2 * WIDTH * k, 2 * WIDTH * count + WIDTH * k
        for e, (in_ref, out_ref) in enumerate(((own_ref, out_own_ref), (sib_ref, out_sib_ref))):
            in_ref[:, kv_at : kv_at + 2 * WIDTH] = matmul_tn(nkv_ref[...], dkv_ref[e]).astype(BF)
            in_ref[:, q_at : q_at + WIDTH] = matmul_tn(nq_ref[...], dq_ref[e]).astype(BF)
            out_ref[k] = matmul_tn(ctx_ref[e].astype(BF), low_ref[...]).astype(BF)


def attend_weights(name, *attentions):
    count, rows = len(attentions), attentions[0][0].shape[0]
    inner, outer = ((D, 3 * count * WIDTH), BF), ((count, WIDTH, D), BF)
    own, sib, out_own, out_sib = call(
        functools.partial(attend_weights_kernel, count),
        name,
        [inner, inner, outer, outer],
        [a for attention in attentions for a in attention],
        1.0 * count,
    )
    return own, out_own, sib, out_sib


IN_ORDER = (8, 6, 7, 4, 0, 1, 5, 2, 3)


def sums_kernel(own, enc_ref, dec_ref, rest_ref, self_ref, out_ref):
    inner = 6 * WIDTH
    third, half = D // 3, D // 2
    wide = enc_ref.shape[1] - 2 * third
    rows = enc_ref.shape[0] * 2 // 3
    out_ref[...] = jnp.zeros_like(out_ref)

    def line(values):
        return jnp.sum(values * values, axis=0, keepdims=True)

    def put(at, values):
        for k in range(0, values.shape[1], 128):
            width = min(128, values.shape[1] - k)
            out_ref[at + k // 128 : at + k // 128 + 1, :width] = values[:, k : k + width]

    put(0, line(enc_ref[:, :wide]))
    put(wide // 128, line(dec_ref[:, :wide]))
    at = 2 * wide // 128
    put(at, line(rest_ref[:, :inner]))
    put(at + inner // 128, line(self_ref[:, third : third + 3 * WIDTH]))
    at = 30
    for ref in (enc_ref, dec_ref):
        put(at, line(ref[:rows, wide:]))
        last = line(ref[rows:, wide : wide + third]) + line(ref[rows:, wide + third :])
        put(at + 2 * third // 128, last)
        at += D // 128
    for k in range(3):
        put(at + k * third // 128, line(self_ref[k * own : (k + 1) * own, :third]))
    at += D // 128
    for k in range(2):
        for side in range(2):
            begin = (2 * side + k) * own
            put(at + side * half // 128, line(rest_ref[begin : begin + own, inner:]))
        at += D // 128


def shards_kernel(ff_own, dec_ref, rest_ref, self_ref, enc_ref, down_enc_ref, down_dec_ref, *outs):
    in_ref, hin_ref, hout_ref = outs
    third = D // 3
    for k, at in enumerate(IN_ORDER):
        ref, at = (rest_ref, at) if at < 6 else (self_ref, at - 6)
        for q in range(WAYS):
            piece = ref[q, :, at * WIDTH : (at + 1) * WIDTH]
            in_ref[k // 3, k % 3, :, q * WIDTH : (q + 1) * WIDTH] = piece
    for layer, ref in enumerate((enc_ref, dec_ref)):
        units = ref.shape[2] // 2
        for j in range(2):
            for k in range(units // ff_own):
                first = j * units + k * ff_own
                for q in range(WAYS):
                    at = (WAYS * k + q) * ff_own
                    hin_ref[layer, j, :, at : at + ff_own] = ref[q, :, first : first + ff_own]
    for layer, ref in enumerate((down_enc_ref, down_dec_ref)):
        hout_ref[layer, :, : 2 * third] = ref[:ff_own, :]
        half = ff_own // 2
        hout_ref[layer, :half, 2 * third :] = ref[ff_own:, :third]
        hout_ref[layer, half:, 2 * third :] = ref[ff_own:, third:]


def input_kernel(gain, up_ref, x_ref, part_ref, got_ref, gains_ref, out_ref, dgain_ref):
    grad, dgain_ref[...] = norm_back(
        x_ref[...].astype(F32),
        gains_ref[gain : gain + 1, :],
        part_ref[...] + got_ref[...].astype(F32),
    )
    out_ref[...] = up_ref[...] + grad


def input_back(gain, upstream, x, part, got, gains, name):
    return call(
        functools.partial(input_kernel, gain),
        name,
        [(upstream.shape, F32), ((1, D), F32)],
        [upstream, x, part, got, gains],
        1.5,
    )


def gather_own_rows(place, mine, other_seq):
    near = pair_up(mine, swap(other_seq, "y"), place.y)
    far = pair_up(near, swap(near, "x"), place.x)
    far = far.transpose(2, 1, 0, 3, 4)
    return far.reshape(far.shape[0], -1, far.shape[4])


def give_back(place, half):
    blocks = half.reshape(2, 2, -1, half.shape[1])
    blocks = pick(blocks, place.x, 1)
    other = swap(pick(blocks, 1 - place.y), "y")
    return pair_up(pick(blocks, place.y), other, place.y)


def sum_everywhere(place, values):
    depth = place.depth
    for axis in ("c", "x", "y"):
        values = values + swap(values, axis)
    return values + sum(shift_z(values, k, depth) for k in range(1, depth))


def pack_down(rows):
    half, third = rows.shape[-2] // 2, rows.shape[-1] // 3
    last = rows[..., 2 * third :]
    last = jnp.concatenate([last[..., :half, :], last[..., half:, :]], axis=-1)
    return jnp.concatenate([rows[..., : 2 * third], last], axis=-2)


def unpack_down(packed):
    half, third = packed.shape[-2] // 3, packed.shape[-1] // 2
    last = packed[..., 2 * half :, :]
    last = jnp.concatenate([last[..., :third], last[..., third:]], axis=-2)
    return jnp.concatenate([packed[..., : 2 * half, :], last], axis=-1)


def pack_out(pair):
    rows = pair.reshape(pair.shape[:-3] + (-1, pair.shape[-1]))
    half = rows.shape[-1] // 2
    return jnp.concatenate([rows[..., :half], rows[..., half:]], axis=-2)


def unpack_out_piece(packed):
    half = packed.shape[-2] // 2
    rows = jnp.concatenate([packed[..., :half, :], packed[..., half:, :]], axis=-1)
    return rows.reshape(rows.shape[:-2] + (2, half // 2, rows.shape[-1]))


def unpack_out(packed, depth):
    pair = unpack_out_piece(packed)
    pair = pair.reshape((depth, 2) + pair.shape[1:])
    pair = pair.transpose(2, 1, 0, 3, 4)
    return pair.reshape(2, -1, pair.shape[-1])


def turned_parts(grads, depth):
    parts = grads.reshape(2, depth, -1, grads.shape[1]).transpose(1, 0, 2, 3)
    return parts.reshape(2 * depth, -1, grads.shape[1])


def grouped(
    depth,
    enc_input,
    dec_input,
    enc_lengths,
    dec_lengths,
    enc_buckets,
    dec_buckets,
    attention_in,
    attention_out,
    hidden_in,
    hidden_out,
    norm_gains,
    position_bias,
    enc_cotangent,
    dec_cotangent,
):
    place = Place(depth)
    y, q = place.y, place.q
    block = enc_input.shape[1]
    length = block * 8
    own = attention_in.shape[2]
    ff_own = hidden_out.shape[1]
    units = ff_own * 2 * depth
    group = WAYS * own

    pieces = attention_in.reshape(3, 3, own, WAYS, WIDTH).transpose(3, 0, 1, 2, 4)
    queries, keys, values = pieces[:, :, 0], pieces[:, :, 1], pieces[:, :, 2]
    gain_piece = jnp.pad(norm_gains.T, ((0, 0), (0, 64 - norm_gains.shape[0])))
    gain_piece = jnp.broadcast_to(gain_piece[None], (WAYS,) + gain_piece.shape)
    turned = turn(attention_out, depth)
    hidden_pieces = hidden_in.reshape(2, 2, own, 2 * depth, WAYS, ff_own)
    hidden_pieces = hidden_pieces.transpose(4, 0, 2, 1, 3, 5).reshape(WAYS, 2, own, 2 * units)
    blocks_in = [keys[:, 0], values[:, 0], queries[:, 0], gain_piece]
    blocks_in += [keys[:, 1], values[:, 1], keys[:, 2], values[:, 2], queries[:, 1], queries[:, 2]]
    blocks_in += [hidden_pieces[:, 0], hidden_pieces[:, 1]]
    everything = exchange_columns(place, jnp.concatenate(blocks_in, axis=2)).reshape(group, -1)
    cuts = [3 * WIDTH + 64, 9 * WIDTH + 64, 9 * WIDTH + 64 + 2 * units]
    enc_piece, rest, ffn_enc, ffn_dec = jnp.split(everything, cuts, axis=1)
    third = turned[0].reshape(own, 3, D // 3).transpose(1, 0, 2).reshape(3 * own, D // 3)
    third = jnp.pad(third, ((0, group - 3 * own), (0, 0)))
    enc_piece = jnp.concatenate([enc_piece, third], axis=1)
    rest = jnp.concatenate([rest, pack_out(turned[1:])], axis=1)
    ffn_enc = jnp.concatenate([ffn_enc, pack_down(hidden_out[0])], axis=1)
    ffn_dec = jnp.concatenate([ffn_dec, pack_down(hidden_out[1])], axis=1)

    line = along_z(place, enc_piece)
    w_enc = along_y(place, line)
    w_enc_sib = swap(w_enc, "c")

    def out_rows(whole):
        rows = whole[:, 3 * WIDTH + 64 :].reshape(depth, 2, group, D // 3)[:, :, : 3 * own]
        rows = rows.reshape(depth, 2, 3, own, D // 3).transpose(1, 0, 3, 2, 4)
        return rows.reshape(WIDTH, D)

    def gather(piece):
        return lax.all_gather(piece, ("dp", "y"), axis=0, tiled=True)

    first = gather(jnp.concatenate([rest, ffn_enc], axis=1))
    out_enc, out_enc_sib = out_rows(w_enc), out_rows(w_enc_sib)
    gains = w_enc[:, 3 * WIDTH : 3 * WIDTH + norm_gains.shape[0]].astype(F32).T

    w_self = [w_enc, w_enc, w_enc_sib, w_enc_sib]

    def own_rows(*arrays):
        mine = jnp.stack([pick(a, y) for a in arrays])
        other = jnp.stack([pick(a, 1 - y) for a in arrays])
        return gather_own_rows(place, mine, other)

    enc_rows, dec_rows, *cots = own_rows(enc_input, dec_input, dec_cotangent, enc_cotangent)
    enc_scalars = jnp.stack([place.c, pick(enc_lengths, y)]).astype(jnp.int32)
    dec_scalars = jnp.stack([place.c, pick(dec_lengths, y)]).astype(jnp.int32)

    def head_rows(table):
        mine = lax.dynamic_slice_in_dim(table, q * SETS, SETS, 0)
        theirs = lax.dynamic_slice_in_dim(table, (q + 1 - 2 * place.c) * SETS, SETS, 0)
        table = jnp.concatenate([mine, theirs])
        table = jnp.pad(table, ((0, 0), (0, block)))
        return lax.dynamic_slice_in_dim(table, block * (1 - place.c), 2 * length, 1)

    enc_table = offset_table(enc_buckets, position_bias[0])
    enc_table = head_rows(jnp.pad(enc_table, ((0, 0), (0, 1))))
    dec_table = offset_table(dec_buckets, position_bias[1])
    dec_table = jnp.concatenate(
        [dec_table[:, ::-1], jnp.broadcast_to(dec_table[:, :1], (HEADS, length))], axis=1
    )
    dec_table = head_rows(dec_table)

    n_a, q_enc, kv_enc = self_project(enc_rows, gains, 0, *w_self, 2 * WIDTH, "enc_project")
    kv_enc_got = swap(kv_enc, "c")
    ctx_enc, p_enc, part, low = attend_local(
        enc_scalars, q_enc, kv_enc, kv_enc_got, enc_table, out_enc, out_enc_sib, False, "enc_attend"
    )
    low_enc, part_enc = low, part
    ffn_dec = gather(after(ffn_dec, low_enc))
    first = after(first, low_enc)
    first_sib = swap(first, "c")
    rest, rest_sib = first[:, : ffn_enc.shape[1]], first_sib[:, : ffn_enc.shape[1]]

    out_rest = unpack_out(rest[:, 6 * WIDTH :].reshape(2 * depth, group, -1), depth)
    out_rest_sib = unpack_out(rest_sib[:, 6 * WIDTH :].reshape(2 * depth, group, -1), depth)
    w_dec = [column_block(w, k) for w in (first, first_sib) for k in (0, 2)]
    w_cross = [column_block(w, k) for w in (first, first_sib) for k in (1, 2)]
    ffn_width = ffn_enc.shape[1]
    ffn_enc, ffn_enc_sib = [
        (w, pl.BlockSpec((D, ffn_width), lambda _: (0, 1))) for w in (first, first_sib)
    ]
    out_dec, out_cross = [[(w, pl.BlockSpec((None, WIDTH, D), f)) for w in (out_rest, out_rest_sib)]
        for f in (lambda _: (0, 0, 0), lambda _: (1, 0, 0))]

    enc_mid, n_1, gu_enc, hid_enc, part, low = ffn_local(
        enc_rows, part_enc, swap(low_enc, "x"), gains, 1, ffn_enc, ffn_enc_sib, units, "enc_ffn"
    )
    n_b, q_dec, kv_dec = self_project(after(dec_rows, n_1), gains, 3, *w_dec, 0, "dec_project")
    kv_dec_got = swap(kv_dec, "c")
    ctx_dec, p_dec, part_dec, low_dec = attend_local(
        dec_scalars, q_dec, kv_dec, kv_dec_got, dec_table, *out_dec, True, "dec_attend"
    )

    rows = enc_rows.shape[0]
    enc_last, memory_low, kv_cross = call(
        memory_kernel,
        "memory",
        [((rows, D), F32), ((rows, D), BF), ((2, rows, 2 * WIDTH), BF)],
        [enc_mid, part, swap(low, "x"), gains, w_cross[0], w_cross[2]],
        2.0,
    )
    kv_cross_got = swap(kv_cross, "c")

    dec_mid, n_c, q_cross = call(
        functools.partial(cross_kernel, WIDTH),
        "cross_project",
        [((rows, D), F32), ((rows, D), BF), ((2, rows, WIDTH), BF)],
        [dec_rows, part_dec, swap(low_dec, "x"), gains, w_cross[1], w_cross[3]],
        2.0,
    )
    ffn_dec = after(ffn_dec, q_cross, kv_cross)
    ffn_dec_sib = swap(ffn_dec, "c")
    ctx_cross, p_cross, part, low = attend_local(
        enc_scalars, q_cross, kv_cross, kv_cross_got, None, *out_cross, False, "cross_attend"
    )
    dec_cross, n_5, gu_dec, hid_dec, part, low = ffn_local(
        dec_mid, part, swap(low, "x"), gains, 5, ffn_dec, ffn_dec_sib, units, "dec_ffn"
    )

    def both(own_grads, sib_grads):
        return (own_grads.astype(F32) + swap(sib_grads, "c").astype(F32)).astype(BF)

    def blocks(grads):
        return grads.reshape(2 * depth, -1, grads.shape[1])

    def scatter(grads):
        return lax.psum_scatter(grads, ("dp", "y"), scatter_dimension=0, tiled=False)

    dec_final, g, gg6, low_d, dgu_dec, part, low = ffn_back(
        True, dec_cross, part, swap(low, "x"), cots[0], gains, gu_dec, ffn_dec, ffn_dec_sib, "dec_ffn_back"
    )
    d_ffn_dec = ffn_weights(n_5, dgu_dec, hid_dec, low_d, "dec_ffn_weights")
    d_ffn_dec = both(*d_ffn_dec)
    got = after(swap(low, "x"), d_ffn_dec)
    g, gg5, low_x, dq_cross, mine, other = attend_local_back(
        5,
        False,
        enc_scalars,
        g,
        dec_cross,
        part,
        got,
        gains,
        *out_cross,
        q_cross,
        kv_cross,
        kv_cross_got,
        p_cross,
        ctx_cross,
        name="cross_attend_back",
    )
    got = swap(other, "c")
    d_ffn_dec = scatter(blocks(d_ffn_dec))
    dkv_cross, part_m, low_m, part_c, low_c = project_back(
        True, dq_cross, mine, got, *w_cross, WIDTH, "cross_project_back"
    )
    got_m = swap(low_m, "x")
    got_c = swap(low_c, "x")
    g_last, gg2, low_e, dgu_enc, part, part_low = ffn_back(
        False, enc_last, part_m, got_m, cots[1], gains, gu_enc, ffn_enc, ffn_enc_sib, "enc_ffn_back"
    )
    d_ffn_enc = ffn_weights(n_1, dgu_enc, hid_enc, low_e, "enc_ffn_weights")
    got_e = swap(part_low, "x")
    got_c = after(got_c, got_e, *d_ffn_enc)
    d_ffn_enc = both(*d_ffn_enc)
    g_dec, gg4, low_b, dq_dec, mine, other, d_table_dec = attend_local_back(
        4,
        True,
        dec_scalars,
        g,
        dec_mid,
        part_c,
        got_c,
        gains,
        *out_dec,
        q_dec,
        kv_dec,
        kv_dec_got,
        p_dec,
        ctx_dec,
        name="dec_attend_back",
    )
    got_e = after(got_e, dq_dec, d_ffn_dec)
    dec_other = swap(other, "c")
    dec_mine = mine
    g_enc, gg1, low_a, dq_enc, mine, other, d_table_enc = attend_local_back(
        1,
        True,
        enc_scalars,
        g_last,
        enc_mid,
        part,
        got_e,
        gains,
        out_enc,
        out_enc_sib,
        q_enc,
        kv_enc,
        kv_enc_got,
        p_enc,
        ctx_enc,
        name="enc_attend_back",
    )
    dkv_dec, part_d, low = project_back(
        False, dq_dec, dec_mine, dec_other, *w_dec, 0, "dec_project_back"
    )
    got_d = swap(low, "x")
    d_in, d_out, d_in_sib, d_out_sib = attend_weights(
        "attend_weights",
        (n_b, n_b, dq_dec, dkv_dec, ctx_dec, low_b),
        (n_c, memory_low, dq_cross, dkv_cross, ctx_cross, low_x),
    )
    d_out = both(d_out, d_out_sib)
    d_out = jnp.stack([turned_parts(d_out[k], depth) for k in range(2)], 1)
    late = [blocks(d_ffn_enc), blocks(both(d_in, d_in_sib)), pack_out(d_out)]
    late = scatter(jnp.concatenate(late, axis=2)).astype(F32)
    got = after(swap(other, "c"), dkv_dec)
    dkv_enc, part, low = project_back(
        False, dq_enc, mine, got, *w_self, 2 * WIDTH, "enc_project_back"
    )
    d_in, d_out, d_in_sib, d_out_sib = attend_weights(
        "enc_attend_weights", (n_a, n_a, dq_enc, dkv_enc, ctx_enc, low_a)
    )
    got = after(swap(low, "x"), d_in, d_out)
    got_d = after(got_d, dkv_enc)
    grad_dec, gg3 = input_back(3, g_dec, dec_rows, part_d, got_d, gains, "dec_input_back")
    grad_enc, gg0 = input_back(0, g_enc, enc_rows, part, got, gains, "enc_input_back")
    thirds = turned_parts(both(d_out, d_out_sib)[0], depth).reshape(2 * depth, own, 3, D // 3)
    thirds = thirds.transpose(0, 2, 1, 3).reshape(2 * depth, 3 * own, D // 3)
    thirds = jnp.pad(thirds, ((0, 0), (0, group - 3 * own), (0, 0)))
    d_enc = jnp.concatenate([thirds, blocks(both(d_in, d_in_sib))], axis=2)
    d_enc = scatter_z(place, scatter_y(place, d_enc))
    d_ffn_dec = d_ffn_dec.astype(F32)
    d_ffn_enc, d_rest = jnp.split(late, [d_ffn_dec.shape[1]], axis=1)

    def to_rows(shard):
        return exchange_columns(place, rounded(shard).reshape(WAYS, own, -1)).astype(F32)

    wide, inner = 2 * units, 6 * WIDTH
    (sums,) = call(
        functools.partial(sums_kernel, own),
        "column_sums",
        [((64, 128), F32)],
        [d_ffn_enc, d_ffn_dec, d_rest, d_enc],
        1.0,
    )
    out_enc_mine = d_enc[: 3 * own, : D // 3].reshape(3, own, D // 3).transpose(1, 0, 2)
    out_mine = unpack_out_piece(d_rest[:, inner:])
    shard_out = jnp.concatenate([out_enc_mine.reshape(1, own, D), out_mine])
    shard_out = turn(rounded(shard_out), depth).astype(F32)
    columns = [d_ffn_dec[:, :wide], d_rest[:, :inner], d_enc[:, D // 3 :], d_ffn_enc[:, :wide]]
    ends = [wide, wide + inner, wide + inner + 3 * WIDTH]
    columns = jnp.split(to_rows(jnp.concatenate(columns, axis=1)), ends, axis=2)
    shard_in, shard_hin, shard_hout = call(
        functools.partial(shards_kernel, ff_own),
        "shards",
        [((3, 3, own, D), F32), ((2, 2, own, WAYS * units), F32), ((2, ff_own, D), F32)],
        columns + [d_ffn_enc[:, wide:], d_ffn_dec[:, wide:]],
        2.0,
    )
    sums = sums + sum(shift_z(sums, k, depth) for k in range(1, depth))
    sums = sums + swap(sums, "y")
    sums = pair_up(sums, swap(sums, "x"), place.x)
    sums = pair_up(sums, swap(sums, "c"), place.c)
    sums = sums.swapaxes(0, 1).reshape(WAYS, -1)
    cuts = [2 * wide, 2 * wide + 9 * WIDTH, 30 * 128, 30 * 128 + 2 * D, 30 * 128 + 5 * D]
    col_hin, col_in, _, col_hout, col_out, _ = jnp.split(sums, cuts, axis=1)
    col_hin = col_hin.reshape(WAYS, 2, 2, 2 * depth, ff_own).transpose(1, 2, 3, 0, 4)
    col_hin = col_hin.reshape(2, 2, WAYS * units)
    col_in = col_in.reshape(WAYS, 9, WIDTH)
    col_in = jnp.stack([col_in[:, k] for k in IN_ORDER]).reshape(3, 3, D)
    col_hout = jnp.sum(col_hout, axis=0).reshape(2, D)
    col_out = jnp.sum(col_out, axis=0).reshape(3, D)

    buckets = position_bias.shape[1]

    def head_table(d_table):
        wide_table = jnp.zeros((2 * SETS, 2 * length + block), F32)
        return lax.dynamic_update_slice_in_dim(wide_table, d_table, block * (1 - place.c), 1)

    grad_enc_bias = head_table(d_table_enc)[:, : 2 * length - 1]
    grad_dec_bias = head_table(d_table_dec)[:, :length][:, ::-1]
    by_set = jnp.stack(
        [
            bucket_grad(enc_buckets, grad_enc_bias, buckets),
            bucket_grad(dec_buckets, grad_dec_bias, buckets),
        ]
    )
    grad_position = lax.dynamic_update_slice_in_dim(
        jnp.zeros_like(position_bias), by_set[:, :, :SETS], q * SETS, 2
    )
    grad_position = lax.dynamic_update_slice_in_dim(
        grad_position, by_set[:, :, SETS:], (q + 1 - 2 * place.c) * SETS, 2
    )
    grad_gains = jnp.concatenate([gg0, gg1, gg2, gg3, gg4, gg5, gg6])
    grad_gains = jnp.where(place.x == 0, grad_gains, 0.0)
    small = jnp.concatenate([grad_gains.reshape(-1, 128), grad_position.reshape(-1, 128)])
    small = sum_everywhere(place, small)
    cut = grad_gains.size // 128
    grad_gains = small[:cut].reshape(grad_gains.shape)
    grad_position = small[cut:].reshape(grad_position.shape)
    shard_gains = lax.dynamic_slice_in_dim(grad_gains, place.index * own, own, 1)

    def mean_rows(v):
        return 0.5 * jnp.mean(v * v, axis=-1)

    return (
        give_back(place, after(memory_low, dkv_enc)),
        give_back(place, after(dec_final, dkv_enc)),
        give_back(place, grad_enc),
        give_back(place, grad_dec),
        shard_in,
        shard_out,
        shard_hin,
        shard_hout,
        shard_gains,
        grad_position,
        mean_rows(shard_in),
        0.5 * col_in / D,
        mean_rows(shard_out),
        0.5 * col_out / D,
        mean_rows(shard_hin),
        0.5 * col_hin / D,
        mean_rows(shard_hout),
        0.5 * col_hout / FF,
    )


def specs(seq):
    rows = P("dp", seq, None)
    every = ("dp",) + (seq if isinstance(seq, tuple) else (seq,))
    second, third = P(None, every, None), P(None, None, every, None)
    ins = (rows, rows, P("dp"), P("dp"), P(), P(), third, second, third, second)
    ins += (P(None, every), P(), rows, rows)
    outs = (rows, rows, rows, rows, third, second, third, second, P(None, every), P())
    outs += (P(None, None, every), P(), P(None, every), P())
    outs += (P(None, None, every), P(), P(None, every), P())
    return ins, outs


def solution(mesh):
    depth, seq = mesh.shape["dp"], mesh.shape["seq"]

    def wrap(function, over, axes):
        ins, outs = specs(axes)
        return jax.shard_map(function, mesh=over, in_specs=ins, out_specs=outs, check_vma=False)

    def run(*args):
        seqs, length = args[0].shape[0] // depth, args[0].shape[1]
        fits = depth == WAYS and seq == 8 and seqs == 2 and length % 512 == 0
        if fits and args[1].shape == args[0].shape:
            axes = ("y", "x", "c")
            split = Mesh(mesh.devices.reshape(depth, 2, 2, 2), ("dp",) + axes)
            return wrap(functools.partial(grouped, depth), split, axes)(*args)
        return wrap(local, mesh, "seq")(*args)

    return run
```

```python
import functools
import math

import jax
import jax.numpy as jnp
from jax import lax
from jax.experimental import pallas as pl
from jax.experimental.pallas import tpu as pltpu
from jax.sharding import Mesh, PartitionSpec as P

D = 768
HEADS = 12
HEAD = 64
FF = 2048


EPSILON = 1e-06
NEGATIVE = -1e30
HIGHEST = lax.Precision.HIGHEST


def rounded(values):
    return values.astype(jnp.bfloat16)


def rows_first(values):
    return values.transpose(0, 2, 1)


def rms_norm(values, gain_row):
    return (
        values * lax.rsqrt(jnp.mean(values * values, axis=-1, keepdims=True) + EPSILON) * gain_row
    )


def rms_back(values, gain_row, upstream):
    _, pullback = jax.vjp(rms_norm, values, gain_row)
    return pullback(upstream)


def gated_unit(gate_up):
    return jax.nn.gelu(gate_up[0], approximate=True) * gate_up[1]


def offset_table(buckets, layer_bias):
    choose = (buckets[:, None] == jnp.arange(layer_bias.shape[0], dtype=jnp.int32)[None, :]).astype(
        jnp.float32
    )
    return jnp.dot(choose, layer_bias, precision=HIGHEST).T


def bucket_grad(buckets, grad_bias, bucket_count):
    choose = (buckets[:, None] == jnp.arange(bucket_count, dtype=jnp.int32)[None, :]).astype(
        jnp.float32
    )
    return jnp.dot(choose.T, grad_bias.T, precision=HIGHEST)


def hankel_block(window, rows, cols):
    heads_here, length = (window.shape[0], window.shape[1])
    tiled = jnp.tile(window, (1, rows + 1))[:, : rows * (length + 1)]
    return tiled.reshape(heads_here, rows, length + 1)[:, :, :cols]


def bias_block(variant, table, row_start, col_start, rows, cols, extent):
    span = rows + cols - 1
    if variant == "enc":
        base = col_start - row_start - (rows - 1) + (extent - 1)
        window = lax.dynamic_slice_in_dim(table, base, span, 1)
        return hankel_block(window, rows, cols)[:, ::-1, :]
    widened = jnp.concatenate(
        [jnp.broadcast_to(table[:, :1], (table.shape[0], extent - 1)), table], axis=1
    )
    base = row_start - col_start - (cols - 1) + (extent - 1)
    window = lax.dynamic_slice_in_dim(widened, base, span, 1)
    return hankel_block(window, rows, cols)[:, :, ::-1]


def visible_mask(variant, row_ids, col_ids, lengths):
    visible = col_ids[None, None, :] < lengths[:, None, None]
    if variant == "dec":
        visible = visible & (col_ids[None, None, :] <= row_ids[None, :, None])
    return visible[:, None]


def block_scores(query_heads, key_heads, row_ids, col_ids, lengths, variant, offset_bias, extent):
    factor = HEAD ** (-0.5)
    scores = (
        jnp.einsum("sqhe,skhe->shqk", query_heads, key_heads, preferred_element_type=jnp.float32)
        * factor
    )
    if offset_bias is not None:
        scores = (
            scores
            + bias_block(
                variant,
                offset_bias,
                row_ids[0],
                col_ids[0],
                row_ids.shape[0],
                col_ids.shape[0],
                extent,
            )[None]
        )
    return (scores, visible_mask(variant, row_ids, col_ids, lengths))


def row_products(grad_context, context):
    seqs_here, rows_here = (context.shape[0], context.shape[1])
    return jnp.sum(
        (grad_context.astype(jnp.float32) * context).reshape(seqs_here, rows_here, HEADS, HEAD),
        axis=-1,
    ).transpose(0, 2, 1)


def attend(queries, row_ids, lengths, variant, offset_bias, extent, fold_keys):
    seqs_here, rows_here = (queries.shape[0], queries.shape[1])
    query_heads = queries.reshape(seqs_here, rows_here, HEADS, HEAD)

    def fold_step(carried, pieces, begin_at):
        key_rows, value_rows = pieces
        block_len = math.gcd(key_rows.shape[1], 512)

        def block_step(block_id, running):
            row_max, row_sum, weighted = running
            offset_in = block_id * block_len
            key_heads = lax.dynamic_slice_in_dim(key_rows, offset_in, block_len, 1).reshape(
                seqs_here, block_len, HEADS, HEAD
            )
            value_heads = lax.dynamic_slice_in_dim(value_rows, offset_in, block_len, 1).reshape(
                seqs_here, block_len, HEADS, HEAD
            )
            col_ids = offset_in + jnp.arange(block_len, dtype=jnp.int32)
            scores, visible = block_scores(
                query_heads, key_heads, row_ids, col_ids, lengths, variant, offset_bias, extent
            )
            new_max = jnp.maximum(row_max, jnp.max(jnp.where(visible, scores, NEGATIVE), axis=-1))
            weights = jnp.where(visible, jnp.exp(scores - new_max[..., None]), 0.0)
            shrink = jnp.exp(row_max - new_max)
            row_sum = row_sum * shrink + jnp.sum(weights, axis=-1)
            weighted = weighted * shrink[..., None] + jnp.einsum(
                "shqk,skhe->shqe", rounded(weights), value_heads, preferred_element_type=jnp.float32
            )
            return (new_max, row_sum, weighted)

        return lax.fori_loop(0, key_rows.shape[1] // block_len, block_step, carried)

    initial = (
        jnp.full((seqs_here, HEADS, rows_here), NEGATIVE, jnp.float32),
        jnp.zeros((seqs_here, HEADS, rows_here), jnp.float32),
        jnp.zeros((seqs_here, HEADS, rows_here, HEAD), jnp.float32),
    )
    row_max, row_sum, weighted = fold_keys(fold_step, initial)
    context = (
        (weighted / row_sum[..., None])
        .transpose(0, 2, 1, 3)
        .reshape(seqs_here, rows_here, HEADS * HEAD)
    )
    return (context, row_max + jnp.log(row_sum))


def attend_back(
    queries,
    log_sums,
    row_dots,
    grad_context,
    row_ids,
    lengths,
    variant,
    offset_bias,
    extent,
    fold_keys,
):
    seqs_here, rows_here = (queries.shape[0], queries.shape[1])
    query_heads = queries.reshape(seqs_here, rows_here, HEADS, HEAD)
    grad_heads = grad_context.reshape(seqs_here, rows_here, HEADS, HEAD)
    bias_width = offset_bias.shape[1] if offset_bias is not None else 1
    factor = HEAD ** (-0.5)

    def fold_step(carried, pieces, begin_at):
        key_rows, value_rows = pieces
        block_len = math.gcd(key_rows.shape[1], 512)

        def block_step(block_id, running):
            grad_query, grad_bias = (running[0], running[-1])
            offset_in = block_id * block_len
            key_heads = lax.dynamic_slice_in_dim(key_rows, offset_in, block_len, 1).reshape(
                seqs_here, block_len, HEADS, HEAD
            )
            value_heads = lax.dynamic_slice_in_dim(value_rows, offset_in, block_len, 1).reshape(
                seqs_here, block_len, HEADS, HEAD
            )
            col_ids = offset_in + jnp.arange(block_len, dtype=jnp.int32)
            scores, visible = block_scores(
                query_heads, key_heads, row_ids, col_ids, lengths, variant, offset_bias, extent
            )
            weights = jnp.where(visible, jnp.exp(scores - log_sums[..., None]), 0.0)
            grad_weights = jnp.einsum(
                "sqhe,skhe->shqk", grad_heads, value_heads, preferred_element_type=jnp.float32
            )
            grad_scores = weights * (grad_weights - row_dots[..., None])
            if offset_bias is not None:

                def table_block(table_values):
                    return bias_block(
                        variant,
                        table_values,
                        row_ids[0],
                        col_ids[0],
                        row_ids.shape[0],
                        col_ids.shape[0],
                        extent,
                    )

                _, table_pull = jax.vjp(table_block, offset_bias)
                grad_bias = grad_bias + table_pull(jnp.sum(grad_scores, axis=0))[0]
            grad_raw = rounded(grad_scores * factor)
            grad_query = grad_query + jnp.einsum(
                "shqk,skhe->shqe", grad_raw, key_heads, preferred_element_type=jnp.float32
            )
            return (grad_query, grad_bias)

        return lax.fori_loop(0, key_rows.shape[1] // block_len, block_step, carried)

    query_start = jnp.zeros((seqs_here, HEADS, rows_here, HEAD), jnp.float32)
    bias_start = jnp.zeros((HEADS, bias_width), jnp.float32)
    initial = (query_start, bias_start)
    result = fold_keys(fold_step, initial)
    grad_query = result[0].transpose(0, 2, 1, 3).reshape(seqs_here, rows_here, HEADS * HEAD)
    return (grad_query, None, None, result[1])


def owned_key_grads(
    key_rows, value_rows, col_ids, lengths, variant, offset_bias, extent, fold_queries
):
    seqs_here, keys_here = (key_rows.shape[0], key_rows.shape[1])
    key_heads = key_rows.reshape(seqs_here, keys_here, HEADS, HEAD)
    value_heads = value_rows.reshape(seqs_here, keys_here, HEADS, HEAD)
    factor = HEAD ** (-0.5)

    def fold_step(carried, pieces, begin_at):
        query_rows, grad_rows, log_rows, dot_rows = pieces
        block_len = math.gcd(query_rows.shape[1], 512)

        def block_step(block_id, running):
            grad_keys, grad_values = running
            offset_in = block_id * block_len
            query_heads = lax.dynamic_slice_in_dim(query_rows, offset_in, block_len, 1).reshape(
                seqs_here, block_len, HEADS, HEAD
            )
            grad_heads = lax.dynamic_slice_in_dim(grad_rows, offset_in, block_len, 1).reshape(
                seqs_here, block_len, HEADS, HEAD
            )
            log_block = lax.dynamic_slice_in_dim(log_rows, offset_in, block_len, 1).transpose(
                0, 2, 1
            )
            dot_block = lax.dynamic_slice_in_dim(dot_rows, offset_in, block_len, 1).transpose(
                0, 2, 1
            )
            row_ids = offset_in + jnp.arange(block_len, dtype=jnp.int32)
            scores, visible = block_scores(
                query_heads, key_heads, row_ids, col_ids, lengths, variant, offset_bias, extent
            )
            weights = jnp.where(visible, jnp.exp(scores - log_block[..., None]), 0.0)
            grad_weights = jnp.einsum(
                "sqhe,skhe->shqk", grad_heads, value_heads, preferred_element_type=jnp.float32
            )
            grad_scores = weights * (grad_weights - dot_block[..., None])
            grad_raw = rounded(grad_scores * factor)
            grad_keys = grad_keys + jnp.einsum(
                "shqk,sqhe->skhe", grad_raw, query_heads, preferred_element_type=jnp.float32
            ).reshape(seqs_here, keys_here, HEADS * HEAD)
            grad_values = grad_values + jnp.einsum(
                "shqk,sqhe->skhe", rounded(weights), grad_heads, preferred_element_type=jnp.float32
            ).reshape(seqs_here, keys_here, HEADS * HEAD)
            return (grad_keys, grad_values)

        return lax.fori_loop(0, query_rows.shape[1] // block_len, block_step, carried)

    initial = (
        jnp.zeros((seqs_here, keys_here, HEADS * HEAD), jnp.float32),
        jnp.zeros((seqs_here, keys_here, HEADS * HEAD), jnp.float32),
    )
    return fold_queries(fold_step, initial)


def feed_forward(residual, gain_row, weights_in, weights_out):
    normed_low = rounded(rms_norm(residual, gain_row))
    gate_up = jnp.einsum(
        "srd,jdf->jsrf", normed_low, weights_in, preferred_element_type=jnp.float32
    )
    hidden = rounded(gated_unit(gate_up))
    output = jnp.einsum("srf,fd->srd", hidden, weights_out, preferred_element_type=jnp.float32)
    return (residual + output, (normed_low, gate_up, hidden))


def feed_back(residual, gain_row, weights_in, weights_out, kept_values, upstream):
    normed_low, gate_up, hidden = kept_values
    upstream_low = rounded(upstream)
    grad_out_weights = jnp.einsum(
        "srf,srd->fd", hidden, upstream_low, preferred_element_type=jnp.float32
    )
    grad_hidden = jnp.einsum(
        "srd,fd->srf", upstream_low, weights_out, preferred_element_type=jnp.float32
    )
    _, pullback = jax.vjp(gated_unit, gate_up)
    grad_gate_up = rounded(pullback(grad_hidden)[0])
    grad_in_weights = jnp.einsum(
        "srd,jsrf->jdf", normed_low, grad_gate_up, preferred_element_type=jnp.float32
    )
    grad_normed = jnp.einsum(
        "jsrf,jdf->srd", grad_gate_up, weights_in, preferred_element_type=jnp.float32
    )
    grad_residual, grad_gain = rms_back(residual, gain_row, grad_normed)
    return (upstream + grad_residual, grad_gain, grad_in_weights, grad_out_weights)


def local(
    enc_input,
    dec_input,
    enc_lengths,
    dec_lengths,
    enc_buckets,
    dec_buckets,
    attention_in,
    attention_out,
    hidden_in,
    hidden_out,
    norm_gains,
    position_bias,
    enc_cotangent,
    dec_cotangent,
):
    full_in, full_out, full_hidden_in, full_hidden_out, full_gains = (
        lax.all_gather(attention_in, ("dp", "seq"), axis=2, tiled=True),
        lax.all_gather(attention_out, ("dp", "seq"), axis=1, tiled=True),
        lax.all_gather(hidden_in, ("dp", "seq"), axis=2, tiled=True),
        lax.all_gather(hidden_out, ("dp", "seq"), axis=1, tiled=True),
        lax.all_gather(norm_gains, ("dp", "seq"), axis=1, tiled=True),
    )
    gain_rows = full_gains.astype(jnp.float32)
    enc_rows = enc_input.shape[1]
    dec_rows = dec_input.shape[1]
    seq_index = lax.axis_index("seq")
    enc_ids = seq_index * enc_rows + jnp.arange(enc_rows, dtype=jnp.int32)
    dec_ids = seq_index * dec_rows + jnp.arange(dec_rows, dtype=jnp.int32)
    enc_extent = (enc_buckets.shape[0] + 1) // 2
    dec_extent = dec_buckets.shape[0]
    enc_table = offset_table(enc_buckets, position_bias[0])
    dec_table = offset_table(dec_buckets, position_bias[1])
    enc_values = enc_input.astype(jnp.float32)
    norm_a_low = rounded(rms_norm(enc_values, gain_rows[0]))
    enc_qkv = rounded(
        jnp.einsum("srd,jde->jsre", norm_a_low, full_in[0], preferred_element_type=jnp.float32)
    )
    enc_context, enc_logs = attend(
        enc_qkv[0],
        enc_ids,
        enc_lengths,
        "enc",
        enc_table,
        enc_extent,
        lambda folder, initial: folder(
            initial,
            (
                lax.all_gather(enc_qkv[1], "seq", axis=1, tiled=True),
                lax.all_gather(enc_qkv[2], "seq", axis=1, tiled=True),
            ),
            jnp.int32(0),
        ),
    )
    enc_context_low = rounded(enc_context)
    enc_mid = enc_values + jnp.einsum(
        "srd,de->sre", enc_context_low, full_out[0], preferred_element_type=jnp.float32
    )
    enc_last, enc_ffn_kept = feed_forward(
        enc_mid, gain_rows[1], full_hidden_in[0], full_hidden_out[0]
    )
    memory = rms_norm(enc_last, gain_rows[2])
    memory_low = rounded(memory)
    dec_values = dec_input.astype(jnp.float32)
    norm_b_low = rounded(rms_norm(dec_values, gain_rows[3]))
    dec_qkv = rounded(
        jnp.einsum("srd,jde->jsre", norm_b_low, full_in[1], preferred_element_type=jnp.float32)
    )
    dec_context, dec_logs = attend(
        dec_qkv[0],
        dec_ids,
        dec_lengths,
        "dec",
        dec_table,
        dec_extent,
        lambda folder, initial: folder(
            initial,
            (
                lax.all_gather(dec_qkv[1], "seq", axis=1, tiled=True),
                lax.all_gather(dec_qkv[2], "seq", axis=1, tiled=True),
            ),
            jnp.int32(0),
        ),
    )
    dec_context_low = rounded(dec_context)
    dec_mid = dec_values + jnp.einsum(
        "srd,de->sre", dec_context_low, full_out[1], preferred_element_type=jnp.float32
    )
    norm_c_low = rounded(rms_norm(dec_mid, gain_rows[4]))
    cross_query = rounded(
        jnp.einsum("srd,de->sre", norm_c_low, full_in[2, 0], preferred_element_type=jnp.float32)
    )
    cross_pair = rounded(
        jnp.einsum("srd,jde->jsre", memory_low, full_in[2, 1:], preferred_element_type=jnp.float32)
    )
    cross_context, cross_logs = attend(
        cross_query,
        dec_ids,
        enc_lengths,
        "cross",
        None,
        0,
        lambda folder, initial: folder(
            initial,
            (
                lax.all_gather(cross_pair[0], "seq", axis=1, tiled=True),
                lax.all_gather(cross_pair[1], "seq", axis=1, tiled=True),
            ),
            jnp.int32(0),
        ),
    )
    cross_low = rounded(cross_context)
    dec_cross = dec_mid + jnp.einsum(
        "srd,de->sre", cross_low, full_out[2], preferred_element_type=jnp.float32
    )
    dec_last, dec_ffn_kept = feed_forward(
        dec_cross, gain_rows[5], full_hidden_in[1], full_hidden_out[1]
    )
    dec_final = rms_norm(dec_last, gain_rows[6])
    grad_dec_last, grad_gain_six = rms_back(
        dec_last, gain_rows[6], dec_cotangent.astype(jnp.float32)
    )
    grad_dec_cross, grad_gain_five, grad_hin_one, grad_hout_one = feed_back(
        dec_cross, gain_rows[5], full_hidden_in[1], full_hidden_out[1], dec_ffn_kept, grad_dec_last
    )
    upstream_low = rounded(grad_dec_cross)
    grad_out_two = jnp.einsum(
        "srd,sre->de", cross_low, upstream_low, preferred_element_type=jnp.float32
    )
    grad_cross_context = rounded(
        jnp.einsum("sre,de->srd", upstream_low, full_out[2], preferred_element_type=jnp.float32)
    )
    cross_dots = row_products(grad_cross_context, cross_context)
    cross_grad_query, cross_grad_keys, cross_grad_values, _ = attend_back(
        cross_query,
        cross_logs,
        cross_dots,
        grad_cross_context,
        dec_ids,
        enc_lengths,
        "cross",
        None,
        0,
        lambda folder, initial: folder(
            initial,
            (
                lax.all_gather(cross_pair[0], "seq", axis=1, tiled=True),
                lax.all_gather(cross_pair[1], "seq", axis=1, tiled=True),
            ),
            jnp.int32(0),
        ),
    )
    cross_query_low = rounded(cross_grad_query)
    grad_query_two = jnp.einsum(
        "srd,sre->de", norm_c_low, cross_query_low, preferred_element_type=jnp.float32
    )
    grad_norm_c = jnp.einsum(
        "sre,de->srd", cross_query_low, full_in[2, 0], preferred_element_type=jnp.float32
    )
    grad_mid_part, grad_gain_four = rms_back(dec_mid, gain_rows[4], grad_norm_c)
    grad_dec_mid = grad_dec_cross + grad_mid_part
    upstream_low = rounded(grad_dec_mid)
    grad_out_one = jnp.einsum(
        "srd,sre->de", dec_context_low, upstream_low, preferred_element_type=jnp.float32
    )
    grad_dec_context = rounded(
        jnp.einsum("sre,de->srd", upstream_low, full_out[1], preferred_element_type=jnp.float32)
    )
    dec_dots = row_products(grad_dec_context, dec_context)
    dec_grad_query, dec_grad_keys, dec_grad_values, grad_dec_bias = attend_back(
        dec_qkv[0],
        dec_logs,
        dec_dots,
        grad_dec_context,
        dec_ids,
        dec_lengths,
        "dec",
        dec_table,
        dec_extent,
        lambda folder, initial: folder(
            initial,
            (
                lax.all_gather(dec_qkv[1], "seq", axis=1, tiled=True),
                lax.all_gather(dec_qkv[2], "seq", axis=1, tiled=True),
            ),
            jnp.int32(0),
        ),
    )
    cross_key_grad, cross_value_grad = owned_key_grads(
        cross_pair[0],
        cross_pair[1],
        enc_ids,
        enc_lengths,
        "cross",
        None,
        0,
        lambda folder, initial: folder(
            initial,
            (
                lax.all_gather(cross_query, "seq", axis=1, tiled=True),
                lax.all_gather(grad_cross_context, "seq", axis=1, tiled=True),
                lax.all_gather(
                    rows_first(cross_logs).astype(jnp.bfloat16), "seq", axis=1, tiled=True
                ).astype(jnp.float32),
                lax.all_gather(
                    rows_first(cross_dots).astype(jnp.bfloat16), "seq", axis=1, tiled=True
                ).astype(jnp.float32),
            ),
            jnp.int32(0),
        ),
    )
    dec_key_grad, dec_value_grad = owned_key_grads(
        dec_qkv[1],
        dec_qkv[2],
        dec_ids,
        dec_lengths,
        "dec",
        dec_table,
        dec_extent,
        lambda folder, initial: folder(
            initial,
            (
                lax.all_gather(dec_qkv[0], "seq", axis=1, tiled=True),
                lax.all_gather(grad_dec_context, "seq", axis=1, tiled=True),
                lax.all_gather(
                    rows_first(dec_logs).astype(jnp.bfloat16), "seq", axis=1, tiled=True
                ).astype(jnp.float32),
                lax.all_gather(
                    rows_first(dec_dots).astype(jnp.bfloat16), "seq", axis=1, tiled=True
                ).astype(jnp.float32),
            ),
            jnp.int32(0),
        ),
    )
    pair_grads = rounded(jnp.stack([cross_key_grad, cross_value_grad]))
    grad_pair_two = jnp.einsum(
        "srd,jsre->jde", memory_low, pair_grads, preferred_element_type=jnp.float32
    )
    grad_memory = jnp.einsum(
        "jsre,jde->srd", pair_grads, full_in[2, 1:], preferred_element_type=jnp.float32
    )
    dec_grads = rounded(jnp.stack([dec_grad_query, dec_key_grad, dec_value_grad]))
    grad_in_one = jnp.einsum(
        "srd,jsre->jde", norm_b_low, dec_grads, preferred_element_type=jnp.float32
    )
    grad_norm_b = jnp.einsum(
        "jsre,jde->srd", dec_grads, full_in[1], preferred_element_type=jnp.float32
    )
    grad_dec_part, grad_gain_three = rms_back(dec_values, gain_rows[3], grad_norm_b)
    grad_dec_input = grad_dec_mid + grad_dec_part
    grad_memory_total = enc_cotangent.astype(jnp.float32) + grad_memory
    grad_enc_last, grad_gain_two = rms_back(enc_last, gain_rows[2], grad_memory_total)
    grad_enc_mid, grad_gain_one, grad_hin_zero, grad_hout_zero = feed_back(
        enc_mid, gain_rows[1], full_hidden_in[0], full_hidden_out[0], enc_ffn_kept, grad_enc_last
    )
    upstream_low = rounded(grad_enc_mid)
    grad_out_zero = jnp.einsum(
        "srd,sre->de", enc_context_low, upstream_low, preferred_element_type=jnp.float32
    )
    grad_enc_context = rounded(
        jnp.einsum("sre,de->srd", upstream_low, full_out[0], preferred_element_type=jnp.float32)
    )
    enc_dots = row_products(grad_enc_context, enc_context)
    enc_grad_query, enc_grad_keys, enc_grad_values, grad_enc_bias = attend_back(
        enc_qkv[0],
        enc_logs,
        enc_dots,
        grad_enc_context,
        enc_ids,
        enc_lengths,
        "enc",
        enc_table,
        enc_extent,
        lambda folder, initial: folder(
            initial,
            (
                lax.all_gather(enc_qkv[1], "seq", axis=1, tiled=True),
                lax.all_gather(enc_qkv[2], "seq", axis=1, tiled=True),
            ),
            jnp.int32(0),
        ),
    )
    enc_key_grad, enc_value_grad = owned_key_grads(
        enc_qkv[1],
        enc_qkv[2],
        enc_ids,
        enc_lengths,
        "enc",
        enc_table,
        enc_extent,
        lambda folder, initial: folder(
            initial,
            (
                lax.all_gather(enc_qkv[0], "seq", axis=1, tiled=True),
                lax.all_gather(grad_enc_context, "seq", axis=1, tiled=True),
                lax.all_gather(
                    rows_first(enc_logs).astype(jnp.bfloat16), "seq", axis=1, tiled=True
                ).astype(jnp.float32),
                lax.all_gather(
                    rows_first(enc_dots).astype(jnp.bfloat16), "seq", axis=1, tiled=True
                ).astype(jnp.float32),
            ),
            jnp.int32(0),
        ),
    )
    enc_grads = rounded(jnp.stack([enc_grad_query, enc_key_grad, enc_value_grad]))
    grad_in_zero = jnp.einsum(
        "srd,jsre->jde", norm_a_low, enc_grads, preferred_element_type=jnp.float32
    )
    grad_norm_a = jnp.einsum(
        "jsre,jde->srd", enc_grads, full_in[0], preferred_element_type=jnp.float32
    )
    grad_enc_part, grad_gain_zero = rms_back(enc_values, gain_rows[0], grad_norm_a)
    grad_enc_input = grad_enc_mid + grad_enc_part
    grad_cross_in = jnp.concatenate([grad_query_two[None], grad_pair_two], axis=0)
    grad_attention_in = jnp.stack([grad_in_zero, grad_in_one, grad_cross_in])
    grad_attention_out = jnp.stack([grad_out_zero, grad_out_one, grad_out_two])
    grad_hidden_in = jnp.stack([grad_hin_zero, grad_hin_one])
    grad_hidden_out = jnp.stack([grad_hout_zero, grad_hout_one])
    grad_gains = jnp.stack(
        [
            grad_gain_zero,
            grad_gain_one,
            grad_gain_two,
            grad_gain_three,
            grad_gain_four,
            grad_gain_five,
            grad_gain_six,
        ]
    )
    shard_in, shard_out, shard_hin, shard_hout, shard_gains = (
        lax.psum_scatter(grad_attention_in, ("dp", "seq"), scatter_dimension=2, tiled=True),
        lax.psum_scatter(grad_attention_out, ("dp", "seq"), scatter_dimension=1, tiled=True),
        lax.psum_scatter(grad_hidden_in, ("dp", "seq"), scatter_dimension=2, tiled=True),
        lax.psum_scatter(grad_hidden_out, ("dp", "seq"), scatter_dimension=1, tiled=True),
        lax.psum_scatter(grad_gains, ("dp", "seq"), scatter_dimension=1, tiled=True),
    )
    bucket_count = position_bias.shape[1]
    grad_position = jnp.stack(
        [
            bucket_grad(enc_buckets, grad_enc_bias, bucket_count),
            bucket_grad(dec_buckets, grad_dec_bias, bucket_count),
        ]
    )
    squares_in = shard_in * shard_in
    squares_out = shard_out * shard_out
    squares_hin = shard_hin * shard_hin
    squares_hout = shard_hout * shard_hout
    col_in, col_out, col_hin, col_hout, grad_position = lax.psum(
        (
            jnp.sum(squares_in, axis=2),
            jnp.sum(squares_out, axis=1),
            jnp.sum(squares_hin, axis=2),
            jnp.sum(squares_hout, axis=1),
            grad_position,
        ),
        ("dp", "seq"),
    )
    return (
        rounded(memory),
        rounded(dec_final),
        grad_enc_input,
        grad_dec_input,
        shard_in,
        shard_out,
        shard_hin,
        shard_hout,
        shard_gains,
        grad_position,
        0.5 * jnp.mean(squares_in, axis=-1),
        0.5 * col_in / D,
        0.5 * jnp.mean(squares_out, axis=-1),
        0.5 * col_out / D,
        0.5 * jnp.mean(squares_hin, axis=-1),
        0.5 * col_hin / D,
        0.5 * jnp.mean(squares_hout, axis=-1),
        0.5 * col_hout / FF,
    )


WAYS = 4
SETS = HEADS // WAYS
WIDTH = SETS * HEAD
VMEM_LIMIT = 16 * 2**20


def swap(values, axis):
    return lax.ppermute(values, axis, [(0, 1), (1, 0)])


def shift_z(values, hops, count):
    return lax.ppermute(values, "dp", [(i, (i + hops) % count) for i in range(count)])


def pair_up(mine, other, bit):
    first = bit == 0
    return jnp.stack([jnp.where(first, mine, other), jnp.where(first, other, mine)])


def pick(values, index, axis=0):
    return lax.dynamic_index_in_dim(values, index, axis, keepdims=False)


class Place:
    def __init__(self, depth):
        self.depth = depth
        self.z, self.y, self.x, self.c = [lax.axis_index(a) for a in ("dp", "y", "x", "c")]
        self.q = 2 * self.x + self.c
        self.index = (self.z * 2 + self.y) * WAYS + self.q


def exchange_over_x(place, pieces):
    halves = pieces.reshape((2, 2) + pieces.shape[1:])
    got = swap(pick(halves, 1 - place.x), "x")
    return pair_up(pick(halves, place.x), got, place.x)


def exchange_over_cores(place, both):
    got = swap(pick(both, 1 - place.c, 1), "c")
    whole = pair_up(pick(both, place.c, 1), got, place.c)
    return jnp.swapaxes(whole, 0, 1).reshape((4,) + both.shape[2:])


def exchange_columns(place, pieces):
    return exchange_over_cores(place, exchange_over_x(place, pieces))


def along_z(place, piece, *earlier):
    depth = place.depth
    held = jnp.zeros((depth,) + piece.shape, piece.dtype)
    arrivals = [shift_z(piece, k, depth) for k in range(1, depth)]
    if earlier:
        arrivals = [after(block, *earlier) for block in arrivals]
    for hops, block in enumerate([piece] + arrivals):
        held = lax.dynamic_update_index_in_dim(held, block, (place.z - hops) % depth, 0)
    return held


def along_y(place, held):
    other = swap(held, "y")
    first = place.y == 0
    pair = [jnp.where(first, held, other), jnp.where(first, other, held)]
    return jnp.stack(pair, axis=1).reshape(-1, held.shape[-1])


def scatter_y(place, parts):
    parts = parts.reshape((place.depth, 2) + parts.shape[1:])
    sent = swap(pick(parts, 1 - place.y, 1), "y")
    return pick(parts, place.y, 1).astype(F32) + sent.astype(F32)


def scatter_z(place, halves):
    depth = place.depth
    low = rounded(halves)
    total = pick(halves, place.z)
    for hops in range(1, depth):
        sent = shift_z(pick(low, (place.z + hops) % depth), hops, depth)
        total = total + sent.astype(F32)
    return total


def after(values, *earlier):
    return lax.optimization_barrier((values,) + earlier)[0]


def turn(values, depth):
    pairs = []
    for d in range(depth):
        for y in range(2):
            for q in range(WAYS):
                pairs.append((d * 8 + y * 4 + q, q * 8 + y * 4 + d))
    return lax.ppermute(values, ("dp", "y", "x", "c"), pairs)


def matmul(a, b):
    return jnp.dot(a, b, preferred_element_type=jnp.float32)


def matmul_nt(a, b):
    return lax.dot_general(a, b, (((1,), (1,)), ((), ())), preferred_element_type=jnp.float32)


def matmul_tn(a, b):
    return lax.dot_general(a, b, (((0,), (0,)), ((), ())), preferred_element_type=jnp.float32)


def call(kernel, name, outs, args, micros, scratch=()):
    whole = pl.BlockSpec(memory_space=pltpu.VMEM)
    arrays = [a[0] if isinstance(a, tuple) else a for a in args]
    specs = [a[1] if isinstance(a, tuple) else whole for a in args]
    late = [k for k, spec in enumerate(specs) if spec is LATE]
    plain = (whole, SCALARS, LATE, ANYWHERE)
    windows = any(all(spec is not p for p in plain) for spec in specs)
    shapes = tuple(jax.ShapeDtypeStruct(s, t) for s, t in outs)
    moved = sum(a.size * a.dtype.itemsize for a in list(arrays) + list(shapes))
    buffers = [pltpu.VMEM(arrays[k].shape, arrays[k].dtype) for k in late]

    def bring_in(*refs):
        if not late:
            return kernel(*refs)
        refs, places, semaphores = list(refs[: -len(late) - 1]), refs[-len(late) - 1 : -1], refs[-1]
        copies = [
            pltpu.make_async_copy(refs[k], place, semaphores.at[n])
            for n, (k, place) in enumerate(zip(late, places))
        ]
        for copy in copies:
            copy.start()
        for copy in copies:
            copy.wait()
        for k, place in zip(late, places):
            refs[k] = place
        return kernel(*refs)

    if late:
        buffers.append(pltpu.SemaphoreType.DMA((len(late),)))
    return pl.pallas_call(
        bring_in,
        grid=(1,) if windows else (),
        out_shape=shapes,
        in_specs=specs,
        out_specs=(whole,) * len(shapes),
        scratch_shapes=list(scratch) + buffers,
        compiler_params=pltpu.CompilerParams(vmem_limit_bytes=VMEM_LIMIT),
        cost_estimate=pl.CostEstimate(
            flops=int(micros * 1e7), bytes_accessed=moved // 32, transcendentals=0
        ),
        name=name,
    )(*arrays)


LATE = pl.BlockSpec(memory_space=pltpu.HBM)
ANYWHERE = pl.BlockSpec(memory_space=pl.ANY)
SCALARS = pl.BlockSpec(memory_space=pltpu.SMEM)
BF, F32 = jnp.bfloat16, jnp.float32


def column_block(array, index):
    rows, columns = array.shape
    return (array, pl.BlockSpec((rows, 2 * WIDTH), lambda _: (0, index)))


def norm_rows(values, gain):
    return values * lax.rsqrt(jnp.mean(values * values, axis=-1, keepdims=True) + EPSILON) * gain


def norm_back(values, gain, upstream):
    scale = lax.rsqrt(jnp.mean(values * values, axis=-1, keepdims=True) + EPSILON)
    unit = values * scale
    inner = upstream * gain
    grad = scale * (inner - unit * jnp.mean(inner * unit, axis=-1, keepdims=True))
    return grad, jnp.sum(upstream * unit, axis=0, keepdims=True)


def self_kernel(gain, q_at, x_ref, gains_ref, kva_ref, qa_ref, kvb_ref, qb_ref, *outs):
    n_ref, q_ref, kv_ref = outs
    n = norm_rows(x_ref[...].astype(F32), gains_ref[gain : gain + 1, :]).astype(BF)
    n_ref[...] = n
    for e, (kv, q) in enumerate(((kva_ref, qa_ref), (kvb_ref, qb_ref))):
        kv_ref[e] = matmul(n, kv[:, : 2 * WIDTH]).astype(BF)
        q_ref[e] = matmul(n, q[:, q_at : q_at + WIDTH]).astype(BF)


def self_project(x, gains, gain, kv_own, q_own, kv_sib, q_sib, q_at, name):
    rows = x.shape[0]
    return call(
        functools.partial(self_kernel, gain, q_at),
        name,
        [((rows, D), BF), ((2, rows, WIDTH), BF), ((2, rows, 2 * WIDTH), BF)],
        [x, gains, kv_own, q_own, kv_sib, q_sib],
        2.5,
    )


def memory_kernel(res_ref, part_ref, got_ref, gains_ref, kva_ref, kvb_ref, *outs):
    last_ref, low_ref, kv_ref = outs
    last = res_ref[...].astype(F32) + part_ref[...] + got_ref[...].astype(F32)
    last_ref[...] = last
    low = norm_rows(last, gains_ref[2:3, :]).astype(BF)
    low_ref[...] = low
    for e, kv in enumerate((kva_ref, kvb_ref)):
        kv_ref[e] = matmul(low, kv[...]).astype(BF)


def cross_kernel(q_at, res_ref, part_ref, got_ref, gains_ref, qa_ref, qb_ref, *outs):
    mid_ref, low_ref, q_ref = outs
    mid = res_ref[...].astype(F32) + part_ref[...] + got_ref[...].astype(F32)
    mid_ref[...] = mid
    low = norm_rows(mid, gains_ref[4:5, :]).astype(BF)
    low_ref[...] = low
    for e, q in enumerate((qa_ref, qb_ref)):
        q_ref[e] = matmul(low, q[:, q_at : q_at + WIDTH]).astype(BF)


def lay_out_keys(core, kv_ref, got_ref, keys):
    block = kv_ref.shape[1] // 4
    for e in range(2):
        for k in range(4):
            at = pl.multiple_of(block * (2 * k + core), block)
            keys[e, pl.ds(at, block), :] = kv_ref[e, k * block : (k + 1) * block, :]
            at = pl.multiple_of(block * (2 * k + 1 - core), block)
            keys[e, pl.ds(at, block), :] = got_ref[1 - e, k * block : (k + 1) * block, :]


def attend_kernel(causal, biased, *refs):
    if biased:
        scalars, q_ref, kv_ref, got_ref, table_ref, oa_ref, ob_ref = refs[:7]
    else:
        scalars, q_ref, kv_ref, got_ref, oa_ref, ob_ref = refs[:6]
    ctx_ref, p_ref, part_ref, low_ref, keys = refs[-5:]
    core, length = scalars[0], scalars[1]
    lay_out_keys(core, kv_ref, got_ref, keys)
    rows, extent = q_ref.shape[1], keys.shape[1]
    block = rows // 4
    cols = lax.broadcasted_iota(jnp.int32, (block, extent), 1)
    ids = lax.broadcasted_iota(jnp.int32, (block, extent), 0)
    total = None
    for e in range(2):
        for h in range(SETS):
            at = slice(h * HEAD, (h + 1) * HEAD)
            k = keys[e, :, at]
            v = keys[e, :, WIDTH + h * HEAD : WIDTH + (h + 1) * HEAD]
            scores = matmul_nt(q_ref[e, :, at], k)
            if biased:
                line = table_ref[e * SETS + h : e * SETS + h + 1, :]
                skew = pltpu.roll(
                    jnp.broadcast_to(line, (block, 2 * extent)),
                    2 * extent - (block - 1),
                    1,
                    stride=1,
                    stride_axis=0,
                )
            for i in range(4):
                here = slice(i * block, (i + 1) * block)
                s = scores[here] * (HEAD**-0.5)
                if biased:
                    begin = (3 - i) * 2 * block
                    s = s + skew[:, begin : begin + extent]
                visible = cols < length
                if causal:
                    visible = visible & (cols <= ids + (i * 2 * block + core * block))
                s = jnp.where(visible, s, NEGATIVE)
                weights = jnp.exp(s - jnp.max(s, axis=-1, keepdims=True))
                weights = weights * (1.0 / jnp.sum(weights, axis=-1, keepdims=True))
                p_ref[e * SETS + h, here, :] = weights.astype(BF)
            ctx_ref[e, :, at] = matmul(p_ref[e * SETS + h], v)
        term = matmul(ctx_ref[e].astype(BF), (oa_ref, ob_ref)[e][...])
        total = term if total is None else total + term
    part_ref[...] = total
    low_ref[...] = total.astype(BF)


def attend_local(scalars, q, kv, got, table, out_own, out_sib, causal, name):
    rows = q.shape[1]
    extent = 2 * rows
    args = [(scalars, SCALARS), q, kv, got] + ([] if table is None else [table])
    return call(
        functools.partial(attend_kernel, causal, table is not None),
        name,
        [
            ((2, rows, WIDTH), F32),
            ((2 * SETS, rows, extent), BF),
            ((rows, D), F32),
            ((rows, D), BF),
        ],
        args + [out_own, out_sib],
        5.5,
        [pltpu.VMEM((2, extent, 2 * WIDTH), BF)],
    )


def unpack_into(w_ref, columns, down):
    blocks, rows = 8, down.shape[0] // 8
    half, third = rows // 2, down.shape[1] // 3
    step = rows + half
    for b in range(blocks):
        down[b * rows : (b + 1) * rows, : 2 * third] = w_ref[
            b * step : b * step + rows, columns : columns + 2 * third
        ]
        for k in range(2):
            down[b * rows + k * half : b * rows + (k + 1) * half, 2 * third :] = w_ref[
                b * step + rows : (b + 1) * step,
                columns + k * third : columns + (k + 1) * third,
            ]


GELU_A, GELU_B = (2 / math.pi) ** 0.5, 0.044715


def gelu_tanh(gate):
    return jnp.tanh(GELU_A * (gate + GELU_B * gate * gate * gate))


def ffn_kernel(gain, res_ref, part_ref, got_ref, gains_ref, wa_ref, wb_ref, *refs):
    mid_ref, n_ref, gu_ref, hid_ref, out_ref, low_ref, down = refs
    mid = res_ref[...].astype(F32) + part_ref[...] + got_ref[...].astype(F32)
    mid_ref[...] = mid
    n = norm_rows(mid, gains_ref[gain : gain + 1, :]).astype(BF)
    n_ref[...] = n
    units = down.shape[0]
    total = None
    for e, w_ref in enumerate((wa_ref, wb_ref)):
        gu_ref[e] = matmul(n, w_ref[:, : 2 * units])
        gate, up = gu_ref[e, :, :units], gu_ref[e, :, units:]
        hid_ref[e] = (0.5 * gate * (1.0 + gelu_tanh(gate)) * up).astype(BF)
        unpack_into(w_ref, 2 * units, down)
        term = matmul(hid_ref[e], down[...])
        total = term if total is None else total + term
    out_ref[...] = total
    low_ref[...] = total.astype(BF)


def ffn_local(res, part, got, gains, gain, w_own, w_sib, units, name):
    rows = res.shape[0]
    return call(
        functools.partial(ffn_kernel, gain),
        name,
        [
            ((rows, D), F32),
            ((rows, D), BF),
            ((2, rows, 2 * units), F32),
            ((2, rows, units), BF),
            ((rows, D), F32),
            ((rows, D), BF),
        ],
        [res, part, got, gains, w_own, w_sib],
        3.0,
        [pltpu.VMEM((units, D), BF)],
    )


def ffn_back_kernel(decoder, val_ref, part_ref, got_ref, cot_ref, gains_ref, *refs):
    gu_ref, wa_ref, wb_ref = refs[:3]
    down = refs[-1]
    sent = part_ref[...] + got_ref[...].astype(F32)
    if decoder:
        final_ref, g_ref, dgain_ref, low_ref, dgu_ref, out_ref, out_low_ref = refs[3:-1]
        gain = gains_ref[6:7, :]
        values = val_ref[...] + sent
        upstream = cot_ref[...].astype(F32)
        final_ref[...] = norm_rows(values, gain).astype(BF)
    else:
        g_ref, dgain_ref, low_ref, dgu_ref, out_ref, out_low_ref = refs[3:-1]
        gain = gains_ref[2:3, :]
        values = val_ref[...]
        upstream = cot_ref[...].astype(F32) + sent
    grad, dgain_ref[...] = norm_back(values, gain, upstream)
    g_ref[...] = grad
    low = grad.astype(BF)
    low_ref[...] = low
    units = down.shape[0]
    total = None
    for e, w_ref in enumerate((wa_ref, wb_ref)):
        unpack_into(w_ref, 2 * units, down)
        grad_hidden = matmul_nt(low, down[...])
        gate, up = gu_ref[e, :, :units], gu_ref[e, :, units:]
        t = gelu_tanh(gate)
        slope = 0.5 * (1.0 + t) + 0.5 * gate * (1.0 - t * t) * GELU_A * (
            1.0 + 3.0 * GELU_B * gate * gate
        )
        dgu_ref[e, :, :units] = (grad_hidden * up * slope).astype(BF)
        dgu_ref[e, :, units:] = (grad_hidden * (0.5 * gate * (1.0 + t))).astype(BF)
        term = matmul_nt(dgu_ref[e], w_ref[:, : 2 * units])
        total = term if total is None else total + term
    out_ref[...] = total
    out_low_ref[...] = total.astype(BF)


def ffn_back(decoder, values, part, got, cot, gains, gate_up, w_own, w_sib, name):
    rows, units = values.shape[0], gate_up.shape[2] // 2
    outs = [((rows, D), BF)] if decoder else []
    outs += [
        ((rows, D), F32),
        ((1, D), F32),
        ((rows, D), BF),
        ((2, rows, 2 * units), BF),
        ((rows, D), F32),
        ((rows, D), BF),
    ]
    return call(
        functools.partial(ffn_back_kernel, decoder),
        name,
        outs,
        [values, part, got, cot, gains, gate_up, w_own, w_sib],
        4.0,
        [pltpu.VMEM((units, D), BF)],
    )


def ffn_weights_kernel(n_ref, dgu_ref, hid_ref, low_ref, own_ref, sib_ref):
    units = hid_ref.shape[2]
    rows, half, third = units // 8, units // 16, D // 3
    step = rows + half
    for e, out in enumerate((own_ref, sib_ref)):
        out[:, : 2 * units] = matmul_tn(n_ref[...], dgu_ref[e]).astype(BF)
        down = matmul_tn(hid_ref[e], low_ref[...]).astype(BF)
        for b in range(8):
            out[b * step : b * step + rows, 2 * units :] = down[
                b * rows : (b + 1) * rows, : 2 * third
            ]
            for k in range(2):
                out[
                    b * step + rows : (b + 1) * step,
                    2 * units + k * third : 2 * units + (k + 1) * third,
                ] = down[b * rows + k * half : b * rows + (k + 1) * half, 2 * third :]


def ffn_weights(n, dgu, hid, low, name):
    units = hid.shape[2]
    shape = ((D, 2 * units + 2 * D // 3), BF)
    return call(
        ffn_weights_kernel, name, [shape, shape], [n, dgu, hid, low], 1.5
    )


def attend_back_kernel(gain, biased, scalars, up_ref, val_ref, part_ref, got_ref, *refs):
    gains_ref, oa_ref, ob_ref, q_ref, kv_ref, kvgot_ref, p_ref, ctx_ref = refs[:8]
    g_ref, dgain_ref, low_ref, dq_ref, mine_ref, other_ref = refs[8:14]
    keys, dkeys, ds_ref = refs[-3:]
    core = scalars[0]
    grad, dgain_ref[...] = norm_back(
        val_ref[...], gains_ref[gain : gain + 1, :], part_ref[...] + got_ref[...].astype(F32)
    )
    grad = up_ref[...] + grad
    g_ref[...] = grad
    low = grad.astype(BF)
    low_ref[...] = low
    lay_out_keys(core, kv_ref, kvgot_ref, keys)
    rows, extent = q_ref.shape[1], keys.shape[1]
    block = rows // 4
    factor = HEAD**-0.5
    for e in range(2):
        g = matmul_nt(low, (oa_ref, ob_ref)[e][...]).astype(BF)
        products = g.astype(F32) * ctx_ref[e]
        for h in range(SETS):
            at = slice(h * HEAD, (h + 1) * HEAD)
            k = keys[e, :, at]
            v = keys[e, :, WIDTH + h * HEAD : WIDTH + (h + 1) * HEAD]
            dots = jnp.sum(products[:, at], axis=-1, keepdims=True)
            dp = matmul_nt(g[:, at], v)
            sums = [None] * 7
            for i in range(4):
                here = slice(i * block, (i + 1) * block)
                ds = p_ref[e * SETS + h, here, :].astype(F32) * (dp[here] - dots[here])
                if biased:
                    for j in range(4):
                        part = ds[:, j * 2 * block : (j + 1) * 2 * block]
                        slot = 3 - i + j
                        sums[slot] = part if sums[slot] is None else sums[slot] + part
                ds_ref[here, :] = (ds * factor).astype(BF)
            dq_ref[e, :, at] = matmul(ds_ref[...], k).astype(BF)
            dkeys[:, at] = matmul_tn(ds_ref[...], q_ref[e, :, at])
            dkeys[:, WIDTH + h * HEAD : WIDTH + (h + 1) * HEAD] = matmul_tn(
                p_ref[e * SETS + h], g[:, at]
            )
            if biased:
                dtable_ref = refs[14]
                band = jnp.concatenate(sums + [jnp.zeros_like(sums[0])], axis=1)
                ids = lax.broadcasted_iota(jnp.int32, band.shape, 0)
                bit = 1
                while bit < block:
                    moved = pltpu.roll(band, 2 * extent - bit, 1)
                    band = jnp.where((ids & bit) != 0, moved, band)
                    bit *= 2
                line = jnp.sum(band, axis=0, keepdims=True)
                dtable_ref[e * SETS + h : e * SETS + h + 1, :] = pltpu.roll(line, block - 1, 1)
        for k in range(4):
            at = pl.multiple_of(block * (2 * k + core), block)
            mine_ref[e, k * block : (k + 1) * block, :] = dkeys[pl.ds(at, block), :]
            at = pl.multiple_of(block * (2 * k + 1 - core), block)
            other_ref[1 - e, k * block : (k + 1) * block, :] = dkeys[
                pl.ds(at, block), :
            ].astype(BF)


def attend_local_back(gain, biased, scalars, upstream, values, part, got, gains, *rest, name):
    rows, extent = upstream.shape[0], 2 * upstream.shape[0]
    outs = [
        ((rows, D), F32),
        ((1, D), F32),
        ((rows, D), BF),
        ((2, rows, WIDTH), BF),
        ((2, rows, 2 * WIDTH), F32),
        ((2, rows, 2 * WIDTH), BF),
    ]
    if biased:
        outs.append(((2 * SETS, 2 * extent), F32))
    return call(
        functools.partial(attend_back_kernel, gain, biased),
        name,
        outs,
        [(scalars, SCALARS), (upstream, LATE), (values, LATE), part, got, gains]
        + list(rest[:2])
        + [(a, LATE) for a in rest[2:]],
        9.0 if biased else 6.0,
        [
            pltpu.VMEM((2, extent, 2 * WIDTH), BF),
            pltpu.VMEM((extent, 2 * WIDTH), F32),
            pltpu.VMEM((rows, extent), BF),
        ],
    )


def project_back_kernel(split, q_at, dq_ref, mine_ref, got_ref, *refs):
    kva_ref, qa_ref, kvb_ref, qb_ref = refs[:4]
    dkv_ref = refs[4]
    from_keys = from_queries = None
    for e, (kv, q) in enumerate(((kva_ref, qa_ref), (kvb_ref, qb_ref))):
        dkv = (mine_ref[e] + got_ref[e].astype(F32)).astype(BF)
        dkv_ref[e] = dkv
        term = matmul_nt(dkv, kv[:, : 2 * WIDTH])
        from_keys = term if e == 0 else from_keys + term
        term = matmul_nt(dq_ref[e], q[:, q_at : q_at + WIDTH])
        from_queries = term if e == 0 else from_queries + term
    outs = [from_keys, from_queries] if split else [from_keys + from_queries]
    for k, total in enumerate(outs):
        refs[5 + 2 * k][...] = total
        refs[6 + 2 * k][...] = total.astype(BF)


def project_back(split, dq, mine, got, kv_own, q_own, kv_sib, q_sib, q_at, name):
    rows = dq.shape[1]
    outs = [((2, rows, 2 * WIDTH), BF)] + [((rows, D), F32), ((rows, D), BF)] * (1 + split)
    return call(
        functools.partial(project_back_kernel, split, q_at),
        name,
        outs,
        [dq, mine, got, kv_own, q_own, kv_sib, q_sib],
        2.5,
    )


def attend_weights_kernel(count, *refs):
    ins, (own_ref, sib_ref, out_own_ref, out_sib_ref) = refs[:-4], refs[-4:]
    for k in range(count):
        nq_ref, nkv_ref, dq_ref, dkv_ref, ctx_ref, low_ref = ins[6 * k : 6 * k + 6]
        kv_at, q_at = 2 * WIDTH * k, 2 * WIDTH * count + WIDTH * k
        for e, (in_ref, out_ref) in enumerate(((own_ref, out_own_ref), (sib_ref, out_sib_ref))):
            if k == 0 and in_ref.shape[1] > 3 * count * WIDTH:
                in_ref[...] = jnp.zeros_like(in_ref)
            in_ref[:, kv_at : kv_at + 2 * WIDTH] = matmul_tn(nkv_ref[...], dkv_ref[e]).astype(BF)
            in_ref[:, q_at : q_at + WIDTH] = matmul_tn(nq_ref[...], dq_ref[e]).astype(BF)
            out_ref[k] = matmul_tn(ctx_ref[e].astype(BF), low_ref[...]).astype(BF)


def attend_weights(name, *attentions):
    count, rows = len(attentions), attentions[0][0].shape[0]
    inner, outer = ((D, -(-3 * count * WIDTH // 128) * 128), BF), ((count, WIDTH, D), BF)
    own, sib, out_own, out_sib = call(
        functools.partial(attend_weights_kernel, count),
        name,
        [inner, inner, outer, outer],
        [a for attention in attentions for a in attention],
        1.0 * count,
    )
    return own, out_own, sib, out_sib


IN_ORDER = (8, 6, 7, 4, 0, 1, 5, 2, 3)


def sums_kernel(own, late_ref, dec_ref, self_ref, out_ref):
    inner, third, half = 6 * WIDTH, D // 3, D // 2
    width = dec_ref.shape[1]
    wide, rows = width - 2 * third, dec_ref.shape[0] * 2 // 3
    out_ref[...] = jnp.zeros_like(out_ref)

    def squares(values, rows_in_all):
        values = values.astype(F32)
        return values * values * (0.5 / rows_in_all)

    def line(values):
        return jnp.sum(values, axis=0, keepdims=True)

    def put(at, values):
        for k in range(0, values.shape[1], 128):
            size = min(128, values.shape[1] - k)
            out_ref[at + k // 128 : at + k // 128 + 1, :size] = values[:, k : k + size]

    put(0, line(squares(late_ref[:, :wide], D)))
    put(wide // 128, line(squares(dec_ref[:, :wide], D)))
    at = 2 * wide // 128
    put(at, line(squares(late_ref[:, width : width + inner], D)))
    put(at + inner // 128, line(squares(self_ref[:, third : third + 3 * WIDTH], D)))
    at = 30
    for ref in (late_ref, dec_ref):
        down = squares(ref[:, wide:width], FF)
        put(at, line(down[:rows]))
        put(at + 2 * third // 128, line(down[rows:, :third]) + line(down[rows:, third:]))
        at += D // 128
    outer = squares(self_ref[:, :third], D)
    for k in range(3):
        put(at + k * third // 128, line(outer[k * own : (k + 1) * own]))
    at += D // 128
    outer = squares(late_ref[:, width + inner :], D)
    for k in range(2):
        for side in range(2):
            begin = (2 * side + k) * own
            put(at + side * half // 128, line(outer[begin : begin + own]))
        at += D // 128


def hold_kernel(values_ref, earlier_ref, out_ref):
    out_ref[...] = values_ref[...]


def half_mean_rows(values):
    ones = jnp.full((8, values.shape[1]), 0.5 / values.shape[1], F32)
    sums = lax.dot_general(
        ones,
        values * values,
        (((1,), (1,)), ((), ())),
        precision=HIGHEST,
        preferred_element_type=F32,
    )
    return sums[:1]


def shards_kernel(ff_own, columns_ref, turned_ref, late_ref, dec_ref, *outs):
    in_ref, out_ref, hin_ref, hout_ref, row_in_ref, row_out_ref, row_hin_ref, row_hout_ref = outs
    third = D // 3
    width = dec_ref.shape[1]
    wide = width - 2 * third
    units = wide // 2
    for k, at in enumerate(IN_ORDER):
        at = wide + at * WIDTH
        for q in range(WAYS):
            piece = columns_ref[q, :, at : at + WIDTH]
            in_ref[k // 3, k % 3, :, q * WIDTH : (q + 1) * WIDTH] = piece
        row_in_ref[k : k + 1, :] = half_mean_rows(in_ref[k // 3, k % 3])
    out_ref[...] = turned_ref[...]
    for k in range(3):
        row_out_ref[k : k + 1, :] = half_mean_rows(turned_ref[k])
    for layer in range(2):
        begin = wide + 9 * WIDTH if layer == 0 else 0
        for j in range(2):
            for k in range(units // ff_own):
                first = begin + j * units + k * ff_own
                for q in range(WAYS):
                    at = (WAYS * k + q) * ff_own
                    piece = columns_ref[q, :, first : first + ff_own]
                    hin_ref[layer, j, :, at : at + ff_own] = piece
            row_hin_ref[2 * layer + j : 2 * layer + j + 1, :] = half_mean_rows(hin_ref[layer, j])
    for layer, ref in enumerate((late_ref, dec_ref)):
        down = ref[:, wide:width].astype(F32)
        hout_ref[layer, :, : 2 * third] = down[:ff_own]
        half = ff_own // 2
        hout_ref[layer, :half, 2 * third :] = down[ff_own:, :third]
        hout_ref[layer, half:, 2 * third :] = down[ff_own:, third:]
        row_hout_ref[layer : layer + 1, :] = half_mean_rows(hout_ref[layer])


def input_kernel(gain, up_ref, x_ref, part_ref, got_ref, gains_ref, out_ref, dgain_ref):
    grad, dgain_ref[...] = norm_back(
        x_ref[...].astype(F32),
        gains_ref[gain : gain + 1, :],
        part_ref[...] + got_ref[...].astype(F32),
    )
    out_ref[...] = up_ref[...] + grad


def input_back(gain, upstream, x, part, got, gains, name):
    return call(
        functools.partial(input_kernel, gain),
        name,
        [(upstream.shape, F32), ((1, D), F32)],
        [upstream, x, part, got, gains],
        1.5,
    )


def gather_own_rows(place, mine, other_seq):
    near = pair_up(mine, swap(other_seq, "y"), place.y)
    far = pair_up(near, swap(near, "x"), place.x)
    far = far.transpose(2, 1, 0, 3, 4)
    return far.reshape(far.shape[0], -1, far.shape[4])


def give_back(place, half):
    blocks = half.reshape(2, 2, -1, half.shape[1])
    blocks = pick(blocks, place.x, 1)
    other = swap(pick(blocks, 1 - place.y), "y")
    return pair_up(pick(blocks, place.y), other, place.y)


def sum_everywhere(place, values):
    depth = place.depth
    for axis in ("c", "x", "y"):
        values = values + swap(values, axis)
    return values + sum(shift_z(values, k, depth) for k in range(1, depth))


def pack_down(rows):
    half, third = rows.shape[-2] // 2, rows.shape[-1] // 3
    last = rows[..., 2 * third :]
    last = jnp.concatenate([last[..., :half, :], last[..., half:, :]], axis=-1)
    return jnp.concatenate([rows[..., : 2 * third], last], axis=-2)


def unpack_down(packed):
    half, third = packed.shape[-2] // 3, packed.shape[-1] // 2
    last = packed[..., 2 * half :, :]
    last = jnp.concatenate([last[..., :third], last[..., third:]], axis=-2)
    return jnp.concatenate([packed[..., : 2 * half, :], last], axis=-1)


def pack_out(pair):
    rows = pair.reshape(pair.shape[:-3] + (-1, pair.shape[-1]))
    half = rows.shape[-1] // 2
    return jnp.concatenate([rows[..., :half], rows[..., half:]], axis=-2)


def unpack_out_piece(packed):
    half = packed.shape[-2] // 2
    rows = jnp.concatenate([packed[..., :half, :], packed[..., half:, :]], axis=-1)
    return rows.reshape(rows.shape[:-2] + (2, half // 2, rows.shape[-1]))


def unpack_out(packed, depth):
    pair = unpack_out_piece(packed)
    pair = pair.reshape((depth, 2) + pair.shape[1:])
    pair = pair.transpose(2, 1, 0, 3, 4)
    return pair.reshape(2, -1, pair.shape[-1])


def turned_parts(grads, depth):
    parts = grads.reshape(2, depth, -1, grads.shape[1]).transpose(1, 0, 2, 3)
    return parts.reshape(2 * depth, -1, grads.shape[1])


def grouped(
    depth,
    enc_input,
    dec_input,
    enc_lengths,
    dec_lengths,
    enc_buckets,
    dec_buckets,
    attention_in,
    attention_out,
    hidden_in,
    hidden_out,
    norm_gains,
    position_bias,
    enc_cotangent,
    dec_cotangent,
):
    place = Place(depth)
    y, q = place.y, place.q
    block = enc_input.shape[1]
    length = block * 8
    own = attention_in.shape[2]
    ff_own = hidden_out.shape[1]
    units = ff_own * 2 * depth
    group = WAYS * own

    pieces = attention_in.reshape(3, 3, own, WAYS, WIDTH).transpose(3, 0, 1, 2, 4)
    queries, keys, values = pieces[:, :, 0], pieces[:, :, 1], pieces[:, :, 2]
    gain_piece = jnp.pad(norm_gains.T, ((0, 0), (0, 64 - norm_gains.shape[0])))
    gain_piece = jnp.broadcast_to(gain_piece[None], (WAYS,) + gain_piece.shape)
    turned = turn(attention_out, depth)
    hidden_pieces = hidden_in.reshape(2, 2, own, 2 * depth, WAYS, ff_own)
    hidden_pieces = hidden_pieces.transpose(4, 0, 2, 1, 3, 5).reshape(WAYS, 2, own, 2 * units)
    blocks_in = [keys[:, 0], values[:, 0], queries[:, 0], gain_piece]
    blocks_in += [keys[:, 1], values[:, 1], keys[:, 2], values[:, 2], queries[:, 1], queries[:, 2]]
    blocks_in += [hidden_pieces[:, 0], hidden_pieces[:, 1]]
    everything = exchange_columns(place, jnp.concatenate(blocks_in, axis=2)).reshape(group, -1)
    cuts = [3 * WIDTH + 64, 9 * WIDTH + 64, 9 * WIDTH + 64 + 2 * units]
    enc_piece, rest, ffn_enc, ffn_dec = jnp.split(everything, cuts, axis=1)
    third = turned[0].reshape(own, 3, D // 3).transpose(1, 0, 2).reshape(3 * own, D // 3)
    third = jnp.pad(third, ((0, group - 3 * own), (0, 0)))
    enc_piece = jnp.concatenate([enc_piece, third], axis=1)
    rest = jnp.concatenate([rest, pack_out(turned[1:])], axis=1)
    ffn_enc = jnp.concatenate([ffn_enc, pack_down(hidden_out[0])], axis=1)
    ffn_dec = jnp.concatenate([ffn_dec, pack_down(hidden_out[1])], axis=1)

    line = along_z(place, enc_piece)
    w_enc = along_y(place, line)
    w_enc_sib = swap(w_enc, "c")

    def out_rows(whole):
        rows = whole[:, 3 * WIDTH + 64 :].reshape(depth, 2, group, D // 3)[:, :, : 3 * own]
        rows = rows.reshape(depth, 2, 3, own, D // 3).transpose(1, 0, 3, 2, 4)
        return rows.reshape(WIDTH, D)

    def gather(piece):
        return lax.all_gather(piece, ("dp", "y"), axis=0, tiled=True)

    first = gather(jnp.concatenate([rest, ffn_enc], axis=1))
    out_enc, out_enc_sib = out_rows(w_enc), out_rows(w_enc_sib)
    gains = w_enc[:, 3 * WIDTH : 3 * WIDTH + norm_gains.shape[0]].astype(F32).T

    w_self = [w_enc, w_enc, w_enc_sib, w_enc_sib]

    def own_rows(*arrays):
        mine = jnp.stack([pick(a, y) for a in arrays])
        other = jnp.stack([pick(a, 1 - y) for a in arrays])
        return gather_own_rows(place, mine, other)

    enc_rows, dec_rows, *cots = own_rows(enc_input, dec_input, dec_cotangent, enc_cotangent)
    enc_scalars = jnp.stack([place.c, pick(enc_lengths, y)]).astype(jnp.int32)
    dec_scalars = jnp.stack([place.c, pick(dec_lengths, y)]).astype(jnp.int32)

    def head_rows(table):
        mine = lax.dynamic_slice_in_dim(table, q * SETS, SETS, 0)
        theirs = lax.dynamic_slice_in_dim(table, (q + 1 - 2 * place.c) * SETS, SETS, 0)
        table = jnp.concatenate([mine, theirs])
        table = jnp.pad(table, ((0, 0), (0, block)))
        return lax.dynamic_slice_in_dim(table, block * (1 - place.c), 2 * length, 1)

    enc_table = offset_table(enc_buckets, position_bias[0])
    enc_table = head_rows(jnp.pad(enc_table, ((0, 0), (0, 1))))
    dec_table = offset_table(dec_buckets, position_bias[1])
    dec_table = jnp.concatenate(
        [dec_table[:, ::-1], jnp.broadcast_to(dec_table[:, :1], (HEADS, length))], axis=1
    )
    dec_table = head_rows(dec_table)

    n_a, q_enc, kv_enc = self_project(enc_rows, gains, 0, *w_self, 2 * WIDTH, "enc_project")
    kv_enc_got = swap(kv_enc, "c")
    ctx_enc, p_enc, part, low = attend_local(
        enc_scalars, q_enc, kv_enc, kv_enc_got, enc_table, out_enc, out_enc_sib, False, "enc_attend"
    )
    low_enc, part_enc = low, part
    ffn_dec = gather(after(ffn_dec, low_enc))
    got_enc = swap(low_enc, "x")
    first = after(first, got_enc)
    first_sib = swap(first, "c")
    rest, rest_sib = first[:, : ffn_enc.shape[1]], first_sib[:, : ffn_enc.shape[1]]

    out_rest = unpack_out(rest[:, 6 * WIDTH :].reshape(2 * depth, group, -1), depth)
    out_rest_sib = unpack_out(rest_sib[:, 6 * WIDTH :].reshape(2 * depth, group, -1), depth)
    w_dec = [column_block(w, k) for w in (first, first_sib) for k in (0, 2)]
    w_cross = [column_block(w, k) for w in (first, first_sib) for k in (1, 2)]
    ffn_width = ffn_enc.shape[1]
    ffn_enc, ffn_enc_sib = [
        (w, pl.BlockSpec((D, ffn_width), lambda _: (0, 1))) for w in (first, first_sib)
    ]
    out_dec, out_cross = [[(w, pl.BlockSpec((None, WIDTH, D), f)) for w in (out_rest, out_rest_sib)]
        for f in (lambda _: (0, 0, 0), lambda _: (1, 0, 0))]

    n_b, q_dec, kv_dec = self_project(dec_rows, gains, 3, *w_dec, 0, "dec_project")
    kv_dec_got = swap(kv_dec, "c")
    ctx_dec, p_dec, part_dec, low_dec = attend_local(
        dec_scalars, q_dec, kv_dec, kv_dec_got, dec_table, *out_dec, True, "dec_attend"
    )

    enc_mid, n_1, gu_enc, hid_enc, part, low = ffn_local(
        enc_rows, part_enc, after(got_enc, low_dec), gains, 1, ffn_enc, ffn_enc_sib, units, "enc_ffn"
    )
    rows = enc_rows.shape[0]
    dec_mid, n_c, q_cross = call(
        functools.partial(cross_kernel, WIDTH),
        "cross_project",
        [((rows, D), F32), ((rows, D), BF), ((2, rows, WIDTH), BF)],
        [dec_rows, part_dec, swap(low_dec, "x"), gains, w_cross[1], w_cross[3]],
        2.0,
    )
    enc_last, memory_low, kv_cross = call(
        memory_kernel,
        "memory",
        [((rows, D), F32), ((rows, D), BF), ((2, rows, 2 * WIDTH), BF)],
        [enc_mid, part, after(swap(low, "x"), q_cross), gains, w_cross[0], w_cross[2]],
        2.0,
    )
    kv_cross_got = swap(kv_cross, "c")

    ctx_cross, p_cross, part, low = attend_local(
        enc_scalars, q_cross, kv_cross, kv_cross_got, None, *out_cross, False, "cross_attend"
    )
    ffn_dec = after(ffn_dec, low)
    ffn_dec_sib = swap(ffn_dec, "c")
    dec_cross, n_5, gu_dec, hid_dec, part, low = ffn_local(
        dec_mid, part, swap(low, "x"), gains, 5, ffn_dec, ffn_dec_sib, units, "dec_ffn"
    )

    def both(own_grads, sib_grads):
        return (own_grads.astype(F32) + swap(sib_grads, "c").astype(F32)).astype(BF)

    def blocks(grads):
        return grads.reshape(2 * depth, -1, grads.shape[1])

    def scatter(grads):
        return lax.psum_scatter(grads, ("dp", "y"), scatter_dimension=0, tiled=False)

    dec_final, g, gg6, low_d, dgu_dec, part, low = ffn_back(
        True, dec_cross, part, swap(low, "x"), cots[0], gains, gu_dec, ffn_dec, ffn_dec_sib, "dec_ffn_back"
    )
    d_ffn_dec = ffn_weights(n_5, dgu_dec, hid_dec, low_d, "dec_ffn_weights")
    d_ffn_dec = both(*d_ffn_dec)
    got_f = after(swap(low, "x"), d_ffn_dec)
    got = got_f
    g, gg5, low_x, dq_cross, mine, other = attend_local_back(
        5,
        False,
        enc_scalars,
        g,
        dec_cross,
        part,
        got,
        gains,
        *out_cross,
        q_cross,
        kv_cross,
        kv_cross_got,
        p_cross,
        ctx_cross,
        name="cross_attend_back",
    )
    got = swap(other, "c")
    d_ffn_dec = scatter(after(blocks(d_ffn_dec), got_f))
    dkv_cross, part_m, low_m, part_c, low_c = project_back(
        True, dq_cross, mine, got, *w_cross, WIDTH, "cross_project_back"
    )
    got_c = swap(low_c, "x")
    got_m = after(swap(low_m, "x"), got_c)
    g_last, gg2, low_e, dgu_enc, part, part_low = ffn_back(
        False, enc_last, part_m, got_m, cots[1], gains, gu_enc, ffn_enc, ffn_enc_sib, "enc_ffn_back"
    )
    d_ffn_enc = ffn_weights(n_1, dgu_enc, hid_enc, low_e, "enc_ffn_weights")
    got_e = swap(part_low, "x")
    got_c = after(got_c, *d_ffn_enc)
    d_ffn_enc = both(*d_ffn_enc)
    g_dec, gg4, low_b, dq_dec, mine, other, d_table_dec = attend_local_back(
        4,
        True,
        dec_scalars,
        g,
        dec_mid,
        part_c,
        got_c,
        gains,
        *out_dec,
        q_dec,
        kv_dec,
        kv_dec_got,
        p_dec,
        ctx_dec,
        name="dec_attend_back",
    )
    got_e = after(got_e, dq_dec, d_ffn_dec)
    dec_other = swap(other, "c")
    dec_mine = mine
    g_enc, gg1, low_a, dq_enc, mine, other, d_table_enc = attend_local_back(
        1,
        True,
        enc_scalars,
        g_last,
        enc_mid,
        part,
        got_e,
        gains,
        out_enc,
        out_enc_sib,
        q_enc,
        kv_enc,
        kv_enc_got,
        p_enc,
        ctx_enc,
        name="enc_attend_back",
    )
    dkv_dec, part_d, low = project_back(
        False, dq_dec, dec_mine, dec_other, *w_dec, 0, "dec_project_back"
    )
    got_d = swap(low, "x")
    d_in, d_out, d_in_sib, d_out_sib = attend_weights(
        "attend_weights",
        (n_b, n_b, dq_dec, dkv_dec, ctx_dec, low_b),
        (n_c, memory_low, dq_cross, dkv_cross, ctx_cross, low_x),
    )
    d_out = both(d_out, d_out_sib)
    d_out = jnp.stack([turned_parts(d_out[k], depth) for k in range(2)], 1)
    late = [blocks(d_ffn_enc), blocks(both(d_in, d_in_sib)), pack_out(d_out)]
    late = scatter(jnp.concatenate(late, axis=2))
    got = after(swap(other, "c"), dkv_dec)
    dkv_enc, part, low = project_back(
        False, dq_enc, mine, got, *w_self, 2 * WIDTH, "enc_project_back"
    )
    d_in, d_out, d_in_sib, d_out_sib = attend_weights(
        "enc_attend_weights", (n_a, n_a, dq_enc, dkv_enc, ctx_enc, low_a)
    )
    got = after(swap(low, "x"), d_in, d_out)
    thirds = turned_parts(both(d_out, d_out_sib)[0], depth).reshape(2 * depth, own, 3, D // 3)
    thirds = thirds.transpose(0, 2, 1, 3).reshape(2 * depth, 3 * own, D // 3)
    thirds = jnp.pad(thirds, ((0, 0), (0, group - 3 * own), (0, 0)))
    d_enc = jnp.concatenate([thirds, blocks(both(d_in, d_in_sib))], axis=2)
    d_enc = scatter_y(place, d_enc)
    got_d = after(got_d, d_in)
    grad_dec, gg3 = input_back(3, g_dec, dec_rows, part_d, got_d, gains, "dec_input_back")
    grad_enc, gg0 = input_back(0, g_enc, enc_rows, part, got, gains, "enc_input_back")
    memory_low, dec_final, grad_enc, grad_dec, gg0, gg3 = after(
        (memory_low, dec_final, grad_enc, grad_dec, gg0, gg3), d_enc
    )
    d_enc = scatter_z(place, d_enc)

    wide, inner = 2 * units, 6 * WIDTH
    down = wide + 2 * D // 3
    (sums,) = call(
        functools.partial(sums_kernel, own),
        "column_sums",
        [((64, 128), F32)],
        [late, d_ffn_dec, d_enc],
        1.0,
    )
    out_enc_mine = d_enc[: 3 * own, : D // 3].reshape(3, own, D // 3).transpose(1, 0, 2)
    out_mine = unpack_out_piece(late[:, down + inner :])
    turned_out = jnp.concatenate([rounded(out_enc_mine.reshape(1, own, D)), out_mine])
    turned_out = turn(turned_out, depth).astype(F32)
    columns = [d_ffn_dec[:, :wide], late[:, down : down + inner]]
    columns += [rounded(d_enc[:, D // 3 : D // 3 + 3 * WIDTH]), late[:, :wide]]
    columns = jnp.concatenate(columns, axis=1).reshape(WAYS, own, -1)
    columns = exchange_over_x(place, columns)
    columns_here = columns
    columns = exchange_over_cores(place, columns).astype(F32)
    shard_in, shard_out, shard_hin, shard_hout, row_in, row_out, row_hin, row_hout = call(
        functools.partial(shards_kernel, ff_own),
        "shards",
        [
            ((3, 3, own, D), F32),
            ((3, own, D), F32),
            ((2, 2, own, WAYS * units), F32),
            ((2, ff_own, D), F32),
            ((9, own), F32),
            ((3, own), F32),
            ((4, own), F32),
            ((2, ff_own), F32),
        ],
        [columns, turned_out, late, d_ffn_dec],
        2.0,
    )
    sums = sums + sum(shift_z(sums, k, depth) for k in range(1, depth))
    sums = sums + swap(sums, "y")
    (sums,) = call(hold_kernel, "hold", [(sums.shape, F32)], [sums, (columns_here, ANYWHERE)], 0.3)
    sums = pair_up(sums, swap(sums, "x"), place.x)
    sums = pair_up(sums, swap(sums, "c"), place.c)
    sums = sums.swapaxes(0, 1).reshape(WAYS, -1)
    cuts = [2 * wide, 2 * wide + 9 * WIDTH, 30 * 128, 30 * 128 + 2 * D, 30 * 128 + 5 * D]
    col_hin, col_in, _, col_hout, col_out, _ = jnp.split(sums, cuts, axis=1)
    col_hin = col_hin.reshape(WAYS, 2, 2, 2 * depth, ff_own).transpose(1, 2, 3, 0, 4)
    col_hin = col_hin.reshape(2, 2, WAYS * units)
    col_in = col_in.reshape(WAYS, 9, WIDTH)
    col_in = jnp.stack([col_in[:, k] for k in IN_ORDER]).reshape(3, 3, D)
    col_hout = jnp.sum(col_hout, axis=0).reshape(2, D)
    col_out = jnp.sum(col_out, axis=0).reshape(3, D)

    buckets = position_bias.shape[1]

    def head_table(d_table):
        wide_table = jnp.zeros((2 * SETS, 2 * length + block), F32)
        return lax.dynamic_update_slice_in_dim(wide_table, d_table, block * (1 - place.c), 1)

    grad_enc_bias = head_table(d_table_enc)[:, : 2 * length - 1]
    grad_dec_bias = head_table(d_table_dec)[:, :length][:, ::-1]
    by_set = jnp.stack(
        [
            bucket_grad(enc_buckets, grad_enc_bias, buckets),
            bucket_grad(dec_buckets, grad_dec_bias, buckets),
        ]
    )
    grad_position = lax.dynamic_update_slice_in_dim(
        jnp.zeros_like(position_bias), by_set[:, :, :SETS], q * SETS, 2
    )
    grad_position = lax.dynamic_update_slice_in_dim(
        grad_position, by_set[:, :, SETS:], (q + 1 - 2 * place.c) * SETS, 2
    )
    grad_gains = jnp.concatenate([gg0, gg1, gg2, gg3, gg4, gg5, gg6])
    grad_gains = jnp.where(place.x == 0, grad_gains, 0.0)
    small = jnp.concatenate([grad_gains.reshape(-1, 128), grad_position.reshape(-1, 128)])
    small = sum_everywhere(place, small)
    cut = grad_gains.size // 128
    grad_gains = small[:cut].reshape(grad_gains.shape)
    grad_position = small[cut:].reshape(grad_position.shape)
    shard_gains = lax.dynamic_slice_in_dim(grad_gains, place.index * own, own, 1)

    return (
        give_back(place, memory_low),
        give_back(place, dec_final),
        give_back(place, grad_enc),
        give_back(place, grad_dec),
        shard_in,
        shard_out,
        shard_hin,
        shard_hout,
        shard_gains,
        grad_position,
        row_in.reshape(3, 3, own),
        col_in,
        row_out,
        col_out,
        row_hin.reshape(2, 2, own),
        col_hin,
        row_hout,
        col_hout,
    )


def specs(seq):
    rows = P("dp", seq, None)
    every = ("dp",) + (seq if isinstance(seq, tuple) else (seq,))
    second, third = P(None, every, None), P(None, None, every, None)
    ins = (rows, rows, P("dp"), P("dp"), P(), P(), third, second, third, second)
    ins += (P(None, every), P(), rows, rows)
    outs = (rows, rows, rows, rows, third, second, third, second, P(None, every), P())
    outs += (P(None, None, every), P(), P(None, every), P())
    outs += (P(None, None, every), P(), P(None, every), P())
    return ins, outs


def solution(mesh):
    depth, seq = mesh.shape["dp"], mesh.shape["seq"]

    def wrap(function, over, axes):
        ins, outs = specs(axes)
        return jax.shard_map(function, mesh=over, in_specs=ins, out_specs=outs, check_vma=False)

    def run(*args):
        seqs, length = args[0].shape[0] // depth, args[0].shape[1]
        fits = depth == WAYS and seq == 8 and seqs == 2 and length % 512 == 0
        if fits and args[1].shape == args[0].shape:
            axes = ("y", "x", "c")
            split = Mesh(mesh.devices.reshape(depth, 2, 2, 2), ("dp",) + axes)
            return wrap(functools.partial(grouped, depth), split, axes)(*args)
        return wrap(local, mesh, "seq")(*args)

    return run
```

```python
import functools
import math

import jax
import jax.numpy as jnp
from jax import lax
from jax.experimental import pallas as pl
from jax.experimental.pallas import tpu as pltpu
from jax.sharding import Mesh, PartitionSpec as P

D = 768
HEADS = 12
HEAD = 64
FF = 2048


EPSILON = 1e-06
NEGATIVE = -1e30
HIGHEST = lax.Precision.HIGHEST


def rounded(values):
    return values.astype(jnp.bfloat16)


def rows_first(values):
    return values.transpose(0, 2, 1)


def rms_norm(values, gain_row):
    return (
        values * lax.rsqrt(jnp.mean(values * values, axis=-1, keepdims=True) + EPSILON) * gain_row
    )


def rms_back(values, gain_row, upstream):
    _, pullback = jax.vjp(rms_norm, values, gain_row)
    return pullback(upstream)


def gated_unit(gate_up):
    return jax.nn.gelu(gate_up[0], approximate=True) * gate_up[1]


def offset_table(buckets, layer_bias):
    choose = (buckets[:, None] == jnp.arange(layer_bias.shape[0], dtype=jnp.int32)[None, :]).astype(
        jnp.float32
    )
    return jnp.dot(choose, layer_bias, precision=HIGHEST).T


def bucket_grad(buckets, grad_bias, bucket_count):
    choose = (buckets[:, None] == jnp.arange(bucket_count, dtype=jnp.int32)[None, :]).astype(
        jnp.float32
    )
    return jnp.dot(choose.T, grad_bias.T, precision=HIGHEST)


def hankel_block(window, rows, cols):
    heads_here, length = (window.shape[0], window.shape[1])
    tiled = jnp.tile(window, (1, rows + 1))[:, : rows * (length + 1)]
    return tiled.reshape(heads_here, rows, length + 1)[:, :, :cols]


def bias_block(variant, table, row_start, col_start, rows, cols, extent):
    span = rows + cols - 1
    if variant == "enc":
        base = col_start - row_start - (rows - 1) + (extent - 1)
        window = lax.dynamic_slice_in_dim(table, base, span, 1)
        return hankel_block(window, rows, cols)[:, ::-1, :]
    widened = jnp.concatenate(
        [jnp.broadcast_to(table[:, :1], (table.shape[0], extent - 1)), table], axis=1
    )
    base = row_start - col_start - (cols - 1) + (extent - 1)
    window = lax.dynamic_slice_in_dim(widened, base, span, 1)
    return hankel_block(window, rows, cols)[:, :, ::-1]


def visible_mask(variant, row_ids, col_ids, lengths):
    visible = col_ids[None, None, :] < lengths[:, None, None]
    if variant == "dec":
        visible = visible & (col_ids[None, None, :] <= row_ids[None, :, None])
    return visible[:, None]


def block_scores(query_heads, key_heads, row_ids, col_ids, lengths, variant, offset_bias, extent):
    factor = HEAD ** (-0.5)
    scores = (
        jnp.einsum("sqhe,skhe->shqk", query_heads, key_heads, preferred_element_type=jnp.float32)
        * factor
    )
    if offset_bias is not None:
        scores = (
            scores
            + bias_block(
                variant,
                offset_bias,
                row_ids[0],
                col_ids[0],
                row_ids.shape[0],
                col_ids.shape[0],
                extent,
            )[None]
        )
    return (scores, visible_mask(variant, row_ids, col_ids, lengths))


def row_products(grad_context, context):
    seqs_here, rows_here = (context.shape[0], context.shape[1])
    return jnp.sum(
        (grad_context.astype(jnp.float32) * context).reshape(seqs_here, rows_here, HEADS, HEAD),
        axis=-1,
    ).transpose(0, 2, 1)


def attend(queries, row_ids, lengths, variant, offset_bias, extent, fold_keys):
    seqs_here, rows_here = (queries.shape[0], queries.shape[1])
    query_heads = queries.reshape(seqs_here, rows_here, HEADS, HEAD)

    def fold_step(carried, pieces, begin_at):
        key_rows, value_rows = pieces
        block_len = math.gcd(key_rows.shape[1], 512)

        def block_step(block_id, running):
            row_max, row_sum, weighted = running
            offset_in = block_id * block_len
            key_heads = lax.dynamic_slice_in_dim(key_rows, offset_in, block_len, 1).reshape(
                seqs_here, block_len, HEADS, HEAD
            )
            value_heads = lax.dynamic_slice_in_dim(value_rows, offset_in, block_len, 1).reshape(
                seqs_here, block_len, HEADS, HEAD
            )
            col_ids = offset_in + jnp.arange(block_len, dtype=jnp.int32)
            scores, visible = block_scores(
                query_heads, key_heads, row_ids, col_ids, lengths, variant, offset_bias, extent
            )
            new_max = jnp.maximum(row_max, jnp.max(jnp.where(visible, scores, NEGATIVE), axis=-1))
            weights = jnp.where(visible, jnp.exp(scores - new_max[..., None]), 0.0)
            shrink = jnp.exp(row_max - new_max)
            row_sum = row_sum * shrink + jnp.sum(weights, axis=-1)
            weighted = weighted * shrink[..., None] + jnp.einsum(
                "shqk,skhe->shqe", rounded(weights), value_heads, preferred_element_type=jnp.float32
            )
            return (new_max, row_sum, weighted)

        return lax.fori_loop(0, key_rows.shape[1] // block_len, block_step, carried)

    initial = (
        jnp.full((seqs_here, HEADS, rows_here), NEGATIVE, jnp.float32),
        jnp.zeros((seqs_here, HEADS, rows_here), jnp.float32),
        jnp.zeros((seqs_here, HEADS, rows_here, HEAD), jnp.float32),
    )
    row_max, row_sum, weighted = fold_keys(fold_step, initial)
    context = (
        (weighted / row_sum[..., None])
        .transpose(0, 2, 1, 3)
        .reshape(seqs_here, rows_here, HEADS * HEAD)
    )
    return (context, row_max + jnp.log(row_sum))


def attend_back(
    queries,
    log_sums,
    row_dots,
    grad_context,
    row_ids,
    lengths,
    variant,
    offset_bias,
    extent,
    fold_keys,
):
    seqs_here, rows_here = (queries.shape[0], queries.shape[1])
    query_heads = queries.reshape(seqs_here, rows_here, HEADS, HEAD)
    grad_heads = grad_context.reshape(seqs_here, rows_here, HEADS, HEAD)
    bias_width = offset_bias.shape[1] if offset_bias is not None else 1
    factor = HEAD ** (-0.5)

    def fold_step(carried, pieces, begin_at):
        key_rows, value_rows = pieces
        block_len = math.gcd(key_rows.shape[1], 512)

        def block_step(block_id, running):
            grad_query, grad_bias = (running[0], running[-1])
            offset_in = block_id * block_len
            key_heads = lax.dynamic_slice_in_dim(key_rows, offset_in, block_len, 1).reshape(
                seqs_here, block_len, HEADS, HEAD
            )
            value_heads = lax.dynamic_slice_in_dim(value_rows, offset_in, block_len, 1).reshape(
                seqs_here, block_len, HEADS, HEAD
            )
            col_ids = offset_in + jnp.arange(block_len, dtype=jnp.int32)
            scores, visible = block_scores(
                query_heads, key_heads, row_ids, col_ids, lengths, variant, offset_bias, extent
            )
            weights = jnp.where(visible, jnp.exp(scores - log_sums[..., None]), 0.0)
            grad_weights = jnp.einsum(
                "sqhe,skhe->shqk", grad_heads, value_heads, preferred_element_type=jnp.float32
            )
            grad_scores = weights * (grad_weights - row_dots[..., None])
            if offset_bias is not None:

                def table_block(table_values):
                    return bias_block(
                        variant,
                        table_values,
                        row_ids[0],
                        col_ids[0],
                        row_ids.shape[0],
                        col_ids.shape[0],
                        extent,
                    )

                _, table_pull = jax.vjp(table_block, offset_bias)
                grad_bias = grad_bias + table_pull(jnp.sum(grad_scores, axis=0))[0]
            grad_raw = rounded(grad_scores * factor)
            grad_query = grad_query + jnp.einsum(
                "shqk,skhe->shqe", grad_raw, key_heads, preferred_element_type=jnp.float32
            )
            return (grad_query, grad_bias)

        return lax.fori_loop(0, key_rows.shape[1] // block_len, block_step, carried)

    query_start = jnp.zeros((seqs_here, HEADS, rows_here, HEAD), jnp.float32)
    bias_start = jnp.zeros((HEADS, bias_width), jnp.float32)
    initial = (query_start, bias_start)
    result = fold_keys(fold_step, initial)
    grad_query = result[0].transpose(0, 2, 1, 3).reshape(seqs_here, rows_here, HEADS * HEAD)
    return (grad_query, None, None, result[1])


def owned_key_grads(
    key_rows, value_rows, col_ids, lengths, variant, offset_bias, extent, fold_queries
):
    seqs_here, keys_here = (key_rows.shape[0], key_rows.shape[1])
    key_heads = key_rows.reshape(seqs_here, keys_here, HEADS, HEAD)
    value_heads = value_rows.reshape(seqs_here, keys_here, HEADS, HEAD)
    factor = HEAD ** (-0.5)

    def fold_step(carried, pieces, begin_at):
        query_rows, grad_rows, log_rows, dot_rows = pieces
        block_len = math.gcd(query_rows.shape[1], 512)

        def block_step(block_id, running):
            grad_keys, grad_values = running
            offset_in = block_id * block_len
            query_heads = lax.dynamic_slice_in_dim(query_rows, offset_in, block_len, 1).reshape(
                seqs_here, block_len, HEADS, HEAD
            )
            grad_heads = lax.dynamic_slice_in_dim(grad_rows, offset_in, block_len, 1).reshape(
                seqs_here, block_len, HEADS, HEAD
            )
            log_block = lax.dynamic_slice_in_dim(log_rows, offset_in, block_len, 1).transpose(
                0, 2, 1
            )
            dot_block = lax.dynamic_slice_in_dim(dot_rows, offset_in, block_len, 1).transpose(
                0, 2, 1
            )
            row_ids = offset_in + jnp.arange(block_len, dtype=jnp.int32)
            scores, visible = block_scores(
                query_heads, key_heads, row_ids, col_ids, lengths, variant, offset_bias, extent
            )
            weights = jnp.where(visible, jnp.exp(scores - log_block[..., None]), 0.0)
            grad_weights = jnp.einsum(
                "sqhe,skhe->shqk", grad_heads, value_heads, preferred_element_type=jnp.float32
            )
            grad_scores = weights * (grad_weights - dot_block[..., None])
            grad_raw = rounded(grad_scores * factor)
            grad_keys = grad_keys + jnp.einsum(
                "shqk,sqhe->skhe", grad_raw, query_heads, preferred_element_type=jnp.float32
            ).reshape(seqs_here, keys_here, HEADS * HEAD)
            grad_values = grad_values + jnp.einsum(
                "shqk,sqhe->skhe", rounded(weights), grad_heads, preferred_element_type=jnp.float32
            ).reshape(seqs_here, keys_here, HEADS * HEAD)
            return (grad_keys, grad_values)

        return lax.fori_loop(0, query_rows.shape[1] // block_len, block_step, carried)

    initial = (
        jnp.zeros((seqs_here, keys_here, HEADS * HEAD), jnp.float32),
        jnp.zeros((seqs_here, keys_here, HEADS * HEAD), jnp.float32),
    )
    return fold_queries(fold_step, initial)


def feed_forward(residual, gain_row, weights_in, weights_out):
    normed_low = rounded(rms_norm(residual, gain_row))
    gate_up = jnp.einsum(
        "srd,jdf->jsrf", normed_low, weights_in, preferred_element_type=jnp.float32
    )
    hidden = rounded(gated_unit(gate_up))
    output = jnp.einsum("srf,fd->srd", hidden, weights_out, preferred_element_type=jnp.float32)
    return (residual + output, (normed_low, gate_up, hidden))


def feed_back(residual, gain_row, weights_in, weights_out, kept_values, upstream):
    normed_low, gate_up, hidden = kept_values
    upstream_low = rounded(upstream)
    grad_out_weights = jnp.einsum(
        "srf,srd->fd", hidden, upstream_low, preferred_element_type=jnp.float32
    )
    grad_hidden = jnp.einsum(
        "srd,fd->srf", upstream_low, weights_out, preferred_element_type=jnp.float32
    )
    _, pullback = jax.vjp(gated_unit, gate_up)
    grad_gate_up = rounded(pullback(grad_hidden)[0])
    grad_in_weights = jnp.einsum(
        "srd,jsrf->jdf", normed_low, grad_gate_up, preferred_element_type=jnp.float32
    )
    grad_normed = jnp.einsum(
        "jsrf,jdf->srd", grad_gate_up, weights_in, preferred_element_type=jnp.float32
    )
    grad_residual, grad_gain = rms_back(residual, gain_row, grad_normed)
    return (upstream + grad_residual, grad_gain, grad_in_weights, grad_out_weights)


def local(
    enc_input,
    dec_input,
    enc_lengths,
    dec_lengths,
    enc_buckets,
    dec_buckets,
    attention_in,
    attention_out,
    hidden_in,
    hidden_out,
    norm_gains,
    position_bias,
    enc_cotangent,
    dec_cotangent,
):
    full_in, full_out, full_hidden_in, full_hidden_out, full_gains = (
        lax.all_gather(attention_in, ("dp", "seq"), axis=2, tiled=True),
        lax.all_gather(attention_out, ("dp", "seq"), axis=1, tiled=True),
        lax.all_gather(hidden_in, ("dp", "seq"), axis=2, tiled=True),
        lax.all_gather(hidden_out, ("dp", "seq"), axis=1, tiled=True),
        lax.all_gather(norm_gains, ("dp", "seq"), axis=1, tiled=True),
    )
    gain_rows = full_gains.astype(jnp.float32)
    enc_rows = enc_input.shape[1]
    dec_rows = dec_input.shape[1]
    seq_index = lax.axis_index("seq")
    enc_ids = seq_index * enc_rows + jnp.arange(enc_rows, dtype=jnp.int32)
    dec_ids = seq_index * dec_rows + jnp.arange(dec_rows, dtype=jnp.int32)
    enc_extent = (enc_buckets.shape[0] + 1) // 2
    dec_extent = dec_buckets.shape[0]
    enc_table = offset_table(enc_buckets, position_bias[0])
    dec_table = offset_table(dec_buckets, position_bias[1])
    enc_values = enc_input.astype(jnp.float32)
    norm_a_low = rounded(rms_norm(enc_values, gain_rows[0]))
    enc_qkv = rounded(
        jnp.einsum("srd,jde->jsre", norm_a_low, full_in[0], preferred_element_type=jnp.float32)
    )
    enc_context, enc_logs = attend(
        enc_qkv[0],
        enc_ids,
        enc_lengths,
        "enc",
        enc_table,
        enc_extent,
        lambda folder, initial: folder(
            initial,
            (
                lax.all_gather(enc_qkv[1], "seq", axis=1, tiled=True),
                lax.all_gather(enc_qkv[2], "seq", axis=1, tiled=True),
            ),
            jnp.int32(0),
        ),
    )
    enc_context_low = rounded(enc_context)
    enc_mid = enc_values + jnp.einsum(
        "srd,de->sre", enc_context_low, full_out[0], preferred_element_type=jnp.float32
    )
    enc_last, enc_ffn_kept = feed_forward(
        enc_mid, gain_rows[1], full_hidden_in[0], full_hidden_out[0]
    )
    memory = rms_norm(enc_last, gain_rows[2])
    memory_low = rounded(memory)
    dec_values = dec_input.astype(jnp.float32)
    norm_b_low = rounded(rms_norm(dec_values, gain_rows[3]))
    dec_qkv = rounded(
        jnp.einsum("srd,jde->jsre", norm_b_low, full_in[1], preferred_element_type=jnp.float32)
    )
    dec_context, dec_logs = attend(
        dec_qkv[0],
        dec_ids,
        dec_lengths,
        "dec",
        dec_table,
        dec_extent,
        lambda folder, initial: folder(
            initial,
            (
                lax.all_gather(dec_qkv[1], "seq", axis=1, tiled=True),
                lax.all_gather(dec_qkv[2], "seq", axis=1, tiled=True),
            ),
            jnp.int32(0),
        ),
    )
    dec_context_low = rounded(dec_context)
    dec_mid = dec_values + jnp.einsum(
        "srd,de->sre", dec_context_low, full_out[1], preferred_element_type=jnp.float32
    )
    norm_c_low = rounded(rms_norm(dec_mid, gain_rows[4]))
    cross_query = rounded(
        jnp.einsum("srd,de->sre", norm_c_low, full_in[2, 0], preferred_element_type=jnp.float32)
    )
    cross_pair = rounded(
        jnp.einsum("srd,jde->jsre", memory_low, full_in[2, 1:], preferred_element_type=jnp.float32)
    )
    cross_context, cross_logs = attend(
        cross_query,
        dec_ids,
        enc_lengths,
        "cross",
        None,
        0,
        lambda folder, initial: folder(
            initial,
            (
                lax.all_gather(cross_pair[0], "seq", axis=1, tiled=True),
                lax.all_gather(cross_pair[1], "seq", axis=1, tiled=True),
            ),
            jnp.int32(0),
        ),
    )
    cross_low = rounded(cross_context)
    dec_cross = dec_mid + jnp.einsum(
        "srd,de->sre", cross_low, full_out[2], preferred_element_type=jnp.float32
    )
    dec_last, dec_ffn_kept = feed_forward(
        dec_cross, gain_rows[5], full_hidden_in[1], full_hidden_out[1]
    )
    dec_final = rms_norm(dec_last, gain_rows[6])
    grad_dec_last, grad_gain_six = rms_back(
        dec_last, gain_rows[6], dec_cotangent.astype(jnp.float32)
    )
    grad_dec_cross, grad_gain_five, grad_hin_one, grad_hout_one = feed_back(
        dec_cross, gain_rows[5], full_hidden_in[1], full_hidden_out[1], dec_ffn_kept, grad_dec_last
    )
    upstream_low = rounded(grad_dec_cross)
    grad_out_two = jnp.einsum(
        "srd,sre->de", cross_low, upstream_low, preferred_element_type=jnp.float32
    )
    grad_cross_context = rounded(
        jnp.einsum("sre,de->srd", upstream_low, full_out[2], preferred_element_type=jnp.float32)
    )
    cross_dots = row_products(grad_cross_context, cross_context)
    cross_grad_query, cross_grad_keys, cross_grad_values, _ = attend_back(
        cross_query,
        cross_logs,
        cross_dots,
        grad_cross_context,
        dec_ids,
        enc_lengths,
        "cross",
        None,
        0,
        lambda folder, initial: folder(
            initial,
            (
                lax.all_gather(cross_pair[0], "seq", axis=1, tiled=True),
                lax.all_gather(cross_pair[1], "seq", axis=1, tiled=True),
            ),
            jnp.int32(0),
        ),
    )
    cross_query_low = rounded(cross_grad_query)
    grad_query_two = jnp.einsum(
        "srd,sre->de", norm_c_low, cross_query_low, preferred_element_type=jnp.float32
    )
    grad_norm_c = jnp.einsum(
        "sre,de->srd", cross_query_low, full_in[2, 0], preferred_element_type=jnp.float32
    )
    grad_mid_part, grad_gain_four = rms_back(dec_mid, gain_rows[4], grad_norm_c)
    grad_dec_mid = grad_dec_cross + grad_mid_part
    upstream_low = rounded(grad_dec_mid)
    grad_out_one = jnp.einsum(
        "srd,sre->de", dec_context_low, upstream_low, preferred_element_type=jnp.float32
    )
    grad_dec_context = rounded(
        jnp.einsum("sre,de->srd", upstream_low, full_out[1], preferred_element_type=jnp.float32)
    )
    dec_dots = row_products(grad_dec_context, dec_context)
    dec_grad_query, dec_grad_keys, dec_grad_values, grad_dec_bias = attend_back(
        dec_qkv[0],
        dec_logs,
        dec_dots,
        grad_dec_context,
        dec_ids,
        dec_lengths,
        "dec",
        dec_table,
        dec_extent,
        lambda folder, initial: folder(
            initial,
            (
                lax.all_gather(dec_qkv[1], "seq", axis=1, tiled=True),
                lax.all_gather(dec_qkv[2], "seq", axis=1, tiled=True),
            ),
            jnp.int32(0),
        ),
    )
    cross_key_grad, cross_value_grad = owned_key_grads(
        cross_pair[0],
        cross_pair[1],
        enc_ids,
        enc_lengths,
        "cross",
        None,
        0,
        lambda folder, initial: folder(
            initial,
            (
                lax.all_gather(cross_query, "seq", axis=1, tiled=True),
                lax.all_gather(grad_cross_context, "seq", axis=1, tiled=True),
                lax.all_gather(
                    rows_first(cross_logs).astype(jnp.bfloat16), "seq", axis=1, tiled=True
                ).astype(jnp.float32),
                lax.all_gather(
                    rows_first(cross_dots).astype(jnp.bfloat16), "seq", axis=1, tiled=True
                ).astype(jnp.float32),
            ),
            jnp.int32(0),
        ),
    )
    dec_key_grad, dec_value_grad = owned_key_grads(
        dec_qkv[1],
        dec_qkv[2],
        dec_ids,
        dec_lengths,
        "dec",
        dec_table,
        dec_extent,
        lambda folder, initial: folder(
            initial,
            (
                lax.all_gather(dec_qkv[0], "seq", axis=1, tiled=True),
                lax.all_gather(grad_dec_context, "seq", axis=1, tiled=True),
                lax.all_gather(
                    rows_first(dec_logs).astype(jnp.bfloat16), "seq", axis=1, tiled=True
                ).astype(jnp.float32),
                lax.all_gather(
                    rows_first(dec_dots).astype(jnp.bfloat16), "seq", axis=1, tiled=True
                ).astype(jnp.float32),
            ),
            jnp.int32(0),
        ),
    )
    pair_grads = rounded(jnp.stack([cross_key_grad, cross_value_grad]))
    grad_pair_two = jnp.einsum(
        "srd,jsre->jde", memory_low, pair_grads, preferred_element_type=jnp.float32
    )
    grad_memory = jnp.einsum(
        "jsre,jde->srd", pair_grads, full_in[2, 1:], preferred_element_type=jnp.float32
    )
    dec_grads = rounded(jnp.stack([dec_grad_query, dec_key_grad, dec_value_grad]))
    grad_in_one = jnp.einsum(
        "srd,jsre->jde", norm_b_low, dec_grads, preferred_element_type=jnp.float32
    )
    grad_norm_b = jnp.einsum(
        "jsre,jde->srd", dec_grads, full_in[1], preferred_element_type=jnp.float32
    )
    grad_dec_part, grad_gain_three = rms_back(dec_values, gain_rows[3], grad_norm_b)
    grad_dec_input = grad_dec_mid + grad_dec_part
    grad_memory_total = enc_cotangent.astype(jnp.float32) + grad_memory
    grad_enc_last, grad_gain_two = rms_back(enc_last, gain_rows[2], grad_memory_total)
    grad_enc_mid, grad_gain_one, grad_hin_zero, grad_hout_zero = feed_back(
        enc_mid, gain_rows[1], full_hidden_in[0], full_hidden_out[0], enc_ffn_kept, grad_enc_last
    )
    upstream_low = rounded(grad_enc_mid)
    grad_out_zero = jnp.einsum(
        "srd,sre->de", enc_context_low, upstream_low, preferred_element_type=jnp.float32
    )
    grad_enc_context = rounded(
        jnp.einsum("sre,de->srd", upstream_low, full_out[0], preferred_element_type=jnp.float32)
    )
    enc_dots = row_products(grad_enc_context, enc_context)
    enc_grad_query, enc_grad_keys, enc_grad_values, grad_enc_bias = attend_back(
        enc_qkv[0],
        enc_logs,
        enc_dots,
        grad_enc_context,
        enc_ids,
        enc_lengths,
        "enc",
        enc_table,
        enc_extent,
        lambda folder, initial: folder(
            initial,
            (
                lax.all_gather(enc_qkv[1], "seq", axis=1, tiled=True),
                lax.all_gather(enc_qkv[2], "seq", axis=1, tiled=True),
            ),
            jnp.int32(0),
        ),
    )
    enc_key_grad, enc_value_grad = owned_key_grads(
        enc_qkv[1],
        enc_qkv[2],
        enc_ids,
        enc_lengths,
        "enc",
        enc_table,
        enc_extent,
        lambda folder, initial: folder(
            initial,
            (
                lax.all_gather(enc_qkv[0], "seq", axis=1, tiled=True),
                lax.all_gather(grad_enc_context, "seq", axis=1, tiled=True),
                lax.all_gather(
                    rows_first(enc_logs).astype(jnp.bfloat16), "seq", axis=1, tiled=True
                ).astype(jnp.float32),
                lax.all_gather(
                    rows_first(enc_dots).astype(jnp.bfloat16), "seq", axis=1, tiled=True
                ).astype(jnp.float32),
            ),
            jnp.int32(0),
        ),
    )
    enc_grads = rounded(jnp.stack([enc_grad_query, enc_key_grad, enc_value_grad]))
    grad_in_zero = jnp.einsum(
        "srd,jsre->jde", norm_a_low, enc_grads, preferred_element_type=jnp.float32
    )
    grad_norm_a = jnp.einsum(
        "jsre,jde->srd", enc_grads, full_in[0], preferred_element_type=jnp.float32
    )
    grad_enc_part, grad_gain_zero = rms_back(enc_values, gain_rows[0], grad_norm_a)
    grad_enc_input = grad_enc_mid + grad_enc_part
    grad_cross_in = jnp.concatenate([grad_query_two[None], grad_pair_two], axis=0)
    grad_attention_in = jnp.stack([grad_in_zero, grad_in_one, grad_cross_in])
    grad_attention_out = jnp.stack([grad_out_zero, grad_out_one, grad_out_two])
    grad_hidden_in = jnp.stack([grad_hin_zero, grad_hin_one])
    grad_hidden_out = jnp.stack([grad_hout_zero, grad_hout_one])
    grad_gains = jnp.stack(
        [
            grad_gain_zero,
            grad_gain_one,
            grad_gain_two,
            grad_gain_three,
            grad_gain_four,
            grad_gain_five,
            grad_gain_six,
        ]
    )
    shard_in, shard_out, shard_hin, shard_hout, shard_gains = (
        lax.psum_scatter(grad_attention_in, ("dp", "seq"), scatter_dimension=2, tiled=True),
        lax.psum_scatter(grad_attention_out, ("dp", "seq"), scatter_dimension=1, tiled=True),
        lax.psum_scatter(grad_hidden_in, ("dp", "seq"), scatter_dimension=2, tiled=True),
        lax.psum_scatter(grad_hidden_out, ("dp", "seq"), scatter_dimension=1, tiled=True),
        lax.psum_scatter(grad_gains, ("dp", "seq"), scatter_dimension=1, tiled=True),
    )
    bucket_count = position_bias.shape[1]
    grad_position = jnp.stack(
        [
            bucket_grad(enc_buckets, grad_enc_bias, bucket_count),
            bucket_grad(dec_buckets, grad_dec_bias, bucket_count),
        ]
    )
    squares_in = shard_in * shard_in
    squares_out = shard_out * shard_out
    squares_hin = shard_hin * shard_hin
    squares_hout = shard_hout * shard_hout
    col_in, col_out, col_hin, col_hout, grad_position = lax.psum(
        (
            jnp.sum(squares_in, axis=2),
            jnp.sum(squares_out, axis=1),
            jnp.sum(squares_hin, axis=2),
            jnp.sum(squares_hout, axis=1),
            grad_position,
        ),
        ("dp", "seq"),
    )
    return (
        rounded(memory),
        rounded(dec_final),
        grad_enc_input,
        grad_dec_input,
        shard_in,
        shard_out,
        shard_hin,
        shard_hout,
        shard_gains,
        grad_position,
        0.5 * jnp.mean(squares_in, axis=-1),
        0.5 * col_in / D,
        0.5 * jnp.mean(squares_out, axis=-1),
        0.5 * col_out / D,
        0.5 * jnp.mean(squares_hin, axis=-1),
        0.5 * col_hin / D,
        0.5 * jnp.mean(squares_hout, axis=-1),
        0.5 * col_hout / FF,
    )


WAYS = 4
SETS = HEADS // WAYS
WIDTH = SETS * HEAD
VMEM_LIMIT = 16 * 2**20


def swap(values, axis):
    return lax.ppermute(values, axis, [(0, 1), (1, 0)])


def shift_z(values, hops, count):
    return lax.ppermute(values, "dp", [(i, (i + hops) % count) for i in range(count)])


def pair_up(mine, other, bit):
    first = bit == 0
    return jnp.stack([jnp.where(first, mine, other), jnp.where(first, other, mine)])


def pick(values, index, axis=0):
    return lax.dynamic_index_in_dim(values, index, axis, keepdims=False)


class Place:
    def __init__(self, depth):
        self.depth = depth
        self.z, self.y, self.x, self.c = [lax.axis_index(a) for a in ("dp", "y", "x", "c")]
        self.q = 2 * self.x + self.c
        self.index = (self.z * 2 + self.y) * WAYS + self.q


def exchange_over_x(place, pieces):
    halves = pieces.reshape((2, 2) + pieces.shape[1:])
    got = swap(pick(halves, 1 - place.x), "x")
    return pair_up(pick(halves, place.x), got, place.x)


def exchange_over_cores(place, both):
    got = swap(pick(both, 1 - place.c, 1), "c")
    whole = pair_up(pick(both, place.c, 1), got, place.c)
    return jnp.swapaxes(whole, 0, 1).reshape((4,) + both.shape[2:])


def exchange_columns(place, pieces):
    return exchange_over_cores(place, exchange_over_x(place, pieces))


def along_z(place, piece, *earlier):
    depth = place.depth
    held = jnp.zeros((depth,) + piece.shape, piece.dtype)
    arrivals = [shift_z(piece, k, depth) for k in range(1, depth)]
    if earlier:
        arrivals = [after(block, *earlier) for block in arrivals]
    for hops, block in enumerate([piece] + arrivals):
        held = lax.dynamic_update_index_in_dim(held, block, (place.z - hops) % depth, 0)
    return held


def along_y(place, held):
    other = swap(held, "y")
    first = place.y == 0
    pair = [jnp.where(first, held, other), jnp.where(first, other, held)]
    return jnp.stack(pair, axis=1).reshape(-1, held.shape[-1])


def scatter_y(place, parts):
    parts = parts.reshape((place.depth, 2) + parts.shape[1:])
    sent = swap(pick(parts, 1 - place.y, 1), "y")
    return pick(parts, place.y, 1).astype(F32) + sent.astype(F32)


def scatter_z(place, halves):
    depth = place.depth
    low = rounded(halves)
    total = pick(halves, place.z)
    for hops in range(1, depth):
        sent = shift_z(pick(low, (place.z + hops) % depth), hops, depth)
        total = total + sent.astype(F32)
    return total


def after(values, *earlier):
    return lax.optimization_barrier((values,) + earlier)[0]


def turn(values, depth):
    pairs = []
    for d in range(depth):
        for y in range(2):
            for q in range(WAYS):
                pairs.append((d * 8 + y * 4 + q, q * 8 + y * 4 + d))
    return lax.ppermute(values, ("dp", "y", "x", "c"), pairs)


def matmul(a, b):
    return jnp.dot(a, b, preferred_element_type=jnp.float32)


def matmul_nt(a, b):
    return lax.dot_general(a, b, (((1,), (1,)), ((), ())), preferred_element_type=jnp.float32)


def matmul_tn(a, b):
    return lax.dot_general(a, b, (((0,), (0,)), ((), ())), preferred_element_type=jnp.float32)


def call(kernel, name, outs, args, micros, scratch=()):
    whole = pl.BlockSpec(memory_space=pltpu.VMEM)
    arrays = [a[0] if isinstance(a, tuple) else a for a in args]
    specs = [a[1] if isinstance(a, tuple) else whole for a in args]
    late = [k for k, spec in enumerate(specs) if spec is LATE]
    plain = (whole, SCALARS, LATE, ANYWHERE)
    windows = any(all(spec is not p for p in plain) for spec in specs)
    shapes = tuple(jax.ShapeDtypeStruct(s, t) for s, t in outs)
    moved = sum(a.size * a.dtype.itemsize for a in list(arrays) + list(shapes))
    buffers = [pltpu.VMEM(arrays[k].shape, arrays[k].dtype) for k in late]

    def bring_in(*refs):
        if not late:
            return kernel(*refs)
        refs, places, semaphores = list(refs[: -len(late) - 1]), refs[-len(late) - 1 : -1], refs[-1]
        copies = [
            pltpu.make_async_copy(refs[k], place, semaphores.at[n])
            for n, (k, place) in enumerate(zip(late, places))
        ]
        for copy in copies:
            copy.start()
        for copy in copies:
            copy.wait()
        for k, place in zip(late, places):
            refs[k] = place
        return kernel(*refs)

    if late:
        buffers.append(pltpu.SemaphoreType.DMA((len(late),)))
    return pl.pallas_call(
        bring_in,
        grid=(1,) if windows else (),
        out_shape=shapes,
        in_specs=specs,
        out_specs=(whole,) * len(shapes),
        scratch_shapes=list(scratch) + buffers,
        compiler_params=pltpu.CompilerParams(vmem_limit_bytes=VMEM_LIMIT),
        cost_estimate=pl.CostEstimate(
            flops=int(micros * 1e7), bytes_accessed=moved // 32, transcendentals=0
        ),
        name=name,
    )(*arrays)


LATE = pl.BlockSpec(memory_space=pltpu.HBM)
ANYWHERE = pl.BlockSpec(memory_space=pl.ANY)
SCALARS = pl.BlockSpec(memory_space=pltpu.SMEM)
BF, F32 = jnp.bfloat16, jnp.float32


def column_block(array, index):
    rows, columns = array.shape
    return (array, pl.BlockSpec((rows, 2 * WIDTH), lambda _: (0, index)))


def norm_rows(values, gain):
    return values * lax.rsqrt(jnp.mean(values * values, axis=-1, keepdims=True) + EPSILON) * gain


def norm_back(values, gain, upstream):
    scale = lax.rsqrt(jnp.mean(values * values, axis=-1, keepdims=True) + EPSILON)
    unit = values * scale
    inner = upstream * gain
    grad = scale * (inner - unit * jnp.mean(inner * unit, axis=-1, keepdims=True))
    return grad, jnp.sum(upstream * unit, axis=0, keepdims=True)


def self_kernel(gain, q_at, x_ref, gains_ref, kva_ref, qa_ref, kvb_ref, qb_ref, *outs):
    n_ref, q_ref, kv_ref = outs
    n = norm_rows(x_ref[...].astype(F32), gains_ref[gain : gain + 1, :]).astype(BF)
    n_ref[...] = n
    for e, (kv, q) in enumerate(((kva_ref, qa_ref), (kvb_ref, qb_ref))):
        kv_ref[e] = matmul(n, kv[:, : 2 * WIDTH]).astype(BF)
        q_ref[e] = matmul(n, q[:, q_at : q_at + WIDTH]).astype(BF)


def self_project(x, gains, gain, kv_own, q_own, kv_sib, q_sib, q_at, name):
    rows = x.shape[0]
    return call(
        functools.partial(self_kernel, gain, q_at),
        name,
        [((rows, D), BF), ((2, rows, WIDTH), BF), ((2, rows, 2 * WIDTH), BF)],
        [x, gains, kv_own, q_own, kv_sib, q_sib],
        2.5,
    )


def memory_kernel(res_ref, part_ref, got_ref, gains_ref, kva_ref, kvb_ref, *outs):
    last_ref, low_ref, kv_ref = outs
    last = res_ref[...].astype(F32) + part_ref[...] + got_ref[...].astype(F32)
    last_ref[...] = last
    low = norm_rows(last, gains_ref[2:3, :]).astype(BF)
    low_ref[...] = low
    for e, kv in enumerate((kva_ref, kvb_ref)):
        kv_ref[e] = matmul(low, kv[...]).astype(BF)


def cross_kernel(q_at, res_ref, part_ref, got_ref, gains_ref, qa_ref, qb_ref, *outs):
    mid_ref, low_ref, q_ref = outs
    mid = res_ref[...].astype(F32) + part_ref[...] + got_ref[...].astype(F32)
    mid_ref[...] = mid
    low = norm_rows(mid, gains_ref[4:5, :]).astype(BF)
    low_ref[...] = low
    for e, q in enumerate((qa_ref, qb_ref)):
        q_ref[e] = matmul(low, q[:, q_at : q_at + WIDTH]).astype(BF)


def lay_out_keys(core, kv_ref, got_ref, keys):
    block = kv_ref.shape[1] // 4
    for e in range(2):
        for k in range(4):
            at = pl.multiple_of(block * (2 * k + core), block)
            keys[e, pl.ds(at, block), :] = kv_ref[e, k * block : (k + 1) * block, :]
            at = pl.multiple_of(block * (2 * k + 1 - core), block)
            keys[e, pl.ds(at, block), :] = got_ref[1 - e, k * block : (k + 1) * block, :]


def attend_kernel(causal, biased, *refs):
    if biased:
        scalars, q_ref, kv_ref, got_ref, table_ref, oa_ref, ob_ref = refs[:7]
    else:
        scalars, q_ref, kv_ref, got_ref, oa_ref, ob_ref = refs[:6]
    ctx_ref, p_ref, part_ref, low_ref, keys = refs[-5:]
    core, length = scalars[0], scalars[1]
    lay_out_keys(core, kv_ref, got_ref, keys)
    rows, extent = q_ref.shape[1], keys.shape[1]
    block = rows // 4
    cols = lax.broadcasted_iota(jnp.int32, (block, extent), 1)
    ids = lax.broadcasted_iota(jnp.int32, (block, extent), 0)
    total = None
    for e in range(2):
        for h in range(SETS):
            at = slice(h * HEAD, (h + 1) * HEAD)
            k = keys[e, :, at]
            v = keys[e, :, WIDTH + h * HEAD : WIDTH + (h + 1) * HEAD]
            scores = matmul_nt(q_ref[e, :, at], k)
            if biased:
                line = table_ref[e * SETS + h : e * SETS + h + 1, :]
                skew = pltpu.roll(
                    jnp.broadcast_to(line, (block, 2 * extent)),
                    2 * extent - (block - 1),
                    1,
                    stride=1,
                    stride_axis=0,
                )
            for i in range(4):
                here = slice(i * block, (i + 1) * block)
                s = scores[here] * (HEAD**-0.5)
                if biased:
                    begin = (3 - i) * 2 * block
                    s = s + skew[:, begin : begin + extent]
                visible = cols < length
                if causal:
                    visible = visible & (cols <= ids + (i * 2 * block + core * block))
                s = jnp.where(visible, s, NEGATIVE)
                weights = jnp.exp(s - jnp.max(s, axis=-1, keepdims=True))
                weights = weights * (1.0 / jnp.sum(weights, axis=-1, keepdims=True))
                p_ref[e * SETS + h, here, :] = weights.astype(BF)
            ctx_ref[e, :, at] = matmul(p_ref[e * SETS + h], v)
        term = matmul(ctx_ref[e].astype(BF), (oa_ref, ob_ref)[e][...])
        total = term if total is None else total + term
    part_ref[...] = total
    low_ref[...] = total.astype(BF)


def attend_local(scalars, q, kv, got, table, out_own, out_sib, causal, name):
    rows = q.shape[1]
    extent = 2 * rows
    args = [(scalars, SCALARS), q, kv, got] + ([] if table is None else [table])
    return call(
        functools.partial(attend_kernel, causal, table is not None),
        name,
        [
            ((2, rows, WIDTH), F32),
            ((2 * SETS, rows, extent), BF),
            ((rows, D), F32),
            ((rows, D), BF),
        ],
        args + [out_own, out_sib],
        5.5,
        [pltpu.VMEM((2, extent, 2 * WIDTH), BF)],
    )


def unpack_into(w_ref, columns, down):
    blocks, rows = 8, down.shape[0] // 8
    half, third = rows // 2, down.shape[1] // 3
    step = rows + half
    for b in range(blocks):
        down[b * rows : (b + 1) * rows, : 2 * third] = w_ref[
            b * step : b * step + rows, columns : columns + 2 * third
        ]
        for k in range(2):
            down[b * rows + k * half : b * rows + (k + 1) * half, 2 * third :] = w_ref[
                b * step + rows : (b + 1) * step,
                columns + k * third : columns + (k + 1) * third,
            ]


GELU_A, GELU_B = (2 / math.pi) ** 0.5, 0.044715


def gelu_tanh(gate):
    return jnp.tanh(GELU_A * (gate + GELU_B * gate * gate * gate))


def ffn_kernel(gain, res_ref, part_ref, got_ref, gains_ref, wa_ref, wb_ref, *refs):
    mid_ref, n_ref, gu_ref, hid_ref, out_ref, low_ref, down = refs
    mid = res_ref[...].astype(F32) + part_ref[...] + got_ref[...].astype(F32)
    mid_ref[...] = mid
    n = norm_rows(mid, gains_ref[gain : gain + 1, :]).astype(BF)
    n_ref[...] = n
    units = down.shape[0]
    total = None
    for e, w_ref in enumerate((wa_ref, wb_ref)):
        gu_ref[e] = matmul(n, w_ref[:, : 2 * units])
        gate, up = gu_ref[e, :, :units], gu_ref[e, :, units:]
        hid_ref[e] = (0.5 * gate * (1.0 + gelu_tanh(gate)) * up).astype(BF)
        unpack_into(w_ref, 2 * units, down)
        term = matmul(hid_ref[e], down[...])
        total = term if total is None else total + term
    out_ref[...] = total
    low_ref[...] = total.astype(BF)


def ffn_local(res, part, got, gains, gain, w_own, w_sib, units, name):
    rows = res.shape[0]
    return call(
        functools.partial(ffn_kernel, gain),
        name,
        [
            ((rows, D), F32),
            ((rows, D), BF),
            ((2, rows, 2 * units), F32),
            ((2, rows, units), BF),
            ((rows, D), F32),
            ((rows, D), BF),
        ],
        [res, part, got, gains, w_own, w_sib],
        3.0,
        [pltpu.VMEM((units, D), BF)],
    )


def ffn_back_kernel(decoder, val_ref, part_ref, got_ref, cot_ref, gains_ref, *refs):
    gu_ref, wa_ref, wb_ref = refs[:3]
    down = refs[-1]
    sent = part_ref[...] + got_ref[...].astype(F32)
    if decoder:
        final_ref, g_ref, dgain_ref, low_ref, dgu_ref, out_ref, out_low_ref = refs[3:-1]
        gain = gains_ref[6:7, :]
        values = val_ref[...] + sent
        upstream = cot_ref[...].astype(F32)
        final_ref[...] = norm_rows(values, gain).astype(BF)
    else:
        g_ref, dgain_ref, low_ref, dgu_ref, out_ref, out_low_ref = refs[3:-1]
        gain = gains_ref[2:3, :]
        values = val_ref[...]
        upstream = cot_ref[...].astype(F32) + sent
    grad, dgain_ref[...] = norm_back(values, gain, upstream)
    g_ref[...] = grad
    low = grad.astype(BF)
    low_ref[...] = low
    units = down.shape[0]
    total = None
    for e, w_ref in enumerate((wa_ref, wb_ref)):
        unpack_into(w_ref, 2 * units, down)
        grad_hidden = matmul_nt(low, down[...])
        gate, up = gu_ref[e, :, :units], gu_ref[e, :, units:]
        t = gelu_tanh(gate)
        slope = 0.5 * (1.0 + t) + 0.5 * gate * (1.0 - t * t) * GELU_A * (
            1.0 + 3.0 * GELU_B * gate * gate
        )
        dgu_ref[e, :, :units] = (grad_hidden * up * slope).astype(BF)
        dgu_ref[e, :, units:] = (grad_hidden * (0.5 * gate * (1.0 + t))).astype(BF)
        term = matmul_nt(dgu_ref[e], w_ref[:, : 2 * units])
        total = term if total is None else total + term
    out_ref[...] = total
    out_low_ref[...] = total.astype(BF)


def ffn_back(decoder, values, part, got, cot, gains, gate_up, w_own, w_sib, name):
    rows, units = values.shape[0], gate_up.shape[2] // 2
    outs = [((rows, D), BF)] if decoder else []
    outs += [
        ((rows, D), F32),
        ((1, D), F32),
        ((rows, D), BF),
        ((2, rows, 2 * units), BF),
        ((rows, D), F32),
        ((rows, D), BF),
    ]
    return call(
        functools.partial(ffn_back_kernel, decoder),
        name,
        outs,
        [values, part, got, cot, gains, gate_up, w_own, w_sib],
        4.0,
        [pltpu.VMEM((units, D), BF)],
    )


def ffn_weights_kernel(n_ref, dgu_ref, hid_ref, low_ref, own_ref, sib_ref):
    units = hid_ref.shape[2]
    rows, half, third = units // 8, units // 16, D // 3
    step = rows + half
    for e, out in enumerate((own_ref, sib_ref)):
        out[:, : 2 * units] = matmul_tn(n_ref[...], dgu_ref[e]).astype(BF)
        down = matmul_tn(hid_ref[e], low_ref[...]).astype(BF)
        for b in range(8):
            out[b * step : b * step + rows, 2 * units :] = down[
                b * rows : (b + 1) * rows, : 2 * third
            ]
            for k in range(2):
                out[
                    b * step + rows : (b + 1) * step,
                    2 * units + k * third : 2 * units + (k + 1) * third,
                ] = down[b * rows + k * half : b * rows + (k + 1) * half, 2 * third :]


def ffn_weights(n, dgu, hid, low, name):
    units = hid.shape[2]
    shape = ((D, 2 * units + 2 * D // 3), BF)
    return call(
        ffn_weights_kernel, name, [shape, shape], [n, dgu, hid, low], 1.5
    )


def attend_back_kernel(gain, biased, scalars, up_ref, val_ref, part_ref, got_ref, *refs):
    gains_ref, oa_ref, ob_ref, q_ref, kv_ref, kvgot_ref, p_ref, ctx_ref = refs[:8]
    g_ref, dgain_ref, low_ref, dq_ref, mine_ref, other_ref = refs[8:14]
    keys, dkeys, ds_ref = refs[-3:]
    core = scalars[0]
    grad, dgain_ref[...] = norm_back(
        val_ref[...], gains_ref[gain : gain + 1, :], part_ref[...] + got_ref[...].astype(F32)
    )
    grad = up_ref[...] + grad
    g_ref[...] = grad
    low = grad.astype(BF)
    low_ref[...] = low
    lay_out_keys(core, kv_ref, kvgot_ref, keys)
    rows, extent = q_ref.shape[1], keys.shape[1]
    block = rows // 4
    factor = HEAD**-0.5
    for e in range(2):
        g = matmul_nt(low, (oa_ref, ob_ref)[e][...]).astype(BF)
        products = g.astype(F32) * ctx_ref[e]
        for h in range(SETS):
            at = slice(h * HEAD, (h + 1) * HEAD)
            k = keys[e, :, at]
            v = keys[e, :, WIDTH + h * HEAD : WIDTH + (h + 1) * HEAD]
            dots = jnp.sum(products[:, at], axis=-1, keepdims=True)
            dp = matmul_nt(g[:, at], v)
            sums = [None] * 7
            for i in range(4):
                here = slice(i * block, (i + 1) * block)
                ds = p_ref[e * SETS + h, here, :].astype(F32) * (dp[here] - dots[here])
                if biased:
                    for j in range(4):
                        part = ds[:, j * 2 * block : (j + 1) * 2 * block]
                        slot = 3 - i + j
                        sums[slot] = part if sums[slot] is None else sums[slot] + part
                ds_ref[here, :] = (ds * factor).astype(BF)
            dq_ref[e, :, at] = matmul(ds_ref[...], k).astype(BF)
            dkeys[:, at] = matmul_tn(ds_ref[...], q_ref[e, :, at])
            dkeys[:, WIDTH + h * HEAD : WIDTH + (h + 1) * HEAD] = matmul_tn(
                p_ref[e * SETS + h], g[:, at]
            )
            if biased:
                dtable_ref = refs[14]
                band = jnp.concatenate(sums + [jnp.zeros_like(sums[0])], axis=1)
                ids = lax.broadcasted_iota(jnp.int32, band.shape, 0)
                bit = 1
                while bit < block:
                    moved = pltpu.roll(band, 2 * extent - bit, 1)
                    band = jnp.where((ids & bit) != 0, moved, band)
                    bit *= 2
                line = jnp.sum(band, axis=0, keepdims=True)
                dtable_ref[e * SETS + h : e * SETS + h + 1, :] = pltpu.roll(line, block - 1, 1)
        for k in range(4):
            at = pl.multiple_of(block * (2 * k + core), block)
            mine_ref[e, k * block : (k + 1) * block, :] = dkeys[pl.ds(at, block), :]
            at = pl.multiple_of(block * (2 * k + 1 - core), block)
            other_ref[1 - e, k * block : (k + 1) * block, :] = dkeys[
                pl.ds(at, block), :
            ].astype(BF)


def attend_local_back(gain, biased, scalars, upstream, values, part, got, gains, *rest, name):
    rows, extent = upstream.shape[0], 2 * upstream.shape[0]
    outs = [
        ((rows, D), F32),
        ((1, D), F32),
        ((rows, D), BF),
        ((2, rows, WIDTH), BF),
        ((2, rows, 2 * WIDTH), F32),
        ((2, rows, 2 * WIDTH), BF),
    ]
    if biased:
        outs.append(((2 * SETS, 2 * extent), F32))
    return call(
        functools.partial(attend_back_kernel, gain, biased),
        name,
        outs,
        [(scalars, SCALARS), (upstream, LATE), (values, LATE), part, got, gains]
        + list(rest[:2])
        + [(a, LATE) for a in rest[2:]],
        9.0 if biased else 6.0,
        [
            pltpu.VMEM((2, extent, 2 * WIDTH), BF),
            pltpu.VMEM((extent, 2 * WIDTH), F32),
            pltpu.VMEM((rows, extent), BF),
        ],
    )


def project_back_kernel(split, q_at, dq_ref, mine_ref, got_ref, *refs):
    kva_ref, qa_ref, kvb_ref, qb_ref = refs[:4]
    dkv_ref = refs[4]
    from_keys = from_queries = None
    for e, (kv, q) in enumerate(((kva_ref, qa_ref), (kvb_ref, qb_ref))):
        dkv = (mine_ref[e] + got_ref[e].astype(F32)).astype(BF)
        dkv_ref[e] = dkv
        term = matmul_nt(dkv, kv[:, : 2 * WIDTH])
        from_keys = term if e == 0 else from_keys + term
        term = matmul_nt(dq_ref[e], q[:, q_at : q_at + WIDTH])
        from_queries = term if e == 0 else from_queries + term
    outs = [from_keys, from_queries] if split else [from_keys + from_queries]
    for k, total in enumerate(outs):
        refs[5 + 2 * k][...] = total
        refs[6 + 2 * k][...] = total.astype(BF)


def project_back(split, dq, mine, got, kv_own, q_own, kv_sib, q_sib, q_at, name):
    rows = dq.shape[1]
    outs = [((2, rows, 2 * WIDTH), BF)] + [((rows, D), F32), ((rows, D), BF)] * (1 + split)
    return call(
        functools.partial(project_back_kernel, split, q_at),
        name,
        outs,
        [dq, mine, got, kv_own, q_own, kv_sib, q_sib],
        2.5,
    )


def attend_weights_kernel(count, *refs):
    ins, (own_ref, sib_ref, out_own_ref, out_sib_ref) = refs[:-4], refs[-4:]
    for k in range(count):
        nq_ref, nkv_ref, dq_ref, dkv_ref, ctx_ref, low_ref = ins[6 * k : 6 * k + 6]
        kv_at, q_at = 2 * WIDTH * k, 2 * WIDTH * count + WIDTH * k
        for e, (in_ref, out_ref) in enumerate(((own_ref, out_own_ref), (sib_ref, out_sib_ref))):
            if k == 0 and in_ref.shape[1] > 3 * count * WIDTH:
                in_ref[...] = jnp.zeros_like(in_ref)
            in_ref[:, kv_at : kv_at + 2 * WIDTH] = matmul_tn(nkv_ref[...], dkv_ref[e]).astype(BF)
            in_ref[:, q_at : q_at + WIDTH] = matmul_tn(nq_ref[...], dq_ref[e]).astype(BF)
            out_ref[k] = matmul_tn(ctx_ref[e].astype(BF), low_ref[...]).astype(BF)


def attend_weights(name, *attentions):
    count, rows = len(attentions), attentions[0][0].shape[0]
    inner, outer = ((D, -(-3 * count * WIDTH // 128) * 128), BF), ((count, WIDTH, D), BF)
    own, sib, out_own, out_sib = call(
        functools.partial(attend_weights_kernel, count),
        name,
        [inner, inner, outer, outer],
        [a for attention in attentions for a in attention],
        1.0 * count,
    )
    return own, out_own, sib, out_sib


IN_ORDER = (8, 6, 7, 4, 0, 1, 5, 2, 3)


def sums_kernel(own, late_ref, dec_ref, self_ref, out_ref):
    inner, third, half = 6 * WIDTH, D // 3, D // 2
    width = dec_ref.shape[1]
    wide, rows = width - 2 * third, dec_ref.shape[0] * 2 // 3
    out_ref[...] = jnp.zeros_like(out_ref)

    def squares(values, rows_in_all):
        values = values.astype(F32)
        return values * values * (0.5 / rows_in_all)

    def line(values):
        return jnp.sum(values, axis=0, keepdims=True)

    def put(at, values):
        for k in range(0, values.shape[1], 128):
            size = min(128, values.shape[1] - k)
            out_ref[at + k // 128 : at + k // 128 + 1, :size] = values[:, k : k + size]

    put(0, line(squares(late_ref[:, :wide], D)))
    put(wide // 128, line(squares(dec_ref[:, :wide], D)))
    at = 2 * wide // 128
    put(at, line(squares(late_ref[:, width : width + inner], D)))
    put(at + inner // 128, line(squares(self_ref[:, third : third + 3 * WIDTH], D)))
    at = 30
    for ref in (late_ref, dec_ref):
        down = squares(ref[:, wide:width], FF)
        put(at, line(down[:rows]))
        put(at + 2 * third // 128, line(down[rows:, :third]) + line(down[rows:, third:]))
        at += D // 128
    outer = squares(self_ref[:, :third], D)
    for k in range(3):
        put(at + k * third // 128, line(outer[k * own : (k + 1) * own]))
    at += D // 128
    outer = squares(late_ref[:, width + inner :], D)
    for k in range(2):
        for side in range(2):
            begin = (2 * side + k) * own
            put(at + side * half // 128, line(outer[begin : begin + own]))
        at += D // 128


def hold_kernel(values_ref, earlier_ref, out_ref):
    out_ref[...] = values_ref[...]


def half_mean_rows(values):
    ones = jnp.full((8, values.shape[1]), 0.5 / values.shape[1], F32)
    sums = lax.dot_general(
        ones,
        values * values,
        (((1,), (1,)), ((), ())),
        precision=HIGHEST,
        preferred_element_type=F32,
    )
    return sums[:1]


def shards_kernel(ff_own, columns_ref, early_ref, turned_ref, late_ref, dec_ref, *outs):
    in_ref, out_ref, hin_ref, hout_ref, row_in_ref, row_out_ref, row_hin_ref, row_hout_ref = outs
    third = D // 3
    width = dec_ref.shape[1]
    wide = width - 2 * third
    units = wide // 2
    for k, at in enumerate(IN_ORDER):
        ref, at = (columns_ref, at * WIDTH) if at < 6 else (early_ref, wide + (at - 6) * WIDTH)
        for q in range(WAYS):
            piece = ref[q, :, at : at + WIDTH]
            in_ref[k // 3, k % 3, :, q * WIDTH : (q + 1) * WIDTH] = piece
        row_in_ref[k : k + 1, :] = half_mean_rows(in_ref[k // 3, k % 3])
    out_ref[...] = turned_ref[...]
    for k in range(3):
        row_out_ref[k : k + 1, :] = half_mean_rows(turned_ref[k])
    for layer in range(2):
        ref, begin = (columns_ref, 6 * WIDTH) if layer == 0 else (early_ref, 0)
        for j in range(2):
            for k in range(units // ff_own):
                first = begin + j * units + k * ff_own
                for q in range(WAYS):
                    at = (WAYS * k + q) * ff_own
                    piece = ref[q, :, first : first + ff_own]
                    hin_ref[layer, j, :, at : at + ff_own] = piece
            row_hin_ref[2 * layer + j : 2 * layer + j + 1, :] = half_mean_rows(hin_ref[layer, j])
    for layer, ref in enumerate((late_ref, dec_ref)):
        down = ref[:, wide:width].astype(F32)
        hout_ref[layer, :, : 2 * third] = down[:ff_own]
        half = ff_own // 2
        hout_ref[layer, :half, 2 * third :] = down[ff_own:, :third]
        hout_ref[layer, half:, 2 * third :] = down[ff_own:, third:]
        row_hout_ref[layer : layer + 1, :] = half_mean_rows(hout_ref[layer])


def input_kernel(gain, up_ref, x_ref, part_ref, got_ref, gains_ref, out_ref, dgain_ref):
    grad, dgain_ref[...] = norm_back(
        x_ref[...].astype(F32),
        gains_ref[gain : gain + 1, :],
        part_ref[...] + got_ref[...].astype(F32),
    )
    out_ref[...] = up_ref[...] + grad


def input_back(gain, upstream, x, part, got, gains, name):
    return call(
        functools.partial(input_kernel, gain),
        name,
        [(upstream.shape, F32), ((1, D), F32)],
        [upstream, x, part, got, gains],
        1.5,
    )


def gather_own_rows(place, mine, other_seq):
    near = pair_up(mine, swap(other_seq, "y"), place.y)
    far = pair_up(near, swap(near, "x"), place.x)
    far = far.transpose(2, 1, 0, 3, 4)
    return far.reshape(far.shape[0], -1, far.shape[4])


def give_back(place, half):
    blocks = half.reshape(2, 2, -1, half.shape[1])
    blocks = pick(blocks, place.x, 1)
    other = swap(pick(blocks, 1 - place.y), "y")
    return pair_up(pick(blocks, place.y), other, place.y)


def sum_everywhere(place, values):
    depth = place.depth
    for axis in ("c", "x", "y"):
        values = values + swap(values, axis)
    return values + sum(shift_z(values, k, depth) for k in range(1, depth))


def pack_down(rows):
    half, third = rows.shape[-2] // 2, rows.shape[-1] // 3
    last = rows[..., 2 * third :]
    last = jnp.concatenate([last[..., :half, :], last[..., half:, :]], axis=-1)
    return jnp.concatenate([rows[..., : 2 * third], last], axis=-2)


def unpack_down(packed):
    half, third = packed.shape[-2] // 3, packed.shape[-1] // 2
    last = packed[..., 2 * half :, :]
    last = jnp.concatenate([last[..., :third], last[..., third:]], axis=-2)
    return jnp.concatenate([packed[..., : 2 * half, :], last], axis=-1)


def pack_out(pair):
    rows = pair.reshape(pair.shape[:-3] + (-1, pair.shape[-1]))
    half = rows.shape[-1] // 2
    return jnp.concatenate([rows[..., :half], rows[..., half:]], axis=-2)


def unpack_out_piece(packed):
    half = packed.shape[-2] // 2
    rows = jnp.concatenate([packed[..., :half, :], packed[..., half:, :]], axis=-1)
    return rows.reshape(rows.shape[:-2] + (2, half // 2, rows.shape[-1]))


def unpack_out(packed, depth):
    pair = unpack_out_piece(packed)
    pair = pair.reshape((depth, 2) + pair.shape[1:])
    pair = pair.transpose(2, 1, 0, 3, 4)
    return pair.reshape(2, -1, pair.shape[-1])


def turned_parts(grads, depth):
    parts = grads.reshape(2, depth, -1, grads.shape[1]).transpose(1, 0, 2, 3)
    return parts.reshape(2 * depth, -1, grads.shape[1])


def grouped(
    depth,
    enc_input,
    dec_input,
    enc_lengths,
    dec_lengths,
    enc_buckets,
    dec_buckets,
    attention_in,
    attention_out,
    hidden_in,
    hidden_out,
    norm_gains,
    position_bias,
    enc_cotangent,
    dec_cotangent,
):
    place = Place(depth)
    y, q = place.y, place.q
    block = enc_input.shape[1]
    length = block * 8
    own = attention_in.shape[2]
    ff_own = hidden_out.shape[1]
    units = ff_own * 2 * depth
    group = WAYS * own

    pieces = attention_in.reshape(3, 3, own, WAYS, WIDTH).transpose(3, 0, 1, 2, 4)
    queries, keys, values = pieces[:, :, 0], pieces[:, :, 1], pieces[:, :, 2]
    gain_piece = jnp.pad(norm_gains.T, ((0, 0), (0, 64 - norm_gains.shape[0])))
    gain_piece = jnp.broadcast_to(gain_piece[None], (WAYS,) + gain_piece.shape)
    turned = turn(attention_out, depth)
    hidden_pieces = hidden_in.reshape(2, 2, own, 2 * depth, WAYS, ff_own)
    hidden_pieces = hidden_pieces.transpose(4, 0, 2, 1, 3, 5).reshape(WAYS, 2, own, 2 * units)
    blocks_in = [keys[:, 0], values[:, 0], queries[:, 0], gain_piece]
    blocks_in += [keys[:, 1], values[:, 1], keys[:, 2], values[:, 2], queries[:, 1], queries[:, 2]]
    blocks_in += [hidden_pieces[:, 0]]
    everything = exchange_columns(place, jnp.concatenate(blocks_in, axis=2)).reshape(group, -1)
    cuts = [3 * WIDTH + 64, 9 * WIDTH + 64]
    enc_piece, rest, ffn_enc = jnp.split(everything, cuts, axis=1)
    ffn_dec = exchange_columns(place, after(hidden_pieces[:, 1], ffn_enc)).reshape(group, -1)
    third = turned[0].reshape(own, 3, D // 3).transpose(1, 0, 2).reshape(3 * own, D // 3)
    third = jnp.pad(third, ((0, group - 3 * own), (0, 0)))
    enc_piece = jnp.concatenate([enc_piece, third], axis=1)
    rest = jnp.concatenate([rest, pack_out(turned[1:])], axis=1)
    ffn_enc = jnp.concatenate([ffn_enc, pack_down(hidden_out[0])], axis=1)
    ffn_dec = jnp.concatenate([ffn_dec, pack_down(hidden_out[1])], axis=1)

    line = along_z(place, enc_piece)
    w_enc = along_y(place, line)
    w_enc_sib = swap(w_enc, "c")

    def out_rows(whole):
        rows = whole[:, 3 * WIDTH + 64 :].reshape(depth, 2, group, D // 3)[:, :, : 3 * own]
        rows = rows.reshape(depth, 2, 3, own, D // 3).transpose(1, 0, 3, 2, 4)
        return rows.reshape(WIDTH, D)

    def gather(piece):
        return lax.all_gather(piece, ("dp", "y"), axis=0, tiled=True)

    first = gather(jnp.concatenate([rest, ffn_enc], axis=1))
    out_enc, out_enc_sib = out_rows(w_enc), out_rows(w_enc_sib)
    gains = w_enc[:, 3 * WIDTH : 3 * WIDTH + norm_gains.shape[0]].astype(F32).T

    w_self = [w_enc, w_enc, w_enc_sib, w_enc_sib]

    def own_rows(*arrays):
        mine = jnp.stack([pick(a, y) for a in arrays])
        other = jnp.stack([pick(a, 1 - y) for a in arrays])
        return gather_own_rows(place, mine, other)

    enc_rows, dec_rows, *cots = own_rows(enc_input, dec_input, dec_cotangent, enc_cotangent)
    enc_scalars = jnp.stack([place.c, pick(enc_lengths, y)]).astype(jnp.int32)
    dec_scalars = jnp.stack([place.c, pick(dec_lengths, y)]).astype(jnp.int32)

    def head_rows(table):
        mine = lax.dynamic_slice_in_dim(table, q * SETS, SETS, 0)
        theirs = lax.dynamic_slice_in_dim(table, (q + 1 - 2 * place.c) * SETS, SETS, 0)
        table = jnp.concatenate([mine, theirs])
        table = jnp.pad(table, ((0, 0), (0, block)))
        return lax.dynamic_slice_in_dim(table, block * (1 - place.c), 2 * length, 1)

    enc_table = offset_table(enc_buckets, position_bias[0])
    enc_table = head_rows(jnp.pad(enc_table, ((0, 0), (0, 1))))
    dec_table = offset_table(dec_buckets, position_bias[1])
    dec_table = jnp.concatenate(
        [dec_table[:, ::-1], jnp.broadcast_to(dec_table[:, :1], (HEADS, length))], axis=1
    )
    dec_table = head_rows(dec_table)

    n_a, q_enc, kv_enc = self_project(enc_rows, gains, 0, *w_self, 2 * WIDTH, "enc_project")
    kv_enc_got = swap(kv_enc, "c")
    ctx_enc, p_enc, part, low = attend_local(
        enc_scalars, q_enc, kv_enc, kv_enc_got, enc_table, out_enc, out_enc_sib, False, "enc_attend"
    )
    low_enc, part_enc = low, part
    ffn_dec = gather(after(ffn_dec, low_enc))
    got_enc = swap(low_enc, "x")
    first = after(first, got_enc)
    rest, ffn_enc = first[:, : ffn_enc.shape[1]], first[:, ffn_enc.shape[1] :]
    rest_sib, ffn_enc_sib = swap(rest, "c"), swap(ffn_enc, "c")
    out_rest = unpack_out(rest[:, 6 * WIDTH :].reshape(2 * depth, group, -1), depth)
    out_rest_sib = unpack_out(rest_sib[:, 6 * WIDTH :].reshape(2 * depth, group, -1), depth)
    w_dec = [column_block(w, k) for w in (rest, rest_sib) for k in (0, 2)]
    w_cross = [column_block(w, k) for w in (rest, rest_sib) for k in (1, 2)]
    out_dec, out_cross = [[(w, pl.BlockSpec((None, WIDTH, D), f)) for w in (out_rest, out_rest_sib)]
        for f in (lambda _: (0, 0, 0), lambda _: (1, 0, 0))]

    n_b, q_dec, kv_dec = self_project(dec_rows, gains, 3, *w_dec, 0, "dec_project")
    kv_dec_got = swap(kv_dec, "c")
    ctx_dec, p_dec, part_dec, low_dec = attend_local(
        dec_scalars, q_dec, kv_dec, kv_dec_got, dec_table, *out_dec, True, "dec_attend"
    )

    enc_mid, n_1, gu_enc, hid_enc, part, low = ffn_local(
        enc_rows, part_enc, after(got_enc, low_dec), gains, 1, ffn_enc, ffn_enc_sib, units, "enc_ffn"
    )
    rows = enc_rows.shape[0]
    dec_mid, n_c, q_cross = call(
        functools.partial(cross_kernel, WIDTH),
        "cross_project",
        [((rows, D), F32), ((rows, D), BF), ((2, rows, WIDTH), BF)],
        [dec_rows, part_dec, swap(low_dec, "x"), gains, w_cross[1], w_cross[3]],
        2.0,
    )
    enc_last, memory_low, kv_cross = call(
        memory_kernel,
        "memory",
        [((rows, D), F32), ((rows, D), BF), ((2, rows, 2 * WIDTH), BF)],
        [enc_mid, part, after(swap(low, "x"), q_cross), gains, w_cross[0], w_cross[2]],
        2.0,
    )
    kv_cross_got = swap(kv_cross, "c")

    ctx_cross, p_cross, part, low = attend_local(
        enc_scalars, q_cross, kv_cross, kv_cross_got, None, *out_cross, False, "cross_attend"
    )
    ffn_dec = after(ffn_dec, low)
    ffn_dec_sib = swap(ffn_dec, "c")
    dec_cross, n_5, gu_dec, hid_dec, part, low = ffn_local(
        dec_mid, part, swap(low, "x"), gains, 5, ffn_dec, ffn_dec_sib, units, "dec_ffn"
    )

    def both(own_grads, sib_grads):
        return (own_grads.astype(F32) + swap(sib_grads, "c").astype(F32)).astype(BF)

    def blocks(grads):
        return grads.reshape(2 * depth, -1, grads.shape[1])

    def scatter(grads):
        return lax.psum_scatter(grads, ("dp", "y"), scatter_dimension=0, tiled=False)

    dec_final, g, gg6, low_d, dgu_dec, part, low = ffn_back(
        True, dec_cross, part, swap(low, "x"), cots[0], gains, gu_dec, ffn_dec, ffn_dec_sib, "dec_ffn_back"
    )
    d_ffn_dec = ffn_weights(n_5, dgu_dec, hid_dec, low_d, "dec_ffn_weights")
    d_ffn_dec = both(*d_ffn_dec)
    got_f = after(swap(low, "x"), d_ffn_dec)
    got = got_f
    g, gg5, low_x, dq_cross, mine, other = attend_local_back(
        5,
        False,
        enc_scalars,
        g,
        dec_cross,
        part,
        got,
        gains,
        *out_cross,
        q_cross,
        kv_cross,
        kv_cross_got,
        p_cross,
        ctx_cross,
        name="cross_attend_back",
    )
    got = swap(other, "c")
    d_ffn_dec = scatter(after(blocks(d_ffn_dec), got_f))
    dkv_cross, part_m, low_m, part_c, low_c = project_back(
        True, dq_cross, mine, got, *w_cross, WIDTH, "cross_project_back"
    )
    got_c = swap(low_c, "x")
    got_m = after(swap(low_m, "x"), got_c)
    g_last, gg2, low_e, dgu_enc, part, part_low = ffn_back(
        False, enc_last, part_m, got_m, cots[1], gains, gu_enc, ffn_enc, ffn_enc_sib, "enc_ffn_back"
    )
    d_ffn_enc = ffn_weights(n_1, dgu_enc, hid_enc, low_e, "enc_ffn_weights")
    got_e = swap(part_low, "x")
    got_c = after(got_c, *d_ffn_enc)
    d_ffn_enc = both(*d_ffn_enc)
    g_dec, gg4, low_b, dq_dec, mine, other, d_table_dec = attend_local_back(
        4,
        True,
        dec_scalars,
        g,
        dec_mid,
        part_c,
        got_c,
        gains,
        *out_dec,
        q_dec,
        kv_dec,
        kv_dec_got,
        p_dec,
        ctx_dec,
        name="dec_attend_back",
    )
    got_e = after(got_e, dq_dec)
    dec_other = swap(other, "c")
    dec_mine = mine
    g_enc, gg1, low_a, dq_enc, mine, other, d_table_enc = attend_local_back(
        1,
        True,
        enc_scalars,
        g_last,
        enc_mid,
        part,
        got_e,
        gains,
        out_enc,
        out_enc_sib,
        q_enc,
        kv_enc,
        kv_enc_got,
        p_enc,
        ctx_enc,
        name="enc_attend_back",
    )
    dkv_dec, part_d, low = project_back(
        False, dq_dec, dec_mine, dec_other, *w_dec, 0, "dec_project_back"
    )
    got_d = swap(low, "x")
    d_in, d_out, d_in_sib, d_out_sib = attend_weights(
        "attend_weights",
        (n_b, n_b, dq_dec, dkv_dec, ctx_dec, low_b),
        (n_c, memory_low, dq_cross, dkv_cross, ctx_cross, low_x),
    )
    d_out = both(d_out, d_out_sib)
    d_out = jnp.stack([turned_parts(d_out[k], depth) for k in range(2)], 1)
    d_in = d_in.astype(F32) + after(swap(d_in_sib, "c"), d_ffn_dec).astype(F32)
    late = [blocks(d_ffn_enc), blocks(rounded(d_in)), pack_out(d_out)]
    late = scatter(jnp.concatenate(late, axis=2))
    got = after(swap(other, "c"), dkv_dec)
    dkv_enc, part, low = project_back(
        False, dq_enc, mine, got, *w_self, 2 * WIDTH, "enc_project_back"
    )
    d_in, d_out, d_in_sib, d_out_sib = attend_weights(
        "enc_attend_weights", (n_a, n_a, dq_enc, dkv_enc, ctx_enc, low_a)
    )
    got = after(swap(low, "x"), d_in, d_out)
    thirds = turned_parts(both(d_out, d_out_sib)[0], depth).reshape(2 * depth, own, 3, D // 3)
    thirds = thirds.transpose(0, 2, 1, 3).reshape(2 * depth, 3 * own, D // 3)
    thirds = jnp.pad(thirds, ((0, 0), (0, group - 3 * own), (0, 0)))
    d_enc = jnp.concatenate([thirds, blocks(both(d_in, d_in_sib))], axis=2)
    d_enc = scatter_y(place, d_enc)
    got_d = after(got_d, d_in)
    grad_dec, gg3 = input_back(3, g_dec, dec_rows, part_d, got_d, gains, "dec_input_back")
    grad_enc, gg0 = input_back(0, g_enc, enc_rows, part, got, gains, "enc_input_back")
    memory_low, dec_final, grad_enc, grad_dec, gg0, gg3 = after(
        (memory_low, dec_final, grad_enc, grad_dec, gg0, gg3), d_enc
    )
    d_enc = scatter_z(place, d_enc)

    wide, inner = 2 * units, 6 * WIDTH
    early = [d_ffn_dec[:, :wide], rounded(d_enc[:, D // 3 : D // 3 + 3 * WIDTH])]
    early = jnp.concatenate(early, axis=1).reshape(WAYS, own, -1)
    early = exchange_columns(place, early).astype(F32)
    late = after(late, early)
    down = wide + 2 * D // 3
    (sums,) = call(
        functools.partial(sums_kernel, own),
        "column_sums",
        [((64, 128), F32)],
        [late, d_ffn_dec, d_enc],
        1.0,
    )
    out_enc_mine = d_enc[: 3 * own, : D // 3].reshape(3, own, D // 3).transpose(1, 0, 2)
    out_mine = unpack_out_piece(late[:, down + inner :])
    turned_out = jnp.concatenate([rounded(out_enc_mine.reshape(1, own, D)), out_mine])
    turned_out = turn(turned_out, depth).astype(F32)
    columns = [late[:, down : down + inner], late[:, :wide]]
    columns = jnp.concatenate(columns, axis=1).reshape(WAYS, own, -1)
    columns = exchange_over_x(place, columns)
    columns_here = columns
    columns = exchange_over_cores(place, columns).astype(F32)
    shard_in, shard_out, shard_hin, shard_hout, row_in, row_out, row_hin, row_hout = call(
        functools.partial(shards_kernel, ff_own),
        "shards",
        [
            ((3, 3, own, D), F32),
            ((3, own, D), F32),
            ((2, 2, own, WAYS * units), F32),
            ((2, ff_own, D), F32),
            ((9, own), F32),
            ((3, own), F32),
            ((4, own), F32),
            ((2, ff_own), F32),
        ],
        [columns, early, turned_out, late, d_ffn_dec],
        2.0,
    )
    sums = sums + sum(shift_z(sums, k, depth) for k in range(1, depth))
    sums = sums + swap(sums, "y")
    (sums,) = call(hold_kernel, "hold", [(sums.shape, F32)], [sums, (columns_here, ANYWHERE)], 0.3)
    sums = pair_up(sums, swap(sums, "x"), place.x)
    sums = pair_up(sums, swap(sums, "c"), place.c)
    sums = sums.swapaxes(0, 1).reshape(WAYS, -1)
    cuts = [2 * wide, 2 * wide + 9 * WIDTH, 30 * 128, 30 * 128 + 2 * D, 30 * 128 + 5 * D]
    col_hin, col_in, _, col_hout, col_out, _ = jnp.split(sums, cuts, axis=1)
    col_hin = col_hin.reshape(WAYS, 2, 2, 2 * depth, ff_own).transpose(1, 2, 3, 0, 4)
    col_hin = col_hin.reshape(2, 2, WAYS * units)
    col_in = col_in.reshape(WAYS, 9, WIDTH)
    col_in = jnp.stack([col_in[:, k] for k in IN_ORDER]).reshape(3, 3, D)
    col_hout = jnp.sum(col_hout, axis=0).reshape(2, D)
    col_out = jnp.sum(col_out, axis=0).reshape(3, D)

    buckets = position_bias.shape[1]

    def head_table(d_table):
        wide_table = jnp.zeros((2 * SETS, 2 * length + block), F32)
        return lax.dynamic_update_slice_in_dim(wide_table, d_table, block * (1 - place.c), 1)

    grad_enc_bias = head_table(d_table_enc)[:, : 2 * length - 1]
    grad_dec_bias = head_table(d_table_dec)[:, :length][:, ::-1]
    by_set = jnp.stack(
        [
            bucket_grad(enc_buckets, grad_enc_bias, buckets),
            bucket_grad(dec_buckets, grad_dec_bias, buckets),
        ]
    )
    grad_position = lax.dynamic_update_slice_in_dim(
        jnp.zeros_like(position_bias), by_set[:, :, :SETS], q * SETS, 2
    )
    grad_position = lax.dynamic_update_slice_in_dim(
        grad_position, by_set[:, :, SETS:], (q + 1 - 2 * place.c) * SETS, 2
    )
    grad_gains = jnp.concatenate([gg0, gg1, gg2, gg3, gg4, gg5, gg6])
    grad_gains = jnp.where(place.x == 0, grad_gains, 0.0)
    small = jnp.concatenate([grad_gains.reshape(-1, 128), grad_position.reshape(-1, 128)])
    small = sum_everywhere(place, small)
    cut = grad_gains.size // 128
    grad_gains = small[:cut].reshape(grad_gains.shape)
    grad_position = small[cut:].reshape(grad_position.shape)
    shard_gains = lax.dynamic_slice_in_dim(grad_gains, place.index * own, own, 1)

    return (
        give_back(place, memory_low),
        give_back(place, dec_final),
        give_back(place, grad_enc),
        give_back(place, grad_dec),
        shard_in,
        shard_out,
        shard_hin,
        shard_hout,
        shard_gains,
        grad_position,
        row_in.reshape(3, 3, own),
        col_in,
        row_out,
        col_out,
        row_hin.reshape(2, 2, own),
        col_hin,
        row_hout,
        col_hout,
    )


def specs(seq):
    rows = P("dp", seq, None)
    every = ("dp",) + (seq if isinstance(seq, tuple) else (seq,))
    second, third = P(None, every, None), P(None, None, every, None)
    ins = (rows, rows, P("dp"), P("dp"), P(), P(), third, second, third, second)
    ins += (P(None, every), P(), rows, rows)
    outs = (rows, rows, rows, rows, third, second, third, second, P(None, every), P())
    outs += (P(None, None, every), P(), P(None, every), P())
    outs += (P(None, None, every), P(), P(None, every), P())
    return ins, outs


def solution(mesh):
    depth, seq = mesh.shape["dp"], mesh.shape["seq"]

    def wrap(function, over, axes):
        ins, outs = specs(axes)
        return jax.shard_map(function, mesh=over, in_specs=ins, out_specs=outs, check_vma=False)

    def run(*args):
        seqs, length = args[0].shape[0] // depth, args[0].shape[1]
        fits = depth == WAYS and seq == 8 and seqs == 2 and length % 512 == 0
        if fits and args[1].shape == args[0].shape:
            axes = ("y", "x", "c")
            split = Mesh(mesh.devices.reshape(depth, 2, 2, 2), ("dp",) + axes)
            return wrap(functools.partial(grouped, depth), split, axes)(*args)
        return wrap(local, mesh, "seq")(*args)

    return run
```

```python
import functools
import math

import jax
import jax.numpy as jnp
from jax import lax
from jax.experimental import pallas as pl
from jax.experimental.pallas import tpu as pltpu
from jax.sharding import Mesh, PartitionSpec as P

D = 768
HEADS = 12
HEAD = 64
FF = 2048


EPSILON = 1e-06
NEGATIVE = -1e30
HIGHEST = lax.Precision.HIGHEST


def rounded(values):
    return values.astype(jnp.bfloat16)


def rows_first(values):
    return values.transpose(0, 2, 1)


def rms_norm(values, gain_row):
    return (
        values * lax.rsqrt(jnp.mean(values * values, axis=-1, keepdims=True) + EPSILON) * gain_row
    )


def rms_back(values, gain_row, upstream):
    _, pullback = jax.vjp(rms_norm, values, gain_row)
    return pullback(upstream)


def gated_unit(gate_up):
    return jax.nn.gelu(gate_up[0], approximate=True) * gate_up[1]


def offset_table(buckets, layer_bias):
    choose = (buckets[:, None] == jnp.arange(layer_bias.shape[0], dtype=jnp.int32)[None, :]).astype(
        jnp.float32
    )
    return jnp.dot(choose, layer_bias, precision=HIGHEST).T


def bucket_grad(buckets, grad_bias, bucket_count):
    choose = (buckets[:, None] == jnp.arange(bucket_count, dtype=jnp.int32)[None, :]).astype(
        jnp.float32
    )
    return jnp.dot(choose.T, grad_bias.T, precision=HIGHEST)


def hankel_block(window, rows, cols):
    heads_here, length = (window.shape[0], window.shape[1])
    tiled = jnp.tile(window, (1, rows + 1))[:, : rows * (length + 1)]
    return tiled.reshape(heads_here, rows, length + 1)[:, :, :cols]


def bias_block(variant, table, row_start, col_start, rows, cols, extent):
    span = rows + cols - 1
    if variant == "enc":
        base = col_start - row_start - (rows - 1) + (extent - 1)
        window = lax.dynamic_slice_in_dim(table, base, span, 1)
        return hankel_block(window, rows, cols)[:, ::-1, :]
    widened = jnp.concatenate(
        [jnp.broadcast_to(table[:, :1], (table.shape[0], extent - 1)), table], axis=1
    )
    base = row_start - col_start - (cols - 1) + (extent - 1)
    window = lax.dynamic_slice_in_dim(widened, base, span, 1)
    return hankel_block(window, rows, cols)[:, :, ::-1]


def visible_mask(variant, row_ids, col_ids, lengths):
    visible = col_ids[None, None, :] < lengths[:, None, None]
    if variant == "dec":
        visible = visible & (col_ids[None, None, :] <= row_ids[None, :, None])
    return visible[:, None]


def block_scores(query_heads, key_heads, row_ids, col_ids, lengths, variant, offset_bias, extent):
    factor = HEAD ** (-0.5)
    scores = (
        jnp.einsum("sqhe,skhe->shqk", query_heads, key_heads, preferred_element_type=jnp.float32)
        * factor
    )
    if offset_bias is not None:
        scores = (
            scores
            + bias_block(
                variant,
                offset_bias,
                row_ids[0],
                col_ids[0],
                row_ids.shape[0],
                col_ids.shape[0],
                extent,
            )[None]
        )
    return (scores, visible_mask(variant, row_ids, col_ids, lengths))


def row_products(grad_context, context):
    seqs_here, rows_here = (context.shape[0], context.shape[1])
    return jnp.sum(
        (grad_context.astype(jnp.float32) * context).reshape(seqs_here, rows_here, HEADS, HEAD),
        axis=-1,
    ).transpose(0, 2, 1)


def attend(queries, row_ids, lengths, variant, offset_bias, extent, fold_keys):
    seqs_here, rows_here = (queries.shape[0], queries.shape[1])
    query_heads = queries.reshape(seqs_here, rows_here, HEADS, HEAD)

    def fold_step(carried, pieces, begin_at):
        key_rows, value_rows = pieces
        block_len = math.gcd(key_rows.shape[1], 512)

        def block_step(block_id, running):
            row_max, row_sum, weighted = running
            offset_in = block_id * block_len
            key_heads = lax.dynamic_slice_in_dim(key_rows, offset_in, block_len, 1).reshape(
                seqs_here, block_len, HEADS, HEAD
            )
            value_heads = lax.dynamic_slice_in_dim(value_rows, offset_in, block_len, 1).reshape(
                seqs_here, block_len, HEADS, HEAD
            )
            col_ids = offset_in + jnp.arange(block_len, dtype=jnp.int32)
            scores, visible = block_scores(
                query_heads, key_heads, row_ids, col_ids, lengths, variant, offset_bias, extent
            )
            new_max = jnp.maximum(row_max, jnp.max(jnp.where(visible, scores, NEGATIVE), axis=-1))
            weights = jnp.where(visible, jnp.exp(scores - new_max[..., None]), 0.0)
            shrink = jnp.exp(row_max - new_max)
            row_sum = row_sum * shrink + jnp.sum(weights, axis=-1)
            weighted = weighted * shrink[..., None] + jnp.einsum(
                "shqk,skhe->shqe", rounded(weights), value_heads, preferred_element_type=jnp.float32
            )
            return (new_max, row_sum, weighted)

        return lax.fori_loop(0, key_rows.shape[1] // block_len, block_step, carried)

    initial = (
        jnp.full((seqs_here, HEADS, rows_here), NEGATIVE, jnp.float32),
        jnp.zeros((seqs_here, HEADS, rows_here), jnp.float32),
        jnp.zeros((seqs_here, HEADS, rows_here, HEAD), jnp.float32),
    )
    row_max, row_sum, weighted = fold_keys(fold_step, initial)
    context = (
        (weighted / row_sum[..., None])
        .transpose(0, 2, 1, 3)
        .reshape(seqs_here, rows_here, HEADS * HEAD)
    )
    return (context, row_max + jnp.log(row_sum))


def attend_back(
    queries,
    log_sums,
    row_dots,
    grad_context,
    row_ids,
    lengths,
    variant,
    offset_bias,
    extent,
    fold_keys,
):
    seqs_here, rows_here = (queries.shape[0], queries.shape[1])
    query_heads = queries.reshape(seqs_here, rows_here, HEADS, HEAD)
    grad_heads = grad_context.reshape(seqs_here, rows_here, HEADS, HEAD)
    bias_width = offset_bias.shape[1] if offset_bias is not None else 1
    factor = HEAD ** (-0.5)

    def fold_step(carried, pieces, begin_at):
        key_rows, value_rows = pieces
        block_len = math.gcd(key_rows.shape[1], 512)

        def block_step(block_id, running):
            grad_query, grad_bias = (running[0], running[-1])
            offset_in = block_id * block_len
            key_heads = lax.dynamic_slice_in_dim(key_rows, offset_in, block_len, 1).reshape(
                seqs_here, block_len, HEADS, HEAD
            )
            value_heads = lax.dynamic_slice_in_dim(value_rows, offset_in, block_len, 1).reshape(
                seqs_here, block_len, HEADS, HEAD
            )
            col_ids = offset_in + jnp.arange(block_len, dtype=jnp.int32)
            scores, visible = block_scores(
                query_heads, key_heads, row_ids, col_ids, lengths, variant, offset_bias, extent
            )
            weights = jnp.where(visible, jnp.exp(scores - log_sums[..., None]), 0.0)
            grad_weights = jnp.einsum(
                "sqhe,skhe->shqk", grad_heads, value_heads, preferred_element_type=jnp.float32
            )
            grad_scores = weights * (grad_weights - row_dots[..., None])
            if offset_bias is not None:

                def table_block(table_values):
                    return bias_block(
                        variant,
                        table_values,
                        row_ids[0],
                        col_ids[0],
                        row_ids.shape[0],
                        col_ids.shape[0],
                        extent,
                    )

                _, table_pull = jax.vjp(table_block, offset_bias)
                grad_bias = grad_bias + table_pull(jnp.sum(grad_scores, axis=0))[0]
            grad_raw = rounded(grad_scores * factor)
            grad_query = grad_query + jnp.einsum(
                "shqk,skhe->shqe", grad_raw, key_heads, preferred_element_type=jnp.float32
            )
            return (grad_query, grad_bias)

        return lax.fori_loop(0, key_rows.shape[1] // block_len, block_step, carried)

    query_start = jnp.zeros((seqs_here, HEADS, rows_here, HEAD), jnp.float32)
    bias_start = jnp.zeros((HEADS, bias_width), jnp.float32)
    initial = (query_start, bias_start)
    result = fold_keys(fold_step, initial)
    grad_query = result[0].transpose(0, 2, 1, 3).reshape(seqs_here, rows_here, HEADS * HEAD)
    return (grad_query, None, None, result[1])


def owned_key_grads(
    key_rows, value_rows, col_ids, lengths, variant, offset_bias, extent, fold_queries
):
    seqs_here, keys_here = (key_rows.shape[0], key_rows.shape[1])
    key_heads = key_rows.reshape(seqs_here, keys_here, HEADS, HEAD)
    value_heads = value_rows.reshape(seqs_here, keys_here, HEADS, HEAD)
    factor = HEAD ** (-0.5)

    def fold_step(carried, pieces, begin_at):
        query_rows, grad_rows, log_rows, dot_rows = pieces
        block_len = math.gcd(query_rows.shape[1], 512)

        def block_step(block_id, running):
            grad_keys, grad_values = running
            offset_in = block_id * block_len
            query_heads = lax.dynamic_slice_in_dim(query_rows, offset_in, block_len, 1).reshape(
                seqs_here, block_len, HEADS, HEAD
            )
            grad_heads = lax.dynamic_slice_in_dim(grad_rows, offset_in, block_len, 1).reshape(
                seqs_here, block_len, HEADS, HEAD
            )
            log_block = lax.dynamic_slice_in_dim(log_rows, offset_in, block_len, 1).transpose(
                0, 2, 1
            )
            dot_block = lax.dynamic_slice_in_dim(dot_rows, offset_in, block_len, 1).transpose(
                0, 2, 1
            )
            row_ids = offset_in + jnp.arange(block_len, dtype=jnp.int32)
            scores, visible = block_scores(
                query_heads, key_heads, row_ids, col_ids, lengths, variant, offset_bias, extent
            )
            weights = jnp.where(visible, jnp.exp(scores - log_block[..., None]), 0.0)
            grad_weights = jnp.einsum(
                "sqhe,skhe->shqk", grad_heads, value_heads, preferred_element_type=jnp.float32
            )
            grad_scores = weights * (grad_weights - dot_block[..., None])
            grad_raw = rounded(grad_scores * factor)
            grad_keys = grad_keys + jnp.einsum(
                "shqk,sqhe->skhe", grad_raw, query_heads, preferred_element_type=jnp.float32
            ).reshape(seqs_here, keys_here, HEADS * HEAD)
            grad_values = grad_values + jnp.einsum(
                "shqk,sqhe->skhe", rounded(weights), grad_heads, preferred_element_type=jnp.float32
            ).reshape(seqs_here, keys_here, HEADS * HEAD)
            return (grad_keys, grad_values)

        return lax.fori_loop(0, query_rows.shape[1] // block_len, block_step, carried)

    initial = (
        jnp.zeros((seqs_here, keys_here, HEADS * HEAD), jnp.float32),
        jnp.zeros((seqs_here, keys_here, HEADS * HEAD), jnp.float32),
    )
    return fold_queries(fold_step, initial)


def feed_forward(residual, gain_row, weights_in, weights_out):
    normed_low = rounded(rms_norm(residual, gain_row))
    gate_up = jnp.einsum(
        "srd,jdf->jsrf", normed_low, weights_in, preferred_element_type=jnp.float32
    )
    hidden = rounded(gated_unit(gate_up))
    output = jnp.einsum("srf,fd->srd", hidden, weights_out, preferred_element_type=jnp.float32)
    return (residual + output, (normed_low, gate_up, hidden))


def feed_back(residual, gain_row, weights_in, weights_out, kept_values, upstream):
    normed_low, gate_up, hidden = kept_values
    upstream_low = rounded(upstream)
    grad_out_weights = jnp.einsum(
        "srf,srd->fd", hidden, upstream_low, preferred_element_type=jnp.float32
    )
    grad_hidden = jnp.einsum(
        "srd,fd->srf", upstream_low, weights_out, preferred_element_type=jnp.float32
    )
    _, pullback = jax.vjp(gated_unit, gate_up)
    grad_gate_up = rounded(pullback(grad_hidden)[0])
    grad_in_weights = jnp.einsum(
        "srd,jsrf->jdf", normed_low, grad_gate_up, preferred_element_type=jnp.float32
    )
    grad_normed = jnp.einsum(
        "jsrf,jdf->srd", grad_gate_up, weights_in, preferred_element_type=jnp.float32
    )
    grad_residual, grad_gain = rms_back(residual, gain_row, grad_normed)
    return (upstream + grad_residual, grad_gain, grad_in_weights, grad_out_weights)


def local(
    enc_input,
    dec_input,
    enc_lengths,
    dec_lengths,
    enc_buckets,
    dec_buckets,
    attention_in,
    attention_out,
    hidden_in,
    hidden_out,
    norm_gains,
    position_bias,
    enc_cotangent,
    dec_cotangent,
):
    full_in, full_out, full_hidden_in, full_hidden_out, full_gains = (
        lax.all_gather(attention_in, ("dp", "seq"), axis=2, tiled=True),
        lax.all_gather(attention_out, ("dp", "seq"), axis=1, tiled=True),
        lax.all_gather(hidden_in, ("dp", "seq"), axis=2, tiled=True),
        lax.all_gather(hidden_out, ("dp", "seq"), axis=1, tiled=True),
        lax.all_gather(norm_gains, ("dp", "seq"), axis=1, tiled=True),
    )
    gain_rows = full_gains.astype(jnp.float32)
    enc_rows = enc_input.shape[1]
    dec_rows = dec_input.shape[1]
    seq_index = lax.axis_index("seq")
    enc_ids = seq_index * enc_rows + jnp.arange(enc_rows, dtype=jnp.int32)
    dec_ids = seq_index * dec_rows + jnp.arange(dec_rows, dtype=jnp.int32)
    enc_extent = (enc_buckets.shape[0] + 1) // 2
    dec_extent = dec_buckets.shape[0]
    enc_table = offset_table(enc_buckets, position_bias[0])
    dec_table = offset_table(dec_buckets, position_bias[1])
    enc_values = enc_input.astype(jnp.float32)
    norm_a_low = rounded(rms_norm(enc_values, gain_rows[0]))
    enc_qkv = rounded(
        jnp.einsum("srd,jde->jsre", norm_a_low, full_in[0], preferred_element_type=jnp.float32)
    )
    enc_context, enc_logs = attend(
        enc_qkv[0],
        enc_ids,
        enc_lengths,
        "enc",
        enc_table,
        enc_extent,
        lambda folder, initial: folder(
            initial,
            (
                lax.all_gather(enc_qkv[1], "seq", axis=1, tiled=True),
                lax.all_gather(enc_qkv[2], "seq", axis=1, tiled=True),
            ),
            jnp.int32(0),
        ),
    )
    enc_context_low = rounded(enc_context)
    enc_mid = enc_values + jnp.einsum(
        "srd,de->sre", enc_context_low, full_out[0], preferred_element_type=jnp.float32
    )
    enc_last, enc_ffn_kept = feed_forward(
        enc_mid, gain_rows[1], full_hidden_in[0], full_hidden_out[0]
    )
    memory = rms_norm(enc_last, gain_rows[2])
    memory_low = rounded(memory)
    dec_values = dec_input.astype(jnp.float32)
    norm_b_low = rounded(rms_norm(dec_values, gain_rows[3]))
    dec_qkv = rounded(
        jnp.einsum("srd,jde->jsre", norm_b_low, full_in[1], preferred_element_type=jnp.float32)
    )
    dec_context, dec_logs = attend(
        dec_qkv[0],
        dec_ids,
        dec_lengths,
        "dec",
        dec_table,
        dec_extent,
        lambda folder, initial: folder(
            initial,
            (
                lax.all_gather(dec_qkv[1], "seq", axis=1, tiled=True),
                lax.all_gather(dec_qkv[2], "seq", axis=1, tiled=True),
            ),
            jnp.int32(0),
        ),
    )
    dec_context_low = rounded(dec_context)
    dec_mid = dec_values + jnp.einsum(
        "srd,de->sre", dec_context_low, full_out[1], preferred_element_type=jnp.float32
    )
    norm_c_low = rounded(rms_norm(dec_mid, gain_rows[4]))
    cross_query = rounded(
        jnp.einsum("srd,de->sre", norm_c_low, full_in[2, 0], preferred_element_type=jnp.float32)
    )
    cross_pair = rounded(
        jnp.einsum("srd,jde->jsre", memory_low, full_in[2, 1:], preferred_element_type=jnp.float32)
    )
    cross_context, cross_logs = attend(
        cross_query,
        dec_ids,
        enc_lengths,
        "cross",
        None,
        0,
        lambda folder, initial: folder(
            initial,
            (
                lax.all_gather(cross_pair[0], "seq", axis=1, tiled=True),
                lax.all_gather(cross_pair[1], "seq", axis=1, tiled=True),
            ),
            jnp.int32(0),
        ),
    )
    cross_low = rounded(cross_context)
    dec_cross = dec_mid + jnp.einsum(
        "srd,de->sre", cross_low, full_out[2], preferred_element_type=jnp.float32
    )
    dec_last, dec_ffn_kept = feed_forward(
        dec_cross, gain_rows[5], full_hidden_in[1], full_hidden_out[1]
    )
    dec_final = rms_norm(dec_last, gain_rows[6])
    grad_dec_last, grad_gain_six = rms_back(
        dec_last, gain_rows[6], dec_cotangent.astype(jnp.float32)
    )
    grad_dec_cross, grad_gain_five, grad_hin_one, grad_hout_one = feed_back(
        dec_cross, gain_rows[5], full_hidden_in[1], full_hidden_out[1], dec_ffn_kept, grad_dec_last
    )
    upstream_low = rounded(grad_dec_cross)
    grad_out_two = jnp.einsum(
        "srd,sre->de", cross_low, upstream_low, preferred_element_type=jnp.float32
    )
    grad_cross_context = rounded(
        jnp.einsum("sre,de->srd", upstream_low, full_out[2], preferred_element_type=jnp.float32)
    )
    cross_dots = row_products(grad_cross_context, cross_context)
    cross_grad_query, cross_grad_keys, cross_grad_values, _ = attend_back(
        cross_query,
        cross_logs,
        cross_dots,
        grad_cross_context,
        dec_ids,
        enc_lengths,
        "cross",
        None,
        0,
        lambda folder, initial: folder(
            initial,
            (
                lax.all_gather(cross_pair[0], "seq", axis=1, tiled=True),
                lax.all_gather(cross_pair[1], "seq", axis=1, tiled=True),
            ),
            jnp.int32(0),
        ),
    )
    cross_query_low = rounded(cross_grad_query)
    grad_query_two = jnp.einsum(
        "srd,sre->de", norm_c_low, cross_query_low, preferred_element_type=jnp.float32
    )
    grad_norm_c = jnp.einsum(
        "sre,de->srd", cross_query_low, full_in[2, 0], preferred_element_type=jnp.float32
    )
    grad_mid_part, grad_gain_four = rms_back(dec_mid, gain_rows[4], grad_norm_c)
    grad_dec_mid = grad_dec_cross + grad_mid_part
    upstream_low = rounded(grad_dec_mid)
    grad_out_one = jnp.einsum(
        "srd,sre->de", dec_context_low, upstream_low, preferred_element_type=jnp.float32
    )
    grad_dec_context = rounded(
        jnp.einsum("sre,de->srd", upstream_low, full_out[1], preferred_element_type=jnp.float32)
    )
    dec_dots = row_products(grad_dec_context, dec_context)
    dec_grad_query, dec_grad_keys, dec_grad_values, grad_dec_bias = attend_back(
        dec_qkv[0],
        dec_logs,
        dec_dots,
        grad_dec_context,
        dec_ids,
        dec_lengths,
        "dec",
        dec_table,
        dec_extent,
        lambda folder, initial: folder(
            initial,
            (
                lax.all_gather(dec_qkv[1], "seq", axis=1, tiled=True),
                lax.all_gather(dec_qkv[2], "seq", axis=1, tiled=True),
            ),
            jnp.int32(0),
        ),
    )
    cross_key_grad, cross_value_grad = owned_key_grads(
        cross_pair[0],
        cross_pair[1],
        enc_ids,
        enc_lengths,
        "cross",
        None,
        0,
        lambda folder, initial: folder(
            initial,
            (
                lax.all_gather(cross_query, "seq", axis=1, tiled=True),
                lax.all_gather(grad_cross_context, "seq", axis=1, tiled=True),
                lax.all_gather(
                    rows_first(cross_logs).astype(jnp.bfloat16), "seq", axis=1, tiled=True
                ).astype(jnp.float32),
                lax.all_gather(
                    rows_first(cross_dots).astype(jnp.bfloat16), "seq", axis=1, tiled=True
                ).astype(jnp.float32),
            ),
            jnp.int32(0),
        ),
    )
    dec_key_grad, dec_value_grad = owned_key_grads(
        dec_qkv[1],
        dec_qkv[2],
        dec_ids,
        dec_lengths,
        "dec",
        dec_table,
        dec_extent,
        lambda folder, initial: folder(
            initial,
            (
                lax.all_gather(dec_qkv[0], "seq", axis=1, tiled=True),
                lax.all_gather(grad_dec_context, "seq", axis=1, tiled=True),
                lax.all_gather(
                    rows_first(dec_logs).astype(jnp.bfloat16), "seq", axis=1, tiled=True
                ).astype(jnp.float32),
                lax.all_gather(
                    rows_first(dec_dots).astype(jnp.bfloat16), "seq", axis=1, tiled=True
                ).astype(jnp.float32),
            ),
            jnp.int32(0),
        ),
    )
    pair_grads = rounded(jnp.stack([cross_key_grad, cross_value_grad]))
    grad_pair_two = jnp.einsum(
        "srd,jsre->jde", memory_low, pair_grads, preferred_element_type=jnp.float32
    )
    grad_memory = jnp.einsum(
        "jsre,jde->srd", pair_grads, full_in[2, 1:], preferred_element_type=jnp.float32
    )
    dec_grads = rounded(jnp.stack([dec_grad_query, dec_key_grad, dec_value_grad]))
    grad_in_one = jnp.einsum(
        "srd,jsre->jde", norm_b_low, dec_grads, preferred_element_type=jnp.float32
    )
    grad_norm_b = jnp.einsum(
        "jsre,jde->srd", dec_grads, full_in[1], preferred_element_type=jnp.float32
    )
    grad_dec_part, grad_gain_three = rms_back(dec_values, gain_rows[3], grad_norm_b)
    grad_dec_input = grad_dec_mid + grad_dec_part
    grad_memory_total = enc_cotangent.astype(jnp.float32) + grad_memory
    grad_enc_last, grad_gain_two = rms_back(enc_last, gain_rows[2], grad_memory_total)
    grad_enc_mid, grad_gain_one, grad_hin_zero, grad_hout_zero = feed_back(
        enc_mid, gain_rows[1], full_hidden_in[0], full_hidden_out[0], enc_ffn_kept, grad_enc_last
    )
    upstream_low = rounded(grad_enc_mid)
    grad_out_zero = jnp.einsum(
        "srd,sre->de", enc_context_low, upstream_low, preferred_element_type=jnp.float32
    )
    grad_enc_context = rounded(
        jnp.einsum("sre,de->srd", upstream_low, full_out[0], preferred_element_type=jnp.float32)
    )
    enc_dots = row_products(grad_enc_context, enc_context)
    enc_grad_query, enc_grad_keys, enc_grad_values, grad_enc_bias = attend_back(
        enc_qkv[0],
        enc_logs,
        enc_dots,
        grad_enc_context,
        enc_ids,
        enc_lengths,
        "enc",
        enc_table,
        enc_extent,
        lambda folder, initial: folder(
            initial,
            (
                lax.all_gather(enc_qkv[1], "seq", axis=1, tiled=True),
                lax.all_gather(enc_qkv[2], "seq", axis=1, tiled=True),
            ),
            jnp.int32(0),
        ),
    )
    enc_key_grad, enc_value_grad = owned_key_grads(
        enc_qkv[1],
        enc_qkv[2],
        enc_ids,
        enc_lengths,
        "enc",
        enc_table,
        enc_extent,
        lambda folder, initial: folder(
            initial,
            (
                lax.all_gather(enc_qkv[0], "seq", axis=1, tiled=True),
                lax.all_gather(grad_enc_context, "seq", axis=1, tiled=True),
                lax.all_gather(
                    rows_first(enc_logs).astype(jnp.bfloat16), "seq", axis=1, tiled=True
                ).astype(jnp.float32),
                lax.all_gather(
                    rows_first(enc_dots).astype(jnp.bfloat16), "seq", axis=1, tiled=True
                ).astype(jnp.float32),
            ),
            jnp.int32(0),
        ),
    )
    enc_grads = rounded(jnp.stack([enc_grad_query, enc_key_grad, enc_value_grad]))
    grad_in_zero = jnp.einsum(
        "srd,jsre->jde", norm_a_low, enc_grads, preferred_element_type=jnp.float32
    )
    grad_norm_a = jnp.einsum(
        "jsre,jde->srd", enc_grads, full_in[0], preferred_element_type=jnp.float32
    )
    grad_enc_part, grad_gain_zero = rms_back(enc_values, gain_rows[0], grad_norm_a)
    grad_enc_input = grad_enc_mid + grad_enc_part
    grad_cross_in = jnp.concatenate([grad_query_two[None], grad_pair_two], axis=0)
    grad_attention_in = jnp.stack([grad_in_zero, grad_in_one, grad_cross_in])
    grad_attention_out = jnp.stack([grad_out_zero, grad_out_one, grad_out_two])
    grad_hidden_in = jnp.stack([grad_hin_zero, grad_hin_one])
    grad_hidden_out = jnp.stack([grad_hout_zero, grad_hout_one])
    grad_gains = jnp.stack(
        [
            grad_gain_zero,
            grad_gain_one,
            grad_gain_two,
            grad_gain_three,
            grad_gain_four,
            grad_gain_five,
            grad_gain_six,
        ]
    )
    shard_in, shard_out, shard_hin, shard_hout, shard_gains = (
        lax.psum_scatter(grad_attention_in, ("dp", "seq"), scatter_dimension=2, tiled=True),
        lax.psum_scatter(grad_attention_out, ("dp", "seq"), scatter_dimension=1, tiled=True),
        lax.psum_scatter(grad_hidden_in, ("dp", "seq"), scatter_dimension=2, tiled=True),
        lax.psum_scatter(grad_hidden_out, ("dp", "seq"), scatter_dimension=1, tiled=True),
        lax.psum_scatter(grad_gains, ("dp", "seq"), scatter_dimension=1, tiled=True),
    )
    bucket_count = position_bias.shape[1]
    grad_position = jnp.stack(
        [
            bucket_grad(enc_buckets, grad_enc_bias, bucket_count),
            bucket_grad(dec_buckets, grad_dec_bias, bucket_count),
        ]
    )
    squares_in = shard_in * shard_in
    squares_out = shard_out * shard_out
    squares_hin = shard_hin * shard_hin
    squares_hout = shard_hout * shard_hout
    col_in, col_out, col_hin, col_hout, grad_position = lax.psum(
        (
            jnp.sum(squares_in, axis=2),
            jnp.sum(squares_out, axis=1),
            jnp.sum(squares_hin, axis=2),
            jnp.sum(squares_hout, axis=1),
            grad_position,
        ),
        ("dp", "seq"),
    )
    return (
        rounded(memory),
        rounded(dec_final),
        grad_enc_input,
        grad_dec_input,
        shard_in,
        shard_out,
        shard_hin,
        shard_hout,
        shard_gains,
        grad_position,
        0.5 * jnp.mean(squares_in, axis=-1),
        0.5 * col_in / D,
        0.5 * jnp.mean(squares_out, axis=-1),
        0.5 * col_out / D,
        0.5 * jnp.mean(squares_hin, axis=-1),
        0.5 * col_hin / D,
        0.5 * jnp.mean(squares_hout, axis=-1),
        0.5 * col_hout / FF,
    )


WAYS = 4
SETS = HEADS // WAYS
WIDTH = SETS * HEAD
VMEM_LIMIT = 16 * 2**20


def swap(values, axis):
    return lax.ppermute(values, axis, [(0, 1), (1, 0)])


def shift_z(values, hops, count):
    return lax.ppermute(values, "dp", [(i, (i + hops) % count) for i in range(count)])


def pair_up(mine, other, bit):
    first = bit == 0
    return jnp.stack([jnp.where(first, mine, other), jnp.where(first, other, mine)])


def pick(values, index, axis=0):
    return lax.dynamic_index_in_dim(values, index, axis, keepdims=False)


class Place:
    def __init__(self, depth):
        self.depth = depth
        self.z, self.y, self.x, self.c = [lax.axis_index(a) for a in ("dp", "y", "x", "c")]
        self.q = 2 * self.x + self.c
        self.index = (self.z * 2 + self.y) * WAYS + self.q


def exchange_over_x(place, pieces):
    halves = pieces.reshape((2, 2) + pieces.shape[1:])
    got = swap(pick(halves, 1 - place.x), "x")
    return pair_up(pick(halves, place.x), got, place.x)


def exchange_over_cores(place, both):
    got = swap(pick(both, 1 - place.c, 1), "c")
    whole = pair_up(pick(both, place.c, 1), got, place.c)
    return jnp.swapaxes(whole, 0, 1).reshape((4,) + both.shape[2:])


def exchange_columns(place, pieces):
    return exchange_over_cores(place, exchange_over_x(place, pieces))


def along_z(place, piece, *earlier):
    depth = place.depth
    held = jnp.zeros((depth,) + piece.shape, piece.dtype)
    arrivals = [shift_z(piece, k, depth) for k in range(1, depth)]
    if earlier:
        arrivals = [after(block, *earlier) for block in arrivals]
    for hops, block in enumerate([piece] + arrivals):
        held = lax.dynamic_update_index_in_dim(held, block, (place.z - hops) % depth, 0)
    return held


def along_y(place, held):
    other = swap(held, "y")
    first = place.y == 0
    pair = [jnp.where(first, held, other), jnp.where(first, other, held)]
    return jnp.stack(pair, axis=1).reshape(-1, held.shape[-1])


def scatter_y(place, parts):
    parts = parts.reshape((place.depth, 2) + parts.shape[1:])
    sent = swap(pick(parts, 1 - place.y, 1), "y")
    return pick(parts, place.y, 1).astype(F32) + sent.astype(F32)


def scatter_z(place, halves):
    depth = place.depth
    low = rounded(halves)
    total = pick(halves, place.z)
    for hops in range(1, depth):
        sent = shift_z(pick(low, (place.z + hops) % depth), hops, depth)
        total = total + sent.astype(F32)
    return total


def after(values, *earlier):
    return lax.optimization_barrier((values,) + earlier)[0]


def turn(values, depth):
    pairs = []
    for d in range(depth):
        for y in range(2):
            for q in range(WAYS):
                pairs.append((d * 8 + y * 4 + q, q * 8 + y * 4 + d))
    return lax.ppermute(values, ("dp", "y", "x", "c"), pairs)


def matmul(a, b):
    return jnp.dot(a, b, preferred_element_type=jnp.float32)


def matmul_nt(a, b):
    return lax.dot_general(a, b, (((1,), (1,)), ((), ())), preferred_element_type=jnp.float32)


def matmul_tn(a, b):
    return lax.dot_general(a, b, (((0,), (0,)), ((), ())), preferred_element_type=jnp.float32)


def call(kernel, name, outs, args, micros, scratch=()):
    whole = pl.BlockSpec(memory_space=pltpu.VMEM)
    arrays = [a[0] if isinstance(a, tuple) else a for a in args]
    specs = [a[1] if isinstance(a, tuple) else whole for a in args]
    late = [k for k, spec in enumerate(specs) if spec is LATE]
    plain = (whole, SCALARS, LATE, ANYWHERE)
    windows = any(all(spec is not p for p in plain) for spec in specs)
    shapes = tuple(jax.ShapeDtypeStruct(s, t) for s, t in outs)
    moved = sum(a.size * a.dtype.itemsize for a in list(arrays) + list(shapes))
    buffers = [pltpu.VMEM(arrays[k].shape, arrays[k].dtype) for k in late]

    def bring_in(*refs):
        if not late:
            return kernel(*refs)
        refs, places, semaphores = list(refs[: -len(late) - 1]), refs[-len(late) - 1 : -1], refs[-1]
        copies = [
            pltpu.make_async_copy(refs[k], place, semaphores.at[n])
            for n, (k, place) in enumerate(zip(late, places))
        ]
        for copy in copies:
            copy.start()
        for copy in copies:
            copy.wait()
        for k, place in zip(late, places):
            refs[k] = place
        return kernel(*refs)

    if late:
        buffers.append(pltpu.SemaphoreType.DMA((len(late),)))
    return pl.pallas_call(
        bring_in,
        grid=(1,) if windows else (),
        out_shape=shapes,
        in_specs=specs,
        out_specs=(whole,) * len(shapes),
        scratch_shapes=list(scratch) + buffers,
        compiler_params=pltpu.CompilerParams(vmem_limit_bytes=VMEM_LIMIT),
        cost_estimate=pl.CostEstimate(
            flops=int(micros * 1e7), bytes_accessed=moved // 32, transcendentals=0
        ),
        name=name,
    )(*arrays)


LATE = pl.BlockSpec(memory_space=pltpu.HBM)
ANYWHERE = pl.BlockSpec(memory_space=pl.ANY)
SCALARS = pl.BlockSpec(memory_space=pltpu.SMEM)
BF, F32 = jnp.bfloat16, jnp.float32


def column_block(array, index):
    rows, columns = array.shape
    return (array, pl.BlockSpec((rows, 2 * WIDTH), lambda _: (0, index)))


def norm_rows(values, gain):
    return values * lax.rsqrt(jnp.mean(values * values, axis=-1, keepdims=True) + EPSILON) * gain


def norm_back(values, gain, upstream):
    scale = lax.rsqrt(jnp.mean(values * values, axis=-1, keepdims=True) + EPSILON)
    unit = values * scale
    inner = upstream * gain
    grad = scale * (inner - unit * jnp.mean(inner * unit, axis=-1, keepdims=True))
    return grad, jnp.sum(upstream * unit, axis=0, keepdims=True)


def self_kernel(gain, q_at, x_ref, gains_ref, kva_ref, qa_ref, kvb_ref, qb_ref, *outs):
    n_ref, q_ref, kv_ref = outs
    n = norm_rows(x_ref[...].astype(F32), gains_ref[gain : gain + 1, :]).astype(BF)
    n_ref[...] = n
    for e, (kv, q) in enumerate(((kva_ref, qa_ref), (kvb_ref, qb_ref))):
        kv_ref[e] = matmul(n, kv[:, : 2 * WIDTH]).astype(BF)
        q_ref[e] = matmul(n, q[:, q_at : q_at + WIDTH]).astype(BF)


def self_project(x, gains, gain, kv_own, q_own, kv_sib, q_sib, q_at, name):
    rows = x.shape[0]
    return call(
        functools.partial(self_kernel, gain, q_at),
        name,
        [((rows, D), BF), ((2, rows, WIDTH), BF), ((2, rows, 2 * WIDTH), BF)],
        [x, gains, kv_own, q_own, kv_sib, q_sib],
        2.5,
    )


def memory_kernel(res_ref, part_ref, got_ref, gains_ref, kva_ref, kvb_ref, *outs):
    last_ref, low_ref, kv_ref = outs
    last = res_ref[...].astype(F32) + part_ref[...] + got_ref[...].astype(F32)
    last_ref[...] = last
    low = norm_rows(last, gains_ref[2:3, :]).astype(BF)
    low_ref[...] = low
    for e, kv in enumerate((kva_ref, kvb_ref)):
        kv_ref[e] = matmul(low, kv[...]).astype(BF)


def cross_kernel(q_at, res_ref, part_ref, got_ref, gains_ref, qa_ref, qb_ref, *outs):
    mid_ref, low_ref, q_ref = outs
    mid = res_ref[...].astype(F32) + part_ref[...] + got_ref[...].astype(F32)
    mid_ref[...] = mid
    low = norm_rows(mid, gains_ref[4:5, :]).astype(BF)
    low_ref[...] = low
    for e, q in enumerate((qa_ref, qb_ref)):
        q_ref[e] = matmul(low, q[:, q_at : q_at + WIDTH]).astype(BF)


def lay_out_keys(core, kv_ref, got_ref, keys):
    block = kv_ref.shape[1] // 4
    for e in range(2):
        for k in range(4):
            at = pl.multiple_of(block * (2 * k + core), block)
            keys[e, pl.ds(at, block), :] = kv_ref[e, k * block : (k + 1) * block, :]
            at = pl.multiple_of(block * (2 * k + 1 - core), block)
            keys[e, pl.ds(at, block), :] = got_ref[1 - e, k * block : (k + 1) * block, :]


def attend_kernel(causal, biased, *refs):
    if biased:
        scalars, q_ref, kv_ref, got_ref, table_ref, oa_ref, ob_ref = refs[:7]
    else:
        scalars, q_ref, kv_ref, got_ref, oa_ref, ob_ref = refs[:6]
    ctx_ref, p_ref, part_ref, low_ref, keys = refs[-5:]
    core, length = scalars[0], scalars[1]
    lay_out_keys(core, kv_ref, got_ref, keys)
    rows, extent = q_ref.shape[1], keys.shape[1]
    block = rows // 4
    cols = lax.broadcasted_iota(jnp.int32, (block, extent), 1)
    ids = lax.broadcasted_iota(jnp.int32, (block, extent), 0)
    total = None
    for e in range(2):
        for h in range(SETS):
            at = slice(h * HEAD, (h + 1) * HEAD)
            k = keys[e, :, at]
            v = keys[e, :, WIDTH + h * HEAD : WIDTH + (h + 1) * HEAD]
            scores = matmul_nt(q_ref[e, :, at], k)
            if biased:
                line = table_ref[e * SETS + h : e * SETS + h + 1, :]
                skew = pltpu.roll(
                    jnp.broadcast_to(line, (block, 2 * extent)),
                    2 * extent - (block - 1),
                    1,
                    stride=1,
                    stride_axis=0,
                )
            for i in range(4):
                here = slice(i * block, (i + 1) * block)
                s = scores[here] * (HEAD**-0.5)
                if biased:
                    begin = (3 - i) * 2 * block
                    s = s + skew[:, begin : begin + extent]
                visible = cols < length
                if causal:
                    visible = visible & (cols <= ids + (i * 2 * block + core * block))
                s = jnp.where(visible, s, NEGATIVE)
                weights = jnp.exp(s - jnp.max(s, axis=-1, keepdims=True))
                weights = weights * (1.0 / jnp.sum(weights, axis=-1, keepdims=True))
                p_ref[e * SETS + h, here, :] = weights.astype(BF)
            ctx_ref[e, :, at] = matmul(p_ref[e * SETS + h], v)
        term = matmul(ctx_ref[e].astype(BF), (oa_ref, ob_ref)[e][...])
        total = term if total is None else total + term
    part_ref[...] = total
    low_ref[...] = total.astype(BF)


def attend_local(scalars, q, kv, got, table, out_own, out_sib, causal, name):
    rows = q.shape[1]
    extent = 2 * rows
    args = [(scalars, SCALARS), q, kv, got] + ([] if table is None else [table])
    return call(
        functools.partial(attend_kernel, causal, table is not None),
        name,
        [
            ((2, rows, WIDTH), F32),
            ((2 * SETS, rows, extent), BF),
            ((rows, D), F32),
            ((rows, D), BF),
        ],
        args + [out_own, out_sib],
        5.5,
        [pltpu.VMEM((2, extent, 2 * WIDTH), BF)],
    )


def unpack_into(w_ref, columns, down):
    blocks, rows = 8, down.shape[0] // 8
    half, third = rows // 2, down.shape[1] // 3
    step = rows + half
    for b in range(blocks):
        down[b * rows : (b + 1) * rows, : 2 * third] = w_ref[
            b * step : b * step + rows, columns : columns + 2 * third
        ]
        for k in range(2):
            down[b * rows + k * half : b * rows + (k + 1) * half, 2 * third :] = w_ref[
                b * step + rows : (b + 1) * step,
                columns + k * third : columns + (k + 1) * third,
            ]


GELU_A, GELU_B = (2 / math.pi) ** 0.5, 0.044715


def gelu_tanh(gate):
    return jnp.tanh(GELU_A * (gate + GELU_B * gate * gate * gate))


def ffn_kernel(gain, res_ref, part_ref, got_ref, gains_ref, wa_ref, wb_ref, *refs):
    mid_ref, n_ref, gu_ref, hid_ref, out_ref, low_ref, down = refs
    mid = res_ref[...].astype(F32) + part_ref[...] + got_ref[...].astype(F32)
    mid_ref[...] = mid
    n = norm_rows(mid, gains_ref[gain : gain + 1, :]).astype(BF)
    n_ref[...] = n
    units = down.shape[0]
    total = None
    for e, w_ref in enumerate((wa_ref, wb_ref)):
        gu_ref[e] = matmul(n, w_ref[:, : 2 * units])
        gate, up = gu_ref[e, :, :units], gu_ref[e, :, units:]
        hid_ref[e] = (0.5 * gate * (1.0 + gelu_tanh(gate)) * up).astype(BF)
        unpack_into(w_ref, 2 * units, down)
        term = matmul(hid_ref[e], down[...])
        total = term if total is None else total + term
    out_ref[...] = total
    low_ref[...] = total.astype(BF)


def ffn_local(res, part, got, gains, gain, w_own, w_sib, units, name):
    rows = res.shape[0]
    return call(
        functools.partial(ffn_kernel, gain),
        name,
        [
            ((rows, D), F32),
            ((rows, D), BF),
            ((2, rows, 2 * units), F32),
            ((2, rows, units), BF),
            ((rows, D), F32),
            ((rows, D), BF),
        ],
        [res, part, got, gains, w_own, w_sib],
        3.0,
        [pltpu.VMEM((units, D), BF)],
    )


def ffn_back_kernel(decoder, val_ref, part_ref, got_ref, cot_ref, gains_ref, *refs):
    gu_ref, wa_ref, wb_ref = refs[:3]
    down = refs[-1]
    sent = part_ref[...] + got_ref[...].astype(F32)
    if decoder:
        final_ref, g_ref, dgain_ref, low_ref, dgu_ref, out_ref, out_low_ref = refs[3:-1]
        gain = gains_ref[6:7, :]
        values = val_ref[...] + sent
        upstream = cot_ref[...].astype(F32)
        final_ref[...] = norm_rows(values, gain).astype(BF)
    else:
        g_ref, dgain_ref, low_ref, dgu_ref, out_ref, out_low_ref = refs[3:-1]
        gain = gains_ref[2:3, :]
        values = val_ref[...]
        upstream = cot_ref[...].astype(F32) + sent
    grad, dgain_ref[...] = norm_back(values, gain, upstream)
    g_ref[...] = grad
    low = grad.astype(BF)
    low_ref[...] = low
    units = down.shape[0]
    total = None
    for e, w_ref in enumerate((wa_ref, wb_ref)):
        unpack_into(w_ref, 2 * units, down)
        grad_hidden = matmul_nt(low, down[...])
        gate, up = gu_ref[e, :, :units], gu_ref[e, :, units:]
        t = gelu_tanh(gate)
        slope = 0.5 * (1.0 + t) + 0.5 * gate * (1.0 - t * t) * GELU_A * (
            1.0 + 3.0 * GELU_B * gate * gate
        )
        dgu_ref[e, :, :units] = (grad_hidden * up * slope).astype(BF)
        dgu_ref[e, :, units:] = (grad_hidden * (0.5 * gate * (1.0 + t))).astype(BF)
        term = matmul_nt(dgu_ref[e], w_ref[:, : 2 * units])
        total = term if total is None else total + term
    out_ref[...] = total
    out_low_ref[...] = total.astype(BF)


def ffn_back(decoder, values, part, got, cot, gains, gate_up, w_own, w_sib, name):
    rows, units = values.shape[0], gate_up.shape[2] // 2
    outs = [((rows, D), BF)] if decoder else []
    outs += [
        ((rows, D), F32),
        ((1, D), F32),
        ((rows, D), BF),
        ((2, rows, 2 * units), BF),
        ((rows, D), F32),
        ((rows, D), BF),
    ]
    return call(
        functools.partial(ffn_back_kernel, decoder),
        name,
        outs,
        [values, part, got, cot, gains, gate_up, w_own, w_sib],
        4.0,
        [pltpu.VMEM((units, D), BF)],
    )


def ffn_weights_kernel(n_ref, dgu_ref, hid_ref, low_ref, own_ref, sib_ref):
    units = hid_ref.shape[2]
    rows, half, third = units // 8, units // 16, D // 3
    step = rows + half
    for e, out in enumerate((own_ref, sib_ref)):
        out[:, : 2 * units] = matmul_tn(n_ref[...], dgu_ref[e]).astype(BF)
        down = matmul_tn(hid_ref[e], low_ref[...]).astype(BF)
        for b in range(8):
            out[b * step : b * step + rows, 2 * units :] = down[
                b * rows : (b + 1) * rows, : 2 * third
            ]
            for k in range(2):
                out[
                    b * step + rows : (b + 1) * step,
                    2 * units + k * third : 2 * units + (k + 1) * third,
                ] = down[b * rows + k * half : b * rows + (k + 1) * half, 2 * third :]


def ffn_weights(n, dgu, hid, low, name):
    units = hid.shape[2]
    shape = ((D, 2 * units + 2 * D // 3), BF)
    return call(
        ffn_weights_kernel, name, [shape, shape], [n, dgu, hid, low], 1.5
    )


def attend_back_kernel(gain, biased, scalars, up_ref, val_ref, part_ref, got_ref, *refs):
    gains_ref, oa_ref, ob_ref, q_ref, kv_ref, kvgot_ref, p_ref, ctx_ref = refs[:8]
    g_ref, dgain_ref, low_ref, dq_ref, mine_ref, other_ref = refs[8:14]
    keys, dkeys, ds_ref = refs[-3:]
    core = scalars[0]
    grad, dgain_ref[...] = norm_back(
        val_ref[...], gains_ref[gain : gain + 1, :], part_ref[...] + got_ref[...].astype(F32)
    )
    grad = up_ref[...] + grad
    g_ref[...] = grad
    low = grad.astype(BF)
    low_ref[...] = low
    lay_out_keys(core, kv_ref, kvgot_ref, keys)
    rows, extent = q_ref.shape[1], keys.shape[1]
    block = rows // 4
    factor = HEAD**-0.5
    for e in range(2):
        g = matmul_nt(low, (oa_ref, ob_ref)[e][...]).astype(BF)
        products = g.astype(F32) * ctx_ref[e]
        for h in range(SETS):
            at = slice(h * HEAD, (h + 1) * HEAD)
            k = keys[e, :, at]
            v = keys[e, :, WIDTH + h * HEAD : WIDTH + (h + 1) * HEAD]
            dots = jnp.sum(products[:, at], axis=-1, keepdims=True)
            dp = matmul_nt(g[:, at], v)
            sums = [None] * 7
            for i in range(4):
                here = slice(i * block, (i + 1) * block)
                ds = p_ref[e * SETS + h, here, :].astype(F32) * (dp[here] - dots[here])
                if biased:
                    for j in range(4):
                        part = ds[:, j * 2 * block : (j + 1) * 2 * block]
                        slot = 3 - i + j
                        sums[slot] = part if sums[slot] is None else sums[slot] + part
                ds_ref[here, :] = (ds * factor).astype(BF)
            dq_ref[e, :, at] = matmul(ds_ref[...], k).astype(BF)
            dkeys[:, at] = matmul_tn(ds_ref[...], q_ref[e, :, at])
            dkeys[:, WIDTH + h * HEAD : WIDTH + (h + 1) * HEAD] = matmul_tn(
                p_ref[e * SETS + h], g[:, at]
            )
            if biased:
                dtable_ref = refs[14]
                band = jnp.concatenate(sums + [jnp.zeros_like(sums[0])], axis=1)
                ids = lax.broadcasted_iota(jnp.int32, band.shape, 0)
                bit = 1
                while bit < block:
                    moved = pltpu.roll(band, 2 * extent - bit, 1)
                    band = jnp.where((ids & bit) != 0, moved, band)
                    bit *= 2
                line = jnp.sum(band, axis=0, keepdims=True)
                dtable_ref[e * SETS + h : e * SETS + h + 1, :] = pltpu.roll(line, block - 1, 1)
        for k in range(4):
            at = pl.multiple_of(block * (2 * k + core), block)
            mine_ref[e, k * block : (k + 1) * block, :] = dkeys[pl.ds(at, block), :]
            at = pl.multiple_of(block * (2 * k + 1 - core), block)
            other_ref[1 - e, k * block : (k + 1) * block, :] = dkeys[
                pl.ds(at, block), :
            ].astype(BF)


def attend_local_back(gain, biased, scalars, upstream, values, part, got, gains, *rest, name):
    rows, extent = upstream.shape[0], 2 * upstream.shape[0]
    outs = [
        ((rows, D), F32),
        ((1, D), F32),
        ((rows, D), BF),
        ((2, rows, WIDTH), BF),
        ((2, rows, 2 * WIDTH), F32),
        ((2, rows, 2 * WIDTH), BF),
    ]
    if biased:
        outs.append(((2 * SETS, 2 * extent), F32))
    return call(
        functools.partial(attend_back_kernel, gain, biased),
        name,
        outs,
        [(scalars, SCALARS), (upstream, LATE), (values, LATE), part, got, gains]
        + list(rest[:2])
        + [(a, LATE) for a in rest[2:]],
        9.0 if biased else 6.0,
        [
            pltpu.VMEM((2, extent, 2 * WIDTH), BF),
            pltpu.VMEM((extent, 2 * WIDTH), F32),
            pltpu.VMEM((rows, extent), BF),
        ],
    )


def project_back_kernel(split, q_at, dq_ref, mine_ref, got_ref, *refs):
    kva_ref, qa_ref, kvb_ref, qb_ref = refs[:4]
    dkv_ref = refs[4]
    from_keys = from_queries = None
    for e, (kv, q) in enumerate(((kva_ref, qa_ref), (kvb_ref, qb_ref))):
        dkv = (mine_ref[e] + got_ref[e].astype(F32)).astype(BF)
        dkv_ref[e] = dkv
        term = matmul_nt(dkv, kv[:, : 2 * WIDTH])
        from_keys = term if e == 0 else from_keys + term
        term = matmul_nt(dq_ref[e], q[:, q_at : q_at + WIDTH])
        from_queries = term if e == 0 else from_queries + term
    outs = [from_keys, from_queries] if split else [from_keys + from_queries]
    for k, total in enumerate(outs):
        refs[5 + 2 * k][...] = total
        refs[6 + 2 * k][...] = total.astype(BF)


def project_back(split, dq, mine, got, kv_own, q_own, kv_sib, q_sib, q_at, name):
    rows = dq.shape[1]
    outs = [((2, rows, 2 * WIDTH), BF)] + [((rows, D), F32), ((rows, D), BF)] * (1 + split)
    return call(
        functools.partial(project_back_kernel, split, q_at),
        name,
        outs,
        [dq, mine, got, kv_own, q_own, kv_sib, q_sib],
        2.5,
    )


def attend_weights_kernel(count, *refs):
    ins, (own_ref, sib_ref, out_own_ref, out_sib_ref) = refs[:-4], refs[-4:]
    for k in range(count):
        nq_ref, nkv_ref, dq_ref, dkv_ref, ctx_ref, low_ref = ins[6 * k : 6 * k + 6]
        kv_at, q_at = 2 * WIDTH * k, 2 * WIDTH * count + WIDTH * k
        for e, (in_ref, out_ref) in enumerate(((own_ref, out_own_ref), (sib_ref, out_sib_ref))):
            if k == 0 and in_ref.shape[1] > 3 * count * WIDTH:
                in_ref[...] = jnp.zeros_like(in_ref)
            in_ref[:, kv_at : kv_at + 2 * WIDTH] = matmul_tn(nkv_ref[...], dkv_ref[e]).astype(BF)
            in_ref[:, q_at : q_at + WIDTH] = matmul_tn(nq_ref[...], dq_ref[e]).astype(BF)
            out_ref[k] = matmul_tn(ctx_ref[e].astype(BF), low_ref[...]).astype(BF)


def attend_weights(name, *attentions):
    count, rows = len(attentions), attentions[0][0].shape[0]
    inner, outer = ((D, -(-3 * count * WIDTH // 128) * 128), BF), ((count, WIDTH, D), BF)
    own, sib, out_own, out_sib = call(
        functools.partial(attend_weights_kernel, count),
        name,
        [inner, inner, outer, outer],
        [a for attention in attentions for a in attention],
        1.0 * count,
    )
    return own, out_own, sib, out_sib


IN_ORDER = (8, 6, 7, 4, 0, 1, 5, 2, 3)


def sums_kernel(own, late_ref, dec_ref, self_ref, out_ref):
    inner, third, half = 6 * WIDTH, D // 3, D // 2
    width = dec_ref.shape[1]
    wide, rows = width - 2 * third, dec_ref.shape[0] * 2 // 3
    out_ref[...] = jnp.zeros_like(out_ref)

    def squares(values, rows_in_all):
        values = values.astype(F32)
        return values * values * (0.5 / rows_in_all)

    def line(values):
        return jnp.sum(values, axis=0, keepdims=True)

    def put(at, values):
        for k in range(0, values.shape[1], 128):
            size = min(128, values.shape[1] - k)
            out_ref[at + k // 128 : at + k // 128 + 1, :size] = values[:, k : k + size]

    put(0, line(squares(late_ref[:, inner : inner + wide], D)))
    put(wide // 128, line(squares(dec_ref[:, :wide], D)))
    at = 2 * wide // 128
    put(at, line(squares(late_ref[:, :inner], D)))
    put(at + inner // 128, line(squares(self_ref[:, third : third + 3 * WIDTH], D)))
    at = 30
    for ref, begin in ((late_ref, inner), (dec_ref, 0)):
        down = squares(ref[:, begin + wide : begin + width], FF)
        put(at, line(down[:rows]))
        put(at + 2 * third // 128, line(down[rows:, :third]) + line(down[rows:, third:]))
        at += D // 128
    outer = squares(self_ref[:, :third], D)
    for k in range(3):
        put(at + k * third // 128, line(outer[k * own : (k + 1) * own]))
    at += D // 128
    outer = squares(late_ref[:, width + inner :], D)
    for k in range(2):
        for side in range(2):
            begin = (2 * side + k) * own
            put(at + side * half // 128, line(outer[begin : begin + own]))
        at += D // 128


def hold_kernel(values_ref, earlier_ref, out_ref):
    out_ref[...] = values_ref[...]


def half_mean_rows(values):
    ones = jnp.full((8, values.shape[1]), 0.5 / values.shape[1], F32)
    sums = lax.dot_general(
        ones,
        values * values,
        (((1,), (1,)), ((), ())),
        precision=HIGHEST,
        preferred_element_type=F32,
    )
    return sums[:1]


def shards_kernel(ff_own, columns_ref, early_ref, turned_ref, late_ref, dec_ref, *outs):
    in_ref, out_ref, hin_ref, hout_ref, row_in_ref, row_out_ref, row_hin_ref, row_hout_ref = outs
    third = D // 3
    width = dec_ref.shape[1]
    wide = width - 2 * third
    units = wide // 2
    for k, at in enumerate(IN_ORDER):
        ref, at = (columns_ref, at * WIDTH) if at < 6 else (early_ref, wide + (at - 6) * WIDTH)
        for q in range(WAYS):
            piece = ref[q, :, at : at + WIDTH]
            in_ref[k // 3, k % 3, :, q * WIDTH : (q + 1) * WIDTH] = piece
        row_in_ref[k : k + 1, :] = half_mean_rows(in_ref[k // 3, k % 3])
    out_ref[...] = turned_ref[...]
    for k in range(3):
        row_out_ref[k : k + 1, :] = half_mean_rows(turned_ref[k])
    for layer in range(2):
        ref, begin = (columns_ref, 6 * WIDTH) if layer == 0 else (early_ref, 0)
        for j in range(2):
            for k in range(units // ff_own):
                first = begin + j * units + k * ff_own
                for q in range(WAYS):
                    at = (WAYS * k + q) * ff_own
                    piece = ref[q, :, first : first + ff_own]
                    hin_ref[layer, j, :, at : at + ff_own] = piece
            row_hin_ref[2 * layer + j : 2 * layer + j + 1, :] = half_mean_rows(hin_ref[layer, j])
    for layer, (ref, begin) in enumerate(((late_ref, 6 * WIDTH), (dec_ref, 0))):
        down = ref[:, begin + wide : begin + width].astype(F32)
        hout_ref[layer, :, : 2 * third] = down[:ff_own]
        half = ff_own // 2
        hout_ref[layer, :half, 2 * third :] = down[ff_own:, :third]
        hout_ref[layer, half:, 2 * third :] = down[ff_own:, third:]
        row_hout_ref[layer : layer + 1, :] = half_mean_rows(hout_ref[layer])


def input_kernel(gain, up_ref, x_ref, part_ref, got_ref, gains_ref, out_ref, dgain_ref):
    grad, dgain_ref[...] = norm_back(
        x_ref[...].astype(F32),
        gains_ref[gain : gain + 1, :],
        part_ref[...] + got_ref[...].astype(F32),
    )
    out_ref[...] = up_ref[...] + grad


def input_back(gain, upstream, x, part, got, gains, name):
    return call(
        functools.partial(input_kernel, gain),
        name,
        [(upstream.shape, F32), ((1, D), F32)],
        [upstream, x, part, got, gains],
        1.5,
    )


def gather_own_rows(place, mine, other_seq):
    near = pair_up(mine, swap(other_seq, "y"), place.y)
    far = pair_up(near, swap(near, "x"), place.x)
    far = far.transpose(2, 1, 0, 3, 4)
    return far.reshape(far.shape[0], -1, far.shape[4])


def give_back(place, half):
    blocks = half.reshape(2, 2, -1, half.shape[1])
    blocks = pick(blocks, place.x, 1)
    other = swap(pick(blocks, 1 - place.y), "y")
    return pair_up(pick(blocks, place.y), other, place.y)


def sum_everywhere(place, values):
    depth = place.depth
    for axis in ("c", "x", "y"):
        values = values + swap(values, axis)
    return values + sum(shift_z(values, k, depth) for k in range(1, depth))


def pack_down(rows):
    half, third = rows.shape[-2] // 2, rows.shape[-1] // 3
    last = rows[..., 2 * third :]
    last = jnp.concatenate([last[..., :half, :], last[..., half:, :]], axis=-1)
    return jnp.concatenate([rows[..., : 2 * third], last], axis=-2)


def unpack_down(packed):
    half, third = packed.shape[-2] // 3, packed.shape[-1] // 2
    last = packed[..., 2 * half :, :]
    last = jnp.concatenate([last[..., :third], last[..., third:]], axis=-2)
    return jnp.concatenate([packed[..., : 2 * half, :], last], axis=-1)


def pack_out(pair):
    rows = pair.reshape(pair.shape[:-3] + (-1, pair.shape[-1]))
    half = rows.shape[-1] // 2
    return jnp.concatenate([rows[..., :half], rows[..., half:]], axis=-2)


def unpack_out_piece(packed):
    half = packed.shape[-2] // 2
    rows = jnp.concatenate([packed[..., :half, :], packed[..., half:, :]], axis=-1)
    return rows.reshape(rows.shape[:-2] + (2, half // 2, rows.shape[-1]))


def unpack_out(packed, depth):
    pair = unpack_out_piece(packed)
    pair = pair.reshape((depth, 2) + pair.shape[1:])
    pair = pair.transpose(2, 1, 0, 3, 4)
    return pair.reshape(2, -1, pair.shape[-1])


def turned_parts(grads, depth):
    parts = grads.reshape(2, depth, -1, grads.shape[1]).transpose(1, 0, 2, 3)
    return parts.reshape(2 * depth, -1, grads.shape[1])


def grouped(
    depth,
    enc_input,
    dec_input,
    enc_lengths,
    dec_lengths,
    enc_buckets,
    dec_buckets,
    attention_in,
    attention_out,
    hidden_in,
    hidden_out,
    norm_gains,
    position_bias,
    enc_cotangent,
    dec_cotangent,
):
    place = Place(depth)
    y, q = place.y, place.q
    block = enc_input.shape[1]
    length = block * 8
    own = attention_in.shape[2]
    ff_own = hidden_out.shape[1]
    units = ff_own * 2 * depth
    group = WAYS * own

    pieces = attention_in.reshape(3, 3, own, WAYS, WIDTH).transpose(3, 0, 1, 2, 4)
    queries, keys, values = pieces[:, :, 0], pieces[:, :, 1], pieces[:, :, 2]
    gain_piece = jnp.pad(norm_gains.T, ((0, 0), (0, 64 - norm_gains.shape[0])))
    gain_piece = jnp.broadcast_to(gain_piece[None], (WAYS,) + gain_piece.shape)
    turned = turn(attention_out, depth)
    hidden_pieces = hidden_in.reshape(2, 2, own, 2 * depth, WAYS, ff_own)
    hidden_pieces = hidden_pieces.transpose(4, 0, 2, 1, 3, 5).reshape(WAYS, 2, own, 2 * units)
    blocks_in = [keys[:, 0], values[:, 0], queries[:, 0], gain_piece]
    blocks_in += [keys[:, 1], values[:, 1], keys[:, 2], values[:, 2], queries[:, 1], queries[:, 2]]
    blocks_in += [hidden_pieces[:, 0]]
    everything = exchange_columns(place, jnp.concatenate(blocks_in, axis=2)).reshape(group, -1)
    cuts = [3 * WIDTH + 64, 9 * WIDTH + 64]
    enc_piece, rest, ffn_enc = jnp.split(everything, cuts, axis=1)
    ffn_dec = exchange_columns(place, after(hidden_pieces[:, 1], ffn_enc)).reshape(group, -1)
    third = turned[0].reshape(own, 3, D // 3).transpose(1, 0, 2).reshape(3 * own, D // 3)
    third = jnp.pad(third, ((0, group - 3 * own), (0, 0)))
    enc_piece = jnp.concatenate([enc_piece, third], axis=1)
    rest = jnp.concatenate([rest, pack_out(turned[1:])], axis=1)
    ffn_enc = jnp.concatenate([ffn_enc, pack_down(hidden_out[0])], axis=1)
    ffn_dec = jnp.concatenate([ffn_dec, pack_down(hidden_out[1])], axis=1)

    line = along_z(place, enc_piece)
    w_enc = along_y(place, line)
    w_enc_sib = swap(w_enc, "c")

    def out_rows(whole):
        rows = whole[:, 3 * WIDTH + 64 :].reshape(depth, 2, group, D // 3)[:, :, : 3 * own]
        rows = rows.reshape(depth, 2, 3, own, D // 3).transpose(1, 0, 3, 2, 4)
        return rows.reshape(WIDTH, D)

    def gather(piece):
        return lax.all_gather(piece, ("dp", "y"), axis=0, tiled=True)

    first = gather(jnp.concatenate([rest, ffn_enc], axis=1))
    out_enc, out_enc_sib = out_rows(w_enc), out_rows(w_enc_sib)
    gains = w_enc[:, 3 * WIDTH : 3 * WIDTH + norm_gains.shape[0]].astype(F32).T

    w_self = [w_enc, w_enc, w_enc_sib, w_enc_sib]

    def own_rows(*arrays):
        mine = jnp.stack([pick(a, y) for a in arrays])
        other = jnp.stack([pick(a, 1 - y) for a in arrays])
        return gather_own_rows(place, mine, other)

    enc_rows, dec_rows, *cots = own_rows(enc_input, dec_input, dec_cotangent, enc_cotangent)
    enc_scalars = jnp.stack([place.c, pick(enc_lengths, y)]).astype(jnp.int32)
    dec_scalars = jnp.stack([place.c, pick(dec_lengths, y)]).astype(jnp.int32)

    def head_rows(table):
        mine = lax.dynamic_slice_in_dim(table, q * SETS, SETS, 0)
        theirs = lax.dynamic_slice_in_dim(table, (q + 1 - 2 * place.c) * SETS, SETS, 0)
        table = jnp.concatenate([mine, theirs])
        table = jnp.pad(table, ((0, 0), (0, block)))
        return lax.dynamic_slice_in_dim(table, block * (1 - place.c), 2 * length, 1)

    enc_table = offset_table(enc_buckets, position_bias[0])
    enc_table = head_rows(jnp.pad(enc_table, ((0, 0), (0, 1))))
    dec_table = offset_table(dec_buckets, position_bias[1])
    dec_table = jnp.concatenate(
        [dec_table[:, ::-1], jnp.broadcast_to(dec_table[:, :1], (HEADS, length))], axis=1
    )
    dec_table = head_rows(dec_table)

    n_a, q_enc, kv_enc = self_project(enc_rows, gains, 0, *w_self, 2 * WIDTH, "enc_project")
    kv_enc_got = swap(kv_enc, "c")
    ctx_enc, p_enc, part, low = attend_local(
        enc_scalars, q_enc, kv_enc, kv_enc_got, enc_table, out_enc, out_enc_sib, False, "enc_attend"
    )
    low_enc, part_enc = low, part
    ffn_dec = gather(after(ffn_dec, low_enc))
    got_enc = swap(low_enc, "x")
    first = after(first, got_enc)
    rest, ffn_enc = first[:, : ffn_enc.shape[1]], first[:, ffn_enc.shape[1] :]
    rest_sib, ffn_enc_sib = swap(rest, "c"), swap(ffn_enc, "c")
    out_rest = unpack_out(rest[:, 6 * WIDTH :].reshape(2 * depth, group, -1), depth)
    out_rest_sib = unpack_out(rest_sib[:, 6 * WIDTH :].reshape(2 * depth, group, -1), depth)
    w_dec = [column_block(w, k) for w in (rest, rest_sib) for k in (0, 2)]
    w_cross = [column_block(w, k) for w in (rest, rest_sib) for k in (1, 2)]
    out_dec, out_cross = [[(w, pl.BlockSpec((None, WIDTH, D), f)) for w in (out_rest, out_rest_sib)]
        for f in (lambda _: (0, 0, 0), lambda _: (1, 0, 0))]

    n_b, q_dec, kv_dec = self_project(dec_rows, gains, 3, *w_dec, 0, "dec_project")
    kv_dec_got = swap(kv_dec, "c")
    ctx_dec, p_dec, part_dec, low_dec = attend_local(
        dec_scalars, q_dec, kv_dec, kv_dec_got, dec_table, *out_dec, True, "dec_attend"
    )

    enc_mid, n_1, gu_enc, hid_enc, part, low = ffn_local(
        enc_rows, part_enc, after(got_enc, low_dec), gains, 1, ffn_enc, ffn_enc_sib, units, "enc_ffn"
    )
    rows = enc_rows.shape[0]
    dec_mid, n_c, q_cross = call(
        functools.partial(cross_kernel, WIDTH),
        "cross_project",
        [((rows, D), F32), ((rows, D), BF), ((2, rows, WIDTH), BF)],
        [dec_rows, part_dec, swap(low_dec, "x"), gains, w_cross[1], w_cross[3]],
        2.0,
    )
    enc_last, memory_low, kv_cross = call(
        memory_kernel,
        "memory",
        [((rows, D), F32), ((rows, D), BF), ((2, rows, 2 * WIDTH), BF)],
        [enc_mid, part, after(swap(low, "x"), q_cross), gains, w_cross[0], w_cross[2]],
        2.0,
    )
    kv_cross_got = swap(kv_cross, "c")

    ctx_cross, p_cross, part, low = attend_local(
        enc_scalars, q_cross, kv_cross, kv_cross_got, None, *out_cross, False, "cross_attend"
    )
    ffn_dec = after(ffn_dec, low)
    ffn_dec_sib = swap(ffn_dec, "c")
    dec_cross, n_5, gu_dec, hid_dec, part, low = ffn_local(
        dec_mid, part, swap(low, "x"), gains, 5, ffn_dec, ffn_dec_sib, units, "dec_ffn"
    )

    def both(own_grads, sib_grads):
        return (own_grads.astype(F32) + swap(sib_grads, "c").astype(F32)).astype(BF)

    def blocks(grads):
        return grads.reshape(2 * depth, -1, grads.shape[1])

    def scatter(grads):
        return lax.psum_scatter(grads, ("dp", "y"), scatter_dimension=0, tiled=False)

    dec_final, g, gg6, low_d, dgu_dec, part, low = ffn_back(
        True, dec_cross, part, swap(low, "x"), cots[0], gains, gu_dec, ffn_dec, ffn_dec_sib, "dec_ffn_back"
    )
    d_ffn_dec = ffn_weights(n_5, dgu_dec, hid_dec, low_d, "dec_ffn_weights")
    d_ffn_dec = both(*d_ffn_dec)
    got_f = after(swap(low, "x"), d_ffn_dec)
    got = got_f
    g, gg5, low_x, dq_cross, mine, other = attend_local_back(
        5,
        False,
        enc_scalars,
        g,
        dec_cross,
        part,
        got,
        gains,
        *out_cross,
        q_cross,
        kv_cross,
        kv_cross_got,
        p_cross,
        ctx_cross,
        name="cross_attend_back",
    )
    got = swap(other, "c")
    d_ffn_dec = scatter(after(blocks(d_ffn_dec), got_f))
    dkv_cross, part_m, low_m, part_c, low_c = project_back(
        True, dq_cross, mine, got, *w_cross, WIDTH, "cross_project_back"
    )
    got_c = swap(low_c, "x")
    got_m = after(swap(low_m, "x"), got_c)
    g_last, gg2, low_e, dgu_enc, part, part_low = ffn_back(
        False, enc_last, part_m, got_m, cots[1], gains, gu_enc, ffn_enc, ffn_enc_sib, "enc_ffn_back"
    )
    d_ffn_enc = ffn_weights(n_1, dgu_enc, hid_enc, low_e, "enc_ffn_weights")
    got_e = swap(part_low, "x")
    got_c = after(got_c, *d_ffn_enc)
    d_ffn_enc = both(*d_ffn_enc)
    g_dec, gg4, low_b, dq_dec, mine, other, d_table_dec = attend_local_back(
        4,
        True,
        dec_scalars,
        g,
        dec_mid,
        part_c,
        got_c,
        gains,
        *out_dec,
        q_dec,
        kv_dec,
        kv_dec_got,
        p_dec,
        ctx_dec,
        name="dec_attend_back",
    )
    got_e = after(got_e, dq_dec)
    dec_other = swap(other, "c")
    dec_mine = mine
    g_enc, gg1, low_a, dq_enc, mine, other, d_table_enc = attend_local_back(
        1,
        True,
        enc_scalars,
        g_last,
        enc_mid,
        part,
        got_e,
        gains,
        out_enc,
        out_enc_sib,
        q_enc,
        kv_enc,
        kv_enc_got,
        p_enc,
        ctx_enc,
        name="enc_attend_back",
    )
    dkv_dec, part_d, low = project_back(
        False, dq_dec, dec_mine, dec_other, *w_dec, 0, "dec_project_back"
    )
    got_d = swap(low, "x")
    d_in, d_out, d_in_sib, d_out_sib = attend_weights(
        "attend_weights",
        (n_b, n_b, dq_dec, dkv_dec, ctx_dec, low_b),
        (n_c, memory_low, dq_cross, dkv_cross, ctx_cross, low_x),
    )
    d_out = both(d_out, d_out_sib)
    d_out = jnp.stack([turned_parts(d_out[k], depth) for k in range(2)], 1)
    d_in = d_in.astype(F32) + after(swap(d_in_sib, "c"), d_ffn_dec).astype(F32)
    late = [blocks(rounded(d_in)), blocks(d_ffn_enc), pack_out(d_out)]
    late = scatter(jnp.concatenate(late, axis=2))
    got = after(swap(other, "c"), dkv_dec)
    dkv_enc, part, low = project_back(
        False, dq_enc, mine, got, *w_self, 2 * WIDTH, "enc_project_back"
    )
    d_in, d_out, d_in_sib, d_out_sib = attend_weights(
        "enc_attend_weights", (n_a, n_a, dq_enc, dkv_enc, ctx_enc, low_a)
    )
    got = after(swap(low, "x"), d_in, d_out)
    thirds = turned_parts(both(d_out, d_out_sib)[0], depth).reshape(2 * depth, own, 3, D // 3)
    thirds = thirds.transpose(0, 2, 1, 3).reshape(2 * depth, 3 * own, D // 3)
    thirds = jnp.pad(thirds, ((0, 0), (0, group - 3 * own), (0, 0)))
    d_enc = jnp.concatenate([thirds, blocks(both(d_in, d_in_sib))], axis=2)
    d_enc = scatter_y(place, d_enc)
    got_d = after(got_d, d_in)
    grad_dec, gg3 = input_back(3, g_dec, dec_rows, part_d, got_d, gains, "dec_input_back")
    grad_enc, gg0 = input_back(0, g_enc, enc_rows, part, got, gains, "enc_input_back")
    memory_low, dec_final, grad_enc, grad_dec, gg0, gg3 = after(
        (memory_low, dec_final, grad_enc, grad_dec, gg0, gg3), d_enc
    )
    d_enc = scatter_z(place, d_enc)

    wide, inner = 2 * units, 6 * WIDTH
    early = [d_ffn_dec[:, :wide], rounded(d_enc[:, D // 3 : D // 3 + 3 * WIDTH])]
    early = jnp.concatenate(early, axis=1).reshape(WAYS, own, -1)
    early = exchange_columns(place, early).astype(F32)
    late = after(late, early)
    down = wide + 2 * D // 3
    (sums,) = call(
        functools.partial(sums_kernel, own),
        "column_sums",
        [((64, 128), F32)],
        [late, d_ffn_dec, d_enc],
        1.0,
    )
    out_enc_mine = d_enc[: 3 * own, : D // 3].reshape(3, own, D // 3).transpose(1, 0, 2)
    out_mine = unpack_out_piece(late[:, down + inner :])
    turned_out = jnp.concatenate([rounded(out_enc_mine.reshape(1, own, D)), out_mine])
    turned_out = turn(turned_out, depth).astype(F32)
    columns = late[:, : inner + wide].reshape(WAYS, own, -1)
    columns = exchange_over_x(place, columns)
    columns_here = columns
    columns = exchange_over_cores(place, columns).astype(F32)
    shard_in, shard_out, shard_hin, shard_hout, row_in, row_out, row_hin, row_hout = call(
        functools.partial(shards_kernel, ff_own),
        "shards",
        [
            ((3, 3, own, D), F32),
            ((3, own, D), F32),
            ((2, 2, own, WAYS * units), F32),
            ((2, ff_own, D), F32),
            ((9, own), F32),
            ((3, own), F32),
            ((4, own), F32),
            ((2, ff_own), F32),
        ],
        [columns, early, turned_out, late, d_ffn_dec],
        2.0,
    )
    sums = sums + sum(shift_z(sums, k, depth) for k in range(1, depth))
    sums = sums + swap(sums, "y")
    (sums,) = call(hold_kernel, "hold", [(sums.shape, F32)], [sums, (columns_here, ANYWHERE)], 0.3)
    sums = pair_up(sums, swap(sums, "x"), place.x)
    sums = pair_up(sums, swap(sums, "c"), place.c)
    sums = sums.swapaxes(0, 1).reshape(WAYS, -1)
    cuts = [2 * wide, 2 * wide + 9 * WIDTH, 30 * 128, 30 * 128 + 2 * D, 30 * 128 + 5 * D]
    col_hin, col_in, _, col_hout, col_out, _ = jnp.split(sums, cuts, axis=1)
    col_hin = col_hin.reshape(WAYS, 2, 2, 2 * depth, ff_own).transpose(1, 2, 3, 0, 4)
    col_hin = col_hin.reshape(2, 2, WAYS * units)
    col_in = col_in.reshape(WAYS, 9, WIDTH)
    col_in = jnp.stack([col_in[:, k] for k in IN_ORDER]).reshape(3, 3, D)
    col_hout = jnp.sum(col_hout, axis=0).reshape(2, D)
    col_out = jnp.sum(col_out, axis=0).reshape(3, D)

    buckets = position_bias.shape[1]

    def head_table(d_table):
        wide_table = jnp.zeros((2 * SETS, 2 * length + block), F32)
        return lax.dynamic_update_slice_in_dim(wide_table, d_table, block * (1 - place.c), 1)

    grad_enc_bias = head_table(d_table_enc)[:, : 2 * length - 1]
    grad_dec_bias = head_table(d_table_dec)[:, :length][:, ::-1]
    by_set = jnp.stack(
        [
            bucket_grad(enc_buckets, grad_enc_bias, buckets),
            bucket_grad(dec_buckets, grad_dec_bias, buckets),
        ]
    )
    grad_position = lax.dynamic_update_slice_in_dim(
        jnp.zeros_like(position_bias), by_set[:, :, :SETS], q * SETS, 2
    )
    grad_position = lax.dynamic_update_slice_in_dim(
        grad_position, by_set[:, :, SETS:], (q + 1 - 2 * place.c) * SETS, 2
    )
    grad_gains = jnp.concatenate([gg0, gg1, gg2, gg3, gg4, gg5, gg6])
    grad_gains = jnp.where(place.x == 0, grad_gains, 0.0)
    small = jnp.concatenate([grad_gains.reshape(-1, 128), grad_position.reshape(-1, 128)])
    small = sum_everywhere(place, small)
    cut = grad_gains.size // 128
    grad_gains = small[:cut].reshape(grad_gains.shape)
    grad_position = small[cut:].reshape(grad_position.shape)
    shard_gains = lax.dynamic_slice_in_dim(grad_gains, place.index * own, own, 1)

    return (
        give_back(place, memory_low),
        give_back(place, dec_final),
        give_back(place, grad_enc),
        give_back(place, grad_dec),
        shard_in,
        shard_out,
        shard_hin,
        shard_hout,
        shard_gains,
        grad_position,
        row_in.reshape(3, 3, own),
        col_in,
        row_out,
        col_out,
        row_hin.reshape(2, 2, own),
        col_hin,
        row_hout,
        col_hout,
    )


def specs(seq):
    rows = P("dp", seq, None)
    every = ("dp",) + (seq if isinstance(seq, tuple) else (seq,))
    second, third = P(None, every, None), P(None, None, every, None)
    ins = (rows, rows, P("dp"), P("dp"), P(), P(), third, second, third, second)
    ins += (P(None, every), P(), rows, rows)
    outs = (rows, rows, rows, rows, third, second, third, second, P(None, every), P())
    outs += (P(None, None, every), P(), P(None, every), P())
    outs += (P(None, None, every), P(), P(None, every), P())
    return ins, outs


def solution(mesh):
    depth, seq = mesh.shape["dp"], mesh.shape["seq"]

    def wrap(function, over, axes):
        ins, outs = specs(axes)
        return jax.shard_map(function, mesh=over, in_specs=ins, out_specs=outs, check_vma=False)

    def run(*args):
        seqs, length = args[0].shape[0] // depth, args[0].shape[1]
        fits = depth == WAYS and seq == 8 and seqs == 2 and length % 512 == 0
        if fits and args[1].shape == args[0].shape:
            axes = ("y", "x", "c")
            split = Mesh(mesh.devices.reshape(depth, 2, 2, 2), ("dp",) + axes)
            return wrap(functools.partial(grouped, depth), split, axes)(*args)
        return wrap(local, mesh, "seq")(*args)

    return run
```

```python
import functools
import math

import jax
import jax.numpy as jnp
from jax import lax
from jax.experimental import pallas as pl
from jax.experimental.pallas import tpu as pltpu
from jax.sharding import Mesh, PartitionSpec as P

D = 768
HEADS = 12
HEAD = 64
FF = 2048


EPSILON = 1e-06
NEGATIVE = -1e30
HIGHEST = lax.Precision.HIGHEST


def rounded(values):
    return values.astype(jnp.bfloat16)


def rows_first(values):
    return values.transpose(0, 2, 1)


def rms_norm(values, gain_row):
    return (
        values * lax.rsqrt(jnp.mean(values * values, axis=-1, keepdims=True) + EPSILON) * gain_row
    )


def rms_back(values, gain_row, upstream):
    _, pullback = jax.vjp(rms_norm, values, gain_row)
    return pullback(upstream)


def gated_unit(gate_up):
    return jax.nn.gelu(gate_up[0], approximate=True) * gate_up[1]


def offset_table(buckets, layer_bias):
    choose = (buckets[:, None] == jnp.arange(layer_bias.shape[0], dtype=jnp.int32)[None, :]).astype(
        jnp.float32
    )
    return jnp.dot(choose, layer_bias, precision=HIGHEST).T


def bucket_grad(buckets, grad_bias, bucket_count):
    choose = (buckets[:, None] == jnp.arange(bucket_count, dtype=jnp.int32)[None, :]).astype(
        jnp.float32
    )
    return jnp.dot(choose.T, grad_bias.T, precision=HIGHEST)


def hankel_block(window, rows, cols):
    heads_here, length = (window.shape[0], window.shape[1])
    tiled = jnp.tile(window, (1, rows + 1))[:, : rows * (length + 1)]
    return tiled.reshape(heads_here, rows, length + 1)[:, :, :cols]


def bias_block(variant, table, row_start, col_start, rows, cols, extent):
    span = rows + cols - 1
    if variant == "enc":
        base = col_start - row_start - (rows - 1) + (extent - 1)
        window = lax.dynamic_slice_in_dim(table, base, span, 1)
        return hankel_block(window, rows, cols)[:, ::-1, :]
    widened = jnp.concatenate(
        [jnp.broadcast_to(table[:, :1], (table.shape[0], extent - 1)), table], axis=1
    )
    base = row_start - col_start - (cols - 1) + (extent - 1)
    window = lax.dynamic_slice_in_dim(widened, base, span, 1)
    return hankel_block(window, rows, cols)[:, :, ::-1]


def visible_mask(variant, row_ids, col_ids, lengths):
    visible = col_ids[None, None, :] < lengths[:, None, None]
    if variant == "dec":
        visible = visible & (col_ids[None, None, :] <= row_ids[None, :, None])
    return visible[:, None]


def block_scores(query_heads, key_heads, row_ids, col_ids, lengths, variant, offset_bias, extent):
    factor = HEAD ** (-0.5)
    scores = (
        jnp.einsum("sqhe,skhe->shqk", query_heads, key_heads, preferred_element_type=jnp.float32)
        * factor
    )
    if offset_bias is not None:
        scores = (
            scores
            + bias_block(
                variant,
                offset_bias,
                row_ids[0],
                col_ids[0],
                row_ids.shape[0],
                col_ids.shape[0],
                extent,
            )[None]
        )
    return (scores, visible_mask(variant, row_ids, col_ids, lengths))


def row_products(grad_context, context):
    seqs_here, rows_here = (context.shape[0], context.shape[1])
    return jnp.sum(
        (grad_context.astype(jnp.float32) * context).reshape(seqs_here, rows_here, HEADS, HEAD),
        axis=-1,
    ).transpose(0, 2, 1)


def attend(queries, row_ids, lengths, variant, offset_bias, extent, fold_keys):
    seqs_here, rows_here = (queries.shape[0], queries.shape[1])
    query_heads = queries.reshape(seqs_here, rows_here, HEADS, HEAD)

    def fold_step(carried, pieces, begin_at):
        key_rows, value_rows = pieces
        block_len = math.gcd(key_rows.shape[1], 512)

        def block_step(block_id, running):
            row_max, row_sum, weighted = running
            offset_in = block_id * block_len
            key_heads = lax.dynamic_slice_in_dim(key_rows, offset_in, block_len, 1).reshape(
                seqs_here, block_len, HEADS, HEAD
            )
            value_heads = lax.dynamic_slice_in_dim(value_rows, offset_in, block_len, 1).reshape(
                seqs_here, block_len, HEADS, HEAD
            )
            col_ids = offset_in + jnp.arange(block_len, dtype=jnp.int32)
            scores, visible = block_scores(
                query_heads, key_heads, row_ids, col_ids, lengths, variant, offset_bias, extent
            )
            new_max = jnp.maximum(row_max, jnp.max(jnp.where(visible, scores, NEGATIVE), axis=-1))
            weights = jnp.where(visible, jnp.exp(scores - new_max[..., None]), 0.0)
            shrink = jnp.exp(row_max - new_max)
            row_sum = row_sum * shrink + jnp.sum(weights, axis=-1)
            weighted = weighted * shrink[..., None] + jnp.einsum(
                "shqk,skhe->shqe", rounded(weights), value_heads, preferred_element_type=jnp.float32
            )
            return (new_max, row_sum, weighted)

        return lax.fori_loop(0, key_rows.shape[1] // block_len, block_step, carried)

    initial = (
        jnp.full((seqs_here, HEADS, rows_here), NEGATIVE, jnp.float32),
        jnp.zeros((seqs_here, HEADS, rows_here), jnp.float32),
        jnp.zeros((seqs_here, HEADS, rows_here, HEAD), jnp.float32),
    )
    row_max, row_sum, weighted = fold_keys(fold_step, initial)
    context = (
        (weighted / row_sum[..., None])
        .transpose(0, 2, 1, 3)
        .reshape(seqs_here, rows_here, HEADS * HEAD)
    )
    return (context, row_max + jnp.log(row_sum))


def attend_back(
    queries,
    log_sums,
    row_dots,
    grad_context,
    row_ids,
    lengths,
    variant,
    offset_bias,
    extent,
    fold_keys,
):
    seqs_here, rows_here = (queries.shape[0], queries.shape[1])
    query_heads = queries.reshape(seqs_here, rows_here, HEADS, HEAD)
    grad_heads = grad_context.reshape(seqs_here, rows_here, HEADS, HEAD)
    bias_width = offset_bias.shape[1] if offset_bias is not None else 1
    factor = HEAD ** (-0.5)

    def fold_step(carried, pieces, begin_at):
        key_rows, value_rows = pieces
        block_len = math.gcd(key_rows.shape[1], 512)

        def block_step(block_id, running):
            grad_query, grad_bias = (running[0], running[-1])
            offset_in = block_id * block_len
            key_heads = lax.dynamic_slice_in_dim(key_rows, offset_in, block_len, 1).reshape(
                seqs_here, block_len, HEADS, HEAD
            )
            value_heads = lax.dynamic_slice_in_dim(value_rows, offset_in, block_len, 1).reshape(
                seqs_here, block_len, HEADS, HEAD
            )
            col_ids = offset_in + jnp.arange(block_len, dtype=jnp.int32)
            scores, visible = block_scores(
                query_heads, key_heads, row_ids, col_ids, lengths, variant, offset_bias, extent
            )
            weights = jnp.where(visible, jnp.exp(scores - log_sums[..., None]), 0.0)
            grad_weights = jnp.einsum(
                "sqhe,skhe->shqk", grad_heads, value_heads, preferred_element_type=jnp.float32
            )
            grad_scores = weights * (grad_weights - row_dots[..., None])
            if offset_bias is not None:

                def table_block(table_values):
                    return bias_block(
                        variant,
                        table_values,
                        row_ids[0],
                        col_ids[0],
                        row_ids.shape[0],
                        col_ids.shape[0],
                        extent,
                    )

                _, table_pull = jax.vjp(table_block, offset_bias)
                grad_bias = grad_bias + table_pull(jnp.sum(grad_scores, axis=0))[0]
            grad_raw = rounded(grad_scores * factor)
            grad_query = grad_query + jnp.einsum(
                "shqk,skhe->shqe", grad_raw, key_heads, preferred_element_type=jnp.float32
            )
            return (grad_query, grad_bias)

        return lax.fori_loop(0, key_rows.shape[1] // block_len, block_step, carried)

    query_start = jnp.zeros((seqs_here, HEADS, rows_here, HEAD), jnp.float32)
    bias_start = jnp.zeros((HEADS, bias_width), jnp.float32)
    initial = (query_start, bias_start)
    result = fold_keys(fold_step, initial)
    grad_query = result[0].transpose(0, 2, 1, 3).reshape(seqs_here, rows_here, HEADS * HEAD)
    return (grad_query, None, None, result[1])


def owned_key_grads(
    key_rows, value_rows, col_ids, lengths, variant, offset_bias, extent, fold_queries
):
    seqs_here, keys_here = (key_rows.shape[0], key_rows.shape[1])
    key_heads = key_rows.reshape(seqs_here, keys_here, HEADS, HEAD)
    value_heads = value_rows.reshape(seqs_here, keys_here, HEADS, HEAD)
    factor = HEAD ** (-0.5)

    def fold_step(carried, pieces, begin_at):
        query_rows, grad_rows, log_rows, dot_rows = pieces
        block_len = math.gcd(query_rows.shape[1], 512)

        def block_step(block_id, running):
            grad_keys, grad_values = running
            offset_in = block_id * block_len
            query_heads = lax.dynamic_slice_in_dim(query_rows, offset_in, block_len, 1).reshape(
                seqs_here, block_len, HEADS, HEAD
            )
            grad_heads = lax.dynamic_slice_in_dim(grad_rows, offset_in, block_len, 1).reshape(
                seqs_here, block_len, HEADS, HEAD
            )
            log_block = lax.dynamic_slice_in_dim(log_rows, offset_in, block_len, 1).transpose(
                0, 2, 1
            )
            dot_block = lax.dynamic_slice_in_dim(dot_rows, offset_in, block_len, 1).transpose(
                0, 2, 1
            )
            row_ids = offset_in + jnp.arange(block_len, dtype=jnp.int32)
            scores, visible = block_scores(
                query_heads, key_heads, row_ids, col_ids, lengths, variant, offset_bias, extent
            )
            weights = jnp.where(visible, jnp.exp(scores - log_block[..., None]), 0.0)
            grad_weights = jnp.einsum(
                "sqhe,skhe->shqk", grad_heads, value_heads, preferred_element_type=jnp.float32
            )
            grad_scores = weights * (grad_weights - dot_block[..., None])
            grad_raw = rounded(grad_scores * factor)
            grad_keys = grad_keys + jnp.einsum(
                "shqk,sqhe->skhe", grad_raw, query_heads, preferred_element_type=jnp.float32
            ).reshape(seqs_here, keys_here, HEADS * HEAD)
            grad_values = grad_values + jnp.einsum(
                "shqk,sqhe->skhe", rounded(weights), grad_heads, preferred_element_type=jnp.float32
            ).reshape(seqs_here, keys_here, HEADS * HEAD)
            return (grad_keys, grad_values)

        return lax.fori_loop(0, query_rows.shape[1] // block_len, block_step, carried)

    initial = (
        jnp.zeros((seqs_here, keys_here, HEADS * HEAD), jnp.float32),
        jnp.zeros((seqs_here, keys_here, HEADS * HEAD), jnp.float32),
    )
    return fold_queries(fold_step, initial)


def feed_forward(residual, gain_row, weights_in, weights_out):
    normed_low = rounded(rms_norm(residual, gain_row))
    gate_up = jnp.einsum(
        "srd,jdf->jsrf", normed_low, weights_in, preferred_element_type=jnp.float32
    )
    hidden = rounded(gated_unit(gate_up))
    output = jnp.einsum("srf,fd->srd", hidden, weights_out, preferred_element_type=jnp.float32)
    return (residual + output, (normed_low, gate_up, hidden))


def feed_back(residual, gain_row, weights_in, weights_out, kept_values, upstream):
    normed_low, gate_up, hidden = kept_values
    upstream_low = rounded(upstream)
    grad_out_weights = jnp.einsum(
        "srf,srd->fd", hidden, upstream_low, preferred_element_type=jnp.float32
    )
    grad_hidden = jnp.einsum(
        "srd,fd->srf", upstream_low, weights_out, preferred_element_type=jnp.float32
    )
    _, pullback = jax.vjp(gated_unit, gate_up)
    grad_gate_up = rounded(pullback(grad_hidden)[0])
    grad_in_weights = jnp.einsum(
        "srd,jsrf->jdf", normed_low, grad_gate_up, preferred_element_type=jnp.float32
    )
    grad_normed = jnp.einsum(
        "jsrf,jdf->srd", grad_gate_up, weights_in, preferred_element_type=jnp.float32
    )
    grad_residual, grad_gain = rms_back(residual, gain_row, grad_normed)
    return (upstream + grad_residual, grad_gain, grad_in_weights, grad_out_weights)


def local(
    enc_input,
    dec_input,
    enc_lengths,
    dec_lengths,
    enc_buckets,
    dec_buckets,
    attention_in,
    attention_out,
    hidden_in,
    hidden_out,
    norm_gains,
    position_bias,
    enc_cotangent,
    dec_cotangent,
):
    full_in, full_out, full_hidden_in, full_hidden_out, full_gains = (
        lax.all_gather(attention_in, ("dp", "seq"), axis=2, tiled=True),
        lax.all_gather(attention_out, ("dp", "seq"), axis=1, tiled=True),
        lax.all_gather(hidden_in, ("dp", "seq"), axis=2, tiled=True),
        lax.all_gather(hidden_out, ("dp", "seq"), axis=1, tiled=True),
        lax.all_gather(norm_gains, ("dp", "seq"), axis=1, tiled=True),
    )
    gain_rows = full_gains.astype(jnp.float32)
    enc_rows = enc_input.shape[1]
    dec_rows = dec_input.shape[1]
    seq_index = lax.axis_index("seq")
    enc_ids = seq_index * enc_rows + jnp.arange(enc_rows, dtype=jnp.int32)
    dec_ids = seq_index * dec_rows + jnp.arange(dec_rows, dtype=jnp.int32)
    enc_extent = (enc_buckets.shape[0] + 1) // 2
    dec_extent = dec_buckets.shape[0]
    enc_table = offset_table(enc_buckets, position_bias[0])
    dec_table = offset_table(dec_buckets, position_bias[1])
    enc_values = enc_input.astype(jnp.float32)
    norm_a_low = rounded(rms_norm(enc_values, gain_rows[0]))
    enc_qkv = rounded(
        jnp.einsum("srd,jde->jsre", norm_a_low, full_in[0], preferred_element_type=jnp.float32)
    )
    enc_context, enc_logs = attend(
        enc_qkv[0],
        enc_ids,
        enc_lengths,
        "enc",
        enc_table,
        enc_extent,
        lambda folder, initial: folder(
            initial,
            (
                lax.all_gather(enc_qkv[1], "seq", axis=1, tiled=True),
                lax.all_gather(enc_qkv[2], "seq", axis=1, tiled=True),
            ),
            jnp.int32(0),
        ),
    )
    enc_context_low = rounded(enc_context)
    enc_mid = enc_values + jnp.einsum(
        "srd,de->sre", enc_context_low, full_out[0], preferred_element_type=jnp.float32
    )
    enc_last, enc_ffn_kept = feed_forward(
        enc_mid, gain_rows[1], full_hidden_in[0], full_hidden_out[0]
    )
    memory = rms_norm(enc_last, gain_rows[2])
    memory_low = rounded(memory)
    dec_values = dec_input.astype(jnp.float32)
    norm_b_low = rounded(rms_norm(dec_values, gain_rows[3]))
    dec_qkv = rounded(
        jnp.einsum("srd,jde->jsre", norm_b_low, full_in[1], preferred_element_type=jnp.float32)
    )
    dec_context, dec_logs = attend(
        dec_qkv[0],
        dec_ids,
        dec_lengths,
        "dec",
        dec_table,
        dec_extent,
        lambda folder, initial: folder(
            initial,
            (
                lax.all_gather(dec_qkv[1], "seq", axis=1, tiled=True),
                lax.all_gather(dec_qkv[2], "seq", axis=1, tiled=True),
            ),
            jnp.int32(0),
        ),
    )
    dec_context_low = rounded(dec_context)
    dec_mid = dec_values + jnp.einsum(
        "srd,de->sre", dec_context_low, full_out[1], preferred_element_type=jnp.float32
    )
    norm_c_low = rounded(rms_norm(dec_mid, gain_rows[4]))
    cross_query = rounded(
        jnp.einsum("srd,de->sre", norm_c_low, full_in[2, 0], preferred_element_type=jnp.float32)
    )
    cross_pair = rounded(
        jnp.einsum("srd,jde->jsre", memory_low, full_in[2, 1:], preferred_element_type=jnp.float32)
    )
    cross_context, cross_logs = attend(
        cross_query,
        dec_ids,
        enc_lengths,
        "cross",
        None,
        0,
        lambda folder, initial: folder(
            initial,
            (
                lax.all_gather(cross_pair[0], "seq", axis=1, tiled=True),
                lax.all_gather(cross_pair[1], "seq", axis=1, tiled=True),
            ),
            jnp.int32(0),
        ),
    )
    cross_low = rounded(cross_context)
    dec_cross = dec_mid + jnp.einsum(
        "srd,de->sre", cross_low, full_out[2], preferred_element_type=jnp.float32
    )
    dec_last, dec_ffn_kept = feed_forward(
        dec_cross, gain_rows[5], full_hidden_in[1], full_hidden_out[1]
    )
    dec_final = rms_norm(dec_last, gain_rows[6])
    grad_dec_last, grad_gain_six = rms_back(
        dec_last, gain_rows[6], dec_cotangent.astype(jnp.float32)
    )
    grad_dec_cross, grad_gain_five, grad_hin_one, grad_hout_one = feed_back(
        dec_cross, gain_rows[5], full_hidden_in[1], full_hidden_out[1], dec_ffn_kept, grad_dec_last
    )
    upstream_low = rounded(grad_dec_cross)
    grad_out_two = jnp.einsum(
        "srd,sre->de", cross_low, upstream_low, preferred_element_type=jnp.float32
    )
    grad_cross_context = rounded(
        jnp.einsum("sre,de->srd", upstream_low, full_out[2], preferred_element_type=jnp.float32)
    )
    cross_dots = row_products(grad_cross_context, cross_context)
    cross_grad_query, cross_grad_keys, cross_grad_values, _ = attend_back(
        cross_query,
        cross_logs,
        cross_dots,
        grad_cross_context,
        dec_ids,
        enc_lengths,
        "cross",
        None,
        0,
        lambda folder, initial: folder(
            initial,
            (
                lax.all_gather(cross_pair[0], "seq", axis=1, tiled=True),
                lax.all_gather(cross_pair[1], "seq", axis=1, tiled=True),
            ),
            jnp.int32(0),
        ),
    )
    cross_query_low = rounded(cross_grad_query)
    grad_query_two = jnp.einsum(
        "srd,sre->de", norm_c_low, cross_query_low, preferred_element_type=jnp.float32
    )
    grad_norm_c = jnp.einsum(
        "sre,de->srd", cross_query_low, full_in[2, 0], preferred_element_type=jnp.float32
    )
    grad_mid_part, grad_gain_four = rms_back(dec_mid, gain_rows[4], grad_norm_c)
    grad_dec_mid = grad_dec_cross + grad_mid_part
    upstream_low = rounded(grad_dec_mid)
    grad_out_one = jnp.einsum(
        "srd,sre->de", dec_context_low, upstream_low, preferred_element_type=jnp.float32
    )
    grad_dec_context = rounded(
        jnp.einsum("sre,de->srd", upstream_low, full_out[1], preferred_element_type=jnp.float32)
    )
    dec_dots = row_products(grad_dec_context, dec_context)
    dec_grad_query, dec_grad_keys, dec_grad_values, grad_dec_bias = attend_back(
        dec_qkv[0],
        dec_logs,
        dec_dots,
        grad_dec_context,
        dec_ids,
        dec_lengths,
        "dec",
        dec_table,
        dec_extent,
        lambda folder, initial: folder(
            initial,
            (
                lax.all_gather(dec_qkv[1], "seq", axis=1, tiled=True),
                lax.all_gather(dec_qkv[2], "seq", axis=1, tiled=True),
            ),
            jnp.int32(0),
        ),
    )
    cross_key_grad, cross_value_grad = owned_key_grads(
        cross_pair[0],
        cross_pair[1],
        enc_ids,
        enc_lengths,
        "cross",
        None,
        0,
        lambda folder, initial: folder(
            initial,
            (
                lax.all_gather(cross_query, "seq", axis=1, tiled=True),
                lax.all_gather(grad_cross_context, "seq", axis=1, tiled=True),
                lax.all_gather(
                    rows_first(cross_logs).astype(jnp.bfloat16), "seq", axis=1, tiled=True
                ).astype(jnp.float32),
                lax.all_gather(
                    rows_first(cross_dots).astype(jnp.bfloat16), "seq", axis=1, tiled=True
                ).astype(jnp.float32),
            ),
            jnp.int32(0),
        ),
    )
    dec_key_grad, dec_value_grad = owned_key_grads(
        dec_qkv[1],
        dec_qkv[2],
        dec_ids,
        dec_lengths,
        "dec",
        dec_table,
        dec_extent,
        lambda folder, initial: folder(
            initial,
            (
                lax.all_gather(dec_qkv[0], "seq", axis=1, tiled=True),
                lax.all_gather(grad_dec_context, "seq", axis=1, tiled=True),
                lax.all_gather(
                    rows_first(dec_logs).astype(jnp.bfloat16), "seq", axis=1, tiled=True
                ).astype(jnp.float32),
                lax.all_gather(
                    rows_first(dec_dots).astype(jnp.bfloat16), "seq", axis=1, tiled=True
                ).astype(jnp.float32),
            ),
            jnp.int32(0),
        ),
    )
    pair_grads = rounded(jnp.stack([cross_key_grad, cross_value_grad]))
    grad_pair_two = jnp.einsum(
        "srd,jsre->jde", memory_low, pair_grads, preferred_element_type=jnp.float32
    )
    grad_memory = jnp.einsum(
        "jsre,jde->srd", pair_grads, full_in[2, 1:], preferred_element_type=jnp.float32
    )
    dec_grads = rounded(jnp.stack([dec_grad_query, dec_key_grad, dec_value_grad]))
    grad_in_one = jnp.einsum(
        "srd,jsre->jde", norm_b_low, dec_grads, preferred_element_type=jnp.float32
    )
    grad_norm_b = jnp.einsum(
        "jsre,jde->srd", dec_grads, full_in[1], preferred_element_type=jnp.float32
    )
    grad_dec_part, grad_gain_three = rms_back(dec_values, gain_rows[3], grad_norm_b)
    grad_dec_input = grad_dec_mid + grad_dec_part
    grad_memory_total = enc_cotangent.astype(jnp.float32) + grad_memory
    grad_enc_last, grad_gain_two = rms_back(enc_last, gain_rows[2], grad_memory_total)
    grad_enc_mid, grad_gain_one, grad_hin_zero, grad_hout_zero = feed_back(
        enc_mid, gain_rows[1], full_hidden_in[0], full_hidden_out[0], enc_ffn_kept, grad_enc_last
    )
    upstream_low = rounded(grad_enc_mid)
    grad_out_zero = jnp.einsum(
        "srd,sre->de", enc_context_low, upstream_low, preferred_element_type=jnp.float32
    )
    grad_enc_context = rounded(
        jnp.einsum("sre,de->srd", upstream_low, full_out[0], preferred_element_type=jnp.float32)
    )
    enc_dots = row_products(grad_enc_context, enc_context)
    enc_grad_query, enc_grad_keys, enc_grad_values, grad_enc_bias = attend_back(
        enc_qkv[0],
        enc_logs,
        enc_dots,
        grad_enc_context,
        enc_ids,
        enc_lengths,
        "enc",
        enc_table,
        enc_extent,
        lambda folder, initial: folder(
            initial,
            (
                lax.all_gather(enc_qkv[1], "seq", axis=1, tiled=True),
                lax.all_gather(enc_qkv[2], "seq", axis=1, tiled=True),
            ),
            jnp.int32(0),
        ),
    )
    enc_key_grad, enc_value_grad = owned_key_grads(
        enc_qkv[1],
        enc_qkv[2],
        enc_ids,
        enc_lengths,
        "enc",
        enc_table,
        enc_extent,
        lambda folder, initial: folder(
            initial,
            (
                lax.all_gather(enc_qkv[0], "seq", axis=1, tiled=True),
                lax.all_gather(grad_enc_context, "seq", axis=1, tiled=True),
                lax.all_gather(
                    rows_first(enc_logs).astype(jnp.bfloat16), "seq", axis=1, tiled=True
                ).astype(jnp.float32),
                lax.all_gather(
                    rows_first(enc_dots).astype(jnp.bfloat16), "seq", axis=1, tiled=True
                ).astype(jnp.float32),
            ),
            jnp.int32(0),
        ),
    )
    enc_grads = rounded(jnp.stack([enc_grad_query, enc_key_grad, enc_value_grad]))
    grad_in_zero = jnp.einsum(
        "srd,jsre->jde", norm_a_low, enc_grads, preferred_element_type=jnp.float32
    )
    grad_norm_a = jnp.einsum(
        "jsre,jde->srd", enc_grads, full_in[0], preferred_element_type=jnp.float32
    )
    grad_enc_part, grad_gain_zero = rms_back(enc_values, gain_rows[0], grad_norm_a)
    grad_enc_input = grad_enc_mid + grad_enc_part
    grad_cross_in = jnp.concatenate([grad_query_two[None], grad_pair_two], axis=0)
    grad_attention_in = jnp.stack([grad_in_zero, grad_in_one, grad_cross_in])
    grad_attention_out = jnp.stack([grad_out_zero, grad_out_one, grad_out_two])
    grad_hidden_in = jnp.stack([grad_hin_zero, grad_hin_one])
    grad_hidden_out = jnp.stack([grad_hout_zero, grad_hout_one])
    grad_gains = jnp.stack(
        [
            grad_gain_zero,
            grad_gain_one,
            grad_gain_two,
            grad_gain_three,
            grad_gain_four,
            grad_gain_five,
            grad_gain_six,
        ]
    )
    shard_in, shard_out, shard_hin, shard_hout, shard_gains = (
        lax.psum_scatter(grad_attention_in, ("dp", "seq"), scatter_dimension=2, tiled=True),
        lax.psum_scatter(grad_attention_out, ("dp", "seq"), scatter_dimension=1, tiled=True),
        lax.psum_scatter(grad_hidden_in, ("dp", "seq"), scatter_dimension=2, tiled=True),
        lax.psum_scatter(grad_hidden_out, ("dp", "seq"), scatter_dimension=1, tiled=True),
        lax.psum_scatter(grad_gains, ("dp", "seq"), scatter_dimension=1, tiled=True),
    )
    bucket_count = position_bias.shape[1]
    grad_position = jnp.stack(
        [
            bucket_grad(enc_buckets, grad_enc_bias, bucket_count),
            bucket_grad(dec_buckets, grad_dec_bias, bucket_count),
        ]
    )
    squares_in = shard_in * shard_in
    squares_out = shard_out * shard_out
    squares_hin = shard_hin * shard_hin
    squares_hout = shard_hout * shard_hout
    col_in, col_out, col_hin, col_hout, grad_position = lax.psum(
        (
            jnp.sum(squares_in, axis=2),
            jnp.sum(squares_out, axis=1),
            jnp.sum(squares_hin, axis=2),
            jnp.sum(squares_hout, axis=1),
            grad_position,
        ),
        ("dp", "seq"),
    )
    return (
        rounded(memory),
        rounded(dec_final),
        grad_enc_input,
        grad_dec_input,
        shard_in,
        shard_out,
        shard_hin,
        shard_hout,
        shard_gains,
        grad_position,
        0.5 * jnp.mean(squares_in, axis=-1),
        0.5 * col_in / D,
        0.5 * jnp.mean(squares_out, axis=-1),
        0.5 * col_out / D,
        0.5 * jnp.mean(squares_hin, axis=-1),
        0.5 * col_hin / D,
        0.5 * jnp.mean(squares_hout, axis=-1),
        0.5 * col_hout / FF,
    )


WAYS = 4
SETS = HEADS // WAYS
WIDTH = SETS * HEAD
VMEM_LIMIT = 16 * 2**20


def swap(values, axis):
    return lax.ppermute(values, axis, [(0, 1), (1, 0)])


def shift_z(values, hops, count):
    return lax.ppermute(values, "dp", [(i, (i + hops) % count) for i in range(count)])


def pair_up(mine, other, bit):
    first = bit == 0
    return jnp.stack([jnp.where(first, mine, other), jnp.where(first, other, mine)])


def pick(values, index, axis=0):
    return lax.dynamic_index_in_dim(values, index, axis, keepdims=False)


class Place:
    def __init__(self, depth):
        self.depth = depth
        self.z, self.y, self.x, self.c = [lax.axis_index(a) for a in ("dp", "y", "x", "c")]
        self.q = 2 * self.x + self.c
        self.index = (self.z * 2 + self.y) * WAYS + self.q


def exchange_over_x(place, pieces):
    halves = pieces.reshape((2, 2) + pieces.shape[1:])
    got = swap(pick(halves, 1 - place.x), "x")
    return pair_up(pick(halves, place.x), got, place.x)


def exchange_over_cores(place, both):
    got = swap(pick(both, 1 - place.c, 1), "c")
    whole = pair_up(pick(both, place.c, 1), got, place.c)
    return jnp.swapaxes(whole, 0, 1).reshape((4,) + both.shape[2:])


def exchange_columns(place, pieces):
    return exchange_over_cores(place, exchange_over_x(place, pieces))


def along_z(place, piece, *earlier):
    depth = place.depth
    held = jnp.zeros((depth,) + piece.shape, piece.dtype)
    arrivals = [shift_z(piece, k, depth) for k in range(1, depth)]
    if earlier:
        arrivals = [after(block, *earlier) for block in arrivals]
    for hops, block in enumerate([piece] + arrivals):
        held = lax.dynamic_update_index_in_dim(held, block, (place.z - hops) % depth, 0)
    return held


def along_y(place, held):
    other = swap(held, "y")
    first = place.y == 0
    pair = [jnp.where(first, held, other), jnp.where(first, other, held)]
    return jnp.stack(pair, axis=1).reshape(-1, held.shape[-1])


def scatter_y(place, parts):
    parts = parts.reshape((place.depth, 2) + parts.shape[1:])
    sent = swap(pick(parts, 1 - place.y, 1), "y")
    return pick(parts, place.y, 1).astype(F32) + sent.astype(F32)


def scatter_z(place, halves):
    depth = place.depth
    low = rounded(halves)
    total = pick(halves, place.z)
    for hops in range(1, depth):
        sent = shift_z(pick(low, (place.z + hops) % depth), hops, depth)
        total = total + sent.astype(F32)
    return total


def after(values, *earlier):
    return lax.optimization_barrier((values,) + earlier)[0]


def turn(values, depth):
    pairs = []
    for d in range(depth):
        for y in range(2):
            for q in range(WAYS):
                pairs.append((d * 8 + y * 4 + q, q * 8 + y * 4 + d))
    return lax.ppermute(values, ("dp", "y", "x", "c"), pairs)


def matmul(a, b):
    return jnp.dot(a, b, preferred_element_type=jnp.float32)


def matmul_nt(a, b):
    return lax.dot_general(a, b, (((1,), (1,)), ((), ())), preferred_element_type=jnp.float32)


def matmul_tn(a, b):
    return lax.dot_general(a, b, (((0,), (0,)), ((), ())), preferred_element_type=jnp.float32)


def call(kernel, name, outs, args, micros, scratch=()):
    whole = pl.BlockSpec(memory_space=pltpu.VMEM)
    arrays = [a[0] if isinstance(a, tuple) else a for a in args]
    specs = [a[1] if isinstance(a, tuple) else whole for a in args]
    late = [k for k, spec in enumerate(specs) if spec is LATE]
    plain = (whole, SCALARS, LATE, ANYWHERE)
    windows = any(all(spec is not p for p in plain) for spec in specs)
    shapes = tuple(jax.ShapeDtypeStruct(s, t) for s, t in outs)
    moved = sum(a.size * a.dtype.itemsize for a in list(arrays) + list(shapes))
    buffers = [pltpu.VMEM(arrays[k].shape, arrays[k].dtype) for k in late]

    def bring_in(*refs):
        if not late:
            return kernel(*refs)
        refs, places, semaphores = list(refs[: -len(late) - 1]), refs[-len(late) - 1 : -1], refs[-1]
        copies = [
            pltpu.make_async_copy(refs[k], place, semaphores.at[n])
            for n, (k, place) in enumerate(zip(late, places))
        ]
        for copy in copies:
            copy.start()
        for copy in copies:
            copy.wait()
        for k, place in zip(late, places):
            refs[k] = place
        return kernel(*refs)

    if late:
        buffers.append(pltpu.SemaphoreType.DMA((len(late),)))
    return pl.pallas_call(
        bring_in,
        grid=(1,) if windows else (),
        out_shape=shapes,
        in_specs=specs,
        out_specs=(whole,) * len(shapes),
        scratch_shapes=list(scratch) + buffers,
        compiler_params=pltpu.CompilerParams(vmem_limit_bytes=VMEM_LIMIT),
        cost_estimate=pl.CostEstimate(
            flops=int(micros * 1e7), bytes_accessed=moved // 32, transcendentals=0
        ),
        name=name,
    )(*arrays)


LATE = pl.BlockSpec(memory_space=pltpu.HBM)
ANYWHERE = pl.BlockSpec(memory_space=pl.ANY)
SCALARS = pl.BlockSpec(memory_space=pltpu.SMEM)
BF, F32 = jnp.bfloat16, jnp.float32


def column_block(array, index):
    rows, columns = array.shape
    return (array, pl.BlockSpec((rows, 2 * WIDTH), lambda _: (0, index)))


def norm_rows(values, gain):
    return values * lax.rsqrt(jnp.mean(values * values, axis=-1, keepdims=True) + EPSILON) * gain


def norm_back(values, gain, upstream):
    scale = lax.rsqrt(jnp.mean(values * values, axis=-1, keepdims=True) + EPSILON)
    unit = values * scale
    inner = upstream * gain
    grad = scale * (inner - unit * jnp.mean(inner * unit, axis=-1, keepdims=True))
    return grad, jnp.sum(upstream * unit, axis=0, keepdims=True)


def self_kernel(gain, q_at, x_ref, gains_ref, kva_ref, qa_ref, kvb_ref, qb_ref, *outs):
    n_ref, q_ref, kv_ref = outs
    n = norm_rows(x_ref[...].astype(F32), gains_ref[gain : gain + 1, :]).astype(BF)
    n_ref[...] = n
    for e, (kv, q) in enumerate(((kva_ref, qa_ref), (kvb_ref, qb_ref))):
        kv_ref[e] = matmul(n, kv[:, : 2 * WIDTH]).astype(BF)
        q_ref[e] = matmul(n, q[:, q_at : q_at + WIDTH]).astype(BF)


def self_project(x, gains, gain, kv_own, q_own, kv_sib, q_sib, q_at, name):
    rows = x.shape[0]
    return call(
        functools.partial(self_kernel, gain, q_at),
        name,
        [((rows, D), BF), ((2, rows, WIDTH), BF), ((2, rows, 2 * WIDTH), BF)],
        [x, gains, kv_own, q_own, kv_sib, q_sib],
        2.5,
    )


def memory_kernel(res_ref, part_ref, got_ref, gains_ref, kva_ref, kvb_ref, *outs):
    last_ref, low_ref, kv_ref = outs
    last = res_ref[...].astype(F32) + part_ref[...] + got_ref[...].astype(F32)
    last_ref[...] = last
    low = norm_rows(last, gains_ref[2:3, :]).astype(BF)
    low_ref[...] = low
    for e, kv in enumerate((kva_ref, kvb_ref)):
        kv_ref[e] = matmul(low, kv[...]).astype(BF)


def cross_kernel(q_at, res_ref, part_ref, got_ref, gains_ref, qa_ref, qb_ref, *outs):
    mid_ref, low_ref, q_ref = outs
    mid = res_ref[...].astype(F32) + part_ref[...] + got_ref[...].astype(F32)
    mid_ref[...] = mid
    low = norm_rows(mid, gains_ref[4:5, :]).astype(BF)
    low_ref[...] = low
    for e, q in enumerate((qa_ref, qb_ref)):
        q_ref[e] = matmul(low, q[:, q_at : q_at + WIDTH]).astype(BF)


def lay_out_keys(core, kv_ref, got_ref, keys):
    block = kv_ref.shape[1] // 4
    for e in range(2):
        for k in range(4):
            at = pl.multiple_of(block * (2 * k + core), block)
            keys[e, pl.ds(at, block), :] = kv_ref[e, k * block : (k + 1) * block, :]
            at = pl.multiple_of(block * (2 * k + 1 - core), block)
            keys[e, pl.ds(at, block), :] = got_ref[1 - e, k * block : (k + 1) * block, :]


def attend_kernel(causal, biased, *refs):
    if biased:
        scalars, q_ref, kv_ref, got_ref, table_ref, oa_ref, ob_ref = refs[:7]
    else:
        scalars, q_ref, kv_ref, got_ref, oa_ref, ob_ref = refs[:6]
    ctx_ref, p_ref, part_ref, low_ref, keys = refs[-5:]
    core, length = scalars[0], scalars[1]
    lay_out_keys(core, kv_ref, got_ref, keys)
    rows, extent = q_ref.shape[1], keys.shape[1]
    block = rows // 4
    cols = lax.broadcasted_iota(jnp.int32, (block, extent), 1)
    ids = lax.broadcasted_iota(jnp.int32, (block, extent), 0)
    total = None
    for e in range(2):
        for h in range(SETS):
            at = slice(h * HEAD, (h + 1) * HEAD)
            k = keys[e, :, at]
            v = keys[e, :, WIDTH + h * HEAD : WIDTH + (h + 1) * HEAD]
            scores = matmul_nt(q_ref[e, :, at], k)
            if biased:
                line = table_ref[e * SETS + h : e * SETS + h + 1, :]
                skew = pltpu.roll(
                    jnp.broadcast_to(line, (block, 2 * extent)),
                    2 * extent - (block - 1),
                    1,
                    stride=1,
                    stride_axis=0,
                )
            for i in range(4):
                here = slice(i * block, (i + 1) * block)
                seen = (i + 1) * 2 * block if causal else extent
                s = scores[here, :seen] * (HEAD**-0.5)
                if biased:
                    begin = (3 - i) * 2 * block
                    s = s + skew[:, begin : begin + seen]
                visible = cols[:, :seen] < length
                if causal:
                    visible = visible & (cols[:, :seen] <= ids[:, :seen] + (i * 2 * block + core * block))
                s = jnp.where(visible, s, NEGATIVE)
                weights = jnp.exp(s - jnp.max(s, axis=-1, keepdims=True))
                weights = weights * (1.0 / jnp.sum(weights, axis=-1, keepdims=True))
                p_ref[e * SETS + h, here, :seen] = weights.astype(BF)
                if seen < extent:
                    p_ref[e * SETS + h, here, seen:] = jnp.zeros((block, extent - seen), BF)
            ctx_ref[e, :, at] = matmul(p_ref[e * SETS + h], v)
        term = matmul(ctx_ref[e].astype(BF), (oa_ref, ob_ref)[e][...])
        total = term if total is None else total + term
    part_ref[...] = total
    low_ref[...] = total.astype(BF)


def attend_local(scalars, q, kv, got, table, out_own, out_sib, causal, name):
    rows = q.shape[1]
    extent = 2 * rows
    args = [(scalars, SCALARS), q, kv, got] + ([] if table is None else [table])
    return call(
        functools.partial(attend_kernel, causal, table is not None),
        name,
        [
            ((2, rows, WIDTH), F32),
            ((2 * SETS, rows, extent), BF),
            ((rows, D), F32),
            ((rows, D), BF),
        ],
        args + [out_own, out_sib],
        5.5,
        [pltpu.VMEM((2, extent, 2 * WIDTH), BF)],
    )


def unpack_into(w_ref, columns, down):
    blocks, rows = 8, down.shape[0] // 8
    half, third = rows // 2, down.shape[1] // 3
    step = rows + half
    for b in range(blocks):
        down[b * rows : (b + 1) * rows, : 2 * third] = w_ref[
            b * step : b * step + rows, columns : columns + 2 * third
        ]
        for k in range(2):
            down[b * rows + k * half : b * rows + (k + 1) * half, 2 * third :] = w_ref[
                b * step + rows : (b + 1) * step,
                columns + k * third : columns + (k + 1) * third,
            ]


GELU_A, GELU_B = (2 / math.pi) ** 0.5, 0.044715


def gelu_tanh(gate):
    return jnp.tanh(GELU_A * (gate + GELU_B * gate * gate * gate))


def ffn_kernel(gain, res_ref, part_ref, got_ref, gains_ref, wa_ref, wb_ref, *refs):
    mid_ref, n_ref, gu_ref, hid_ref, out_ref, low_ref, down = refs
    mid = res_ref[...].astype(F32) + part_ref[...] + got_ref[...].astype(F32)
    mid_ref[...] = mid
    n = norm_rows(mid, gains_ref[gain : gain + 1, :]).astype(BF)
    n_ref[...] = n
    units = down.shape[0]
    total = None
    for e, w_ref in enumerate((wa_ref, wb_ref)):
        gu_ref[e] = matmul(n, w_ref[:, : 2 * units])
        gate, up = gu_ref[e, :, :units], gu_ref[e, :, units:]
        hid_ref[e] = (0.5 * gate * (1.0 + gelu_tanh(gate)) * up).astype(BF)
        unpack_into(w_ref, 2 * units, down)
        term = matmul(hid_ref[e], down[...])
        total = term if total is None else total + term
    out_ref[...] = total
    low_ref[...] = total.astype(BF)


def ffn_local(res, part, got, gains, gain, w_own, w_sib, units, name):
    rows = res.shape[0]
    return call(
        functools.partial(ffn_kernel, gain),
        name,
        [
            ((rows, D), F32),
            ((rows, D), BF),
            ((2, rows, 2 * units), F32),
            ((2, rows, units), BF),
            ((rows, D), F32),
            ((rows, D), BF),
        ],
        [res, part, got, gains, w_own, w_sib],
        3.0,
        [pltpu.VMEM((units, D), BF)],
    )


def ffn_back_kernel(decoder, val_ref, part_ref, got_ref, cot_ref, gains_ref, *refs):
    gu_ref, wa_ref, wb_ref = refs[:3]
    down = refs[-1]
    sent = part_ref[...] + got_ref[...].astype(F32)
    if decoder:
        final_ref, g_ref, dgain_ref, low_ref, dgu_ref, out_ref, out_low_ref = refs[3:-1]
        gain = gains_ref[6:7, :]
        values = val_ref[...] + sent
        upstream = cot_ref[...].astype(F32)
        final_ref[...] = norm_rows(values, gain).astype(BF)
    else:
        g_ref, dgain_ref, low_ref, dgu_ref, out_ref, out_low_ref = refs[3:-1]
        gain = gains_ref[2:3, :]
        values = val_ref[...]
        upstream = cot_ref[...].astype(F32) + sent
    grad, dgain_ref[...] = norm_back(values, gain, upstream)
    g_ref[...] = grad
    low = grad.astype(BF)
    low_ref[...] = low
    units = down.shape[0]
    total = None
    for e, w_ref in enumerate((wa_ref, wb_ref)):
        unpack_into(w_ref, 2 * units, down)
        grad_hidden = matmul_nt(low, down[...])
        gate, up = gu_ref[e, :, :units], gu_ref[e, :, units:]
        t = gelu_tanh(gate)
        slope = 0.5 * (1.0 + t) + 0.5 * gate * (1.0 - t * t) * GELU_A * (
            1.0 + 3.0 * GELU_B * gate * gate
        )
        dgu_ref[e, :, :units] = (grad_hidden * up * slope).astype(BF)
        dgu_ref[e, :, units:] = (grad_hidden * (0.5 * gate * (1.0 + t))).astype(BF)
        term = matmul_nt(dgu_ref[e], w_ref[:, : 2 * units])
        total = term if total is None else total + term
    out_ref[...] = total
    out_low_ref[...] = total.astype(BF)


def ffn_back(decoder, values, part, got, cot, gains, gate_up, w_own, w_sib, name):
    rows, units = values.shape[0], gate_up.shape[2] // 2
    outs = [((rows, D), BF)] if decoder else []
    outs += [
        ((rows, D), F32),
        ((1, D), F32),
        ((rows, D), BF),
        ((2, rows, 2 * units), BF),
        ((rows, D), F32),
        ((rows, D), BF),
    ]
    return call(
        functools.partial(ffn_back_kernel, decoder),
        name,
        outs,
        [values, part, got, cot, gains, gate_up, w_own, w_sib],
        4.0,
        [pltpu.VMEM((units, D), BF)],
    )


def ffn_weights_kernel(n_ref, dgu_ref, hid_ref, low_ref, own_ref, sib_ref):
    units = hid_ref.shape[2]
    rows, half, third = units // 8, units // 16, D // 3
    step = rows + half
    for e, out in enumerate((own_ref, sib_ref)):
        out[:, : 2 * units] = matmul_tn(n_ref[...], dgu_ref[e]).astype(BF)
        down = matmul_tn(hid_ref[e], low_ref[...]).astype(BF)
        for b in range(8):
            out[b * step : b * step + rows, 2 * units :] = down[
                b * rows : (b + 1) * rows, : 2 * third
            ]
            for k in range(2):
                out[
                    b * step + rows : (b + 1) * step,
                    2 * units + k * third : 2 * units + (k + 1) * third,
                ] = down[b * rows + k * half : b * rows + (k + 1) * half, 2 * third :]


def ffn_weights(n, dgu, hid, low, name):
    units = hid.shape[2]
    shape = ((D, 2 * units + 2 * D // 3), BF)
    return call(
        ffn_weights_kernel, name, [shape, shape], [n, dgu, hid, low], 1.5
    )


def attend_back_kernel(gain, biased, scalars, up_ref, val_ref, part_ref, got_ref, *refs):
    gains_ref, oa_ref, ob_ref, q_ref, kv_ref, kvgot_ref, p_ref, ctx_ref = refs[:8]
    g_ref, dgain_ref, low_ref, dq_ref, mine_ref, other_ref = refs[8:14]
    keys, dkeys, ds_ref = refs[-3:]
    core = scalars[0]
    grad, dgain_ref[...] = norm_back(
        val_ref[...], gains_ref[gain : gain + 1, :], part_ref[...] + got_ref[...].astype(F32)
    )
    grad = up_ref[...] + grad
    g_ref[...] = grad
    low = grad.astype(BF)
    low_ref[...] = low
    lay_out_keys(core, kv_ref, kvgot_ref, keys)
    rows, extent = q_ref.shape[1], keys.shape[1]
    block = rows // 4
    factor = HEAD**-0.5
    for e in range(2):
        g = matmul_nt(low, (oa_ref, ob_ref)[e][...]).astype(BF)
        products = g.astype(F32) * ctx_ref[e]
        for h in range(SETS):
            at = slice(h * HEAD, (h + 1) * HEAD)
            k = keys[e, :, at]
            v = keys[e, :, WIDTH + h * HEAD : WIDTH + (h + 1) * HEAD]
            dots = jnp.sum(products[:, at], axis=-1, keepdims=True)
            dp = matmul_nt(g[:, at], v)
            sums = [None] * 7
            for i in range(4):
                here = slice(i * block, (i + 1) * block)
                ds = p_ref[e * SETS + h, here, :].astype(F32) * (dp[here] - dots[here])
                if biased:
                    for j in range(4):
                        part = ds[:, j * 2 * block : (j + 1) * 2 * block]
                        slot = 3 - i + j
                        sums[slot] = part if sums[slot] is None else sums[slot] + part
                ds_ref[here, :] = (ds * factor).astype(BF)
            dq_ref[e, :, at] = matmul(ds_ref[...], k).astype(BF)
            dkeys[:, at] = matmul_tn(ds_ref[...], q_ref[e, :, at])
            dkeys[:, WIDTH + h * HEAD : WIDTH + (h + 1) * HEAD] = matmul_tn(
                p_ref[e * SETS + h], g[:, at]
            )
            if biased:
                dtable_ref = refs[14]
                band = jnp.concatenate(sums + [jnp.zeros_like(sums[0])], axis=1)
                ids = lax.broadcasted_iota(jnp.int32, band.shape, 0)
                bit = 1
                while bit < block:
                    moved = pltpu.roll(band, 2 * extent - bit, 1)
                    band = jnp.where((ids & bit) != 0, moved, band)
                    bit *= 2
                line = jnp.sum(band, axis=0, keepdims=True)
                dtable_ref[e * SETS + h : e * SETS + h + 1, :] = pltpu.roll(line, block - 1, 1)
        for k in range(4):
            at = pl.multiple_of(block * (2 * k + core), block)
            mine_ref[e, k * block : (k + 1) * block, :] = dkeys[pl.ds(at, block), :]
            at = pl.multiple_of(block * (2 * k + 1 - core), block)
            other_ref[1 - e, k * block : (k + 1) * block, :] = dkeys[
                pl.ds(at, block), :
            ].astype(BF)


def attend_local_back(gain, biased, scalars, upstream, values, part, got, gains, *rest, name):
    rows, extent = upstream.shape[0], 2 * upstream.shape[0]
    outs = [
        ((rows, D), F32),
        ((1, D), F32),
        ((rows, D), BF),
        ((2, rows, WIDTH), BF),
        ((2, rows, 2 * WIDTH), F32),
        ((2, rows, 2 * WIDTH), BF),
    ]
    if biased:
        outs.append(((2 * SETS, 2 * extent), F32))
    return call(
        functools.partial(attend_back_kernel, gain, biased),
        name,
        outs,
        [(scalars, SCALARS), (upstream, LATE), (values, LATE), part, got, gains]
        + list(rest[:2])
        + [(a, LATE) for a in rest[2:]],
        9.0 if biased else 6.0,
        [
            pltpu.VMEM((2, extent, 2 * WIDTH), BF),
            pltpu.VMEM((extent, 2 * WIDTH), F32),
            pltpu.VMEM((rows, extent), BF),
        ],
    )


def project_back_kernel(split, q_at, dq_ref, mine_ref, got_ref, *refs):
    kva_ref, qa_ref, kvb_ref, qb_ref = refs[:4]
    dkv_ref = refs[4]
    from_keys = from_queries = None
    for e, (kv, q) in enumerate(((kva_ref, qa_ref), (kvb_ref, qb_ref))):
        dkv = (mine_ref[e] + got_ref[e].astype(F32)).astype(BF)
        dkv_ref[e] = dkv
        term = matmul_nt(dkv, kv[:, : 2 * WIDTH])
        from_keys = term if e == 0 else from_keys + term
        term = matmul_nt(dq_ref[e], q[:, q_at : q_at + WIDTH])
        from_queries = term if e == 0 else from_queries + term
    outs = [from_keys, from_queries] if split else [from_keys + from_queries]
    for k, total in enumerate(outs):
        refs[5 + 2 * k][...] = total
        refs[6 + 2 * k][...] = total.astype(BF)


def project_back(split, dq, mine, got, kv_own, q_own, kv_sib, q_sib, q_at, name):
    rows = dq.shape[1]
    outs = [((2, rows, 2 * WIDTH), BF)] + [((rows, D), F32), ((rows, D), BF)] * (1 + split)
    return call(
        functools.partial(project_back_kernel, split, q_at),
        name,
        outs,
        [dq, mine, got, kv_own, q_own, kv_sib, q_sib],
        2.5,
    )


def attend_weights_kernel(count, *refs):
    ins, (own_ref, sib_ref, out_own_ref, out_sib_ref) = refs[:-4], refs[-4:]
    for k in range(count):
        nq_ref, nkv_ref, dq_ref, dkv_ref, ctx_ref, low_ref = ins[6 * k : 6 * k + 6]
        kv_at, q_at = 2 * WIDTH * k, 2 * WIDTH * count + WIDTH * k
        for e, (in_ref, out_ref) in enumerate(((own_ref, out_own_ref), (sib_ref, out_sib_ref))):
            if k == 0 and in_ref.shape[1] > 3 * count * WIDTH:
                in_ref[...] = jnp.zeros_like(in_ref)
            in_ref[:, kv_at : kv_at + 2 * WIDTH] = matmul_tn(nkv_ref[...], dkv_ref[e]).astype(BF)
            in_ref[:, q_at : q_at + WIDTH] = matmul_tn(nq_ref[...], dq_ref[e]).astype(BF)
            out_ref[k] = matmul_tn(ctx_ref[e].astype(BF), low_ref[...]).astype(BF)


def attend_weights(name, *attentions):
    count, rows = len(attentions), attentions[0][0].shape[0]
    inner, outer = ((D, -(-3 * count * WIDTH // 128) * 128), BF), ((count, WIDTH, D), BF)
    own, sib, out_own, out_sib = call(
        functools.partial(attend_weights_kernel, count),
        name,
        [inner, inner, outer, outer],
        [a for attention in attentions for a in attention],
        1.0 * count,
    )
    return own, out_own, sib, out_sib


IN_ORDER = (8, 6, 7, 4, 0, 1, 5, 2, 3)


def sums_kernel(own, late_ref, dec_ref, self_ref, out_ref):
    inner, third, half = 6 * WIDTH, D // 3, D // 2
    width = dec_ref.shape[1]
    wide, rows = width - 2 * third, dec_ref.shape[0] * 2 // 3
    out_ref[...] = jnp.zeros_like(out_ref)

    def squares(values, rows_in_all):
        values = values.astype(F32)
        return values * values * (0.5 / rows_in_all)

    def line(values):
        return jnp.sum(values, axis=0, keepdims=True)

    def put(at, values):
        for k in range(0, values.shape[1], 128):
            size = min(128, values.shape[1] - k)
            out_ref[at + k // 128 : at + k // 128 + 1, :size] = values[:, k : k + size]

    put(0, line(squares(late_ref[:, inner : inner + wide], D)))
    put(wide // 128, line(squares(dec_ref[:, :wide], D)))
    at = 2 * wide // 128
    put(at, line(squares(late_ref[:, :inner], D)))
    put(at + inner // 128, line(squares(self_ref[:, third : third + 3 * WIDTH], D)))
    at = 30
    for ref, begin in ((late_ref, inner), (dec_ref, 0)):
        down = squares(ref[:, begin + wide : begin + width], FF)
        put(at, line(down[:rows]))
        put(at + 2 * third // 128, line(down[rows:, :third]) + line(down[rows:, third:]))
        at += D // 128
    outer = squares(self_ref[:, :third], D)
    for k in range(3):
        put(at + k * third // 128, line(outer[k * own : (k + 1) * own]))
    at += D // 128
    outer = squares(late_ref[:, width + inner :], D)
    for k in range(2):
        for side in range(2):
            begin = (2 * side + k) * own
            put(at + side * half // 128, line(outer[begin : begin + own]))
        at += D // 128


def hold_kernel(values_ref, earlier_ref, out_ref):
    out_ref[...] = values_ref[...]


def half_mean_rows(values):
    ones = jnp.full((8, values.shape[1]), 0.5 / values.shape[1], F32)
    sums = lax.dot_general(
        ones,
        values * values,
        (((1,), (1,)), ((), ())),
        precision=HIGHEST,
        preferred_element_type=F32,
    )
    return sums[:1]


def shards_kernel(ff_own, columns_ref, early_ref, turned_ref, late_ref, dec_ref, *outs):
    in_ref, out_ref, hin_ref, hout_ref, row_in_ref, row_out_ref, row_hin_ref, row_hout_ref = outs
    third = D // 3
    width = dec_ref.shape[1]
    wide = width - 2 * third
    units = wide // 2
    for k, at in enumerate(IN_ORDER):
        ref, at = (columns_ref, at * WIDTH) if at < 6 else (early_ref, wide + (at - 6) * WIDTH)
        for q in range(WAYS):
            piece = ref[q, :, at : at + WIDTH]
            in_ref[k // 3, k % 3, :, q * WIDTH : (q + 1) * WIDTH] = piece
        row_in_ref[k : k + 1, :] = half_mean_rows(in_ref[k // 3, k % 3])
    out_ref[...] = turned_ref[...]
    for k in range(3):
        row_out_ref[k : k + 1, :] = half_mean_rows(turned_ref[k])
    for layer in range(2):
        ref, begin = (columns_ref, 6 * WIDTH) if layer == 0 else (early_ref, 0)
        for j in range(2):
            for k in range(units // ff_own):
                first = begin + j * units + k * ff_own
                for q in range(WAYS):
                    at = (WAYS * k + q) * ff_own
                    piece = ref[q, :, first : first + ff_own]
                    hin_ref[layer, j, :, at : at + ff_own] = piece
            row_hin_ref[2 * layer + j : 2 * layer + j + 1, :] = half_mean_rows(hin_ref[layer, j])
    for layer, (ref, begin) in enumerate(((late_ref, 6 * WIDTH), (dec_ref, 0))):
        down = ref[:, begin + wide : begin + width].astype(F32)
        hout_ref[layer, :, : 2 * third] = down[:ff_own]
        half = ff_own // 2
        hout_ref[layer, :half, 2 * third :] = down[ff_own:, :third]
        hout_ref[layer, half:, 2 * third :] = down[ff_own:, third:]
        row_hout_ref[layer : layer + 1, :] = half_mean_rows(hout_ref[layer])


def input_kernel(gain, up_ref, x_ref, part_ref, got_ref, gains_ref, out_ref, dgain_ref):
    grad, dgain_ref[...] = norm_back(
        x_ref[...].astype(F32),
        gains_ref[gain : gain + 1, :],
        part_ref[...] + got_ref[...].astype(F32),
    )
    out_ref[...] = up_ref[...] + grad


def input_back(gain, upstream, x, part, got, gains, name):
    return call(
        functools.partial(input_kernel, gain),
        name,
        [(upstream.shape, F32), ((1, D), F32)],
        [upstream, x, part, got, gains],
        1.5,
    )


def gather_own_rows(place, mine, other_seq):
    near = pair_up(mine, swap(other_seq, "y"), place.y)
    far = pair_up(near, swap(near, "x"), place.x)
    far = far.transpose(2, 1, 0, 3, 4)
    return far.reshape(far.shape[0], -1, far.shape[4])


def give_back(place, half):
    blocks = half.reshape(2, 2, -1, half.shape[1])
    blocks = pick(blocks, place.x, 1)
    other = swap(pick(blocks, 1 - place.y), "y")
    return pair_up(pick(blocks, place.y), other, place.y)


def sum_everywhere(place, values):
    depth = place.depth
    for axis in ("c", "x", "y"):
        values = values + swap(values, axis)
    return values + sum(shift_z(values, k, depth) for k in range(1, depth))


def pack_down(rows):
    half, third = rows.shape[-2] // 2, rows.shape[-1] // 3
    last = rows[..., 2 * third :]
    last = jnp.concatenate([last[..., :half, :], last[..., half:, :]], axis=-1)
    return jnp.concatenate([rows[..., : 2 * third], last], axis=-2)


def unpack_down(packed):
    half, third = packed.shape[-2] // 3, packed.shape[-1] // 2
    last = packed[..., 2 * half :, :]
    last = jnp.concatenate([last[..., :third], last[..., third:]], axis=-2)
    return jnp.concatenate([packed[..., : 2 * half, :], last], axis=-1)


def pack_out(pair):
    rows = pair.reshape(pair.shape[:-3] + (-1, pair.shape[-1]))
    half = rows.shape[-1] // 2
    return jnp.concatenate([rows[..., :half], rows[..., half:]], axis=-2)


def unpack_out_piece(packed):
    half = packed.shape[-2] // 2
    rows = jnp.concatenate([packed[..., :half, :], packed[..., half:, :]], axis=-1)
    return rows.reshape(rows.shape[:-2] + (2, half // 2, rows.shape[-1]))


def unpack_out(packed, depth):
    pair = unpack_out_piece(packed)
    pair = pair.reshape((depth, 2) + pair.shape[1:])
    pair = pair.transpose(2, 1, 0, 3, 4)
    return pair.reshape(2, -1, pair.shape[-1])


def turned_parts(grads, depth):
    parts = grads.reshape(2, depth, -1, grads.shape[1]).transpose(1, 0, 2, 3)
    return parts.reshape(2 * depth, -1, grads.shape[1])


def grouped(
    depth,
    enc_input,
    dec_input,
    enc_lengths,
    dec_lengths,
    enc_buckets,
    dec_buckets,
    attention_in,
    attention_out,
    hidden_in,
    hidden_out,
    norm_gains,
    position_bias,
    enc_cotangent,
    dec_cotangent,
):
    place = Place(depth)
    y, q = place.y, place.q
    block = enc_input.shape[1]
    length = block * 8
    own = attention_in.shape[2]
    ff_own = hidden_out.shape[1]
    units = ff_own * 2 * depth
    group = WAYS * own

    pieces = attention_in.reshape(3, 3, own, WAYS, WIDTH).transpose(3, 0, 1, 2, 4)
    queries, keys, values = pieces[:, :, 0], pieces[:, :, 1], pieces[:, :, 2]
    gain_piece = jnp.pad(norm_gains.T, ((0, 0), (0, 64 - norm_gains.shape[0])))
    gain_piece = jnp.broadcast_to(gain_piece[None], (WAYS,) + gain_piece.shape)
    turned = turn(attention_out, depth)
    hidden_pieces = hidden_in.reshape(2, 2, own, 2 * depth, WAYS, ff_own)
    hidden_pieces = hidden_pieces.transpose(4, 0, 2, 1, 3, 5).reshape(WAYS, 2, own, 2 * units)
    blocks_in = [keys[:, 0], values[:, 0], queries[:, 0], gain_piece]
    blocks_in += [keys[:, 1], values[:, 1], keys[:, 2], values[:, 2], queries[:, 1], queries[:, 2]]
    blocks_in += [hidden_pieces[:, 0]]
    everything = exchange_columns(place, jnp.concatenate(blocks_in, axis=2)).reshape(group, -1)
    cuts = [3 * WIDTH + 64, 9 * WIDTH + 64]
    enc_piece, rest, ffn_enc = jnp.split(everything, cuts, axis=1)
    ffn_dec = exchange_columns(place, after(hidden_pieces[:, 1], ffn_enc)).reshape(group, -1)
    third = turned[0].reshape(own, 3, D // 3).transpose(1, 0, 2).reshape(3 * own, D // 3)
    third = jnp.pad(third, ((0, group - 3 * own), (0, 0)))
    enc_piece = jnp.concatenate([enc_piece, third], axis=1)
    rest = jnp.concatenate([rest, pack_out(turned[1:])], axis=1)
    ffn_enc = jnp.concatenate([ffn_enc, pack_down(hidden_out[0])], axis=1)
    ffn_dec = jnp.concatenate([ffn_dec, pack_down(hidden_out[1])], axis=1)

    line = along_z(place, enc_piece)
    w_enc = along_y(place, line)
    w_enc_sib = swap(w_enc, "c")

    def out_rows(whole):
        rows = whole[:, 3 * WIDTH + 64 :].reshape(depth, 2, group, D // 3)[:, :, : 3 * own]
        rows = rows.reshape(depth, 2, 3, own, D // 3).transpose(1, 0, 3, 2, 4)
        return rows.reshape(WIDTH, D)

    def gather(piece):
        return lax.all_gather(piece, ("dp", "y"), axis=0, tiled=True)

    first = gather(jnp.concatenate([rest, ffn_enc], axis=1))
    out_enc, out_enc_sib = out_rows(w_enc), out_rows(w_enc_sib)
    gains = w_enc[:, 3 * WIDTH : 3 * WIDTH + norm_gains.shape[0]].astype(F32).T

    w_self = [w_enc, w_enc, w_enc_sib, w_enc_sib]

    def own_rows(*arrays):
        mine = jnp.stack([pick(a, y) for a in arrays])
        other = jnp.stack([pick(a, 1 - y) for a in arrays])
        return gather_own_rows(place, mine, other)

    enc_rows, dec_rows, *cots = own_rows(enc_input, dec_input, dec_cotangent, enc_cotangent)
    enc_scalars = jnp.stack([place.c, pick(enc_lengths, y)]).astype(jnp.int32)
    dec_scalars = jnp.stack([place.c, pick(dec_lengths, y)]).astype(jnp.int32)

    def head_rows(table):
        mine = lax.dynamic_slice_in_dim(table, q * SETS, SETS, 0)
        theirs = lax.dynamic_slice_in_dim(table, (q + 1 - 2 * place.c) * SETS, SETS, 0)
        table = jnp.concatenate([mine, theirs])
        table = jnp.pad(table, ((0, 0), (0, block)))
        return lax.dynamic_slice_in_dim(table, block * (1 - place.c), 2 * length, 1)

    enc_table = offset_table(enc_buckets, position_bias[0])
    enc_table = head_rows(jnp.pad(enc_table, ((0, 0), (0, 1))))
    dec_table = offset_table(dec_buckets, position_bias[1])
    dec_table = jnp.concatenate(
        [dec_table[:, ::-1], jnp.broadcast_to(dec_table[:, :1], (HEADS, length))], axis=1
    )
    dec_table = head_rows(dec_table)

    n_a, q_enc, kv_enc = self_project(enc_rows, gains, 0, *w_self, 2 * WIDTH, "enc_project")
    kv_enc_got = swap(kv_enc, "c")
    ctx_enc, p_enc, part, low = attend_local(
        enc_scalars, q_enc, kv_enc, kv_enc_got, enc_table, out_enc, out_enc_sib, False, "enc_attend"
    )
    low_enc, part_enc = low, part
    ffn_dec = gather(after(ffn_dec, low_enc))
    got_enc = swap(low_enc, "x")
    first = after(first, got_enc)
    rest, ffn_enc = first[:, : ffn_enc.shape[1]], first[:, ffn_enc.shape[1] :]
    rest_sib, ffn_enc_sib = swap(rest, "c"), swap(ffn_enc, "c")
    out_rest = unpack_out(rest[:, 6 * WIDTH :].reshape(2 * depth, group, -1), depth)
    out_rest_sib = unpack_out(rest_sib[:, 6 * WIDTH :].reshape(2 * depth, group, -1), depth)
    w_dec = [column_block(w, k) for w in (rest, rest_sib) for k in (0, 2)]
    w_cross = [column_block(w, k) for w in (rest, rest_sib) for k in (1, 2)]
    out_dec, out_cross = [[(w, pl.BlockSpec((None, WIDTH, D), f)) for w in (out_rest, out_rest_sib)]
        for f in (lambda _: (0, 0, 0), lambda _: (1, 0, 0))]

    n_b, q_dec, kv_dec = self_project(dec_rows, gains, 3, *w_dec, 0, "dec_project")
    kv_dec_got = swap(kv_dec, "c")
    ctx_dec, p_dec, part_dec, low_dec = attend_local(
        dec_scalars, q_dec, kv_dec, kv_dec_got, dec_table, *out_dec, True, "dec_attend"
    )

    enc_mid, n_1, gu_enc, hid_enc, part, low = ffn_local(
        enc_rows, part_enc, after(got_enc, low_dec), gains, 1, ffn_enc, ffn_enc_sib, units, "enc_ffn"
    )
    rows = enc_rows.shape[0]
    dec_mid, n_c, q_cross = call(
        functools.partial(cross_kernel, WIDTH),
        "cross_project",
        [((rows, D), F32), ((rows, D), BF), ((2, rows, WIDTH), BF)],
        [dec_rows, part_dec, swap(low_dec, "x"), gains, w_cross[1], w_cross[3]],
        2.0,
    )
    enc_last, memory_low, kv_cross = call(
        memory_kernel,
        "memory",
        [((rows, D), F32), ((rows, D), BF), ((2, rows, 2 * WIDTH), BF)],
        [enc_mid, part, after(swap(low, "x"), q_cross), gains, w_cross[0], w_cross[2]],
        2.0,
    )
    kv_cross_got = swap(kv_cross, "c")

    ctx_cross, p_cross, part, low = attend_local(
        enc_scalars, q_cross, kv_cross, kv_cross_got, None, *out_cross, False, "cross_attend"
    )
    ffn_dec = after(ffn_dec, low)
    ffn_dec_sib = swap(ffn_dec, "c")
    dec_cross, n_5, gu_dec, hid_dec, part, low = ffn_local(
        dec_mid, part, swap(low, "x"), gains, 5, ffn_dec, ffn_dec_sib, units, "dec_ffn"
    )

    def both(own_grads, sib_grads):
        return (own_grads.astype(F32) + swap(sib_grads, "c").astype(F32)).astype(BF)

    def blocks(grads):
        return grads.reshape(2 * depth, -1, grads.shape[1])

    def scatter(grads):
        return lax.psum_scatter(grads, ("dp", "y"), scatter_dimension=0, tiled=False)

    dec_final, g, gg6, low_d, dgu_dec, part, low = ffn_back(
        True, dec_cross, part, swap(low, "x"), cots[0], gains, gu_dec, ffn_dec, ffn_dec_sib, "dec_ffn_back"
    )
    d_ffn_dec = ffn_weights(n_5, dgu_dec, hid_dec, low_d, "dec_ffn_weights")
    d_ffn_dec = both(*d_ffn_dec)
    got_f = after(swap(low, "x"), d_ffn_dec)
    got = got_f
    g, gg5, low_x, dq_cross, mine, other = attend_local_back(
        5,
        False,
        enc_scalars,
        g,
        dec_cross,
        part,
        got,
        gains,
        *out_cross,
        q_cross,
        kv_cross,
        kv_cross_got,
        p_cross,
        ctx_cross,
        name="cross_attend_back",
    )
    got = swap(other, "c")
    d_ffn_dec = scatter(after(blocks(d_ffn_dec), got_f))
    dkv_cross, part_m, low_m, part_c, low_c = project_back(
        True, dq_cross, mine, got, *w_cross, WIDTH, "cross_project_back"
    )
    got_c = swap(low_c, "x")
    got_m = after(swap(low_m, "x"), got_c)
    g_last, gg2, low_e, dgu_enc, part, part_low = ffn_back(
        False, enc_last, part_m, got_m, cots[1], gains, gu_enc, ffn_enc, ffn_enc_sib, "enc_ffn_back"
    )
    d_ffn_enc = ffn_weights(n_1, dgu_enc, hid_enc, low_e, "enc_ffn_weights")
    got_e = swap(part_low, "x")
    got_c = after(got_c, *d_ffn_enc)
    d_ffn_enc = both(*d_ffn_enc)
    g_dec, gg4, low_b, dq_dec, mine, other, d_table_dec = attend_local_back(
        4,
        True,
        dec_scalars,
        g,
        dec_mid,
        part_c,
        got_c,
        gains,
        *out_dec,
        q_dec,
        kv_dec,
        kv_dec_got,
        p_dec,
        ctx_dec,
        name="dec_attend_back",
    )
    got_e = after(got_e, dq_dec)
    dec_other = swap(other, "c")
    dec_mine = mine
    g_enc, gg1, low_a, dq_enc, mine, other, d_table_enc = attend_local_back(
        1,
        True,
        enc_scalars,
        g_last,
        enc_mid,
        part,
        got_e,
        gains,
        out_enc,
        out_enc_sib,
        q_enc,
        kv_enc,
        kv_enc_got,
        p_enc,
        ctx_enc,
        name="enc_attend_back",
    )
    dkv_dec, part_d, low = project_back(
        False, dq_dec, dec_mine, dec_other, *w_dec, 0, "dec_project_back"
    )
    got_d = swap(low, "x")
    d_in, d_out, d_in_sib, d_out_sib = attend_weights(
        "attend_weights",
        (n_b, n_b, dq_dec, dkv_dec, ctx_dec, low_b),
        (n_c, memory_low, dq_cross, dkv_cross, ctx_cross, low_x),
    )
    d_out = both(d_out, d_out_sib)
    d_out = jnp.stack([turned_parts(d_out[k], depth) for k in range(2)], 1)
    d_in = d_in.astype(F32) + after(swap(d_in_sib, "c"), d_ffn_dec).astype(F32)
    late = [blocks(rounded(d_in)), blocks(d_ffn_enc), pack_out(d_out)]
    late = scatter(jnp.concatenate(late, axis=2))
    got = after(swap(other, "c"), dkv_dec)
    dkv_enc, part, low = project_back(
        False, dq_enc, mine, got, *w_self, 2 * WIDTH, "enc_project_back"
    )
    d_in, d_out, d_in_sib, d_out_sib = attend_weights(
        "enc_attend_weights", (n_a, n_a, dq_enc, dkv_enc, ctx_enc, low_a)
    )
    got = after(swap(low, "x"), d_in, d_out)
    thirds = turned_parts(both(d_out, d_out_sib)[0], depth).reshape(2 * depth, own, 3, D // 3)
    thirds = thirds.transpose(0, 2, 1, 3).reshape(2 * depth, 3 * own, D // 3)
    thirds = jnp.pad(thirds, ((0, 0), (0, group - 3 * own), (0, 0)))
    d_enc = jnp.concatenate([thirds, blocks(both(d_in, d_in_sib))], axis=2)
    d_enc = scatter_y(place, d_enc)
    got_d = after(got_d, d_in)
    grad_dec, gg3 = input_back(3, g_dec, dec_rows, part_d, got_d, gains, "dec_input_back")
    grad_enc, gg0 = input_back(0, g_enc, enc_rows, part, got, gains, "enc_input_back")
    memory_low, dec_final, grad_enc, grad_dec, gg0, gg3 = after(
        (memory_low, dec_final, grad_enc, grad_dec, gg0, gg3), d_enc
    )
    d_enc = scatter_z(place, d_enc)

    wide, inner = 2 * units, 6 * WIDTH
    early = [d_ffn_dec[:, :wide], rounded(d_enc[:, D // 3 : D // 3 + 3 * WIDTH])]
    early = jnp.concatenate(early, axis=1).reshape(WAYS, own, -1)
    early = exchange_columns(place, early).astype(F32)
    late = after(late, early)
    down = wide + 2 * D // 3
    (sums,) = call(
        functools.partial(sums_kernel, own),
        "column_sums",
        [((64, 128), F32)],
        [late, d_ffn_dec, d_enc],
        1.0,
    )
    out_enc_mine = d_enc[: 3 * own, : D // 3].reshape(3, own, D // 3).transpose(1, 0, 2)
    out_mine = unpack_out_piece(late[:, down + inner :])
    turned_out = jnp.concatenate([rounded(out_enc_mine.reshape(1, own, D)), out_mine])
    turned_out = turn(turned_out, depth).astype(F32)
    columns = late[:, : inner + wide].reshape(WAYS, own, -1)
    columns = exchange_over_x(place, columns)
    columns_here = columns
    columns = exchange_over_cores(place, columns).astype(F32)
    shard_in, shard_out, shard_hin, shard_hout, row_in, row_out, row_hin, row_hout = call(
        functools.partial(shards_kernel, ff_own),
        "shards",
        [
            ((3, 3, own, D), F32),
            ((3, own, D), F32),
            ((2, 2, own, WAYS * units), F32),
            ((2, ff_own, D), F32),
            ((9, own), F32),
            ((3, own), F32),
            ((4, own), F32),
            ((2, ff_own), F32),
        ],
        [columns, early, turned_out, late, d_ffn_dec],
        2.0,
    )
    sums = sums + sum(shift_z(sums, k, depth) for k in range(1, depth))
    sums = sums + swap(sums, "y")
    (sums,) = call(hold_kernel, "hold", [(sums.shape, F32)], [sums, (columns_here, ANYWHERE)], 0.3)
    sums = pair_up(sums, swap(sums, "x"), place.x)
    sums = pair_up(sums, swap(sums, "c"), place.c)
    sums = sums.swapaxes(0, 1).reshape(WAYS, -1)
    cuts = [2 * wide, 2 * wide + 9 * WIDTH, 30 * 128, 30 * 128 + 2 * D, 30 * 128 + 5 * D]
    col_hin, col_in, _, col_hout, col_out, _ = jnp.split(sums, cuts, axis=1)
    col_hin = col_hin.reshape(WAYS, 2, 2, 2 * depth, ff_own).transpose(1, 2, 3, 0, 4)
    col_hin = col_hin.reshape(2, 2, WAYS * units)
    col_in = col_in.reshape(WAYS, 9, WIDTH)
    col_in = jnp.stack([col_in[:, k] for k in IN_ORDER]).reshape(3, 3, D)
    col_hout = jnp.sum(col_hout, axis=0).reshape(2, D)
    col_out = jnp.sum(col_out, axis=0).reshape(3, D)

    buckets = position_bias.shape[1]

    def head_table(d_table):
        wide_table = jnp.zeros((2 * SETS, 2 * length + block), F32)
        return lax.dynamic_update_slice_in_dim(wide_table, d_table, block * (1 - place.c), 1)

    grad_enc_bias = head_table(d_table_enc)[:, : 2 * length - 1]
    grad_dec_bias = head_table(d_table_dec)[:, :length][:, ::-1]
    by_set = jnp.stack(
        [
            bucket_grad(enc_buckets, grad_enc_bias, buckets),
            bucket_grad(dec_buckets, grad_dec_bias, buckets),
        ]
    )
    grad_position = lax.dynamic_update_slice_in_dim(
        jnp.zeros_like(position_bias), by_set[:, :, :SETS], q * SETS, 2
    )
    grad_position = lax.dynamic_update_slice_in_dim(
        grad_position, by_set[:, :, SETS:], (q + 1 - 2 * place.c) * SETS, 2
    )
    grad_gains = jnp.concatenate([gg0, gg1, gg2, gg3, gg4, gg5, gg6])
    grad_gains = jnp.where(place.x == 0, grad_gains, 0.0)
    small = jnp.concatenate([grad_gains.reshape(-1, 128), grad_position.reshape(-1, 128)])
    small = sum_everywhere(place, small)
    cut = grad_gains.size // 128
    grad_gains = small[:cut].reshape(grad_gains.shape)
    grad_position = small[cut:].reshape(grad_position.shape)
    shard_gains = lax.dynamic_slice_in_dim(grad_gains, place.index * own, own, 1)

    return (
        give_back(place, memory_low),
        give_back(place, dec_final),
        give_back(place, grad_enc),
        give_back(place, grad_dec),
        shard_in,
        shard_out,
        shard_hin,
        shard_hout,
        shard_gains,
        grad_position,
        row_in.reshape(3, 3, own),
        col_in,
        row_out,
        col_out,
        row_hin.reshape(2, 2, own),
        col_hin,
        row_hout,
        col_hout,
    )


def specs(seq):
    rows = P("dp", seq, None)
    every = ("dp",) + (seq if isinstance(seq, tuple) else (seq,))
    second, third = P(None, every, None), P(None, None, every, None)
    ins = (rows, rows, P("dp"), P("dp"), P(), P(), third, second, third, second)
    ins += (P(None, every), P(), rows, rows)
    outs = (rows, rows, rows, rows, third, second, third, second, P(None, every), P())
    outs += (P(None, None, every), P(), P(None, every), P())
    outs += (P(None, None, every), P(), P(None, every), P())
    return ins, outs


def solution(mesh):
    depth, seq = mesh.shape["dp"], mesh.shape["seq"]

    def wrap(function, over, axes):
        ins, outs = specs(axes)
        return jax.shard_map(function, mesh=over, in_specs=ins, out_specs=outs, check_vma=False)

    def run(*args):
        seqs, length = args[0].shape[0] // depth, args[0].shape[1]
        fits = depth == WAYS and seq == 8 and seqs == 2 and length % 512 == 0
        if fits and args[1].shape == args[0].shape:
            axes = ("y", "x", "c")
            split = Mesh(mesh.devices.reshape(depth, 2, 2, 2), ("dp",) + axes)
            return wrap(functools.partial(grouped, depth), split, axes)(*args)
        return wrap(local, mesh, "seq")(*args)

    return run
```
